32 devices in a mesh: dp: 8 (over z, y), row: 2 (over x), col: 2 (over core).
Axes of the slice: x: 2, y: 2, z: 4, core: 2. Of those that a mesh axis runs over, the one named last changes fastest.
Arguments:
- images: bfloat16 [128, 14, 14, 256], P('dp', 'row', 'col'), may hold values from -6 to 6
- cotangent: bfloat16 [128, 14, 14, 256], P('dp', 'row', 'col'), may hold values from -6 to 6
- mix_partner: int32 [128], replicated, may hold values from 0 to 127, as said below
- cut_partner: int32 [128], replicated, may hold values from 0 to 127, as said below
- ratios: float32 [128], P('dp'), may hold values from 0.3 to 0.9
- corners: int32 [128, 4], P('dp'), may hold values from 0 to 13, as said below
- drop_masks: int32 [128, 4], P('dp'), may hold values 0 or 1
- norm_gains: float32 [2, 2, 256], replicated, may hold values from 0.25 to 1.75
- norm_shifts: float32 [2, 2, 256], replicated, may hold values from -2 to 2
- entry_weight: bfloat16 [2, 256, 768], replicated, may hold values from -0.5 to 0.5
- entry_bias: float32 [2, 512], replicated, may hold values from -3 to 3
- position_kernel: float32 [2, 3, 3, 256], replicated, may hold values from -2 to 2
- position_bias: float32 [2, 256], replicated, may hold values from -2 to 2
- exit_weight: bfloat16 [2, 256, 256], replicated, may hold values from -0.5 to 0.5
- exit_bias: float32 [2, 256], replicated, may hold values from -2 to 2
- expand_weight: bfloat16 [2, 256, 1024], replicated, may hold values from -0.375 to 0.375
- expand_bias: float32 [2, 1024], replicated, may hold values from -2 to 2
- shrink_weight: bfloat16 [2, 1024, 256], replicated, may hold values from -0.25 to 0.25
- shrink_bias: float32 [2, 256], replicated, may hold values from -2 to 2
Outputs:
- activations: bfloat16 [128, 14, 14, 256], P('dp', 'row', 'col')
- input_gradient: float32 [128, 14, 14, 256], P('dp', 'row', 'col')
- norm_gains_gradient: float32 [2, 2, 256], replicated
- norm_shifts_gradient: float32 [2, 2, 256], replicated
- entry_weight_gradient: float32 [2, 256, 768], replicated
- entry_bias_gradient: float32 [2, 512], replicated
- position_kernel_gradient: float32 [2, 3, 3, 256], replicated
- position_bias_gradient: float32 [2, 256], replicated
- exit_weight_gradient: float32 [2, 256, 256], replicated
- exit_bias_gradient: float32 [2, 256], replicated
- expand_weight_gradient: float32 [2, 256, 1024], replicated
- expand_bias_gradient: float32 [2, 1024], replicated
- shrink_weight_gradient: float32 [2, 1024, 256], replicated
- shrink_bias_gradient: float32 [2, 256], replicated
The draws below stay inside these ranges and needn't reach their ends.
Inputs may be any that keep to these rules, and one draw needn't show every extreme that they name: `mix_partner`: of the 32 mixup and cutmix partners of the images of one index of dp, at most 4 lie on any one index of dp, and in every draw some pair of indices reaches 4. `cut_partner`: counted with mix_partner in its bound. `corners`: each box spans 4 to 6 rows and 4 to 6 columns, bottom and right exclusive.
All inputs are finite; a program needn't handle non-finite values. No bound on the sum of `drop_masks` on one device may be relied on, other than what follows from the above.
Results may differ from the reference program's by a relative error of at most 0.017.
Values may be sent and summed in bfloat16 or wider, within the bound.
No kernel may reach another device: no remote copies, remote signals or barrier semaphores. Data moves between devices by JAX's collectives and lax.ppermute only.
A program may use at most 128 MiB of HBM per device.

```python
import jax
import jax.numpy as jnp
from jax import lax

D = 256
FF = 1024
TILE = 7
B_DEV = 16
HEAD_DIM = 32
GRID = 14
IMAGES = 128


def partner_table(key):
    groups = IMAGES // B_DEV
    subkeys = jax.random.split(key, groups)
    orders = jax.vmap(lambda subkey: jax.random.permutation(subkey, groups))(subkeys)
    picked = jnp.arange(2 * B_DEV) % groups
    sources = orders[:, picked]
    within = jax.random.randint(jax.random.fold_in(key, 7), (groups, 2 * B_DEV), 0, B_DEV)
    return (sources * B_DEV + within).astype(jnp.int32)


def draw_mix_partner(key, part):
    partner_rows = partner_table(key)
    return partner_rows[:, :B_DEV].reshape(IMAGES)


def draw_cut_partner(key, part):
    partner_rows = partner_table(key)
    return partner_rows[:, B_DEV:].reshape(IMAGES)


def draw_corners(key, part):
    key = jax.random.fold_in(key, 3)
    key_top, key_height, key_left, key_width = jax.random.split(key, 4)
    top_row = jax.random.randint(key_top, (IMAGES,), 0, GRID - 6)
    height = jax.random.randint(key_height, (IMAGES,), 4, 7)
    left_col = jax.random.randint(key_left, (IMAGES,), 0, GRID - 6)
    width_cols = jax.random.randint(key_width, (IMAGES,), 4, 7)
    return jnp.stack([top_row, top_row + height, left_col, left_col + width_cols], axis=1).astype(jnp.int32)


def plant(array, stream_key, smallest, top_value):
    index_at = [jax.random.randint(jax.random.fold_in(stream_key, axis), (), 0, length) for axis, length in enumerate(array.shape)]
    widest = array.shape.index(max(array.shape))
    next_to = index_at[:widest] + [(index_at[widest] + 1) % array.shape[widest]] + index_at[widest + 1:]
    return array.at[tuple(index_at)].set(smallest).at[tuple(next_to)].set(top_value)


def level_of(own_key, extent, pieces, low, high):
    def one(position, shards_of):
        heights = jax.random.uniform(jax.random.fold_in(jax.random.fold_in(own_key, 6), position), (shards_of,), jnp.float32, low / len(pieces), high / len(pieces))
        return jnp.repeat(jnp.exp(heights), extent[position] // shards_of).reshape((-1,) + (1,) * (len(extent) - position - 1))

    loudness = one(*pieces[0])
    for cut in pieces[1:]:
        loudness = loudness * one(*cut)
    return loudness


def gaussian(stream_key, shape, scale, bound, cuts=(), held_as=jnp.bfloat16):
    loudness = level_of(stream_key, shape, cuts, -0.22, 0.18) if cuts else 1.0
    values = jax.random.normal(stream_key, shape, jnp.float32) * scale * loudness
    return jnp.minimum(jnp.maximum(values, -bound), bound).astype(held_as)


def setup_inputs(seed: int = 0) -> dict:
    splits = jax.random.split(jax.random.key(seed), 20)
    return {
        "images": gaussian(splits[0], (IMAGES, GRID, GRID, D), 1.0, 6.0, ((0, 8), (1, 2), (2, 2))),
        "cotangent": gaussian(splits[1], (IMAGES, GRID, GRID, D), 1.0, 6.0, ((0, 8), (1, 2), (2, 2))),
        "mix_partner": draw_mix_partner(jax.random.fold_in(splits[19], 71), 0),
        "cut_partner": draw_cut_partner(jax.random.fold_in(splits[19], 71), 0),
        "ratios": jnp.clip(0.3 + 0.59999996 * jax.random.uniform(splits[4], (IMAGES,), jnp.float32) ** level_of(splits[4], (IMAGES,), ((0, 8),), -0.2, 0.2), 0.3, 0.9),
        "corners": draw_corners(jax.random.fold_in(splits[19], 71), 0),
        "drop_masks": plant((jax.random.randint(splits[6], (IMAGES, 4), 0, 5) < 4).astype(jnp.int32), jax.random.fold_in(splits[6], 1), 0, 1),
        "norm_gains": jnp.clip(1.0 + 0.15 * jax.random.normal(splits[7], (2, 2, D), jnp.float32), 0.25, 1.75),
        "norm_shifts": gaussian(splits[8], (2, 2, D), 0.3, 2.0, (), jnp.float32),
        "entry_weight": gaussian(splits[9], (2, D, 3 * D), (D // 2) ** -0.5, 0.5),
        "entry_bias": gaussian(splits[10], (2, 2 * D), 0.5, 3.0, (), jnp.float32),
        "position_kernel": gaussian(splits[11], (2, 3, 3, D), 9 ** -0.5, 2.0, (), jnp.float32),
        "position_bias": gaussian(splits[12], (2, D), 0.3, 2.0, (), jnp.float32),
        "exit_weight": gaussian(splits[13], (2, D, D), (D // 2) ** -0.5, 0.5),
        "exit_bias": gaussian(splits[14], (2, D), 0.3, 2.0, (), jnp.float32),
        "expand_weight": gaussian(splits[15], (2, D, FF), D ** -0.5, 0.375),
        "expand_bias": gaussian(splits[16], (2, FF), 0.3, 2.0, (), jnp.float32),
        "shrink_weight": gaussian(splits[17], (2, FF, D), (FF // 2) ** -0.5, 0.25),
        "shrink_bias": gaussian(splits[18], (2, D), 0.3, 2.0, (), jnp.float32),
    }


@jax.custom_vjp
def low(v):
    return lax.optimization_barrier(v.astype(jnp.bfloat16)).astype(jnp.float32)

@jax.custom_vjp
def low_back(v):
    return v

def low_keep(v):
    return (low(v), None)

def low_pass(kept, grad):
    return (grad,)

def back_keep(v):
    return (v, None)

def back_low(kept, grad):
    return (low(grad),)
low.defvjp(low_keep, low_pass)
low_back.defvjp(back_keep, back_low)
precise = lax.Precision.HIGHEST

def norm_rows(values, scale_by, shift_by):
    centre = lax.optimization_barrier(jnp.mean(values, axis=-1, keepdims=True))
    centered = values - centre
    variance = lax.optimization_barrier(jnp.mean(centered * centered, axis=-1, keepdims=True))
    return centered * lax.rsqrt(variance + 1e-05) * scale_by + shift_by

def split_windows(tensor, across):
    images_here = tensor.shape[0]
    channels = tensor.shape[-1]
    if across:
        return tensor.reshape(images_here * 2, TILE, GRID, channels)
    return tensor.reshape(images_here, GRID, 2, TILE, channels).transpose(0, 2, 1, 3, 4).reshape(images_here * 2, GRID, TILE, channels)

def join_windows(tensor, across, images_here):
    channels = tensor.shape[-1]
    if across:
        return tensor.reshape(images_here, GRID, GRID, channels)
    return tensor.reshape(images_here, 2, GRID, TILE, channels).transpose(0, 2, 1, 3, 4).reshape(images_here, GRID, GRID, channels)

def window_attend(queries, key_part, value_part, kernel, bias_row):
    window_total, height, breadth, channels = queries.shape
    head_count = channels // HEAD_DIM
    head_shape = (window_total, height * breadth, head_count, HEAD_DIM)
    scores = low_back(jnp.einsum('wqhd,wkhd->whqk', queries.reshape(head_shape), key_part.reshape(head_shape), precision=precise) * HEAD_DIM ** (-0.5))
    chances = low(jax.nn.softmax(scores, axis=-1))
    output = jnp.einsum('whqk,wkhd->wqhd', chances, value_part.reshape(head_shape), precision=precise).reshape(queries.shape)
    padded = jnp.pad(value_part, ((0, 0), (1, 1), (1, 1), (0, 0)))
    result = bias_row
    for row_step in range(3):
        for col_step in range(3):
            result = result + kernel[row_step, col_step] * padded[:, row_step:row_step + height, col_step:col_step + breadth]
    return output + result

def run_block(hidden, block_index, scales, params):
    norm_gains, norm_shifts, entry_weight, entry_bias, position_kernel, position_bias, exit_weight, exit_bias, expand_weight, expand_bias, shrink_weight, shrink_bias = params
    images_here = hidden.shape[0]
    channel_half = D // 2
    normed = low(norm_rows(hidden, norm_gains[block_index, 0], norm_shifts[block_index, 0]))
    full_bias = jnp.concatenate([entry_bias[block_index, :D], jnp.zeros((D,), jnp.float32), entry_bias[block_index, D:]])
    triple = low_back(low(jnp.einsum('nijd,de->nije', normed, entry_weight[block_index], precision=precise) + full_bias))
    queries = triple[..., :D]
    key_part = triple[..., D:2 * D]
    value_part = triple[..., 2 * D:]
    branches = []
    for across, start_channel, end_channel in ((True, 0, channel_half), (False, channel_half, D)):
        attended = window_attend(split_windows(queries[..., start_channel:end_channel], across), split_windows(key_part[..., start_channel:end_channel], across), split_windows(value_part[..., start_channel:end_channel], across), position_kernel[block_index, :, :, start_channel:end_channel], position_bias[block_index, start_channel:end_channel])
        branches.append(join_windows(attended, across, images_here))
    stripe_out = low_back(low(jnp.concatenate(branches, axis=-1)))
    branch = low_back(jnp.einsum('nijd,de->nije', stripe_out, exit_weight[block_index], precision=precise) + exit_bias[block_index])
    midway = hidden + scales[:, 2 * block_index, None, None, None] * branch
    inner_normed = low(norm_rows(midway, norm_gains[block_index, 1], norm_shifts[block_index, 1]))
    pre_act = low_back(jnp.einsum('nijd,df->nijf', inner_normed, expand_weight[block_index], precision=precise) + expand_bias[block_index])
    activated = low(jax.nn.gelu(pre_act, approximate=False))
    feed_out = low_back(jnp.einsum('nijf,fd->nijd', activated, shrink_weight[block_index], precision=precise) + shrink_bias[block_index])
    return midway + scales[:, 2 * block_index + 1, None, None, None] * feed_out

def reference(images, cotangent, mix_partner, cut_partner, ratios, corners, drop_masks, norm_gains, norm_shifts, entry_weight, entry_bias, position_kernel, position_bias, exit_weight, exit_bias, expand_weight, expand_bias, shrink_weight, shrink_bias):
    grid_rows = jnp.arange(GRID).astype(jnp.int32)
    in_rows = (grid_rows[None, :] >= corners[:, 0:1]) & (grid_rows[None, :] < corners[:, 1:2])
    in_cols = (grid_rows[None, :] >= corners[:, 2:3]) & (grid_rows[None, :] < corners[:, 3:4])
    in_box = (in_rows[:, :, None] & in_cols[:, None, :]).astype(jnp.float32)[..., None]
    ratio_here = ratios.astype(jnp.float32)[:, None, None, None]
    scales = drop_masks.astype(jnp.float32) * 1.25
    groups = IMAGES // B_DEV

    def forward(image_values, *params):
        mixed_input = in_box * image_values[cut_partner] + (1.0 - in_box) * (ratio_here * image_values + (1.0 - ratio_here) * image_values[mix_partner])

        def run_group(group_pair):
            hidden, group_scales = group_pair
            hidden = run_block(hidden, 0, group_scales, params)
            return run_block(hidden, 1, group_scales, params)
        output = lax.map(jax.checkpoint(run_group), (mixed_input.reshape(groups, B_DEV, GRID, GRID, D), scales.reshape(groups, B_DEV, 4)))
        return output.reshape(IMAGES, GRID, GRID, D)
    hidden, pullback = jax.vjp(forward, images.astype(jnp.float32), norm_gains, norm_shifts, entry_weight.astype(jnp.float32), entry_bias, position_kernel, position_bias, exit_weight.astype(jnp.float32), exit_bias, expand_weight.astype(jnp.float32), expand_bias, shrink_weight.astype(jnp.float32), shrink_bias)
    gradients = pullback(cotangent.astype(jnp.float32))
    return (hidden.astype(jnp.bfloat16), gradients[0], gradients[1], gradients[2], gradients[3], gradients[4], gradients[5], gradients[6], gradients[7], gradients[8], gradients[9], gradients[10], gradients[11], gradients[12])
```

```python
import functools

import jax
import jax.numpy as jnp
from jax import lax
from jax.experimental import pallas as pl
from jax.experimental.pallas import tpu as pltpu
from jax.sharding import PartitionSpec as P

TILE = 7
PAD = 56
HEAD_DIM = 32
SIDE_HEADS = 4
HALF = 128
WIN = 2 * PAD
LANES = SIDE_HEADS * 128
SCALE = HEAD_DIM ** (-0.5)
EPS = 1e-05
BF = jnp.bfloat16
F32 = jnp.float32
VMEM_BYTES = 60 * 1024 * 1024


def dot_nn(a, b):
    return lax.dot_general(a, b, (((1,), (0,)), ((), ())), preferred_element_type=F32)


def dot_nt(a, b):
    return lax.dot_general(a, b, (((1,), (1,)), ((), ())), preferred_element_type=F32)


def dot_tn(a, b):
    return lax.dot_general(a, b, (((0,), (0,)), ((), ())), preferred_element_type=F32)


def norm_parts(values):
    centered = values - jnp.mean(values, axis=-1, keepdims=True)
    inverse = lax.rsqrt(jnp.mean(centered * centered, axis=-1, keepdims=True) + EPS)
    return centered * inverse, inverse


def norm_back(delta, hat, inverse, gain):
    scaled = delta * gain
    first = jnp.mean(scaled, axis=-1, keepdims=True)
    second = jnp.mean(scaled * hat, axis=-1, keepdims=True)
    return inverse * (scaled - first - hat * second)


def gelu_parts(values):
    size = jnp.abs(values) * (0.5**0.5)
    fall = jnp.exp(-(size * size))
    step = 1.0 / (1.0 + 0.3275911 * size)
    series = step * (
        0.254829592
        + step * (-0.284496736 + step * (1.421413741 + step * (-1.453152027 + step * 1.061405429)))
    )
    tail = 0.5 * series * fall
    chance = jnp.where(values >= 0.0, 1.0 - tail, tail)
    return chance, fall * 0.3989422804014327


def row_sums(values):
    count, width = values.shape
    return jnp.sum(values.reshape(count // 8, 8, width), axis=0)


def scale_rows(scale_ref, column, rows_of):
    return jnp.concatenate(
        [jnp.full((PAD, 1), scale_ref[i, column], F32) for i in range(rows_of)], axis=0
    )


def add_row(acc_ref, row, values):
    acc_ref[row] += values


def spread_heads(values):
    lane = lax.broadcasted_iota(jnp.int32, values.shape, 1) // HEAD_DIM
    empty = jnp.zeros((128 - WIN, HALF), F32)
    blocks = []
    for head in range(SIDE_HEADS):
        blocks.append(jnp.where(lane == head, values, 0.0))
        blocks.append(empty)
    return jnp.concatenate(blocks, axis=0).astype(BF)


def gather_heads(wide):
    picked = jnp.concatenate(
        [
            wide[head * HEAD_DIM : (head + 1) * HEAD_DIM, head * 128 : (head + 1) * 128]
            for head in range(SIDE_HEADS)
        ],
        axis=0,
    )
    return picked.T[:WIN]


def valid_rows(shape):
    return lax.broadcasted_iota(jnp.int32, shape, 0) % 8 != 7


def column_shifts(values, across):
    cube = values.reshape(2 * TILE, 8, HALF)
    if not across:
        return (pltpu.roll(cube, 1, 1), cube, pltpu.roll(cube, 7, 1))
    left, right = cube[:TILE], cube[TILE:]
    column = lax.broadcasted_iota(jnp.int32, left.shape, 1)
    before = jnp.concatenate(
        [
            pltpu.roll(left, 1, 1),
            jnp.where(column == 0, pltpu.roll(left, 2, 1), pltpu.roll(right, 1, 1)),
        ],
        axis=0,
    )
    after = jnp.concatenate(
        [
            jnp.where(column == 6, pltpu.roll(right, 6, 1), pltpu.roll(left, 7, 1)),
            pltpu.roll(right, 7, 1),
        ],
        axis=0,
    )
    return (before, cube, after)


def row_shift(cube, step, across):
    if step == 0:
        return cube
    empty = jnp.zeros((1, 8, HALF), F32)

    def move(part):
        if step < 0:
            return jnp.concatenate([empty, part[:-1]], axis=0)
        return jnp.concatenate([part[1:], empty], axis=0)

    if across:
        return jnp.concatenate([move(cube[:TILE]), move(cube[TILE:])], axis=0)
    return move(cube)


def window_conv(shifts, kernel_at, across):
    total = None
    for i in range(3):
        part = None
        for j in range(3):
            term = kernel_at(i, j) * shifts[j]
            part = term if part is None else part + term
        part = row_shift(part, i - 1, across)
        total = part if total is None else total + part
    return total.reshape(WIN, HALF)


def window_rows(across, window):
    side, image = window // 4, window % 4
    if across:
        first, second = 2 * side, 2 * side + 1
    else:
        first, second = side, 2 + side
    return (
        pl.multiple_of((first * 4 + image) * PAD, 8),
        pl.multiple_of((second * 4 + image) * PAD, 8),
    )


def take_window(ref, at, lane):
    return jnp.concatenate(
        [ref[pl.ds(at[0], PAD), lane : lane + HALF], ref[pl.ds(at[1], PAD), lane : lane + HALF]],
        axis=0,
    )


def put_window(ref, at, lane, values):
    ref[pl.ds(at[0], PAD), lane : lane + HALF] = values[:PAD]
    ref[pl.ds(at[1], PAD), lane : lane + HALF] = values[PAD:]


def round_bf(values):
    return values.astype(BF).astype(F32)


def attention_forward(
    block, hidden_ref, gains, shifts, entry_w, entry_b, conv_k, conv_b, wide, stripe, win_out, chance_out
):
    width = hidden_ref.shape[1]

    @pl.loop(0, 4)
    def _(t):
        rows = pl.ds(pl.multiple_of(t * 4 * PAD, 4 * PAD), 4 * PAD)
        hat, _ = norm_parts(hidden_ref[rows, :])
        normed = (hat * gains[block, 0:1, :] + shifts[block, 0:1, :]).astype(BF)
        for part in range(3):
            out = dot_nn(normed, entry_w[block, :, part * width : (part + 1) * width])
            if part != 1:
                at = 0 if part == 0 else width
                out = out + entry_b[block : block + 1, at : at + width]
            wide[rows, part * width : (part + 1) * width] = round_bf(out)

    for direction in range(2):
        across = direction == 0
        lane = direction * HALF

        @pl.loop(0, 8)
        def _(window, across=across, lane=lane, direction=direction):
            at = window_rows(across, window)
            queries = take_window(wide, at, lane)
            keys = take_window(wide, at, width + lane)
            values = take_window(wide, at, 2 * width + lane)
            keys_bf = keys.astype(BF)
            win_out[direction * 8 + window, :, 0:HALF] = queries.astype(BF)
            win_out[direction * 8 + window, :, HALF : 2 * HALF] = keys_bf
            win_out[direction * 8 + window, :, 2 * HALF : 3 * HALF] = values.astype(BF)
            scores = dot_nt(keys_bf, spread_heads(queries))
            keep = valid_rows(scores.shape)
            scores = jnp.where(keep, scores, -1e30)
            top = jnp.max(scores, axis=0, keepdims=True)
            lifted = jnp.exp((scores - top) * SCALE)
            totals = jnp.sum(lifted, axis=0, keepdims=True)
            chances = (lifted * (1.0 / totals)).astype(BF)
            chance_out[direction * 8 + window] = chances
            attended = gather_heads(dot_nn(values.T.astype(BF), chances))
            clean = jnp.where(valid_rows(values.shape), values, 0.0)
            position = window_conv(
                column_shifts(clean, across),
                lambda i, j: conv_k[block, 3 * i + j : 3 * i + j + 1, lane : lane + HALF],
                across,
            )
            put_window(
                stripe, at, lane, attended + position + conv_b[block : block + 1, lane : lane + HALF]
            )


def attention_backward(
    block,
    win_in,
    chance_in,
    conv_k,
    stripe_delta,
    wide,
    conv_acc,
):
    width = stripe_delta.shape[1]
    for direction in range(2):
        across = direction == 0
        lane = direction * HALF

        @pl.loop(0, 8)
        def _(window, across=across, lane=lane, direction=direction):
            at = window_rows(across, window)
            out_delta = take_window(stripe_delta, at, lane)
            queries = win_in[direction * 8 + window, :, 0:HALF].astype(F32)
            keys = win_in[direction * 8 + window, :, HALF : 2 * HALF].astype(F32)
            values_bf = win_in[direction * 8 + window, :, 2 * HALF : 3 * HALF]
            values = values_bf.astype(F32)
            chances = chance_in[direction * 8 + window]
            delta_spread = spread_heads(out_delta)
            chance_delta = dot_nt(values_bf, delta_spread)
            wide_chances = chances.astype(F32)
            weighted = wide_chances * chance_delta
            score_delta = (
                weighted - wide_chances * jnp.sum(weighted, axis=0, keepdims=True)
            ).astype(BF)
            values_delta = dot_nn(chances, delta_spread)
            keys_delta = dot_nn(score_delta, spread_heads(queries)) * SCALE
            query_delta = gather_heads(dot_nn(keys.T.astype(BF), score_delta)) * SCALE
            keep = valid_rows(values.shape)
            clean = jnp.where(keep, values, 0.0)
            shifts = column_shifts(clean, across)
            cube = out_delta.reshape(2 * TILE, 8, HALF)
            for i in range(3):
                moved = row_shift(cube, 1 - i, across)
                for j in range(3):
                    conv_acc[3 * i + j, :, lane : lane + HALF] += jnp.sum(moved * shifts[j], axis=0)
            back = window_conv(
                column_shifts(out_delta, across),
                lambda i, j: conv_k[block, 8 - 3 * i - j : 9 - 3 * i - j, lane : lane + HALF],
                across,
            )
            values_delta = jnp.where(keep, values_delta + back, 0.0)
            put_window(wide, at, lane, query_delta)
            put_window(wide, at, width + lane, keys_delta)
            put_window(wide, at, 2 * width + lane, values_delta)


def chunk(t):
    return pl.ds(pl.multiple_of(t * 4 * PAD, 4 * PAD), 4 * PAD)


def put_squares(out_ref, at, values, side):
    for part in range(values.shape[1] // side):
        out_ref[at + part * side : at + (part + 1) * side, :] = values[
            :, part * side : (part + 1) * side
        ].astype(BF)


def first_kernel(
    scale_ref,
    mixed_ref,
    cot_ref,
    gains,
    shifts,
    entry_w,
    entry_b,
    conv_k,
    conv_b,
    exit_w,
    exit_b,
    expand_w,
    expand_b,
    shrink_w,
    shrink_b,
    act_out,
    bundle_out,
    vec_out,
    active0_out,
    slope0_out,
    win0_out,
    chance0_out,
    stripe0_out,
    mid0_out,
    win1_out,
    chance1_out,
    stripe1_out,
    hidden1_out,
    grad_out,
    hidden,
    wide,
    stripe,
    active1,
    pre1,
    feed1,
    inner1,
):
    width = hidden.shape[1]
    hidden_units = expand_w.shape[2]
    vec_out[...] = jnp.zeros(vec_out.shape, F32)

    @pl.loop(0, 16)
    def _(n):
        hidden[pl.ds(pl.multiple_of(n * PAD, 8), PAD), :] = mixed_ref[n // 4, n % 4].astype(F32)

    for block in range(2):
        win_out, chance_out, stripe_out = (
            (win0_out, chance0_out, stripe0_out),
            (win1_out, chance1_out, stripe1_out),
        )[block]
        attention_forward(
            block, hidden, gains, shifts, entry_w, entry_b, conv_k, conv_b, wide, stripe, win_out, chance_out
        )

        @pl.loop(0, 4)
        def _(t, block=block, stripe_out=stripe_out):
            rows = chunk(t)
            striped = stripe[rows, :].astype(BF)
            stripe_out[rows, :] = striped
            branch = dot_nn(striped, exit_w[block]) + exit_b[block : block + 1, :]
            midway = hidden[rows, :] + scale_rows(scale_ref, 2 * block, 4) * branch
            if block == 0:
                mid0_out[rows, :] = midway
            hat, inverse = norm_parts(midway)
            normed = (hat * gains[block, 1:2, :] + shifts[block, 1:2, :]).astype(BF)
            feed_scale = scale_rows(scale_ref, 2 * block + 1, 4)
            feed = shrink_b[block : block + 1, :]
            if block == 1:
                inner1[rows, :] = normed
                gradient = jnp.concatenate([cot_ref[t, i] for i in range(4)], axis=0).astype(F32)
                feed_delta = (feed_scale * gradient).astype(BF)
                feed1[rows, :] = feed_delta
                add_row(vec_out, 4, row_sums(feed_delta.astype(F32)))
                inner_delta = jnp.zeros((4 * PAD, width), F32)
            for part in range(hidden_units // width):
                at = slice(part * width, (part + 1) * width)
                pre_act = dot_nn(normed, expand_w[block, :, at]) + expand_b[block : block + 1, at]
                chance, density = gelu_parts(pre_act)
                active = (pre_act * chance).astype(BF)
                slope = chance + pre_act * density
                if block == 0:
                    active0_out[rows, at] = active
                    slope0_out[rows, at] = slope.astype(BF)
                else:
                    active1[rows, at] = active
                    pre_delta = (dot_nt(feed_delta, shrink_w[block, at, :]) * slope).astype(BF)
                    pre1[rows, at] = pre_delta
                    add_row(vec_out, part, row_sums(pre_delta.astype(F32)))
                    inner_delta = inner_delta + dot_nt(pre_delta, expand_w[block, :, at])
                feed = feed + dot_nn(active, shrink_w[block, at, :])
            output = midway + feed_scale * feed
            if block == 0:
                hidden[rows, :] = output
                hidden1_out[rows, :] = output
            else:
                for i in range(4):
                    act_out[t, i] = output[i * PAD : (i + 1) * PAD].astype(BF)
                add_row(vec_out, 5, row_sums(inner_delta * hat))
                add_row(vec_out, 6, row_sums(inner_delta))
                grad_out[rows, :] = gradient + norm_back(
                    inner_delta, hat, inverse, gains[block, 1:2, :]
                )

    put_squares(bundle_out, 0, dot_tn(inner1[...], pre1[...]), width)
    for part in range(hidden_units // width):
        bundle_out[hidden_units + part * width : hidden_units + (part + 1) * width, :] = dot_tn(
            active1[:, part * width : (part + 1) * width], feed1[...]
        ).astype(BF)


def delta_rows(block, scale_ref, exit_w, grad_ref, stripe_delta, branch_delta, vec_out, at):
    @pl.loop(0, 4)
    def _(t):
        rows = chunk(t)
        rounded = (scale_rows(scale_ref, 2 * block, 4) * grad_ref[rows, :]).astype(BF)
        branch_delta[rows, :] = rounded
        add_row(vec_out, at, row_sums(rounded.astype(F32)))
        out = round_bf(dot_nt(rounded, exit_w[block]))
        stripe_delta[rows, :] = out
        add_row(vec_out, at + 1, row_sums(out))


def entry_backward(block, hidden_ref, gains, shifts, entry_w, grad_ref, wide, wide_bf, normed_bf, vec_out, at, emit):
    width = hidden_ref.shape[1]

    @pl.loop(0, 4)
    def _(t):
        rows = chunk(t)
        hat, inverse = norm_parts(hidden_ref[rows, :])
        normed_bf[rows, :] = (hat * gains[block, 0:1, :] + shifts[block, 0:1, :]).astype(BF)
        delta = jnp.zeros((4 * PAD, width), F32)
        for part in range(3):
            lanes = slice(part * width, (part + 1) * width)
            rounded = wide[rows, lanes].astype(BF)
            wide_bf[rows, lanes] = rounded
            if part != 1:
                add_row(vec_out, at + part // 2, row_sums(rounded.astype(F32)))
            delta = delta + dot_nt(rounded, entry_w[block, :, lanes])
        add_row(vec_out, at + 2, row_sums(delta * hat))
        add_row(vec_out, at + 3, row_sums(delta))
        emit(t, rows, grad_ref[rows, :] + norm_back(delta, hat, inverse, gains[block, 0:1, :]))


def second_kernel(
    scale_ref,
    grad_in,
    hidden1,
    stripe1,
    win1,
    chance1,
    mid0,
    active0,
    slope0,
    stripe0,
    gains,
    shifts,
    entry_w,
    conv_k,
    exit_w,
    expand_w,
    shrink_w,
    bundle_out,
    vec_out,
    conv_out,
    grad_out,
    stripe_delta_out,
    grad,
    stripe_delta,
    branch_delta,
    wide,
    wide_bf,
    normed_bf,
    feed0,
    pre0,
):
    width = grad.shape[1]
    hidden_units = expand_w.shape[2]
    vec_out[...] = jnp.zeros(vec_out.shape, F32)
    conv_out[...] = jnp.zeros(conv_out.shape, F32)
    delta_rows(1, scale_ref, exit_w, grad_in, stripe_delta, branch_delta, vec_out, 0)
    attention_backward(1, win1, chance1, conv_k, stripe_delta, wide, conv_out)

    def emit(t, rows, values):
        grad[rows, :] = values

    entry_backward(
        1, hidden1, gains, shifts, entry_w, grad_in, wide, wide_bf, normed_bf, vec_out, 2, emit
    )
    put_squares(bundle_out, 0, dot_tn(normed_bf[...], wide_bf[...]), width)
    bundle_out[3 * width : 4 * width, :] = dot_tn(stripe1[...], branch_delta[...]).astype(BF)

    @pl.loop(0, 4)
    def _(t):
        rows = chunk(t)
        gradient = grad[rows, :]
        hat, inverse = norm_parts(mid0[rows, :])
        normed_bf[rows, :] = (hat * gains[0, 1:2, :] + shifts[0, 1:2, :]).astype(BF)
        feed_delta = (scale_rows(scale_ref, 1, 4) * gradient).astype(BF)
        feed0[rows, :] = feed_delta
        add_row(vec_out, 6, row_sums(feed_delta.astype(F32)))
        inner_delta = jnp.zeros((4 * PAD, width), F32)
        for part in range(hidden_units // width):
            at = slice(part * width, (part + 1) * width)
            pre_delta = (
                dot_nt(feed_delta, shrink_w[0, at, :]) * slope0[rows, at].astype(F32)
            ).astype(BF)
            pre0[rows, at] = pre_delta
            add_row(vec_out, 7 + part, row_sums(pre_delta.astype(F32)))
            inner_delta = inner_delta + dot_nt(pre_delta, expand_w[0, :, at])
        add_row(vec_out, 11, row_sums(inner_delta * hat))
        add_row(vec_out, 12, row_sums(inner_delta))
        grad[rows, :] = gradient + norm_back(inner_delta, hat, inverse, gains[0, 1:2, :])

    grad_out[...] = grad[...]
    put_squares(bundle_out, 4 * width, dot_tn(normed_bf[...], pre0[...]), width)
    for part in range(hidden_units // width):
        base = 8 * width + part * width
        bundle_out[base : base + width, :] = dot_tn(
            active0[:, part * width : (part + 1) * width], feed0[...]
        ).astype(BF)
    delta_rows(0, scale_ref, exit_w, grad, stripe_delta_out, branch_delta, vec_out, 13)
    bundle_out[12 * width : 13 * width, :] = dot_tn(stripe0[...], branch_delta[...]).astype(BF)


def third_kernel(
    grad_in,
    stripe_delta,
    mixed_ref,
    win0,
    chance0,
    gains,
    shifts,
    entry_w,
    conv_k,
    out_ref,
    bundle_out,
    vec_out,
    conv_out,
    hidden,
    wide,
    wide_bf,
    normed_bf,
):
    width = hidden.shape[1]
    vec_out[...] = jnp.zeros(vec_out.shape, F32)
    conv_out[...] = jnp.zeros(conv_out.shape, F32)

    @pl.loop(0, 16)
    def _(n):
        hidden[pl.ds(pl.multiple_of(n * PAD, 8), PAD), :] = mixed_ref[n // 4, n % 4].astype(F32)

    attention_backward(0, win0, chance0, conv_k, stripe_delta, wide, conv_out)

    def emit(t, rows, values):
        for i in range(4):
            out_ref[t, i] = values[i * PAD : (i + 1) * PAD].astype(BF)

    entry_backward(
        0, hidden, gains, shifts, entry_w, grad_in, wide, wide_bf, normed_bf, vec_out, 0, emit
    )
    put_squares(bundle_out, 0, dot_tn(normed_bf[...], wide_bf[...]), width)


def pick_kernel(index_ref, images_ref, out_ref):
    @pl.loop(0, out_ref.shape[0])
    def _(s):
        out_ref[s] = images_ref[jnp.minimum(index_ref[s], images_ref.shape[0] - 1)]


def inside_box(corner_ref, n, start_ref):
    token = lax.broadcasted_iota(jnp.int32, (PAD, 1), 0)
    row = start_ref[0] + token // 8
    col = start_ref[1] + token % 8
    hit = (
        (row >= corner_ref[n, 0])
        & (row < corner_ref[n, 1])
        & (col >= corner_ref[n, 2])
        & (col < corner_ref[n, 3])
    )
    return jnp.where(hit, 1.0, 0.0)


def mix_kernel(take_ref, corner_ref, ratio_ref, start_ref, arrived, images_ref, out_ref):
    count = images_ref.shape[0]

    @pl.loop(0, count)
    def _(n):
        inside = inside_box(corner_ref, n, start_ref)
        ratio = ratio_ref[n]
        own = images_ref[n].astype(F32)
        blend = arrived[take_ref[n]].astype(F32)
        cut = arrived[take_ref[count + n]].astype(F32)
        mixed = inside * cut + (1.0 - inside) * (ratio * own + (1.0 - ratio) * blend)
        out_ref[n] = mixed.astype(BF)


def split_kernel(take_ref, corner_ref, ratio_ref, start_ref, grad_ref, out_ref):
    count = grad_ref.shape[0]
    out_ref[...] = jnp.zeros(out_ref.shape, BF)

    @pl.loop(0, count)
    def _(n):
        inside = inside_box(corner_ref, n, start_ref)
        gradient = grad_ref[n].astype(F32)
        cut = inside * gradient
        out_ref[take_ref[n]] = ((1.0 - ratio_ref[n]) * (gradient - cut)).astype(BF)
        out_ref[take_ref[count + n]] = cut.astype(BF)


def join_kernel(index_ref, corner_ref, ratio_ref, start_ref, grad_ref, back_ref, out_ref, total):
    count = grad_ref.shape[0]

    @pl.loop(0, count)
    def _(n):
        outside = 1.0 - inside_box(corner_ref, n, start_ref)
        total[n] = ratio_ref[n] * outside * grad_ref[n].astype(F32)

    @pl.loop(0, back_ref.shape[0])
    def _(s):
        total[index_ref[s]] += back_ref[s].astype(F32)

    @pl.loop(0, count)
    def _(n):
        out_ref[n] = total[n].reshape(TILE, 8, total.shape[2])[:, :TILE, :]


SMEM = pl.BlockSpec(memory_space=pltpu.SMEM)
VMEM = pl.BlockSpec(memory_space=pltpu.VMEM)


def run(kernel, scalars, arrays, outs, scratch=(), flops=0, name=None):
    out_shape = [jax.ShapeDtypeStruct(shape, dtype) for shape, dtype in outs]
    moved = sum(a.size * a.dtype.itemsize for a in arrays)
    return pl.pallas_call(
        kernel,
        out_shape=out_shape,
        in_specs=[SMEM] * len(scalars) + [VMEM] * len(arrays),
        out_specs=[VMEM] * len(outs),
        scratch_shapes=[pltpu.VMEM(shape, dtype) for shape, dtype in scratch],
        compiler_params=pltpu.CompilerParams(vmem_limit_bytes=VMEM_BYTES),
        cost_estimate=pl.CostEstimate(flops=flops, bytes_accessed=moved, transcendentals=0),
        name=name,
    )(*scalars, *arrays)


def partner_plan(mix_partner, cut_partner, images_here, groups, device):
    requests = jnp.concatenate(
        [mix_partner.reshape(groups, images_here), cut_partner.reshape(groups, images_here)], axis=1
    )
    owners = requests // images_here
    within = requests % images_here
    wanted = 2 * images_here
    before = jnp.arange(wanted)[None, :] < jnp.arange(wanted)[:, None]
    rank = jnp.sum((owners[:, :, None] == owners[:, None, :]) & before[None], axis=2)
    capacity = (wanted + groups - 1) // groups
    chosen = (owners == device)[:, :, None] & (
        rank[:, :, None] == jnp.arange(capacity)[None, None, :]
    )
    index = images_here + jnp.sum(
        jnp.where(chosen, (within - images_here)[:, :, None], 0), axis=1
    ).reshape(groups * capacity)
    take = lax.dynamic_index_in_dim(owners * capacity + rank, device, 0, keepdims=False)
    return index.astype(jnp.int32), take.astype(jnp.int32), capacity


def swap(values, axis):
    return lax.ppermute(values, axis, [(0, 1), (1, 0)])


def halve(values, axis):
    place = lax.axis_index(axis)
    count = values.shape[0] // 2
    away = lax.dynamic_slice_in_dim(values, (1 - place) * count, count, 0)
    mine = lax.dynamic_slice_in_dim(values, place * count, count, 0)
    return (mine.astype(F32) + swap(away, axis).astype(F32)).astype(BF)


def unhalve(values, axis):
    other = swap(values, axis)
    first = lax.axis_index(axis) == 0
    return jnp.concatenate([jnp.where(first, values, other), jnp.where(first, other, values)])


def sum_spread(values, groups):
    part = halve(halve(values, "col"), "row")
    rows = part.shape[0] // groups
    pieces = lax.all_to_all(
        part.reshape(groups, rows, part.shape[1]), "dp", split_axis=0, concat_axis=0, tiled=True
    )
    mine = jnp.sum(pieces.astype(F32), axis=0).astype(BF)
    full = lax.all_to_all(
        jnp.broadcast_to(mine[None], pieces.shape), "dp", split_axis=0, concat_axis=0, tiled=True
    )
    return unhalve(unhalve(full.reshape(part.shape), "row"), "col")


def sum_doubling(values, groups):
    part = halve(halve(values, "col"), "row")
    step = 1
    while step < groups:
        other = lax.ppermute(part, "dp", [(i, i ^ step) for i in range(groups)])
        part = (part.astype(F32) + other.astype(F32)).astype(BF)
        step *= 2
    return unhalve(unhalve(part, "row"), "col")


def local(
    groups,
    images,
    cotangent,
    mix_partner,
    cut_partner,
    ratios,
    corners,
    drop_masks,
    norm_gains,
    norm_shifts,
    entry_weight,
    entry_bias,
    position_kernel,
    position_bias,
    exit_weight,
    exit_bias,
    expand_weight,
    expand_bias,
    shrink_weight,
    shrink_bias,
):
    images_here = images.shape[0]
    width = images.shape[3]
    units = expand_weight.shape[2]
    device = lax.axis_index("dp")
    row, col = lax.axis_index("row"), lax.axis_index("col")
    start = jnp.stack([row * TILE, col * TILE]).astype(jnp.int32)
    share = images_here // 4
    rows = 4 * share * PAD
    index, take, capacity = partner_plan(mix_partner, cut_partner, images_here, groups, device)
    slots = groups * capacity

    def padded(values):
        wide = jnp.pad(values, ((0, 0), (0, 0), (0, 1), (0, 0)))
        return wide.reshape(images_here, PAD, width)

    def regroup(values):
        return lax.all_to_all(values, ("row", "col"), split_axis=0, concat_axis=0, tiled=True)

    own = padded(images)
    (outgoing,) = run(pick_kernel, [index], [own], [((slots, PAD, width), BF)], name="pick")
    arrived = lax.all_to_all(outgoing, "dp", split_axis=0, concat_axis=0, tiled=True)
    cot = regroup(padded(cotangent).reshape(4, share, PAD, width))
    (mixed,) = run(
        mix_kernel,
        [take, corners, ratios, start],
        [arrived, own],
        [((images_here, PAD, width), BF)],
        name="mix",
    )
    mixed = regroup(mixed.reshape(4, share, PAD, width))
    scales = lax.dynamic_slice_in_dim(
        drop_masks.astype(F32) * 1.25, (2 * row + col) * share, share, 0
    )
    conv_k = position_kernel.reshape(2, 9, width)
    tall = (rows, width)
    (
        act,
        bundle1,
        vec1,
        active0,
        slope0,
        win0,
        chance0,
        stripe0,
        mid0,
        win1,
        chance1,
        stripe1,
        hidden1,
        grad1,
    ) = run(
        first_kernel,
        [scales],
        [
            mixed,
            cot,
            norm_gains,
            norm_shifts,
            entry_weight,
            entry_bias,
            conv_k,
            position_bias,
            exit_weight,
            exit_bias,
            expand_weight,
            expand_bias,
            shrink_weight,
            shrink_bias,
        ],
        [
            ((4, share, PAD, width), BF),
            ((2 * units, width), BF),
            ((7, 8, width), F32),
            ((rows, units), BF),
            ((rows, units), BF),
            ((4 * share, WIN, 3 * HALF), BF),
            ((4 * share, WIN, LANES), BF),
            (tall, BF),
            (tall, F32),
            ((4 * share, WIN, 3 * HALF), BF),
            ((4 * share, WIN, LANES), BF),
            (tall, BF),
            (tall, F32),
            (tall, F32),
        ],
        [
            (tall, F32),
            ((rows, 3 * width), F32),
            (tall, F32),
            ((rows, units), BF),
            ((rows, units), BF),
            (tall, BF),
            (tall, BF),
        ],
        flops=10 * rows * width * width * 12,
        name="first",
    )
    sum1 = sum_spread(bundle1, groups)
    act = regroup(act)
    bundle2, vec2, conv2, grad0, delta0 = run(
        second_kernel,
        [scales],
        [
            grad1,
            hidden1,
            stripe1,
            win1,
            chance1,
            mid0,
            active0,
            slope0,
            stripe0,
            norm_gains,
            norm_shifts,
            entry_weight,
            conv_k,
            exit_weight,
            expand_weight,
            shrink_weight,
        ],
        [
            ((13 * width, width), BF),
            ((15, 8, width), F32),
            ((9, 8, width), F32),
            (tall, F32),
            (tall, F32),
        ],
        [
            (tall, F32),
            (tall, F32),
            (tall, BF),
            ((rows, 3 * width), F32),
            ((rows, 3 * width), BF),
            (tall, BF),
            (tall, BF),
            ((rows, units), BF),
        ],
        flops=6 * rows * width * width * 12,
        name="second",
    )
    sum2 = sum_spread(bundle2, groups)
    out_tiles, bundle3, vec3, conv3 = run(
        third_kernel,
        [],
        [grad0, delta0, mixed, win0, chance0, norm_gains, norm_shifts, entry_weight, conv_k],
        [
            ((4, share, PAD, width), BF),
            ((3 * width, width), BF),
            ((4, 8, width), F32),
            ((9, 8, width), F32),
        ],
        [(tall, F32), ((rows, 3 * width), F32), ((rows, 3 * width), BF), (tall, BF)],
        flops=3 * rows * width * width * 12,
        name="third",
    )
    gradient = regroup(out_tiles).reshape(images_here, PAD, width)
    (parted,) = run(
        split_kernel,
        [take, corners, ratios, start],
        [gradient],
        [((slots, PAD, width), BF)],
        name="split",
    )
    back = lax.all_to_all(parted, "dp", split_axis=0, concat_axis=0, tiled=True)
    (input_gradient,) = run(
        join_kernel,
        [index, corners, ratios, start],
        [gradient, back],
        [((images_here, TILE, TILE, width), F32)],
        [((images_here + 1, PAD, width), F32)],
        name="join",
    )
    vectors = jnp.sum(jnp.concatenate([vec1, vec2, conv2, vec3, conv3]), axis=1)
    count = vectors.shape[0]
    filled = jnp.pad(vectors.astype(BF), ((0, 64 - count), (0, 0)))
    sum3 = sum_doubling(jnp.concatenate([bundle3, filled]), groups)

    def flat(values):
        return values.reshape(-1, width, width).transpose(1, 0, 2).reshape(width, -1)

    sum1, sum2, sum3 = sum1.astype(F32), sum2.astype(F32), sum3.astype(F32)
    v = sum3[3 * width : 3 * width + count]
    v1, v2, c2, v3, c3 = v[0:7], v[7:22], v[22:31], v[31:35], v[35:44]
    return (
        act.reshape(images_here, TILE, 8, width)[:, :, :TILE, :],
        input_gradient,
        jnp.stack([jnp.stack([v3[2], v2[11]]), jnp.stack([v2[4], v1[5]])]),
        jnp.stack([jnp.stack([v3[3], v2[12]]), jnp.stack([v2[5], v1[6]])]),
        jnp.stack([flat(sum3[: 3 * width]), flat(sum2[: 3 * width])]),
        jnp.stack([v3[0:2].reshape(-1), v2[2:4].reshape(-1)]),
        jnp.stack([c3, c2]).reshape(2, 3, 3, width),
        jnp.stack([v2[14], v2[1]]),
        jnp.stack([sum2[12 * width :], sum2[3 * width : 4 * width]]),
        jnp.stack([v2[13], v2[0]]),
        jnp.stack([flat(sum2[4 * width : 8 * width]), flat(sum1[:units])]),
        jnp.stack([v2[7:11].reshape(-1), v1[0:4].reshape(-1)]),
        jnp.stack([sum2[8 * width : 12 * width], sum1[units:]]),
        jnp.stack([v2[6], v1[4]]),
    )


def solution(mesh):
    tiles = P("dp", "row", "col", None)
    return jax.shard_map(
        functools.partial(local, mesh.shape["dp"]),
        mesh=mesh,
        in_specs=(tiles, tiles, P(), P(), P("dp"), P("dp", None), P("dp", None)) + (P(),) * 12,
        out_specs=(tiles, tiles) + (P(),) * 12,
        check_vma=False,
    )
```

```python
import functools

import jax
import jax.numpy as jnp
from jax import lax
from jax.experimental import pallas as pl
from jax.experimental.pallas import tpu as pltpu
from jax.sharding import PartitionSpec as P

TILE = 7
PAD = 56
HEAD_DIM = 32
SIDE_HEADS = 4
HALF = 128
WIN = 2 * PAD
LANES = SIDE_HEADS * 128
SCALE = HEAD_DIM ** (-0.5)
EPS = 1e-05
BF = jnp.bfloat16
F32 = jnp.float32
VMEM_BYTES = 60 * 1024 * 1024


def dot_nn(a, b):
    return lax.dot_general(a, b, (((1,), (0,)), ((), ())), preferred_element_type=F32)


def dot_nt(a, b):
    return lax.dot_general(a, b, (((1,), (1,)), ((), ())), preferred_element_type=F32)


def dot_tn(a, b):
    return lax.dot_general(a, b, (((0,), (0,)), ((), ())), preferred_element_type=F32)


def norm_parts(values):
    centered = values - jnp.mean(values, axis=-1, keepdims=True)
    inverse = lax.rsqrt(jnp.mean(centered * centered, axis=-1, keepdims=True) + EPS)
    return centered * inverse, inverse


def norm_back(delta, hat, inverse, gain):
    scaled = delta * gain
    first = jnp.mean(scaled, axis=-1, keepdims=True)
    second = jnp.mean(scaled * hat, axis=-1, keepdims=True)
    return inverse * (scaled - first - hat * second)


def gelu_parts(values):
    size = jnp.abs(values) * (0.5**0.5)
    fall = jnp.exp(-(size * size))
    step = 1.0 / (1.0 + 0.3275911 * size)
    series = step * (
        0.254829592
        + step * (-0.284496736 + step * (1.421413741 + step * (-1.453152027 + step * 1.061405429)))
    )
    tail = 0.5 * series * fall
    chance = jnp.where(values >= 0.0, 1.0 - tail, tail)
    return chance, fall * 0.3989422804014327


def row_sums(values):
    count, width = values.shape
    return jnp.sum(values.reshape(count // 8, 8, width), axis=0)


def scale_rows(place_ref, mask_ref, column):
    scales = [
        mask_ref[column, 4 * place_ref[3] + i].astype(F32) * 1.25 for i in range(4)
    ]
    return jnp.concatenate([jnp.full((PAD, 1), scale, F32) for scale in scales], axis=0)


def add_row(acc_ref, row, values):
    acc_ref[row] += values


def spread_heads(values):
    lane = lax.broadcasted_iota(jnp.int32, values.shape, 1) // HEAD_DIM
    empty = jnp.zeros((128 - WIN, HALF), F32)
    blocks = []
    for head in range(SIDE_HEADS):
        blocks.append(jnp.where(lane == head, values, 0.0))
        blocks.append(empty)
    return jnp.concatenate(blocks, axis=0).astype(BF)


def gather_heads(wide):
    picked = jnp.concatenate(
        [
            wide[head * HEAD_DIM : (head + 1) * HEAD_DIM, head * 128 : (head + 1) * 128]
            for head in range(SIDE_HEADS)
        ],
        axis=0,
    )
    return picked.T[:WIN]


def valid_rows(shape):
    return lax.broadcasted_iota(jnp.int32, shape, 0) % 8 != 7


def column_shifts(values, across):
    cube = values.reshape(2 * TILE, 8, HALF)
    if not across:
        return (pltpu.roll(cube, 1, 1), cube, pltpu.roll(cube, 7, 1))
    left, right = cube[:TILE], cube[TILE:]
    column = lax.broadcasted_iota(jnp.int32, left.shape, 1)
    before = jnp.concatenate(
        [
            pltpu.roll(left, 1, 1),
            jnp.where(column == 0, pltpu.roll(left, 2, 1), pltpu.roll(right, 1, 1)),
        ],
        axis=0,
    )
    after = jnp.concatenate(
        [
            jnp.where(column == 6, pltpu.roll(right, 6, 1), pltpu.roll(left, 7, 1)),
            pltpu.roll(right, 7, 1),
        ],
        axis=0,
    )
    return (before, cube, after)


def row_shift(cube, step, across):
    if step == 0:
        return cube
    empty = jnp.zeros((1, 8, HALF), F32)

    def move(part):
        if step < 0:
            return jnp.concatenate([empty, part[:-1]], axis=0)
        return jnp.concatenate([part[1:], empty], axis=0)

    if across:
        return jnp.concatenate([move(cube[:TILE]), move(cube[TILE:])], axis=0)
    return move(cube)


def window_conv(shifts, kernel_at, across):
    total = None
    for i in range(3):
        part = None
        for j in range(3):
            term = kernel_at(i, j) * shifts[j]
            part = term if part is None else part + term
        part = row_shift(part, i - 1, across)
        total = part if total is None else total + part
    return total.reshape(WIN, HALF)


def window_rows(across, window):
    side, image = window // 4, window % 4
    if across:
        first, second = 2 * side, 2 * side + 1
    else:
        first, second = side, 2 + side
    return (
        pl.multiple_of((first * 4 + image) * PAD, 8),
        pl.multiple_of((second * 4 + image) * PAD, 8),
    )


def take_window(ref, at, lane):
    return jnp.concatenate(
        [ref[pl.ds(at[0], PAD), lane : lane + HALF], ref[pl.ds(at[1], PAD), lane : lane + HALF]],
        axis=0,
    )


def put_window(ref, at, lane, values):
    ref[pl.ds(at[0], PAD), lane : lane + HALF] = values[:PAD]
    ref[pl.ds(at[1], PAD), lane : lane + HALF] = values[PAD:]


def round_bf(values):
    return values.astype(BF).astype(F32)


def attention_forward(
    block, hidden_ref, gains, shifts, entry_w, entry_b, conv_k, conv_b, wide, stripe, win_out, chance_out
):
    width = hidden_ref.shape[1]

    @pl.loop(0, 4)
    def _(t):
        rows = pl.ds(pl.multiple_of(t * 4 * PAD, 4 * PAD), 4 * PAD)
        hat, _ = norm_parts(hidden_ref[rows, :])
        normed = (hat * gains[block, 0:1, :] + shifts[block, 0:1, :]).astype(BF)
        for part in range(3):
            out = dot_nn(normed, entry_w[block, :, part * width : (part + 1) * width])
            if part != 1:
                at = 0 if part == 0 else width
                out = out + entry_b[block : block + 1, at : at + width]
            wide[rows, part * width : (part + 1) * width] = round_bf(out)

    for direction in range(2):
        across = direction == 0
        lane = direction * HALF

        @pl.loop(0, 8)
        def _(window, across=across, lane=lane, direction=direction):
            at = window_rows(across, window)
            queries = take_window(wide, at, lane)
            keys = take_window(wide, at, width + lane)
            values = take_window(wide, at, 2 * width + lane)
            keys_bf = keys.astype(BF)
            win_out[direction * 8 + window, :, 0:HALF] = queries.astype(BF)
            win_out[direction * 8 + window, :, HALF : 2 * HALF] = keys_bf
            win_out[direction * 8 + window, :, 2 * HALF : 3 * HALF] = values.astype(BF)
            scores = dot_nt(keys_bf, spread_heads(queries))
            keep = valid_rows(scores.shape)
            scores = jnp.where(keep, scores, -1e30)
            top = jnp.max(scores, axis=0, keepdims=True)
            lifted = jnp.exp((scores - top) * SCALE)
            totals = jnp.sum(lifted, axis=0, keepdims=True)
            chances = (lifted * (1.0 / totals)).astype(BF)
            chance_out[direction * 8 + window] = chances
            attended = gather_heads(dot_nn(values.T.astype(BF), chances))
            clean = jnp.where(valid_rows(values.shape), values, 0.0)
            position = window_conv(
                column_shifts(clean, across),
                lambda i, j: conv_k[i, j, block : block + 1, lane : lane + HALF],
                across,
            )
            put_window(
                stripe, at, lane, attended + position + conv_b[block : block + 1, lane : lane + HALF]
            )


def attention_backward(
    block,
    win_in,
    chance_in,
    conv_k,
    stripe_delta,
    wide,
    conv_acc,
):
    width = stripe_delta.shape[1]
    for direction in range(2):
        across = direction == 0
        lane = direction * HALF

        @pl.loop(0, 8)
        def _(window, across=across, lane=lane, direction=direction):
            at = window_rows(across, window)
            out_delta = take_window(stripe_delta, at, lane)
            queries = win_in[direction * 8 + window, :, 0:HALF].astype(F32)
            keys = win_in[direction * 8 + window, :, HALF : 2 * HALF].astype(F32)
            values_bf = win_in[direction * 8 + window, :, 2 * HALF : 3 * HALF]
            values = values_bf.astype(F32)
            chances = chance_in[direction * 8 + window]
            delta_spread = spread_heads(out_delta)
            chance_delta = dot_nt(values_bf, delta_spread)
            wide_chances = chances.astype(F32)
            weighted = wide_chances * chance_delta
            score_delta = (
                weighted - wide_chances * jnp.sum(weighted, axis=0, keepdims=True)
            ).astype(BF)
            values_delta = dot_nn(chances, delta_spread)
            keys_delta = dot_nn(score_delta, spread_heads(queries)) * SCALE
            query_delta = gather_heads(dot_nn(keys.T.astype(BF), score_delta)) * SCALE
            keep = valid_rows(values.shape)
            clean = jnp.where(keep, values, 0.0)
            shifts = column_shifts(clean, across)
            cube = out_delta.reshape(2 * TILE, 8, HALF)
            for i in range(3):
                moved = row_shift(cube, 1 - i, across)
                for j in range(3):
                    conv_acc[3 * i + j, :, lane : lane + HALF] += jnp.sum(moved * shifts[j], axis=0)
            back = window_conv(
                column_shifts(out_delta, across),
                lambda i, j: conv_k[2 - i, 2 - j, block : block + 1, lane : lane + HALF],
                across,
            )
            values_delta = jnp.where(keep, values_delta + back, 0.0)
            put_window(wide, at, lane, query_delta)
            put_window(wide, at, width + lane, keys_delta)
            put_window(wide, at, 2 * width + lane, values_delta)


def chunk(t):
    return pl.ds(pl.multiple_of(t * 4 * PAD, 4 * PAD), 4 * PAD)


def put_rows(bundle, at, values):
    place_ref, keep, away = bundle
    values = values.astype(BF)
    half = keep.shape[0]
    count = values.shape[0]
    cuts = [at, at + count] if at >= half or at + count <= half else [at, half, at + count]
    for first, last in zip(cuts[:-1], cuts[1:]):
        number = first // half
        piece = values[first - at : last - at]
        place = slice(first - number * half, last - number * half)

        @pl.when(place_ref[2] == number)
        def _(piece=piece, place=place):
            keep[place, :] = piece

        @pl.when(place_ref[2] != number)
        def _(piece=piece, place=place):
            away[place, :] = piece


def put_squares(bundle, at, values, side):
    for part in range(values.shape[1] // side):
        put_rows(bundle, at + part * side, values[:, part * side : (part + 1) * side])


def load_tiles(place_ref, tiles, hidden):
    for d, tile in enumerate(tiles):
        rows = chunk(jnp.bitwise_xor(place_ref[3], d))
        hidden[rows, :] = tile[...].astype(F32).reshape(4 * PAD, hidden.shape[1])


def store_tile(place_ref, tiles, t, values):
    values = values.reshape(tiles[0].shape).astype(BF)
    for d, tile in enumerate(tiles):

        @pl.when(jnp.bitwise_xor(place_ref[3], d) == t)
        def _(tile=tile):
            tile[...] = values


def first_kernel(
    place_ref,
    mask_ref,
    mixed_a,
    mixed_b,
    mixed_c,
    mixed_d,
    cot_a,
    cot_b,
    cot_c,
    cot_d,
    gains,
    shifts,
    entry_w,
    entry_b,
    conv_k,
    conv_b,
    exit_w,
    exit_b,
    expand_w,
    expand_b,
    shrink_w,
    shrink_b,
    act_a,
    act_b,
    act_c,
    act_d,
    keep_out,
    away_out,
    vec_out,
    active0_out,
    slope0_out,
    win0_out,
    chance0_out,
    stripe0_out,
    mid0_out,
    win1_out,
    chance1_out,
    stripe1_out,
    hidden1_out,
    grad_out,
    hidden,
    wide,
    stripe,
    active1,
    pre1,
    feed1,
    inner1,
):
    width = hidden.shape[1]
    hidden_units = expand_w.shape[2]
    bundle = (place_ref, keep_out, away_out)
    vec_out[...] = jnp.zeros(vec_out.shape, F32)
    load_tiles(place_ref, (mixed_a, mixed_b, mixed_c, mixed_d), hidden)
    load_tiles(place_ref, (cot_a, cot_b, cot_c, cot_d), grad_out)

    for block in range(2):
        win_out, chance_out, stripe_out = (
            (win0_out, chance0_out, stripe0_out),
            (win1_out, chance1_out, stripe1_out),
        )[block]
        attention_forward(
            block, hidden, gains, shifts, entry_w, entry_b, conv_k, conv_b, wide, stripe, win_out, chance_out
        )

        @pl.loop(0, 4)
        def _(t, block=block, stripe_out=stripe_out):
            rows = chunk(t)
            striped = stripe[rows, :].astype(BF)
            stripe_out[rows, :] = striped
            branch = dot_nn(striped, exit_w[block]) + exit_b[block : block + 1, :]
            midway = hidden[rows, :] + scale_rows(place_ref, mask_ref, 2 * block) * branch
            if block == 0:
                mid0_out[rows, :] = midway
            hat, inverse = norm_parts(midway)
            normed = (hat * gains[block, 1:2, :] + shifts[block, 1:2, :]).astype(BF)
            feed_scale = scale_rows(place_ref, mask_ref, 2 * block + 1)
            feed = shrink_b[block : block + 1, :]
            if block == 1:
                inner1[rows, :] = normed
                gradient = grad_out[rows, :]
                feed_delta = (feed_scale * gradient).astype(BF)
                feed1[rows, :] = feed_delta
                add_row(vec_out, 4, row_sums(feed_delta.astype(F32)))
                inner_delta = jnp.zeros((4 * PAD, width), F32)
            for part in range(hidden_units // width):
                at = slice(part * width, (part + 1) * width)
                pre_act = dot_nn(normed, expand_w[block, :, at]) + expand_b[block : block + 1, at]
                chance, density = gelu_parts(pre_act)
                active = (pre_act * chance).astype(BF)
                slope = chance + pre_act * density
                if block == 0:
                    active0_out[rows, at] = active
                    slope0_out[rows, at] = slope.astype(BF)
                else:
                    active1[rows, at] = active
                    pre_delta = (dot_nt(feed_delta, shrink_w[block, at, :]) * slope).astype(BF)
                    pre1[rows, at] = pre_delta
                    add_row(vec_out, part, row_sums(pre_delta.astype(F32)))
                    inner_delta = inner_delta + dot_nt(pre_delta, expand_w[block, :, at])
                feed = feed + dot_nn(active, shrink_w[block, at, :])
            output = midway + feed_scale * feed
            if block == 0:
                hidden[rows, :] = output
                hidden1_out[rows, :] = output
            else:
                store_tile(place_ref, (act_a, act_b, act_c, act_d), t, output)
                add_row(vec_out, 5, row_sums(inner_delta * hat))
                add_row(vec_out, 6, row_sums(inner_delta))
                grad_out[rows, :] = gradient + norm_back(
                    inner_delta, hat, inverse, gains[block, 1:2, :]
                )

    put_squares(bundle, 0, dot_tn(inner1[...], pre1[...]), width)
    for part in range(hidden_units // width):
        put_rows(
            bundle,
            hidden_units + part * width,
            dot_tn(active1[:, part * width : (part + 1) * width], feed1[...]),
        )


def delta_rows(block, place_ref, mask_ref, exit_w, grad_ref, stripe_delta, branch_delta, vec_out, at):
    @pl.loop(0, 4)
    def _(t):
        rows = chunk(t)
        rounded = (scale_rows(place_ref, mask_ref, 2 * block) * grad_ref[rows, :]).astype(BF)
        branch_delta[rows, :] = rounded
        add_row(vec_out, at, row_sums(rounded.astype(F32)))
        out = round_bf(dot_nt(rounded, exit_w[block]))
        stripe_delta[rows, :] = out
        add_row(vec_out, at + 1, row_sums(out))


def entry_backward(block, hidden_ref, gains, shifts, entry_w, grad_ref, wide, wide_bf, normed_bf, vec_out, at, emit):
    width = hidden_ref.shape[1]

    @pl.loop(0, 4)
    def _(t):
        rows = chunk(t)
        hat, inverse = norm_parts(hidden_ref[rows, :])
        normed_bf[rows, :] = (hat * gains[block, 0:1, :] + shifts[block, 0:1, :]).astype(BF)
        delta = jnp.zeros((4 * PAD, width), F32)
        for part in range(3):
            lanes = slice(part * width, (part + 1) * width)
            rounded = wide[rows, lanes].astype(BF)
            wide_bf[rows, lanes] = rounded
            if part != 1:
                add_row(vec_out, at + part // 2, row_sums(rounded.astype(F32)))
            delta = delta + dot_nt(rounded, entry_w[block, :, lanes])
        add_row(vec_out, at + 2, row_sums(delta * hat))
        add_row(vec_out, at + 3, row_sums(delta))
        emit(t, rows, grad_ref[rows, :] + norm_back(delta, hat, inverse, gains[block, 0:1, :]))


def second_kernel(
    place_ref,
    mask_ref,
    grad_in,
    hidden1,
    stripe1,
    win1,
    chance1,
    mid0,
    active0,
    slope0,
    stripe0,
    gains,
    shifts,
    entry_w,
    conv_k,
    exit_w,
    expand_w,
    shrink_w,
    keep_out,
    away_out,
    vec_out,
    conv_out,
    grad_out,
    stripe_delta_out,
    grad,
    stripe_delta,
    branch_delta,
    wide,
    wide_bf,
    normed_bf,
    feed0,
    pre0,
):
    width = grad.shape[1]
    hidden_units = expand_w.shape[2]
    bundle = (place_ref, keep_out, away_out)
    vec_out[...] = jnp.zeros(vec_out.shape, F32)
    conv_out[...] = jnp.zeros(conv_out.shape, F32)
    delta_rows(1, place_ref, mask_ref, exit_w, grad_in, stripe_delta, branch_delta, vec_out, 0)
    attention_backward(1, win1, chance1, conv_k, stripe_delta, wide, conv_out)

    def emit(t, rows, values):
        grad[rows, :] = values

    entry_backward(
        1, hidden1, gains, shifts, entry_w, grad_in, wide, wide_bf, normed_bf, vec_out, 2, emit
    )
    put_squares(bundle, 0, dot_tn(normed_bf[...], wide_bf[...]), width)
    put_rows(bundle, 3 * width, dot_tn(stripe1[...], branch_delta[...]))

    @pl.loop(0, 4)
    def _(t):
        rows = chunk(t)
        gradient = grad[rows, :]
        hat, inverse = norm_parts(mid0[rows, :])
        normed_bf[rows, :] = (hat * gains[0, 1:2, :] + shifts[0, 1:2, :]).astype(BF)
        feed_delta = (scale_rows(place_ref, mask_ref, 1) * gradient).astype(BF)
        feed0[rows, :] = feed_delta
        add_row(vec_out, 6, row_sums(feed_delta.astype(F32)))
        inner_delta = jnp.zeros((4 * PAD, width), F32)
        for part in range(hidden_units // width):
            at = slice(part * width, (part + 1) * width)
            pre_delta = (
                dot_nt(feed_delta, shrink_w[0, at, :]) * slope0[rows, at].astype(F32)
            ).astype(BF)
            pre0[rows, at] = pre_delta
            add_row(vec_out, 7 + part, row_sums(pre_delta.astype(F32)))
            inner_delta = inner_delta + dot_nt(pre_delta, expand_w[0, :, at])
        add_row(vec_out, 11, row_sums(inner_delta * hat))
        add_row(vec_out, 12, row_sums(inner_delta))
        grad[rows, :] = gradient + norm_back(inner_delta, hat, inverse, gains[0, 1:2, :])

    grad_out[...] = grad[...]
    put_squares(bundle, 4 * width, dot_tn(normed_bf[...], pre0[...]), width)
    for part in range(hidden_units // width):
        put_rows(
            bundle,
            (8 + part) * width,
            dot_tn(active0[:, part * width : (part + 1) * width], feed0[...]),
        )
    delta_rows(0, place_ref, mask_ref, exit_w, grad, stripe_delta_out, branch_delta, vec_out, 13)
    put_rows(bundle, 12 * width, dot_tn(stripe0[...], branch_delta[...]))


def third_kernel(
    place_ref,
    grad_in,
    stripe_delta,
    mixed_a,
    mixed_b,
    mixed_c,
    mixed_d,
    win0,
    chance0,
    gains,
    shifts,
    entry_w,
    conv_k,
    vec1,
    vec2,
    conv2,
    out_a,
    out_b,
    out_c,
    out_d,
    keep_out,
    away_out,
    hidden,
    wide,
    wide_bf,
    normed_bf,
    vec3,
    conv3,
    flat,
):
    width = hidden.shape[1]
    bundle = (place_ref, keep_out, away_out)
    vec3[...] = jnp.zeros(vec3.shape, F32)
    conv3[...] = jnp.zeros(conv3.shape, F32)
    load_tiles(place_ref, (mixed_a, mixed_b, mixed_c, mixed_d), hidden)
    attention_backward(0, win0, chance0, conv_k, stripe_delta, wide, conv3)

    def emit(t, rows, values):
        store_tile(place_ref, (out_a, out_b, out_c, out_d), t, values)

    entry_backward(
        0, hidden, gains, shifts, entry_w, grad_in, wide, wide_bf, normed_bf, vec3, 0, emit
    )
    flat[...] = jnp.zeros(flat.shape, F32)
    at = 0
    for ref in (vec1, vec2, conv2, vec3, conv3):
        flat[at : at + ref.shape[0], :] = jnp.sum(ref[...], axis=1)
        at += ref.shape[0]
    spread = dot_tn(normed_bf[...], wide_bf[...])
    half = keep_out.shape[0]
    middle = width // 2
    lots = flat.shape[0] // 2
    put_rows(bundle, 0, spread[:, :width])
    put_rows(bundle, width, spread[:middle, width : 2 * width])
    put_rows(bundle, width + middle, flat[:lots, :])
    put_rows(bundle, half, spread[middle:, width : 2 * width])
    put_rows(bundle, half + middle, spread[:, 2 * width :])
    put_rows(bundle, half + middle + width, flat[lots:, :])


def untangle(source, flat, target):
    count, width = source.shape[2:]
    lanes = flat.shape[0]
    for row in range(TILE):
        flat[:, pl.ds(row * 8 + 7, count, stride=PAD), :] = jnp.zeros((lanes, count, 128), F32)
        for col in range(TILE):
            token = source[row, col].astype(F32)
            for lane in range(lanes):
                flat[lane, pl.ds(row * 8 + col, count, stride=PAD), :] = token[
                    :, lane * 128 : (lane + 1) * 128
                ]

    @pl.loop(0, count)
    def _(n):
        rows = pl.ds(pl.multiple_of(n * PAD, 8), PAD)
        tile = jnp.concatenate([flat[lane, rows, :] for lane in range(lanes)], axis=1)
        target(n, tile.reshape(TILE, 8, width).astype(BF))


def owner_of(wanted, count):
    if count & (count - 1) == 0:
        return lax.shift_right_logical(wanted, count.bit_length() - 1)
    return lax.div(wanted, count)


def pick_kernel(
    place_ref, mix_ref, cut_ref, images_ref, index_out, take_out, sent_out, own_out, flat, counts
):
    count = images_ref.shape[2]
    slots = sent_out.shape[0]
    capacity = slots // counts.shape[0]
    me = place_ref[0]

    def put(n, tile):
        own_out[n] = tile

    untangle(images_ref, flat, put)

    @pl.loop(0, slots, unroll=8)
    def _(s):
        index_out[s] = count

    @pl.loop(0, counts.shape[0])
    def _(g):
        counts[g] = 0
        rank = g * capacity
        for ref in (mix_ref, cut_ref):
            for j in range(count):
                wanted = ref[g * count + j]
                owner = owner_of(wanted, count)
                hit = owner == me
                index_out[jnp.where(hit, rank, slots)] = wanted - owner * count
                rank = rank + hit.astype(jnp.int32)

    @pl.loop(0, slots)
    def _(s):
        sent_out[s] = own_out[jnp.minimum(index_out[s], count - 1)]

    for part, ref in enumerate((mix_ref, cut_ref)):

        @pl.loop(0, count)
        def _(j, part=part, ref=ref):
            owner = owner_of(ref[me * count + j], count)
            rank = counts[owner]
            take_out[part * count + j] = owner * capacity + rank
            counts[owner] = rank + 1


def deal_kernel(place_ref, source, out_a, out_b, out_c, out_d, flat):
    outs = (out_a, out_b, out_c, out_d)
    share = out_a.shape[0]

    def put(n, tile):
        for d, out in enumerate(outs):

            @pl.when(jnp.bitwise_xor(place_ref[3], d) == n // share)
            def _(out=out):
                out[n % share] = tile

    untangle(source, flat, put)


def inside_box(corner_ref, n, place_ref):
    shape = (TILE, 8, 1)
    row = place_ref[1] * TILE + lax.broadcasted_iota(jnp.int32, shape, 0)
    col = place_ref[2] * TILE + lax.broadcasted_iota(jnp.int32, shape, 1)
    hit = (
        (row >= corner_ref[0, n])
        & (row < corner_ref[1, n])
        & (col >= corner_ref[2, n])
        & (col < corner_ref[3, n])
    )
    return jnp.where(hit, 1.0, 0.0)


def mix_kernel(
    place_ref, take_ref, corner_ref, ratio_ref, arrived, own_ref, out_a, out_b, out_c, out_d
):
    count = own_ref.shape[0]
    share = out_a.shape[0]
    for d, out in enumerate((out_a, out_b, out_c, out_d)):

        @pl.loop(0, share)
        def _(i, d=d, out=out):
            n = jnp.bitwise_xor(place_ref[3], d) * share + i
            inside = inside_box(corner_ref, n, place_ref)
            ratio = ratio_ref[n]
            own = own_ref[n].astype(F32)
            blend = arrived[take_ref[n]].astype(F32)
            cut = arrived[take_ref[count + n]].astype(F32)
            mixed = inside * cut + (1.0 - inside) * (ratio * own + (1.0 - ratio) * blend)
            out[i] = mixed.astype(BF)


def split_kernel(
    place_ref, take_ref, corner_ref, ratio_ref, grad_a, grad_b, grad_c, grad_d, out_ref
):
    share = grad_a.shape[0]
    count = 4 * share
    if out_ref.shape[0] > 2 * count:
        out_ref[...] = jnp.zeros(out_ref.shape, BF)
    for d, grad_ref in enumerate((grad_a, grad_b, grad_c, grad_d)):

        @pl.loop(0, share)
        def _(i, d=d, grad_ref=grad_ref):
            n = jnp.bitwise_xor(place_ref[3], d) * share + i
            inside = inside_box(corner_ref, n, place_ref)
            gradient = grad_ref[i].astype(F32)
            cut = inside * gradient
            out_ref[take_ref[n]] = ((1.0 - ratio_ref[n]) * (gradient - cut)).astype(BF)
            out_ref[take_ref[count + n]] = cut.astype(BF)


def join_kernel(
    place_ref,
    index_ref,
    corner_ref,
    ratio_ref,
    grad_a,
    grad_b,
    grad_c,
    grad_d,
    back_ref,
    out_ref,
    total,
):
    count, width = out_ref.shape[2:]
    share = grad_a.shape[0]

    def tile_rows(n):
        return pl.ds(pl.multiple_of(n * PAD, 8), PAD)

    for d, grad_ref in enumerate((grad_a, grad_b, grad_c, grad_d)):

        @pl.loop(0, share)
        def _(i, d=d, grad_ref=grad_ref):
            n = jnp.bitwise_xor(place_ref[3], d) * share + i
            outside = 1.0 - inside_box(corner_ref, n, place_ref)
            kept = ratio_ref[n] * outside * grad_ref[i].astype(F32)
            kept = kept.reshape(PAD, width)
            for lane in range(total.shape[0]):
                total[lane, tile_rows(n), :] = kept[:, lane * 128 : (lane + 1) * 128]

    @pl.loop(0, back_ref.shape[0])
    def _(s):
        piece = back_ref[s].astype(F32).reshape(PAD, width)
        for lane in range(total.shape[0]):
            total[lane, tile_rows(index_ref[s]), :] += piece[:, lane * 128 : (lane + 1) * 128]

    for row in range(TILE):
        for col in range(TILE):
            out_ref[row, col] = jnp.concatenate(
                [
                    total[lane, pl.ds(row * 8 + col, count, stride=PAD), :]
                    for lane in range(total.shape[0])
                ],
                axis=1,
            )


def lay_kernel(place_ref, act_a, act_b, act_c, act_d, out_ref, flat):
    count, width = out_ref.shape[2:]
    share = act_a.shape[0]
    for d, act_ref in enumerate((act_a, act_b, act_c, act_d)):

        @pl.loop(0, share)
        def _(i, d=d, act_ref=act_ref):
            n = jnp.bitwise_xor(place_ref[3], d) * share + i
            tile = act_ref[i].astype(F32).reshape(PAD, width)
            for lane in range(flat.shape[0]):
                flat[lane, pl.ds(pl.multiple_of(n * PAD, 8), PAD), :] = tile[
                    :, lane * 128 : (lane + 1) * 128
                ]

    for row in range(TILE):
        for col in range(TILE):
            out_ref[row, col] = jnp.concatenate(
                [
                    flat[lane, pl.ds(row * 8 + col, count, stride=PAD), :]
                    for lane in range(flat.shape[0])
                ],
                axis=1,
            ).astype(BF)


def unpack_kernel(
    place_ref,
    mine1,
    other1,
    mine2,
    other2,
    gain_out,
    shift_out,
    entry_out,
    entry_b_out,
    conv_out,
    conv_b_out,
    exit_out,
    exit_b_out,
    expand_out,
    expand_b_out,
    shrink_out,
    shrink_b_out,
    vectors,
):
    width = exit_out.shape[1]
    units = expand_out.shape[2]
    upper = place_ref[2] == 1
    middle = width // 2

    def squares(out_ref, block, count):
        return [(out_ref, block, 0, part * width, width) for part in range(count)]

    def tall(out_ref, block, count):
        return [(out_ref, block, part * width, 0, width) for part in range(count)]

    plans = (
        squares(expand_out, 1, units // width) + tall(shrink_out, 1, units // width),
        squares(entry_out, 1, 3)
        + tall(exit_out, 1, 1)
        + squares(expand_out, 0, units // width)
        + tall(shrink_out, 0, units // width)
        + tall(exit_out, 0, 1),
        [
            (entry_out, 0, 0, 0, width),
            (entry_out, 0, 0, width, middle),
            (vectors, None, 0, 0, middle),
            (entry_out, 0, middle, width, middle),
            (entry_out, 0, 0, 2 * width, width),
        ],
    )
    total = sum(plan[4] for plan in plans[1])
    ranks = mine2.shape[0]
    cut = total // 2 // ranks
    for number, mine, other, base, count in (
        (0, mine1, other1, 0, mine1.shape[1]),
        (1, mine2, other2, 0, cut),
        (2, mine2, other2, cut, mine2.shape[1] - cut),
    ):
        pieces = []
        at = 0
        for out_ref, block, first_row, lane, length in plans[number]:
            done = 0
            while done < length:
                step = min(length - done, count - at % count)
                pieces.append((at, step, out_ref, block, first_row + done, lane))
                at += step
                done += step
        for at, step, out_ref, block, first_row, lane in pieces:
            shard, start = at // count, at % count
            half, shard = shard // ranks, shard % ranks
            if number > 0:
                shard = jnp.bitwise_xor(place_ref[4], shard)
            here = upper if half == 1 else jnp.logical_not(upper)
            rows = slice(base + start, base + start + step)
            values = jnp.where(
                here, mine[shard, rows, :].astype(F32), other[shard, rows, :].astype(F32)
            )
            place = slice(first_row, first_row + step)
            if block is None:
                out_ref[place, :] = values
            else:
                out_ref[block, place, lane : lane + width] = values

    def line(n):
        return vectors[n : n + 1, :]

    gain_out[0] = jnp.concatenate([line(33), line(18)], axis=0)
    gain_out[1] = jnp.concatenate([line(11), line(5)], axis=0)
    shift_out[0] = jnp.concatenate([line(34), line(19)], axis=0)
    shift_out[1] = jnp.concatenate([line(12), line(6)], axis=0)
    for part in range(2):
        lanes = slice(part * width, (part + 1) * width)
        entry_b_out[:, lanes] = jnp.concatenate([line(31 + part), line(9 + part)], axis=0)
    for i in range(3):
        for j in range(3):
            conv_out[i, j] = jnp.concatenate(
                [line(35 + 3 * i + j), line(22 + 3 * i + j)], axis=0
            )
    conv_b_out[...] = jnp.concatenate([line(21), line(8)], axis=0)
    exit_b_out[...] = jnp.concatenate([line(20), line(7)], axis=0)
    for part in range(units // width):
        lanes = slice(part * width, (part + 1) * width)
        expand_b_out[:, lanes] = jnp.concatenate([line(14 + part), line(part)], axis=0)
    shrink_b_out[...] = jnp.concatenate([line(13), line(4)], axis=0)


SMEM = pl.BlockSpec(memory_space=pltpu.SMEM)
VMEM = pl.BlockSpec(memory_space=pltpu.VMEM)


ANYWHERE = pl.BlockSpec(memory_space=pl.ANY)


def run(kernel, scalars, arrays, outs, scratch=(), flops=0, name=None, after=(), scalar_outs=()):
    given = len(scalars) + len(arrays)

    def body(*refs):
        kernel(*refs[:given], *refs[given + len(after) :])

    out_shape = [jax.ShapeDtypeStruct(shape, dtype) for shape, dtype in scalar_outs + tuple(outs)]
    moved = sum(a.size * a.dtype.itemsize for a in arrays)
    return pl.pallas_call(
        body,
        out_shape=out_shape,
        in_specs=[SMEM] * len(scalars) + [VMEM] * len(arrays) + [ANYWHERE] * len(after),
        out_specs=[SMEM] * len(scalar_outs) + [VMEM] * len(outs),
        scratch_shapes=[
            kind if dtype is None else pltpu.VMEM(kind, dtype) for kind, dtype in scratch
        ],
        compiler_params=pltpu.CompilerParams(vmem_limit_bytes=VMEM_BYTES),
        cost_estimate=pl.CostEstimate(flops=flops, bytes_accessed=moved, transcendentals=0),
        name=name,
    )(*scalars, *arrays, *after)


def gate(values, after):
    values, after = list(values), list(after)

    def body(*refs):
        del refs

    return pl.pallas_call(
        body,
        out_shape=[jax.ShapeDtypeStruct(v.shape, v.dtype) for v in values],
        in_specs=[ANYWHERE] * (len(values) + len(after)),
        out_specs=[ANYWHERE] * len(values),
        input_output_aliases={i: i for i in range(len(values))},
        name="gate",
    )(*values, *after)


def swap(values, axis):
    return lax.ppermute(values, axis, [(0, 1), (1, 0)])


def added(values, others):
    return (values.astype(F32) + others.astype(F32)).astype(BF)


def shards(values, ranks):
    return values.reshape(ranks, values.shape[0] // ranks, values.shape[1])


def spread_sum(pieces):
    mine = jnp.sum(pieces.astype(F32), axis=0).astype(BF)
    return jnp.broadcast_to(mine[None], pieces.shape)


def across(values, axes, size, mask):
    return lax.ppermute(values, axes, [(i, i ^ mask) for i in range(size)])


def deal(parts):
    return [parts[0]] + [across(parts[d], ("row", "col"), 4, d) for d in (1, 2, 3)]


RANKS = ("dp", "row")


def stages(ranks):
    bits = ranks.bit_length() - 1
    return [(bit, min(2, bits - bit)) for bit in range(0, bits, 2)]


def scatter_send(values, ranks, stage):
    bit, count = stage
    size = 1 << count
    me = (lax.axis_index(RANKS) >> bit) & (size - 1)
    cut = values.reshape(size, values.shape[0] // size, values.shape[1])
    return [lax.dynamic_index_in_dim(cut, me ^ d, 0, keepdims=False) for d in range(size)]


def scatter_move(parts, ranks, stage):
    return [parts[0]] + [
        across(parts[d], RANKS, ranks, d << stage[0]) for d in range(1, len(parts))
    ]


def scatter_sum(parts):
    return sum(part.astype(F32) for part in parts).astype(BF)


def gather(values, ranks, stage):
    return jnp.stack(
        [values]
        + [across(values, RANKS, ranks, d << stage[0]) for d in range(1, 1 << stage[1])]
    )


def rank_order(rank, ranks):
    order = 0
    for bit, count in stages(ranks):
        order = order * (1 << count) + ((rank >> bit) & ((1 << count) - 1))
    return order


def local(
    groups,
    images,
    cotangent,
    mix_partner,
    cut_partner,
    ratios,
    corners,
    drop_masks,
    norm_gains,
    norm_shifts,
    entry_weight,
    entry_bias,
    position_kernel,
    position_bias,
    exit_weight,
    exit_bias,
    expand_weight,
    expand_bias,
    shrink_weight,
    shrink_bias,
):
    images_here = images.shape[0]
    width = images.shape[3]
    units = expand_weight.shape[2]
    row, col = lax.axis_index("row"), lax.axis_index("col")
    share = images_here // 4
    rows = 4 * share * PAD
    ranks = 2 * groups
    capacity = (2 * images_here + groups - 1) // groups
    slots = groups * capacity
    order = rank_order(lax.axis_index(RANKS), ranks)
    place = jnp.stack([lax.axis_index("dp"), row, col, 2 * row + col, order]).astype(jnp.int32)
    quad = ((share, TILE, 8, width), BF)
    corners = corners.T
    masks = drop_masks.T
    flat = ((width // 128, images_here * PAD, 128), F32)
    index, take, outgoing, own = run(
        pick_kernel,
        [place, mix_partner, cut_partner],
        [images.transpose(1, 2, 0, 3)],
        [((slots, TILE, 8, width), BF), ((images_here, TILE, 8, width), BF)],
        [flat, (pltpu.SMEM((groups,), jnp.int32), None)],
        name="pick",
        scalar_outs=(((slots + 8,), jnp.int32), ((2 * images_here,), jnp.int32)),
    )
    arrived = lax.all_to_all(outgoing, "dp", split_axis=0, concat_axis=0, tiled=True)
    cot = deal(
        run(deal_kernel, [place], [cotangent.transpose(1, 2, 0, 3)], [quad] * 4, [flat], name="deal")
    )
    mixed = deal(
        run(
            mix_kernel,
            [place, take, corners, ratios],
            [arrived, own],
            [quad] * 4,
            name="mix",
            after=cot,
        )
    )
    conv_k = position_kernel.transpose(1, 2, 0, 3)
    tall = (rows, width)
    (
        act_a,
        act_b,
        act_c,
        act_d,
        keep1,
        away1,
        vec1,
        active0,
        slope0,
        win0,
        chance0,
        stripe0,
        mid0,
        win1,
        chance1,
        stripe1,
        hidden1,
        grad1,
    ) = run(
        first_kernel,
        [place, masks],
        [
            *mixed,
            *cot,
            norm_gains,
            norm_shifts,
            entry_weight,
            entry_bias,
            conv_k,
            position_bias,
            exit_weight,
            exit_bias,
            expand_weight,
            expand_bias,
            shrink_weight,
            shrink_bias,
        ],
        [
            *([quad] * 4),
            ((units, width), BF),
            ((units, width), BF),
            ((7, 8, width), F32),
            ((rows, units), BF),
            ((rows, units), BF),
            ((4 * share, WIN, 3 * HALF), BF),
            ((4 * share, WIN, LANES), BF),
            (tall, BF),
            (tall, F32),
            ((4 * share, WIN, 3 * HALF), BF),
            ((4 * share, WIN, LANES), BF),
            (tall, BF),
            (tall, F32),
            (tall, F32),
        ],
        [
            (tall, F32),
            ((rows, 3 * width), F32),
            (tall, F32),
            ((rows, units), BF),
            ((rows, units), BF),
            (tall, BF),
            (tall, BF),
        ],
        flops=10 * rows * width * width * 120,
        name="first",
    )
    sent1 = shards(added(keep1, swap(away1, "col")), ranks)
    pieces1 = lax.all_to_all(sent1, RANKS, split_axis=0, concat_axis=0, tiled=True)
    act = deal([act_a, act_b, act_c, act_d])
    keep2, away2, vec2, conv2, grad0, delta0 = run(
        second_kernel,
        [place, masks],
        [
            grad1,
            hidden1,
            stripe1,
            win1,
            chance1,
            mid0,
            active0,
            slope0,
            stripe0,
            norm_gains,
            norm_shifts,
            entry_weight,
            conv_k,
            exit_weight,
            expand_weight,
            shrink_weight,
        ],
        [
            ((13 * width // 2, width), BF),
            ((13 * width // 2, width), BF),
            ((15, 8, width), F32),
            ((9, 8, width), F32),
            (tall, F32),
            (tall, F32),
        ],
        [
            (tall, F32),
            (tall, F32),
            (tall, BF),
            ((rows, 3 * width), F32),
            ((rows, 3 * width), BF),
            (tall, BF),
            (tall, BF),
            ((rows, units), BF),
        ],
        flops=6 * rows * width * width * 120,
        name="second",
        after=[sent1],
    )
    keep2, away2, grad0, delta0 = gate([keep2, away2, grad0, delta0], [pieces1, *act])
    spread1 = spread_sum(pieces1)
    steps = stages(ranks)
    parts2 = scatter_send(added(keep2, swap(away2, "col")), ranks, steps[0])
    moved2 = scatter_move(parts2, ranks, steps[0])
    *out_tiles, keep3, away3 = run(
        third_kernel,
        [place],
        [
            grad0,
            delta0,
            *mixed,
            win0,
            chance0,
            norm_gains,
            norm_shifts,
            entry_weight,
            conv_k,
            vec1,
            vec2,
            conv2,
        ],
        [quad] * 4 + [((2 * width, width), BF), ((2 * width, width), BF)],
        [
            (tall, F32),
            ((rows, 3 * width), F32),
            ((rows, 3 * width), BF),
            (tall, BF),
            ((4, 8, width), F32),
            ((9, 8, width), F32),
            ((width, width), F32),
        ],
        flops=3 * rows * width * width * 120,
        name="third",
        after=parts2,
    )
    *held, keep3, away3 = gate([*moved2, keep3, away3], [])
    moved2 = held
    gradient = deal(out_tiles)
    (parted,) = run(
        split_kernel,
        [place, take, corners, ratios],
        gradient,
        [((slots, TILE, 8, width), BF)],
        name="split",
    )
    back = lax.all_to_all(parted, "dp", split_axis=0, concat_axis=0, tiled=True)
    (input_gradient,) = run(
        join_kernel,
        [place, index, corners, ratios],
        [*gradient, back],
        [((TILE, TILE, images_here, width), F32)],
        [((width // 128, (images_here + 1) * PAD, 128), F32)],
        name="join",
    )
    full1 = lax.all_to_all(spread1, RANKS, split_axis=0, concat_axis=0, tiled=True)
    mine2 = scatter_sum(moved2)
    moved3 = scatter_move(
        scatter_send(added(keep3, swap(away3, "col")), ranks, steps[0]), ranks, steps[0]
    )
    mine3 = scatter_sum(moved3)
    cut = mine2.shape[0] * 4 // ranks
    lot = mine3.shape[0] * 4 // ranks
    joint = jnp.concatenate(
        [
            mine2.reshape(ranks // 4, cut, width),
            mine3.reshape(ranks // 4, lot, width),
        ],
        axis=1,
    ).reshape(-1, width)
    for step in steps[1:]:
        joint = scatter_sum(scatter_move(scatter_send(joint, ranks, step), ranks, step))
    for step in reversed(steps):
        joint = gather(joint, ranks, step).reshape(-1, width)
    joint = shards(joint, ranks)
    full = [full1, swap(full1, "col"), joint, swap(joint, "col")]
    (activations,) = run(
        lay_kernel, [place], act, [((TILE, TILE, images_here, width), BF)], [flat], name="lay"
    )
    gains, shifts, entry, entry_b, conv, conv_b, exit_, exit_b, expand, expand_b, shrink, shrink_b = run(
        unpack_kernel,
        [place],
        full,
        [
            ((2, 2, width), F32),
            ((2, 2, width), F32),
            ((2, width, 3 * width), F32),
            ((2, 2 * width), F32),
            ((3, 3, 2, width), F32),
            ((2, width), F32),
            ((2, width, width), F32),
            ((2, width), F32),
            ((2, width, units), F32),
            ((2, units), F32),
            ((2, units, width), F32),
            ((2, width), F32),
        ],
        [((width // 2, width), F32)],
        name="unpack",
    )
    return (
        activations.transpose(2, 0, 1, 3),
        input_gradient.transpose(2, 0, 1, 3),
        gains,
        shifts,
        entry,
        entry_b,
        conv.transpose(2, 0, 1, 3),
        conv_b,
        exit_,
        exit_b,
        expand,
        expand_b,
        shrink,
        shrink_b,
    )


def solution(mesh):
    tiles = P("dp", "row", "col", None)
    return jax.shard_map(
        functools.partial(local, mesh.shape["dp"]),
        mesh=mesh,
        in_specs=(tiles, tiles, P(), P(), P("dp"), P("dp", None), P("dp", None)) + (P(),) * 12,
        out_specs=(tiles, tiles) + (P(),) * 12,
        check_vma=False,
    )
```

```python
import functools

import jax
import jax.numpy as jnp
from jax import lax
from jax.experimental import pallas as pl
from jax.experimental.pallas import tpu as pltpu
from jax.sharding import PartitionSpec as P

TILE = 7
PAD = 56
HEAD_DIM = 32
SIDE_HEADS = 4
HALF = 128
WIN = 2 * PAD
CHUNK = 8 * PAD
LANES = SIDE_HEADS * 128
SCALE = HEAD_DIM ** (-0.5)
LOG2E = 1.4426950408889634
EPS = 1e-05
BF = jnp.bfloat16
F32 = jnp.float32
VMEM_BYTES = 60 * 1024 * 1024


def dot_nn(a, b):
    return lax.dot_general(a, b, (((1,), (0,)), ((), ())), preferred_element_type=F32)


def dot_nt(a, b):
    return lax.dot_general(a, b, (((1,), (1,)), ((), ())), preferred_element_type=F32)


def dot_tn(a, b):
    return lax.dot_general(a, b, (((0,), (0,)), ((), ())), preferred_element_type=F32)


def norm_parts(values):
    centered = values - jnp.mean(values, axis=-1, keepdims=True)
    inverse = lax.rsqrt(jnp.mean(centered * centered, axis=-1, keepdims=True) + EPS)
    return centered * inverse, inverse


def norm_back(delta, hat, inverse, gain):
    scaled = delta * gain
    first = jnp.mean(scaled, axis=-1, keepdims=True)
    second = jnp.mean(scaled * hat, axis=-1, keepdims=True)
    return inverse * (scaled - first - hat * second)


def gelu_parts(values):
    size = jnp.abs(values) * (0.5**0.5)
    fall = jnp.exp(-(size * size))
    step = 1.0 / (1.0 + 0.3275911 * size)
    series = step * (
        0.254829592
        + step * (-0.284496736 + step * (1.421413741 + step * (-1.453152027 + step * 1.061405429)))
    )
    tail = 0.5 * series * fall
    chance = jnp.where(values >= 0.0, 1.0 - tail, tail)
    return chance, fall * 0.3989422804014327


def row_sums(values):
    count, width = values.shape
    return jnp.sum(values.reshape(count // 8, 8, width), axis=0)


def scale_rows(place_ref, mask_ref, column):
    scales = [
        mask_ref[column, 4 * place_ref[3] + i].astype(F32) * 1.25 for i in range(4)
    ]
    columns = [jnp.full((PAD, 1), scale, F32) for scale in scales]
    return jnp.concatenate(columns * (CHUNK // (4 * PAD)), axis=0)


def add_row(acc_ref, row, values):
    acc_ref[row] += values


def spread_heads(values):
    lane = lax.broadcasted_iota(jnp.int32, values.shape, 1) // HEAD_DIM
    empty = jnp.zeros((128 - WIN, HALF), F32)
    blocks = []
    for head in range(SIDE_HEADS):
        blocks.append(jnp.where(lane == head, values, 0.0))
        blocks.append(empty)
    return jnp.concatenate(blocks, axis=0).astype(BF)


def gather_heads(wide):
    picked = jnp.concatenate(
        [
            wide[head * HEAD_DIM : (head + 1) * HEAD_DIM, head * 128 : (head + 1) * 128]
            for head in range(SIDE_HEADS)
        ],
        axis=0,
    )
    return picked.T[:WIN]


def turned(values):
    return jnp.concatenate([values, jnp.zeros((128 - WIN, HALF), F32)], axis=0).T.astype(BF)


def fill_rows(values):
    empty = jnp.zeros((128 - WIN, values.shape[1]), values.dtype)
    return jnp.concatenate([values, empty], axis=0)


def valid_column(shape):
    return lax.broadcasted_iota(jnp.int32, shape, 1) != 7


def valid_rows(shape):
    return lax.broadcasted_iota(jnp.int32, shape, 0) % 8 != 7


def column_shifts(values, across):
    cube = values.reshape(2 * TILE, 8, HALF)
    if not across:
        return (pltpu.roll(cube, 1, 1), cube, pltpu.roll(cube, 7, 1))
    left, right = cube[:TILE], cube[TILE:]
    column = lax.broadcasted_iota(jnp.int32, left.shape, 1)
    before = jnp.concatenate(
        [
            pltpu.roll(left, 1, 1),
            jnp.where(column == 0, pltpu.roll(left, 2, 1), pltpu.roll(right, 1, 1)),
        ],
        axis=0,
    )
    after = jnp.concatenate(
        [
            jnp.where(column == 6, pltpu.roll(right, 6, 1), pltpu.roll(left, 7, 1)),
            pltpu.roll(right, 7, 1),
        ],
        axis=0,
    )
    return (before, cube, after)


def row_shift(cube, step, across):
    if step == 0:
        return cube
    empty = jnp.zeros((1, 8, HALF), F32)

    def move(part):
        if step < 0:
            return jnp.concatenate([empty, part[:-1]], axis=0)
        return jnp.concatenate([part[1:], empty], axis=0)

    if across:
        return jnp.concatenate([move(cube[:TILE]), move(cube[TILE:])], axis=0)
    return move(cube)


def window_conv(shifts, kernel_at, across):
    total = None
    for i in range(3):
        part = None
        for j in range(3):
            term = kernel_at(i, j) * shifts[j]
            part = term if part is None else part + term
        part = row_shift(part, i - 1, across)
        total = part if total is None else total + part
    return total.reshape(WIN, HALF)


def window_rows(across, window):
    side, image = window // 4, window % 4
    if across:
        first, second = 2 * side, 2 * side + 1
    else:
        first, second = side, 2 + side
    return (
        pl.multiple_of((first * 4 + image) * PAD, 8),
        pl.multiple_of((second * 4 + image) * PAD, 8),
    )


def take_window(ref, at, lane):
    return jnp.concatenate(
        [ref[pl.ds(at[0], PAD), lane : lane + HALF], ref[pl.ds(at[1], PAD), lane : lane + HALF]],
        axis=0,
    )


def put_window(ref, at, lane, values):
    ref[pl.ds(at[0], PAD), lane : lane + HALF] = values[:PAD]
    ref[pl.ds(at[1], PAD), lane : lane + HALF] = values[PAD:]


def round_bf(values):
    return values.astype(BF).astype(F32)


def attention_forward(
    block, hidden_ref, gains, shifts, entry_w, entry_b, conv_k, conv_b, wide, stripe, win_out, chance_out
):
    width = hidden_ref.shape[1]

    @pl.loop(0, 2)
    def _(t):
        rows = chunk(t)
        hat, _ = norm_parts(hidden_ref[rows, :])
        normed = (hat * gains[block, 0:1, :] + shifts[block, 0:1, :]).astype(BF)
        for part in range(3):
            out = dot_nn(normed, entry_w[block, :, part * width : (part + 1) * width])
            if part != 1:
                at = 0 if part == 0 else width
                out = out + entry_b[block : block + 1, at : at + width]
            wide[rows, part * width : (part + 1) * width] = round_bf(out)

    for direction in range(2):
        across = direction == 0
        lane = direction * HALF

        @pl.loop(0, 8, unroll=4)
        def _(window, across=across, lane=lane, direction=direction):
            at = window_rows(across, window)
            queries = take_window(wide, at, lane)
            keys = take_window(wide, at, width + lane)
            values = take_window(wide, at, 2 * width + lane)
            keys_bf = keys.astype(BF)
            win_out[direction * 8 + window, :, 0:HALF] = queries.astype(BF)
            win_out[direction * 8 + window, :, HALF : 2 * HALF] = keys_bf
            win_out[direction * 8 + window, :, 2 * HALF : 3 * HALF] = values.astype(BF)
            scores = dot_nt(keys_bf, spread_heads(queries)).reshape(2 * TILE, 8, LANES)
            scores = jnp.where(valid_column((1, 8, LANES)), scores, -1e30)
            top = jnp.max(jnp.max(scores, axis=0), axis=0, keepdims=True)
            lifted = jnp.exp2((scores - top) * (SCALE * LOG2E))
            totals = jnp.sum(jnp.sum(lifted, axis=0), axis=0, keepdims=True)
            chances = (lifted * (1.0 / totals)).reshape(WIN, LANES).astype(BF)
            chance_out[direction * 8 + window] = chances
            attended = gather_heads(dot_nn(turned(values), fill_rows(chances)))
            clean = jnp.where(valid_rows(values.shape), values, 0.0)
            position = window_conv(
                column_shifts(clean, across),
                lambda i, j: conv_k[i, j, block : block + 1, lane : lane + HALF],
                across,
            )
            put_window(
                stripe, at, lane, attended + position + conv_b[block : block + 1, lane : lane + HALF]
            )


def attention_backward(
    block,
    win_in,
    chance_in,
    conv_k,
    stripe_delta,
    wide,
    conv_acc,
):
    width = stripe_delta.shape[1]
    for direction in range(2):
        across = direction == 0
        lane = direction * HALF

        @pl.loop(0, 8, unroll=4)
        def _(window, across=across, lane=lane, direction=direction):
            at = window_rows(across, window)
            out_delta = take_window(stripe_delta, at, lane)
            queries = win_in[direction * 8 + window, :, 0:HALF].astype(F32)
            keys = win_in[direction * 8 + window, :, HALF : 2 * HALF].astype(F32)
            values_bf = win_in[direction * 8 + window, :, 2 * HALF : 3 * HALF]
            values = values_bf.astype(F32)
            chances = chance_in[direction * 8 + window]
            delta_spread = spread_heads(out_delta)
            chance_delta = dot_nt(values_bf, delta_spread)
            cubes = (2 * TILE, 8, LANES)
            wide_chances = chances.astype(F32).reshape(cubes)
            weighted = wide_chances * chance_delta.reshape(cubes)
            common = jnp.sum(jnp.sum(weighted, axis=0), axis=0, keepdims=True)
            score_delta = (weighted - wide_chances * common).reshape(WIN, LANES).astype(BF)
            values_delta = dot_nn(chances, delta_spread)
            keys_delta = dot_nn(score_delta, spread_heads(queries)) * SCALE
            query_delta = gather_heads(dot_nn(turned(keys), fill_rows(score_delta))) * SCALE
            keep = valid_rows(values.shape)
            clean = jnp.where(keep, values, 0.0)
            shifts = column_shifts(clean, across)
            cube = out_delta.reshape(2 * TILE, 8, HALF)
            for i in range(3):
                moved = row_shift(cube, 1 - i, across)
                for j in range(3):
                    conv_acc[3 * i + j, :, lane : lane + HALF] += jnp.sum(moved * shifts[j], axis=0)
            back = window_conv(
                column_shifts(out_delta, across),
                lambda i, j: conv_k[2 - i, 2 - j, block : block + 1, lane : lane + HALF],
                across,
            )
            values_delta = jnp.where(keep, values_delta + back, 0.0)
            put_window(wide, at, lane, query_delta)
            put_window(wide, at, width + lane, keys_delta)
            put_window(wide, at, 2 * width + lane, values_delta)


def chunk(t):
    return pl.ds(pl.multiple_of(t * CHUNK, CHUNK), CHUNK)


class Bundle:
    def __init__(self, place_ref, keep, away, chunks=1, spot=lambda chunk: chunk):
        self.place_ref, self.keep, self.away = place_ref, keep, away
        self.step, self.spot = keep.shape[0] // chunks, spot

    def put(self, at, values):
        values = values.astype(BF)
        half, step = self.keep.shape[0], self.step
        last = at + values.shape[0]
        first = at
        while first < last:
            stop = min(last, (first // step + 1) * step)
            number = first // half
            start = self.spot(first % half // step) * step
            inner, count = first % step, stop - first
            if not isinstance(start, int):
                start = pl.multiple_of(start, step)
            rows = pl.ds(start + inner, count)
            piece = values[first - at : stop - at]

            @pl.when(self.place_ref[2] == number)
            def _(piece=piece, rows=rows):
                self.keep[rows, :] = piece

            @pl.when(self.place_ref[2] != number)
            def _(piece=piece, rows=rows):
                self.away[rows, :] = piece

            first = stop


def put_squares(bundle, at, values, side):
    for part in range(values.shape[1] // side):
        bundle.put(at + part * side, values[:, part * side : (part + 1) * side])


def load_tiles(place_ref, tiles, hidden):
    for d, tile in enumerate(tiles):
        at = jnp.bitwise_xor(place_ref[3], d) * (4 * PAD)
        rows = pl.ds(pl.multiple_of(at, 4 * PAD), 4 * PAD)
        hidden[rows, :] = tile[...].astype(F32).reshape(4 * PAD, hidden.shape[1])


def store_tile(place_ref, tiles, t, values):
    count = CHUNK // (4 * PAD)
    values = values.reshape((count,) + tiles[0].shape).astype(BF)
    for part in range(count):
        for d, tile in enumerate(tiles):

            @pl.when(jnp.bitwise_xor(place_ref[3], d) == count * t + part)
            def _(tile=tile, part=part):
                tile[...] = values[part]


def first_kernel(
    spots,
    moves,
    place_ref,
    mask_ref,
    mixed_a,
    mixed_b,
    mixed_c,
    mixed_d,
    gains,
    shifts,
    entry_b,
    conv_k,
    conv_b,
    exit_b,
    expand_b,
    shrink_b,
    entry_w,
    exit_w,
    expand_w,
    shrink_w,
    cot_a,
    cot_b,
    cot_c,
    cot_d,
    vec_out,
    act_a,
    act_b,
    act_c,
    act_d,
    keep_out,
    away_out,
    active0_out,
    slope0_out,
    win0_out,
    chance0_out,
    stripe0_out,
    mid0_out,
    win1_out,
    chance1_out,
    stripe1_out,
    hidden1_out,
    grad_out,
    hidden,
    wide,
    stripe,
    active1,
    pre1,
    feed1,
    inner1,
):
    width = hidden.shape[1]
    hidden_units = expand_w.shape[2]
    bundle = Bundle(place_ref, keep_out, away_out, len(spots), lambda chunk: spots[chunk])
    vec_out[...] = jnp.zeros(vec_out.shape, F32)
    load_tiles(place_ref, (mixed_a, mixed_b, mixed_c, mixed_d), hidden)
    moves.need(entry_w)

    for block in range(2):
        win_out, chance_out, stripe_out = (
            (win0_out, chance0_out, stripe0_out),
            (win1_out, chance1_out, stripe1_out),
        )[block]
        attention_forward(
            block, hidden, gains, shifts, entry_w, entry_b, conv_k, conv_b, wide, stripe, win_out, chance_out
        )
        moves.send(win_out, chance_out)
        moves.need(exit_w, expand_w, shrink_w)
        if block == 1:
            moves.need(cot_a, cot_b, cot_c, cot_d)
            load_tiles(place_ref, (cot_a, cot_b, cot_c, cot_d), grad_out)

        @pl.loop(0, 2)
        def _(t, block=block, stripe_out=stripe_out):
            rows = chunk(t)
            striped = stripe[rows, :].astype(BF)
            stripe_out[rows, :] = striped
            branch = dot_nn(striped, exit_w[block]) + exit_b[block : block + 1, :]
            midway = hidden[rows, :] + scale_rows(place_ref, mask_ref, 2 * block) * branch
            if block == 0:
                mid0_out[rows, :] = midway
            hat, inverse = norm_parts(midway)
            normed = (hat * gains[block, 1:2, :] + shifts[block, 1:2, :]).astype(BF)
            feed_scale = scale_rows(place_ref, mask_ref, 2 * block + 1)
            feed = shrink_b[block : block + 1, :]
            if block == 1:
                inner1[rows, :] = normed
                gradient = grad_out[rows, :]
                feed_delta = (feed_scale * gradient).astype(BF)
                feed1[rows, :] = feed_delta
                add_row(vec_out, 4, row_sums(feed_delta.astype(F32)))
                inner_delta = jnp.zeros((CHUNK, width), F32)
            for part in range(hidden_units // width):
                at = slice(part * width, (part + 1) * width)
                pre_act = dot_nn(normed, expand_w[block, :, at]) + expand_b[block : block + 1, at]
                chance, density = gelu_parts(pre_act)
                active = (pre_act * chance).astype(BF)
                slope = chance + pre_act * density
                if block == 0:
                    active0_out[rows, at] = active
                    slope0_out[rows, at] = slope.astype(BF)
                else:
                    active1[rows, at] = active
                    pre_delta = (dot_nt(feed_delta, shrink_w[block, at, :]) * slope).astype(BF)
                    pre1[rows, at] = pre_delta
                    add_row(vec_out, part, row_sums(pre_delta.astype(F32)))
                    inner_delta = inner_delta + dot_nt(pre_delta, expand_w[block, :, at])
                feed = feed + dot_nn(active, shrink_w[block, at, :])
            output = midway + feed_scale * feed
            if block == 0:
                hidden[rows, :] = output
                hidden1_out[rows, :] = output
            else:
                store_tile(place_ref, (act_a, act_b, act_c, act_d), t, output)
                add_row(vec_out, 5, row_sums(inner_delta * hat))
                add_row(vec_out, 6, row_sums(inner_delta))
                grad_out[rows, :] = gradient + norm_back(
                    inner_delta, hat, inverse, gains[block, 1:2, :]
                )

        moves.send(stripe_out)
        if block == 0:
            moves.send(mid0_out, active0_out, slope0_out, hidden1_out)
        else:
            moves.send(act_a, act_b, act_c, act_d, grad_out)

    put_squares(bundle, 0, dot_tn(inner1[...], pre1[...]), width)
    for part in range(hidden_units // width):
        bundle.put(
            hidden_units + part * width,
            dot_tn(active1[:, part * width : (part + 1) * width], feed1[...]),
        )


def delta_rows(block, place_ref, mask_ref, exit_w, grad_ref, stripe_delta, branch_delta, vec_out, at):
    @pl.loop(0, 2)
    def _(t):
        rows = chunk(t)
        rounded = (scale_rows(place_ref, mask_ref, 2 * block) * grad_ref[rows, :]).astype(BF)
        branch_delta[rows, :] = rounded
        add_row(vec_out, at, row_sums(rounded.astype(F32)))
        out = round_bf(dot_nt(rounded, exit_w[block]))
        stripe_delta[rows, :] = out
        add_row(vec_out, at + 1, row_sums(out))


def entry_backward(block, hidden_ref, gains, shifts, entry_w, grad_ref, wide, wide_bf, normed_bf, vec_out, at, emit):
    width = hidden_ref.shape[1]

    @pl.loop(0, 2)
    def _(t):
        rows = chunk(t)
        hat, inverse = norm_parts(hidden_ref[rows, :])
        normed_bf[rows, :] = (hat * gains[block, 0:1, :] + shifts[block, 0:1, :]).astype(BF)
        delta = jnp.zeros((CHUNK, width), F32)
        for part in range(3):
            lanes = slice(part * width, (part + 1) * width)
            rounded = wide[rows, lanes].astype(BF)
            wide_bf[rows, lanes] = rounded
            if part != 1:
                add_row(vec_out, at + part // 2, row_sums(rounded.astype(F32)))
            delta = delta + dot_nt(rounded, entry_w[block, :, lanes])
        add_row(vec_out, at + 2, row_sums(delta * hat))
        add_row(vec_out, at + 3, row_sums(delta))
        emit(t, rows, grad_ref[rows, :] + norm_back(delta, hat, inverse, gains[block, 0:1, :]))


def second_kernel(
    moves,
    place_ref,
    mask_ref,
    gains,
    shifts,
    conv_k,
    grad_in,
    exit_w,
    win1,
    chance1,
    hidden1,
    entry_w,
    stripe1,
    mid0,
    shrink_w,
    slope0,
    expand_w,
    active0,
    stripe0,
    vec_out,
    conv_out,
    grad_out,
    stripe_delta_out,
    keep_out,
    away_out,
    stripe_delta,
    branch_delta,
    wide,
    wide_bf,
    normed_bf,
    feed0,
    pre0,
):
    grad = grad_out
    width = grad.shape[1]
    hidden_units = expand_w.shape[2]
    bundle = Bundle(
        place_ref, keep_out, away_out, 4, lambda chunk: jnp.bitwise_xor(place_ref[5], chunk)
    )
    vec_out[...] = jnp.zeros(vec_out.shape, F32)
    conv_out[...] = jnp.zeros(conv_out.shape, F32)
    moves.need(grad_in, exit_w)
    delta_rows(1, place_ref, mask_ref, exit_w, grad_in, stripe_delta, branch_delta, vec_out, 0)
    moves.need(win1, chance1)
    attention_backward(1, win1, chance1, conv_k, stripe_delta, wide, conv_out)

    def emit(t, rows, values):
        grad[rows, :] = values

    moves.need(hidden1, entry_w)
    entry_backward(
        1, hidden1, gains, shifts, entry_w, grad_in, wide, wide_bf, normed_bf, vec_out, 2, emit
    )
    put_squares(bundle, 0, dot_tn(normed_bf[...], wide_bf[...]), width)
    moves.need(stripe1)
    bundle.put(3 * width, dot_tn(stripe1[...], branch_delta[...]))
    moves.need(mid0, shrink_w, slope0, expand_w)

    @pl.loop(0, 2)
    def _(t):
        rows = chunk(t)
        gradient = grad[rows, :]
        hat, inverse = norm_parts(mid0[rows, :])
        normed_bf[rows, :] = (hat * gains[0, 1:2, :] + shifts[0, 1:2, :]).astype(BF)
        feed_delta = (scale_rows(place_ref, mask_ref, 1) * gradient).astype(BF)
        feed0[rows, :] = feed_delta
        add_row(vec_out, 6, row_sums(feed_delta.astype(F32)))
        inner_delta = jnp.zeros((CHUNK, width), F32)
        for part in range(hidden_units // width):
            at = slice(part * width, (part + 1) * width)
            pre_delta = (
                dot_nt(feed_delta, shrink_w[0, at, :]) * slope0[rows, at].astype(F32)
            ).astype(BF)
            pre0[rows, at] = pre_delta
            add_row(vec_out, 7 + part, row_sums(pre_delta.astype(F32)))
            inner_delta = inner_delta + dot_nt(pre_delta, expand_w[0, :, at])
        add_row(vec_out, 11, row_sums(inner_delta * hat))
        add_row(vec_out, 12, row_sums(inner_delta))
        grad[rows, :] = gradient + norm_back(inner_delta, hat, inverse, gains[0, 1:2, :])

    delta_rows(0, place_ref, mask_ref, exit_w, grad, stripe_delta_out, branch_delta, vec_out, 13)
    moves.send(grad_out, stripe_delta_out)
    moves.need(active0, stripe0)
    put_squares(bundle, 4 * width, dot_tn(normed_bf[...], pre0[...]), width)
    for part in range(hidden_units // width):
        bundle.put(
            (8 + part) * width,
            dot_tn(active0[:, part * width : (part + 1) * width], feed0[...]),
        )
    bundle.put(12 * width, dot_tn(stripe0[...], branch_delta[...]))


def third_kernel(
    moves,
    place_ref,
    gains,
    shifts,
    conv_k,
    vec1,
    vec2,
    conv2,
    stripe_delta,
    win0,
    chance0,
    mixed_a,
    mixed_b,
    mixed_c,
    mixed_d,
    entry_w,
    grad_in,
    out_a,
    out_b,
    out_c,
    out_d,
    keep_out,
    away_out,
    hidden,
    wide,
    wide_bf,
    normed_bf,
    vec3,
    conv3,
    flat,
):
    width = hidden.shape[1]
    bundle = Bundle(
        place_ref, keep_out, away_out, 4, lambda chunk: jnp.bitwise_xor(place_ref[5], chunk)
    )
    vec3[...] = jnp.zeros(vec3.shape, F32)
    conv3[...] = jnp.zeros(conv3.shape, F32)
    moves.need(stripe_delta, win0, chance0)
    attention_backward(0, win0, chance0, conv_k, stripe_delta, wide, conv3)

    def emit(t, rows, values):
        store_tile(place_ref, (out_a, out_b, out_c, out_d), t, values)

    moves.need(mixed_a, mixed_b, mixed_c, mixed_d, entry_w, grad_in)
    load_tiles(place_ref, (mixed_a, mixed_b, mixed_c, mixed_d), hidden)
    entry_backward(
        0, hidden, gains, shifts, entry_w, grad_in, wide, wide_bf, normed_bf, vec3, 0, emit
    )
    moves.send(out_a, out_b, out_c, out_d)
    flat[...] = jnp.zeros(flat.shape, F32)
    at = 0
    for ref in (vec1, vec2, conv2, vec3, conv3):
        flat[at : at + ref.shape[0], :] = jnp.sum(ref[...], axis=1)
        at += ref.shape[0]
    spread = dot_tn(normed_bf[...], wide_bf[...])
    half = keep_out.shape[0]
    middle = width // 2
    lots = flat.shape[0] // 2
    bundle.put(0, spread[:, :width])
    bundle.put(width, spread[:middle, width : 2 * width])
    bundle.put(width + middle, flat[:lots, :])
    bundle.put(half, spread[middle:, width : 2 * width])
    bundle.put(half + middle, spread[:, 2 * width :])
    bundle.put(half + middle + width, flat[lots:, :])


def untangle(source, flat, target):
    count, width = source.shape[2:]
    lanes = flat.shape[0]
    for row in range(TILE):
        flat[:, pl.ds(row * 8 + 7, count, stride=PAD), :] = jnp.zeros((lanes, count, 128), F32)
        for col in range(TILE):
            token = source[row, col].astype(F32)
            for lane in range(lanes):
                flat[lane, pl.ds(row * 8 + col, count, stride=PAD), :] = token[
                    :, lane * 128 : (lane + 1) * 128
                ]

    @pl.loop(0, count)
    def _(n):
        rows = pl.ds(pl.multiple_of(n * PAD, 8), PAD)
        tile = jnp.concatenate([flat[lane, rows, :] for lane in range(lanes)], axis=1)
        target(n, tile.reshape(TILE, 8, width).astype(BF))


def owner_of(wanted, count):
    if count & (count - 1) == 0:
        return lax.shift_right_logical(wanted, count.bit_length() - 1)
    return lax.div(wanted, count)


def pick_kernel(
    place_ref, mix_ref, cut_ref, images_ref, index_out, take_out, sent_out, own_out, flat, counts
):
    count = images_ref.shape[2]
    slots = sent_out.shape[0]
    capacity = slots // counts.shape[0]
    me = place_ref[0]

    def put(n, tile):
        own_out[n] = tile

    untangle(images_ref, flat, put)

    @pl.loop(0, slots, unroll=8)
    def _(s):
        index_out[s] = count

    @pl.loop(0, counts.shape[0])
    def _(g):
        counts[g] = 0
        rank = g * capacity
        for ref in (mix_ref, cut_ref):
            for j in range(count):
                wanted = ref[g * count + j]
                owner = owner_of(wanted, count)
                hit = owner == me
                index_out[jnp.where(hit, rank, slots)] = wanted - owner * count
                rank = rank + hit.astype(jnp.int32)

    @pl.loop(0, slots)
    def _(s):
        sent_out[s] = own_out[jnp.minimum(index_out[s], count - 1)]

    for part, ref in enumerate((mix_ref, cut_ref)):

        @pl.loop(0, count)
        def _(j, part=part, ref=ref):
            owner = owner_of(ref[me * count + j], count)
            rank = counts[owner]
            take_out[part * count + j] = owner * capacity + rank
            counts[owner] = rank + 1


def deal_kernel(place_ref, source, out_a, out_b, out_c, out_d, flat):
    outs = (out_a, out_b, out_c, out_d)
    share = out_a.shape[0]

    def put(n, tile):
        for d, out in enumerate(outs):

            @pl.when(jnp.bitwise_xor(place_ref[3], d) == n // share)
            def _(out=out):
                out[n % share] = tile

    untangle(source, flat, put)


def inside_box(corner_ref, n, place_ref):
    shape = (TILE, 8, 1)
    row = place_ref[1] * TILE + lax.broadcasted_iota(jnp.int32, shape, 0)
    col = place_ref[2] * TILE + lax.broadcasted_iota(jnp.int32, shape, 1)
    hit = (
        (row >= corner_ref[0, n])
        & (row < corner_ref[1, n])
        & (col >= corner_ref[2, n])
        & (col < corner_ref[3, n])
    )
    return jnp.where(hit, 1.0, 0.0)


def mix_kernel(
    place_ref, take_ref, corner_ref, ratio_ref, arrived, own_ref, out_a, out_b, out_c, out_d
):
    count = own_ref.shape[0]
    share = out_a.shape[0]
    for d, out in enumerate((out_a, out_b, out_c, out_d)):

        @pl.loop(0, share)
        def _(i, d=d, out=out):
            n = jnp.bitwise_xor(place_ref[3], d) * share + i
            inside = inside_box(corner_ref, n, place_ref)
            ratio = ratio_ref[n]
            own = own_ref[n].astype(F32)
            blend = arrived[take_ref[n]].astype(F32)
            cut = arrived[take_ref[count + n]].astype(F32)
            mixed = inside * cut + (1.0 - inside) * (ratio * own + (1.0 - ratio) * blend)
            out[i] = mixed.astype(BF)


def split_kernel(
    place_ref, take_ref, corner_ref, ratio_ref, grad_a, grad_b, grad_c, grad_d, out_ref
):
    share = grad_a.shape[0]
    count = 4 * share
    if out_ref.shape[0] > 2 * count:
        out_ref[...] = jnp.zeros(out_ref.shape, BF)
    for d, grad_ref in enumerate((grad_a, grad_b, grad_c, grad_d)):

        @pl.loop(0, share)
        def _(i, d=d, grad_ref=grad_ref):
            n = jnp.bitwise_xor(place_ref[3], d) * share + i
            inside = inside_box(corner_ref, n, place_ref)
            gradient = grad_ref[i].astype(F32)
            cut = inside * gradient
            out_ref[take_ref[n]] = ((1.0 - ratio_ref[n]) * (gradient - cut)).astype(BF)
            out_ref[take_ref[count + n]] = cut.astype(BF)


def join_kernel(
    place_ref,
    index_ref,
    corner_ref,
    ratio_ref,
    grad_a,
    grad_b,
    grad_c,
    grad_d,
    back_ref,
    out_ref,
    total,
):
    count, width = out_ref.shape[2:]
    share = grad_a.shape[0]

    def tile_rows(n):
        return pl.ds(pl.multiple_of(n * PAD, 8), PAD)

    for d, grad_ref in enumerate((grad_a, grad_b, grad_c, grad_d)):

        @pl.loop(0, share)
        def _(i, d=d, grad_ref=grad_ref):
            n = jnp.bitwise_xor(place_ref[3], d) * share + i
            outside = 1.0 - inside_box(corner_ref, n, place_ref)
            kept = ratio_ref[n] * outside * grad_ref[i].astype(F32)
            kept = kept.reshape(PAD, width)
            for lane in range(total.shape[0]):
                total[lane, tile_rows(n), :] = kept[:, lane * 128 : (lane + 1) * 128]

    @pl.loop(0, back_ref.shape[0])
    def _(s):
        piece = back_ref[s].astype(F32).reshape(PAD, width)
        for lane in range(total.shape[0]):
            total[lane, tile_rows(index_ref[s]), :] += piece[:, lane * 128 : (lane + 1) * 128]

    for row in range(TILE):
        for col in range(TILE):
            out_ref[row, col] = jnp.concatenate(
                [
                    total[lane, pl.ds(row * 8 + col, count, stride=PAD), :]
                    for lane in range(total.shape[0])
                ],
                axis=1,
            )


def lay_kernel(place_ref, act_a, act_b, act_c, act_d, out_ref, flat):
    count, width = out_ref.shape[2:]
    share = act_a.shape[0]
    for d, act_ref in enumerate((act_a, act_b, act_c, act_d)):

        @pl.loop(0, share)
        def _(i, d=d, act_ref=act_ref):
            n = jnp.bitwise_xor(place_ref[3], d) * share + i
            tile = act_ref[i].astype(F32).reshape(PAD, width)
            for lane in range(flat.shape[0]):
                flat[lane, pl.ds(pl.multiple_of(n * PAD, 8), PAD), :] = tile[
                    :, lane * 128 : (lane + 1) * 128
                ]

    for row in range(TILE):
        for col in range(TILE):
            out_ref[row, col] = jnp.concatenate(
                [
                    flat[lane, pl.ds(row * 8 + col, count, stride=PAD), :]
                    for lane in range(flat.shape[0])
                ],
                axis=1,
            ).astype(BF)


def unpack_kernel(
    ranks,
    counts,
    place_ref,
    *refs,
):
    pieces, refs = refs[:8], refs[8:]
    outs, (vectors, held, fetch_sem, *buffers, send_sem) = refs[:12], refs[12:]
    copies = [
        pltpu.make_async_copy(piece, held.at[i], fetch_sem.at[i])
        for i, piece in enumerate(pieces)
    ]
    for copy in copies:
        copy.start()
    (
        gain_out,
        shift_out,
        entry_out,
        entry_b_out,
        conv_out,
        conv_b_out,
        exit_out,
        exit_b_out,
        expand_out,
        expand_b_out,
        shrink_out,
        shrink_b_out,
    ) = buffers
    width = exit_out.shape[1]
    units = expand_out.shape[2]
    middle = width // 2

    def squares(out_ref, block, count):
        return [(out_ref, block, 0, part * width, width) for part in range(count)]

    def tall(out_ref, block, count):
        return [(out_ref, block, part * width, 0, width) for part in range(count)]

    plans = (
        squares(expand_out, 1, units // width) + tall(shrink_out, 1, units // width),
        [
            (entry_out, 0, 0, 0, width),
            (entry_out, 0, 0, width, middle),
            (vectors, None, 0, 0, middle),
            (entry_out, 0, middle, width, middle),
            (entry_out, 0, 0, 2 * width, width),
        ],
        squares(entry_out, 1, 3)
        + tall(exit_out, 1, 1)
        + squares(expand_out, 0, units // width)
        + tall(shrink_out, 0, units // width)
        + tall(exit_out, 0, 1),
    )
    for copy in copies:
        copy.wait()
    inner_ranks = ranks // 4
    moves = []
    base = 0
    for plan, count in zip(plans, counts):
        at = 0
        for out_ref, block, first_row, lane, length in plan:
            done = 0
            while done < length:
                step = min(length - done, count - at % count)
                moves.append((out_ref, block, first_row + done, lane, base, count, at, step))
                at += step
                done += step
        base += count
    sent = []
    for target in (expand_out, shrink_out, entry_out, exit_out, vectors):
        for out_ref, block, first_row, lane, base, count, at, step in moves:
            if out_ref is not target:
                continue
            shard, start = at // count, base + at % count
            half, shard = shard // ranks, shard % ranks
            first, inner = shard // inner_ranks, shard % inner_ranks
            piece = 4 * jnp.bitwise_xor(place_ref[2], half) + jnp.bitwise_xor(place_ref[5], first)
            inner = jnp.bitwise_xor(place_ref[6], inner)
            values = held[piece, inner, start : start + step, :].astype(F32)
            place = slice(first_row, first_row + step)
            if block is None:
                out_ref[place, :] = values
            else:
                out_ref[block, place, lane : lane + width] = values
        if target is not vectors:
            i = [j for j, ref in enumerate(buffers) if ref is target][0]
            copy = pltpu.make_async_copy(target, outs[i], send_sem.at[i])
            copy.start()
            sent.append(i)

    def line(n):
        return vectors[n : n + 1, :]

    gain_out[0] = jnp.concatenate([line(33), line(18)], axis=0)
    gain_out[1] = jnp.concatenate([line(11), line(5)], axis=0)
    shift_out[0] = jnp.concatenate([line(34), line(19)], axis=0)
    shift_out[1] = jnp.concatenate([line(12), line(6)], axis=0)
    for part in range(2):
        lanes = slice(part * width, (part + 1) * width)
        entry_b_out[:, lanes] = jnp.concatenate([line(31 + part), line(9 + part)], axis=0)
    for i in range(3):
        for j in range(3):
            conv_out[i, j] = jnp.concatenate(
                [line(35 + 3 * i + j), line(22 + 3 * i + j)], axis=0
            )
    conv_b_out[...] = jnp.concatenate([line(21), line(8)], axis=0)
    exit_b_out[...] = jnp.concatenate([line(20), line(7)], axis=0)
    for part in range(units // width):
        lanes = slice(part * width, (part + 1) * width)
        expand_b_out[:, lanes] = jnp.concatenate([line(14 + part), line(part)], axis=0)
    shrink_b_out[...] = jnp.concatenate([line(13), line(4)], axis=0)
    for i, (buffer, out) in enumerate(zip(buffers, outs)):
        if i not in sent:
            pltpu.make_async_copy(buffer, out, send_sem.at[i]).start()
    for i, (buffer, out) in enumerate(zip(buffers, outs)):
        pltpu.make_async_copy(buffer, out, send_sem.at[i]).wait()


SMEM = pl.BlockSpec(memory_space=pltpu.SMEM)
VMEM = pl.BlockSpec(memory_space=pltpu.VMEM)


ANYWHERE = pl.BlockSpec(memory_space=pl.ANY)


class Moves:
    def __init__(self, fetched, sent):
        self.fetched, self.sent = dict(fetched), dict(sent)
        self.waited, self.started = [], []
        for copy in self.fetched.values():
            copy.start()

    def need(self, *refs):
        for ref in refs:
            if id(ref) in self.fetched and id(ref) not in self.waited:
                self.fetched[id(ref)].wait()
                self.waited.append(id(ref))

    def send(self, *refs):
        for ref in refs:
            self.sent[id(ref)].start()
            self.started.append(id(ref))

    def finish(self):
        for key, copy in self.fetched.items():
            if key not in self.waited:
                copy.wait()
        for key, copy in self.sent.items():
            if key not in self.started:
                copy.start()
        for copy in self.sent.values():
            copy.wait()


def run(
    kernel,
    scalars,
    arrays,
    outs,
    scratch=(),
    flops=0,
    name=None,
    after=(),
    scalar_outs=(),
    lazy=None,
):
    outs = list(outs)
    first_in, first_out = (len(arrays), len(outs)) if lazy is None else lazy
    eager, late = list(arrays[:first_in]), list(arrays[first_in:])
    n_in = len(scalars) + len(eager)
    scratch_shapes = [
        kind if dtype is None else pltpu.VMEM(kind, dtype) for kind, dtype in scratch
    ]
    n_own = len(scratch_shapes)
    n_late, n_sent = len(late), len(outs) - first_out
    if lazy is not None:
        scratch_shapes += [pltpu.VMEM(a.shape, a.dtype) for a in late]
        scratch_shapes += [pltpu.VMEM(*out) for out in outs[first_out:]]
        scratch_shapes += [pltpu.SemaphoreType.DMA((n_late,)), pltpu.SemaphoreType.DMA((n_sent,))]

    def body(*refs):
        given, refs = refs[:n_in], refs[n_in:]
        sources, refs = refs[:n_late], refs[n_late + len(after) :]
        results, refs = refs[: len(scalar_outs) + first_out], refs[len(scalar_outs) + first_out :]
        targets, refs = refs[:n_sent], refs[n_sent:]
        own, refs = refs[:n_own], refs[n_own:]
        if lazy is None:
            kernel(*given, *results, *own)
            return
        buffers, leaving = refs[:n_late], refs[n_late : n_late + n_sent]
        fetch_sem, send_sem = refs[n_late + n_sent :]
        moves = Moves(
            [
                (id(buffer), pltpu.make_async_copy(source, buffer, fetch_sem.at[i]))
                for i, (source, buffer) in enumerate(zip(sources, buffers))
            ],
            [
                (id(buffer), pltpu.make_async_copy(buffer, target, send_sem.at[i]))
                for i, (buffer, target) in enumerate(zip(leaving, targets))
            ],
        )
        kernel(moves, *given, *buffers, *results, *leaving, *own)
        moves.finish()

    out_shape = [jax.ShapeDtypeStruct(shape, dtype) for shape, dtype in tuple(scalar_outs) + tuple(outs)]
    moved = sum(a.size * a.dtype.itemsize for a in arrays)
    return pl.pallas_call(
        body,
        out_shape=out_shape,
        in_specs=[SMEM] * len(scalars)
        + [VMEM] * len(eager)
        + [ANYWHERE] * (n_late + len(after)),
        out_specs=[SMEM] * len(scalar_outs) + [VMEM] * first_out + [ANYWHERE] * n_sent,
        scratch_shapes=scratch_shapes,
        compiler_params=pltpu.CompilerParams(vmem_limit_bytes=VMEM_BYTES),
        cost_estimate=pl.CostEstimate(flops=flops, bytes_accessed=moved, transcendentals=0),
        name=name,
    )(*scalars, *eager, *late, *after)


def gate(values, after):
    values, after = list(values), list(after)
    return list(lax.optimization_barrier(tuple(values + after)))[: len(values)]


def swap(values, axis):
    return lax.ppermute(values, axis, [(0, 1), (1, 0)])


def added(values, others):
    return (values.astype(F32) + others.astype(F32)).astype(BF)


def shards(values, ranks):
    return values.reshape(ranks, values.shape[0] // ranks, values.shape[1])


def spread_sum(pieces):
    mine = jnp.sum(pieces.astype(F32), axis=0).astype(BF)
    return jnp.broadcast_to(mine[None], pieces.shape)


def across(values, axes, size, mask):
    return lax.ppermute(values, axes, [(i, i ^ mask) for i in range(size)])


def deal(parts):
    return [parts[0]] + [across(parts[d], ("row", "col"), 4, d) for d in (1, 2, 3)]


RANKS = ("dp", "row")


def stages(ranks):
    bits = ranks.bit_length() - 1
    return [(bit, min(2, bits - bit)) for bit in range(0, bits, 2)]


def scatter_send(values, ranks, stage):
    bit, count = stage
    size = 1 << count
    me = (lax.axis_index(RANKS) >> bit) & (size - 1)
    cut = values.reshape(size, values.shape[0] // size, values.shape[1])
    return [lax.dynamic_index_in_dim(cut, me ^ d, 0, keepdims=False) for d in range(size)]


def scatter_move(parts, ranks, stage):
    return [parts[0]] + [
        across(parts[d], RANKS, ranks, d << stage[0]) for d in range(1, len(parts))
    ]


def scatter_sum(parts):
    return sum(part.astype(F32) for part in parts).astype(BF)


def gather(values, ranks, stage):
    return jnp.stack(
        [values]
        + [across(values, RANKS, ranks, d << stage[0]) for d in range(1, 1 << stage[1])]
    )


def rank_order(rank, ranks):
    order = 0
    for bit, count in stages(ranks):
        order = order * (1 << count) + ((rank >> bit) & ((1 << count) - 1))
    return order


def local(
    groups,
    images,
    cotangent,
    mix_partner,
    cut_partner,
    ratios,
    corners,
    drop_masks,
    norm_gains,
    norm_shifts,
    entry_weight,
    entry_bias,
    position_kernel,
    position_bias,
    exit_weight,
    exit_bias,
    expand_weight,
    expand_bias,
    shrink_weight,
    shrink_bias,
):
    images_here = images.shape[0]
    width = images.shape[3]
    units = expand_weight.shape[2]
    row, col = lax.axis_index("row"), lax.axis_index("col")
    share = images_here // 4
    rows = 4 * share * PAD
    ranks = 2 * groups
    capacity = (2 * images_here + groups - 1) // groups
    slots = groups * capacity
    order = rank_order(lax.axis_index(RANKS), ranks)
    place = jnp.stack(
        [
            lax.axis_index("dp"),
            row,
            col,
            2 * row + col,
            order,
            order // (ranks // 4),
            order % (ranks // 4),
        ]
    ).astype(jnp.int32)
    spots = [0] * ranks
    for rank in range(ranks):
        spots[rank_order(rank, ranks)] = rank
    quad = ((share, TILE, 8, width), BF)
    corners = corners.T
    masks = drop_masks.T
    flat = ((width // 128, images_here * PAD, 128), F32)
    index, take, outgoing, own = run(
        pick_kernel,
        [place, mix_partner, cut_partner],
        [images.transpose(1, 2, 0, 3)],
        [((slots, TILE, 8, width), BF), ((images_here, TILE, 8, width), BF)],
        [flat, (pltpu.SMEM((groups,), jnp.int32), None)],
        name="pick",
        scalar_outs=(((slots + 8,), jnp.int32), ((2 * images_here,), jnp.int32)),
    )
    arrived = lax.all_to_all(outgoing, "dp", split_axis=0, concat_axis=0, tiled=True)
    cot = deal(
        run(deal_kernel, [place], [cotangent.transpose(1, 2, 0, 3)], [quad] * 4, [flat], name="deal")
    )
    mixed = deal(
        run(
            mix_kernel,
            [place, take, corners, ratios],
            [arrived, own],
            [quad] * 4,
            name="mix",
            after=cot,
        )
    )
    conv_k = position_kernel.transpose(1, 2, 0, 3)
    tall = (rows, width)
    (
        vec1,
        act_a,
        act_b,
        act_c,
        act_d,
        keep1,
        away1,
        active0,
        slope0,
        win0,
        chance0,
        stripe0,
        mid0,
        win1,
        chance1,
        stripe1,
        hidden1,
        grad1,
    ) = run(
        functools.partial(first_kernel, spots),
        [place, masks],
        [
            *mixed,
            norm_gains,
            norm_shifts,
            entry_bias,
            conv_k,
            position_bias,
            exit_bias,
            expand_bias,
            shrink_bias,
            entry_weight,
            exit_weight,
            expand_weight,
            shrink_weight,
            *cot,
        ],
        [
            ((7, 8, width), F32),
            *([quad] * 4),
            ((units, width), BF),
            ((units, width), BF),
            ((rows, units), BF),
            ((rows, units), BF),
            ((4 * share, WIN, 3 * HALF), BF),
            ((4 * share, WIN, LANES), BF),
            (tall, BF),
            (tall, F32),
            ((4 * share, WIN, 3 * HALF), BF),
            ((4 * share, WIN, LANES), BF),
            (tall, BF),
            (tall, F32),
            (tall, F32),
        ],
        [
            (tall, F32),
            ((rows, 3 * width), F32),
            (tall, F32),
            ((rows, units), BF),
            ((rows, units), BF),
            (tall, BF),
            (tall, BF),
        ],
        flops=10 * rows * width * width * 120,
        name="first",
        lazy=(12, 1),
    )
    sent1 = shards(added(keep1, swap(away1, "col")), ranks)
    pieces1 = lax.all_to_all(sent1, RANKS, split_axis=0, concat_axis=0, tiled=True)
    vec2, conv2, grad0, delta0, keep2, away2 = run(
        second_kernel,
        [place, masks],
        [
            norm_gains,
            norm_shifts,
            conv_k,
            grad1,
            exit_weight,
            win1,
            chance1,
            hidden1,
            entry_weight,
            stripe1,
            mid0,
            shrink_weight,
            slope0,
            expand_weight,
            active0,
            stripe0,
        ],
        [
            ((15, 8, width), F32),
            ((9, 8, width), F32),
            (tall, F32),
            (tall, F32),
            ((13 * width // 2, width), BF),
            ((13 * width // 2, width), BF),
        ],
        [
            (tall, F32),
            (tall, BF),
            ((rows, 3 * width), F32),
            ((rows, 3 * width), BF),
            (tall, BF),
            (tall, BF),
            ((rows, units), BF),
        ],
        flops=6 * rows * width * width * 120,
        name="second",
        after=[sent1],
        lazy=(3, 2),
    )
    act = deal([act_a, act_b, act_c, act_d])
    keep2, away2, grad0, delta0, *act = gate([keep2, away2, grad0, delta0, *act], [pieces1])
    steps = stages(ranks)

    def first_parts(keep, away):
        other = swap(away, "col")
        count = keep.shape[0] // 4
        return [
            added(keep[d * count : (d + 1) * count], other[d * count : (d + 1) * count])
            for d in range(4)
        ]

    parts2 = first_parts(keep2, away2)
    moved2 = scatter_move(parts2, ranks, steps[0])
    *out_tiles, keep3, away3 = run(
        third_kernel,
        [place],
        [
            norm_gains,
            norm_shifts,
            conv_k,
            vec1,
            vec2,
            conv2,
            delta0,
            win0,
            chance0,
            *mixed,
            entry_weight,
            grad0,
        ],
        [quad] * 4 + [((2 * width, width), BF), ((2 * width, width), BF)],
        [
            (tall, F32),
            ((rows, 3 * width), F32),
            ((rows, 3 * width), BF),
            (tall, BF),
            ((4, 8, width), F32),
            ((9, 8, width), F32),
            ((width, width), F32),
        ],
        flops=3 * rows * width * width * 120,
        name="third",
        after=parts2,
        lazy=(6, 0),
    )
    *moved2, keep3, away3 = gate([*moved2, keep3, away3], out_tiles)
    gradient = deal(out_tiles)
    (parted,) = run(
        split_kernel,
        [place, take, corners, ratios],
        gradient,
        [((slots, TILE, 8, width), BF)],
        name="split",
    )
    mine1 = jnp.sum(pieces1.astype(F32), axis=0).astype(BF)
    mine2 = scatter_sum(moved2)
    mine3 = scatter_sum(scatter_move(first_parts(keep3, away3), ranks, steps[0]))
    cut = mine2.shape[0] * 4 // ranks
    lot = mine3.shape[0] * 4 // ranks
    joint = jnp.concatenate(
        [
            mine3.reshape(ranks // 4, lot, width),
            mine2.reshape(ranks // 4, cut, width),
        ],
        axis=1,
    ).reshape(-1, width)
    for step in steps[1:]:
        joint = scatter_sum(scatter_move(scatter_send(joint, ranks, step), ranks, step))
    joint = jnp.concatenate([mine1, joint], axis=0)
    counts = (mine1.shape[0], lot, cut)
    for step in reversed(steps[1:]):
        joint = gather(joint, ranks, step).reshape(-1, width)
    joint = shards(joint, ranks // 4)
    (parted,) = gate([parted], [joint])
    back = lax.all_to_all(parted, "dp", split_axis=0, concat_axis=0, tiled=True)
    (input_gradient,) = run(
        join_kernel,
        [place, index, corners, ratios],
        [*gradient, back],
        [((TILE, TILE, images_here, width), F32)],
        [((width // 128, (images_here + 1) * PAD, 128), F32)],
        name="join",
    )
    full = [joint] + [across(joint, RANKS, ranks, d) for d in (1, 2, 3)]
    full += [swap(piece, "col") for piece in full]
    full = gate(full, [input_gradient])
    (activations,) = run(
        lay_kernel, [place], act, [((TILE, TILE, images_here, width), BF)], [flat], name="lay"
    )
    shapes = [
        (2, 2, width),
        (2, 2, width),
        (2, width, 3 * width),
        (2, 2 * width),
        (3, 3, 2, width),
        (2, width),
        (2, width, width),
        (2, width),
        (2, width, units),
        (2, units),
        (2, units, width),
        (2, width),
    ]
    gains, shifts, entry, entry_b, conv, conv_b, exit_, exit_b, expand, expand_b, shrink, shrink_b = (
        pl.pallas_call(
            functools.partial(unpack_kernel, ranks, counts),
            out_shape=[jax.ShapeDtypeStruct(shape, F32) for shape in shapes],
            in_specs=[SMEM] + [ANYWHERE] * 8,
            out_specs=[ANYWHERE] * 12,
            scratch_shapes=[
                pltpu.VMEM((width // 2, width), F32),
                pltpu.VMEM((8,) + joint.shape, BF),
                pltpu.SemaphoreType.DMA((8,)),
            ]
            + [pltpu.VMEM(shape, F32) for shape in shapes]
            + [pltpu.SemaphoreType.DMA((12,))],
            compiler_params=pltpu.CompilerParams(vmem_limit_bytes=VMEM_BYTES),
            name="unpack",
        )(place, *full)
    )
    return (
        activations.transpose(2, 0, 1, 3),
        input_gradient.transpose(2, 0, 1, 3),
        gains,
        shifts,
        entry,
        entry_b,
        conv.transpose(2, 0, 1, 3),
        conv_b,
        exit_,
        exit_b,
        expand,
        expand_b,
        shrink,
        shrink_b,
    )


def solution(mesh):
    tiles = P("dp", "row", "col", None)
    return jax.shard_map(
        functools.partial(local, mesh.shape["dp"]),
        mesh=mesh,
        in_specs=(tiles, tiles, P(), P(), P("dp"), P("dp", None), P("dp", None)) + (P(),) * 12,
        out_specs=(tiles, tiles) + (P(),) * 12,
        check_vma=False,
    )
```

```python
import functools

import jax
import jax.numpy as jnp
from jax import lax
from jax.experimental import pallas as pl
from jax.experimental.pallas import tpu as pltpu
from jax.sharding import PartitionSpec as P

TILE = 7
PAD = 56
HEAD_DIM = 32
SIDE_HEADS = 4
HALF = 128
WIN = 2 * PAD
CHUNK = 8 * PAD
LANES = SIDE_HEADS * 128
SCALE = HEAD_DIM ** (-0.5)
LOG2E = 1.4426950408889634
EPS = 1e-05
BF = jnp.bfloat16
F32 = jnp.float32


def dot_nn(a, b):
    return lax.dot_general(a, b, (((1,), (0,)), ((), ())), preferred_element_type=F32)


def dot_nt(a, b):
    return lax.dot_general(a, b, (((1,), (1,)), ((), ())), preferred_element_type=F32)


def dot_tn(a, b):
    return lax.dot_general(a, b, (((0,), (0,)), ((), ())), preferred_element_type=F32)


def norm_parts(values):
    centered = values - jnp.mean(values, axis=-1, keepdims=True)
    inverse = lax.rsqrt(jnp.mean(centered * centered, axis=-1, keepdims=True) + EPS)
    return centered * inverse, inverse


def norm_back(delta, hat, inverse, gain):
    scaled = delta * gain
    first = jnp.mean(scaled, axis=-1, keepdims=True)
    second = jnp.mean(scaled * hat, axis=-1, keepdims=True)
    return inverse * (scaled - first - hat * second)


def gelu_parts(values):
    chance = 0.5 + 0.5 * lax.erf(values * (0.5**0.5))
    density = jnp.exp2(values * values * (-0.5 * LOG2E)) * 0.3989422804014327
    return chance, density


def row_sums(values):
    count, width = values.shape
    return jnp.sum(values.reshape(count // 8, 8, width), axis=0)


def scale_rows(place_ref, mask_ref, column):
    scales = [
        mask_ref[column, 4 * place_ref[3] + i].astype(F32) * 1.25 for i in range(4)
    ]
    columns = [jnp.full((PAD, 1), scale, F32) for scale in scales]
    return jnp.concatenate(columns * (CHUNK // (4 * PAD)), axis=0)


def add_row(acc_ref, row, values):
    acc_ref[row] += values


def spread_heads(values):
    lane = lax.broadcasted_iota(jnp.int32, values.shape, 1) // HEAD_DIM
    empty = jnp.zeros((128 - WIN, HALF), F32)
    blocks = []
    for head in range(SIDE_HEADS):
        blocks.append(jnp.where(lane == head, values, 0.0))
        blocks.append(empty)
    return jnp.concatenate(blocks, axis=0).astype(BF)


def gather_heads(wide):
    picked = jnp.concatenate(
        [
            wide[head * HEAD_DIM : (head + 1) * HEAD_DIM, head * 128 : (head + 1) * 128]
            for head in range(SIDE_HEADS)
        ],
        axis=0,
    )
    return picked.T[:WIN]


def turned(values):
    return jnp.concatenate([values, jnp.zeros((128 - WIN, HALF), F32)], axis=0).T.astype(BF)


def fill_rows(values):
    empty = jnp.zeros((128 - WIN, values.shape[1]), values.dtype)
    return jnp.concatenate([values, empty], axis=0)


def valid_column(shape):
    return lax.broadcasted_iota(jnp.int32, shape, 1) != 7


def valid_rows(shape):
    return lax.broadcasted_iota(jnp.int32, shape, 0) % 8 != 7


def column_shifts(values, across):
    cube = values.reshape(2 * TILE, 8, HALF)
    if not across:
        return (pltpu.roll(cube, 1, 1), cube, pltpu.roll(cube, 7, 1))
    left, right = cube[:TILE], cube[TILE:]
    column = lax.broadcasted_iota(jnp.int32, left.shape, 1)
    before = jnp.concatenate(
        [
            pltpu.roll(left, 1, 1),
            jnp.where(column == 0, pltpu.roll(left, 2, 1), pltpu.roll(right, 1, 1)),
        ],
        axis=0,
    )
    after = jnp.concatenate(
        [
            jnp.where(column == 6, pltpu.roll(right, 6, 1), pltpu.roll(left, 7, 1)),
            pltpu.roll(right, 7, 1),
        ],
        axis=0,
    )
    return (before, cube, after)


def row_shift(cube, step, across):
    if step == 0:
        return cube
    empty = jnp.zeros((1, 8, HALF), F32)

    def move(part):
        if step < 0:
            return jnp.concatenate([empty, part[:-1]], axis=0)
        return jnp.concatenate([part[1:], empty], axis=0)

    if across:
        return jnp.concatenate([move(cube[:TILE]), move(cube[TILE:])], axis=0)
    return move(cube)


def window_conv(shifts, kernel_at, across):
    total = None
    for i in range(3):
        part = None
        for j in range(3):
            term = kernel_at(i, j) * shifts[j]
            part = term if part is None else part + term
        part = row_shift(part, i - 1, across)
        total = part if total is None else total + part
    return total.reshape(WIN, HALF)


def window_rows(across, window):
    side, image = window // 4, window % 4
    if across:
        first, second = 2 * side, 2 * side + 1
    else:
        first, second = side, 2 + side
    return (
        pl.multiple_of((first * 4 + image) * PAD, 8),
        pl.multiple_of((second * 4 + image) * PAD, 8),
    )


def take_window(ref, at, lane):
    return jnp.concatenate(
        [ref[pl.ds(at[0], PAD), lane : lane + HALF], ref[pl.ds(at[1], PAD), lane : lane + HALF]],
        axis=0,
    )


def put_window(ref, at, lane, values):
    ref[pl.ds(at[0], PAD), lane : lane + HALF] = values[:PAD]
    ref[pl.ds(at[1], PAD), lane : lane + HALF] = values[PAD:]


def round_bf(values):
    return values.astype(BF).astype(F32)


def attention_forward(
    block, hidden_ref, gains, shifts, entry_w, entry_b, conv_k, conv_b, wide, stripe, win_out, chance_out
):
    width = hidden_ref.shape[1]

    @pl.loop(0, 2)
    def _(t):
        rows = chunk(t)
        hat, _ = norm_parts(hidden_ref[rows, :])
        normed = (hat * gains[block, 0:1, :] + shifts[block, 0:1, :]).astype(BF)
        for part in range(3):
            out = dot_nn(normed, entry_w[block, :, part * width : (part + 1) * width])
            if part != 1:
                at = 0 if part == 0 else width
                out = out + entry_b[block : block + 1, at : at + width]
            wide[rows, part * width : (part + 1) * width] = round_bf(out)

    for direction in range(2):
        across = direction == 0
        lane = direction * HALF

        @pl.loop(0, 8, unroll=4)
        def _(window, across=across, lane=lane, direction=direction):
            at = window_rows(across, window)
            queries = take_window(wide, at, lane)
            keys = take_window(wide, at, width + lane)
            values = take_window(wide, at, 2 * width + lane)
            keys_bf = keys.astype(BF)
            win_out[direction * 8 + window, :, 0:HALF] = queries.astype(BF)
            win_out[direction * 8 + window, :, HALF : 2 * HALF] = keys_bf
            win_out[direction * 8 + window, :, 2 * HALF : 3 * HALF] = values.astype(BF)
            scores = dot_nt(keys_bf, spread_heads(queries)).reshape(2 * TILE, 8, LANES)
            scores = jnp.where(valid_column((1, 8, LANES)), scores, -1e30)
            top = jnp.max(jnp.max(scores, axis=0), axis=0, keepdims=True)
            lifted = jnp.exp2((scores - top) * (SCALE * LOG2E))
            totals = jnp.sum(jnp.sum(lifted, axis=0), axis=0, keepdims=True)
            chances = (lifted * (1.0 / totals)).reshape(WIN, LANES).astype(BF)
            chance_out[direction * 8 + window] = chances
            attended = gather_heads(dot_nn(turned(values), fill_rows(chances)))
            clean = jnp.where(valid_rows(values.shape), values, 0.0)
            position = window_conv(
                column_shifts(clean, across),
                lambda i, j: conv_k[i, j, block : block + 1, lane : lane + HALF],
                across,
            )
            put_window(
                stripe, at, lane, attended + position + conv_b[block : block + 1, lane : lane + HALF]
            )


def attention_backward(
    ready,
    block,
    win_in,
    chance_in,
    conv_k,
    stripe_delta,
    wide,
    conv_acc,
):
    width = stripe_delta.shape[1]
    for direction in range(2):
        ready(direction)
        across = direction == 0
        lane = direction * HALF

        @pl.loop(0, 8, unroll=4)
        def _(window, across=across, lane=lane, direction=direction):
            at = window_rows(across, window)
            out_delta = take_window(stripe_delta, at, lane)
            queries = win_in[direction * 8 + window, :, 0:HALF].astype(F32)
            keys = win_in[direction * 8 + window, :, HALF : 2 * HALF].astype(F32)
            values_bf = win_in[direction * 8 + window, :, 2 * HALF : 3 * HALF]
            values = values_bf.astype(F32)
            chances = chance_in[direction * 8 + window]
            delta_spread = spread_heads(out_delta)
            chance_delta = dot_nt(values_bf, delta_spread)
            cubes = (2 * TILE, 8, LANES)
            wide_chances = chances.astype(F32).reshape(cubes)
            weighted = wide_chances * chance_delta.reshape(cubes)
            common = jnp.sum(jnp.sum(weighted, axis=0), axis=0, keepdims=True)
            score_delta = (weighted - wide_chances * common).reshape(WIN, LANES).astype(BF)
            values_delta = dot_nn(chances, delta_spread)
            keys_delta = dot_nn(score_delta, spread_heads(queries)) * SCALE
            query_delta = gather_heads(dot_nn(turned(keys), fill_rows(score_delta))) * SCALE
            keep = valid_rows(values.shape)
            clean = jnp.where(keep, values, 0.0)
            shifts = column_shifts(clean, across)
            cube = out_delta.reshape(2 * TILE, 8, HALF)
            for i in range(3):
                moved = row_shift(cube, 1 - i, across)
                for j in range(3):
                    conv_acc[3 * i + j, :, lane : lane + HALF] += jnp.sum(moved * shifts[j], axis=0)
            back = window_conv(
                column_shifts(out_delta, across),
                lambda i, j: conv_k[2 - i, 2 - j, block : block + 1, lane : lane + HALF],
                across,
            )
            values_delta = jnp.where(keep, values_delta + back, 0.0)
            put_window(wide, at, lane, query_delta)
            put_window(wide, at, width + lane, keys_delta)
            put_window(wide, at, 2 * width + lane, values_delta)


def chunk(t):
    return pl.ds(pl.multiple_of(t * CHUNK, CHUNK), CHUNK)


class Bundle:
    def __init__(self, place_ref, keep, away, chunks=1, spot=lambda chunk: chunk):
        self.place_ref, self.keep, self.away = place_ref, keep, away
        self.step, self.spot = keep.shape[0] // chunks, spot

    def put(self, at, values):
        values = values.astype(BF)
        half, step = self.keep.shape[0], self.step
        last = at + values.shape[0]
        first = at
        while first < last:
            stop = min(last, (first // step + 1) * step)
            number = first // half
            start = self.spot(first % half // step) * step
            inner, count = first % step, stop - first
            if not isinstance(start, int):
                start = pl.multiple_of(start, step)
            rows = pl.ds(start + inner, count)
            piece = values[first - at : stop - at]

            @pl.when(self.place_ref[2] == number)
            def _(piece=piece, rows=rows):
                self.keep[rows, :] = piece

            @pl.when(self.place_ref[2] != number)
            def _(piece=piece, rows=rows):
                self.away[rows, :] = piece

            first = stop


def put_squares(bundle, at, values, side):
    for part in range(values.shape[1] // side):
        bundle.put(at + part * side, values[:, part * side : (part + 1) * side])


def load_tiles(place_ref, tiles, hidden):
    for d, tile in enumerate(tiles):
        at = jnp.bitwise_xor(place_ref[3], d) * (4 * PAD)
        rows = pl.ds(pl.multiple_of(at, 4 * PAD), 4 * PAD)
        hidden[rows, :] = tile[...].astype(F32).reshape(4 * PAD, hidden.shape[1])


def store_tile(place_ref, tiles, t, values):
    count = CHUNK // (4 * PAD)
    values = values.reshape((count,) + tiles[0].shape).astype(BF)
    for part in range(count):
        for d, tile in enumerate(tiles):

            @pl.when(jnp.bitwise_xor(place_ref[3], d) == count * t + part)
            def _(tile=tile, part=part):
                tile[...] = values[part]


def first_kernel(
    spots,
    moves,
    place_ref,
    mask_ref,
    mixed_a,
    mixed_b,
    mixed_c,
    mixed_d,
    gains,
    shifts,
    entry_b,
    conv_k,
    conv_b,
    exit_b,
    expand_b,
    shrink_b,
    entry_w,
    exit_w,
    expand_w,
    shrink_w,
    cot_a,
    cot_b,
    cot_c,
    cot_d,
    vec_out,
    act_a,
    act_b,
    act_c,
    act_d,
    keep_out,
    away_out,
    active0_out,
    slope0_out,
    win0_out,
    chance0_out,
    stripe0_out,
    mid0_out,
    win1_out,
    chance1_out,
    stripe1_out,
    hidden1_out,
    grad_out,
    hidden,
    wide,
    stripe,
    active1,
    pre1,
    feed1,
    inner1,
):
    width = hidden.shape[1]
    hidden_units = expand_w.shape[2]
    bundle = Bundle(place_ref, keep_out, away_out, len(spots), lambda chunk: spots[chunk])
    vec_out[...] = jnp.zeros(vec_out.shape, F32)
    moves.fetch(entry_w)
    load_tiles(place_ref, (mixed_a, mixed_b, mixed_c, mixed_d), hidden)
    moves.need(entry_w)
    moves.fetch(exit_w, expand_w, shrink_w, cot_a, cot_b, cot_c, cot_d)

    for block in range(2):
        win_out, chance_out, stripe_out = (
            (win0_out, chance0_out, stripe0_out),
            (win1_out, chance1_out, stripe1_out),
        )[block]
        attention_forward(
            block, hidden, gains, shifts, entry_w, entry_b, conv_k, conv_b, wide, stripe, win_out, chance_out
        )
        moves.send(win_out, chance_out)
        moves.need(exit_w, expand_w, shrink_w)
        if block == 1:
            moves.need(cot_a, cot_b, cot_c, cot_d)
            load_tiles(place_ref, (cot_a, cot_b, cot_c, cot_d), grad_out)

        @pl.loop(0, 2)
        def _(t, block=block, stripe_out=stripe_out):
            rows = chunk(t)
            striped = stripe[rows, :].astype(BF)
            stripe_out[rows, :] = striped
            branch = dot_nn(striped, exit_w[block]) + exit_b[block : block + 1, :]
            midway = hidden[rows, :] + scale_rows(place_ref, mask_ref, 2 * block) * branch
            if block == 0:
                mid0_out[rows, :] = midway
            hat, inverse = norm_parts(midway)
            normed = (hat * gains[block, 1:2, :] + shifts[block, 1:2, :]).astype(BF)
            feed_scale = scale_rows(place_ref, mask_ref, 2 * block + 1)
            feed = shrink_b[block : block + 1, :]
            if block == 1:
                inner1[rows, :] = normed
                gradient = grad_out[rows, :]
                feed_delta = (feed_scale * gradient).astype(BF)
                feed1[rows, :] = feed_delta
                add_row(vec_out, 4, row_sums(feed_delta.astype(F32)))
                inner_delta = jnp.zeros((CHUNK, width), F32)
            for part in range(hidden_units // width):
                at = slice(part * width, (part + 1) * width)
                pre_act = dot_nn(normed, expand_w[block, :, at]) + expand_b[block : block + 1, at]
                chance, density = gelu_parts(pre_act)
                active = (pre_act * chance).astype(BF)
                slope = chance + pre_act * density
                if block == 0:
                    active0_out[rows, at] = active
                    slope0_out[rows, at] = slope.astype(BF)
                else:
                    active1[rows, at] = active
                    pre_delta = (dot_nt(feed_delta, shrink_w[block, at, :]) * slope).astype(BF)
                    pre1[rows, at] = pre_delta
                    add_row(vec_out, part, row_sums(pre_delta.astype(F32)))
                    inner_delta = inner_delta + dot_nt(pre_delta, expand_w[block, :, at])
                feed = feed + dot_nn(active, shrink_w[block, at, :])
            output = midway + feed_scale * feed
            if block == 0:
                hidden[rows, :] = output
                hidden1_out[rows, :] = output
            else:
                store_tile(place_ref, (act_a, act_b, act_c, act_d), t, output)
                add_row(vec_out, 5, row_sums(inner_delta * hat))
                add_row(vec_out, 6, row_sums(inner_delta))
                grad_out[rows, :] = gradient + norm_back(
                    inner_delta, hat, inverse, gains[block, 1:2, :]
                )

        moves.send(stripe_out)
        if block == 0:
            moves.send(mid0_out, active0_out, slope0_out, hidden1_out)
        else:
            moves.send(act_a, act_b, act_c, act_d, grad_out)

    put_squares(bundle, 0, dot_tn(inner1[...], pre1[...]), width)
    for part in range(hidden_units // width):
        bundle.put(
            hidden_units + part * width,
            dot_tn(active1[:, part * width : (part + 1) * width], feed1[...]),
        )


def delta_rows(block, place_ref, mask_ref, exit_w, grad_ref, stripe_delta, branch_delta, vec_out, at):
    @pl.loop(0, 2)
    def _(t):
        rows = chunk(t)
        rounded = (scale_rows(place_ref, mask_ref, 2 * block) * grad_ref[rows, :]).astype(BF)
        branch_delta[rows, :] = rounded
        add_row(vec_out, at, row_sums(rounded.astype(F32)))
        out = round_bf(dot_nt(rounded, exit_w[block]))
        stripe_delta[rows, :] = out
        add_row(vec_out, at + 1, row_sums(out))


def entry_backward(block, hidden_ref, gains, shifts, entry_w, grad_ref, wide, wide_bf, normed_bf, vec_out, at, emit):
    width = hidden_ref.shape[1]

    @pl.loop(0, 2)
    def _(t):
        rows = chunk(t)
        hat, inverse = norm_parts(hidden_ref[rows, :])
        normed_bf[rows, :] = (hat * gains[block, 0:1, :] + shifts[block, 0:1, :]).astype(BF)
        delta = jnp.zeros((CHUNK, width), F32)
        for part in range(3):
            lanes = slice(part * width, (part + 1) * width)
            rounded = wide[rows, lanes].astype(BF)
            wide_bf[rows, lanes] = rounded
            if part != 1:
                add_row(vec_out, at + part // 2, row_sums(rounded.astype(F32)))
            delta = delta + dot_nt(rounded, entry_w[block, :, lanes])
        add_row(vec_out, at + 2, row_sums(delta * hat))
        add_row(vec_out, at + 3, row_sums(delta))
        emit(t, rows, grad_ref[rows, :] + norm_back(delta, hat, inverse, gains[block, 0:1, :]))


def second_kernel(
    moves,
    place_ref,
    mask_ref,
    gains,
    shifts,
    conv_k,
    grad_in,
    exit_w,
    win1,
    chance1,
    hidden1,
    entry_w,
    stripe1,
    mid0,
    shrink_w,
    slope0,
    expand_w,
    active0,
    stripe0,
    vec_out,
    conv_out,
    grad_out,
    stripe_delta_out,
    keep_out,
    away_out,
    stripe_delta,
    branch_delta,
    wide,
    wide_bf,
    normed_bf,
    feed0,
    pre0,
):
    grad = grad_out
    width = grad.shape[1]
    hidden_units = expand_w.shape[2]
    bundle = Bundle(
        place_ref, keep_out, away_out, 4, lambda chunk: jnp.bitwise_xor(place_ref[5], chunk)
    )
    vec_out[...] = jnp.zeros(vec_out.shape, F32)
    conv_out[...] = jnp.zeros(conv_out.shape, F32)
    moves.fetch(grad_in, exit_w)
    moves.fetch(win1, chance1, part=0)
    moves.need(grad_in, exit_w)
    moves.fetch(win1, chance1, part=1)
    delta_rows(1, place_ref, mask_ref, exit_w, grad_in, stripe_delta, branch_delta, vec_out, 0)

    def ready(direction):
        moves.need(win1, chance1, part=direction)
        if direction == 0:
            moves.fetch(hidden1, entry_w, stripe1)
        else:
            moves.fetch(mid0, shrink_w, slope0, expand_w, active0, stripe0)

    attention_backward(ready, 1, win1, chance1, conv_k, stripe_delta, wide, conv_out)

    def emit(t, rows, values):
        grad[rows, :] = values

    moves.need(hidden1, entry_w)
    entry_backward(
        1, hidden1, gains, shifts, entry_w, grad_in, wide, wide_bf, normed_bf, vec_out, 2, emit
    )
    put_squares(bundle, 0, dot_tn(normed_bf[...], wide_bf[...]), width)
    moves.need(stripe1)
    bundle.put(3 * width, dot_tn(stripe1[...], branch_delta[...]))
    moves.need(mid0, shrink_w, slope0, expand_w)

    @pl.loop(0, 2)
    def _(t):
        rows = chunk(t)
        gradient = grad[rows, :]
        hat, inverse = norm_parts(mid0[rows, :])
        normed_bf[rows, :] = (hat * gains[0, 1:2, :] + shifts[0, 1:2, :]).astype(BF)
        feed_delta = (scale_rows(place_ref, mask_ref, 1) * gradient).astype(BF)
        feed0[rows, :] = feed_delta
        add_row(vec_out, 6, row_sums(feed_delta.astype(F32)))
        inner_delta = jnp.zeros((CHUNK, width), F32)
        for part in range(hidden_units // width):
            at = slice(part * width, (part + 1) * width)
            pre_delta = (
                dot_nt(feed_delta, shrink_w[0, at, :]) * slope0[rows, at].astype(F32)
            ).astype(BF)
            pre0[rows, at] = pre_delta
            add_row(vec_out, 7 + part, row_sums(pre_delta.astype(F32)))
            inner_delta = inner_delta + dot_nt(pre_delta, expand_w[0, :, at])
        add_row(vec_out, 11, row_sums(inner_delta * hat))
        add_row(vec_out, 12, row_sums(inner_delta))
        grad[rows, :] = gradient + norm_back(inner_delta, hat, inverse, gains[0, 1:2, :])

    delta_rows(0, place_ref, mask_ref, exit_w, grad, stripe_delta_out, branch_delta, vec_out, 13)
    moves.send(grad_out, stripe_delta_out)
    moves.need(active0, stripe0)
    put_squares(bundle, 4 * width, dot_tn(normed_bf[...], pre0[...]), width)
    for part in range(hidden_units // width):
        bundle.put(
            (8 + part) * width,
            dot_tn(active0[:, part * width : (part + 1) * width], feed0[...]),
        )
    bundle.put(12 * width, dot_tn(stripe0[...], branch_delta[...]))


def third_kernel(
    moves,
    place_ref,
    gains,
    shifts,
    conv_k,
    vec1,
    vec2,
    conv2,
    stripe_delta,
    win0,
    chance0,
    mixed_a,
    mixed_b,
    mixed_c,
    mixed_d,
    entry_w,
    grad_in,
    out_a,
    out_b,
    out_c,
    out_d,
    keep_out,
    away_out,
    hidden,
    wide,
    wide_bf,
    normed_bf,
    vec3,
    conv3,
    flat,
):
    width = hidden.shape[1]
    bundle = Bundle(
        place_ref, keep_out, away_out, 4, lambda chunk: jnp.bitwise_xor(place_ref[5], chunk)
    )
    vec3[...] = jnp.zeros(vec3.shape, F32)
    conv3[...] = jnp.zeros(conv3.shape, F32)
    moves.fetch(stripe_delta)
    moves.fetch(win0, chance0, part=0)
    moves.need(stripe_delta)
    moves.fetch(win0, chance0, part=1)

    def ready(direction):
        moves.need(win0, chance0, part=direction)
        if direction == 0:
            moves.fetch(mixed_a, mixed_b, mixed_c, mixed_d, entry_w, grad_in)

    attention_backward(ready, 0, win0, chance0, conv_k, stripe_delta, wide, conv3)

    def emit(t, rows, values):
        store_tile(place_ref, (out_a, out_b, out_c, out_d), t, values)

    moves.need(mixed_a, mixed_b, mixed_c, mixed_d, entry_w, grad_in)
    load_tiles(place_ref, (mixed_a, mixed_b, mixed_c, mixed_d), hidden)
    entry_backward(
        0, hidden, gains, shifts, entry_w, grad_in, wide, wide_bf, normed_bf, vec3, 0, emit
    )
    moves.send(out_a, out_b, out_c, out_d)
    flat[...] = jnp.zeros(flat.shape, F32)
    at = 0
    for ref in (vec1, vec2, conv2, vec3, conv3):
        flat[at : at + ref.shape[0], :] = jnp.sum(ref[...], axis=1)
        at += ref.shape[0]
    spread = dot_tn(normed_bf[...], wide_bf[...])
    half = keep_out.shape[0]
    middle = width // 2
    lots = flat.shape[0] // 2
    bundle.put(0, spread[:, :width])
    bundle.put(width, spread[:middle, width : 2 * width])
    bundle.put(width + middle, flat[:lots, :])
    bundle.put(half, spread[middle:, width : 2 * width])
    bundle.put(half + middle, spread[:, 2 * width :])
    bundle.put(half + middle + width, flat[lots:, :])


def untangle(source, flat, target):
    count, width = source.shape[2:]
    lanes = flat.shape[0]
    for row in range(TILE):
        flat[:, pl.ds(row * 8 + 7, count, stride=PAD), :] = jnp.zeros((lanes, count, 128), F32)
        for col in range(TILE):
            token = source[row, col].astype(F32)
            for lane in range(lanes):
                flat[lane, pl.ds(row * 8 + col, count, stride=PAD), :] = token[
                    :, lane * 128 : (lane + 1) * 128
                ]

    @pl.loop(0, count)
    def _(n):
        rows = pl.ds(pl.multiple_of(n * PAD, 8), PAD)
        tile = jnp.concatenate([flat[lane, rows, :] for lane in range(lanes)], axis=1)
        target(n, tile.reshape(TILE, 8, width).astype(BF))


def owner_of(wanted, count):
    if count & (count - 1) == 0:
        return lax.shift_right_logical(wanted, count.bit_length() - 1)
    return lax.div(wanted, count)


def pick_kernel(
    place_ref, mix_ref, cut_ref, images_ref, index_out, take_out, sent_out, own_out, flat, counts
):
    count = images_ref.shape[2]
    slots = sent_out.shape[0]
    capacity = slots // counts.shape[0]
    me = place_ref[0]

    def put(n, tile):
        own_out[n] = tile

    untangle(images_ref, flat, put)

    @pl.loop(0, slots, unroll=8)
    def _(s):
        index_out[s] = count

    @pl.loop(0, counts.shape[0])
    def _(g):
        counts[g] = 0
        rank = g * capacity
        for ref in (mix_ref, cut_ref):
            for j in range(count):
                wanted = ref[g * count + j]
                owner = owner_of(wanted, count)
                hit = owner == me
                index_out[jnp.where(hit, rank, slots)] = wanted - owner * count
                rank = rank + hit.astype(jnp.int32)

    @pl.loop(0, slots)
    def _(s):
        sent_out[s] = own_out[jnp.minimum(index_out[s], count - 1)]

    for part, ref in enumerate((mix_ref, cut_ref)):

        @pl.loop(0, count)
        def _(j, part=part, ref=ref):
            owner = owner_of(ref[me * count + j], count)
            rank = counts[owner]
            take_out[part * count + j] = owner * capacity + rank
            counts[owner] = rank + 1


def deal_kernel(place_ref, source, out_a, out_b, out_c, out_d, flat):
    outs = (out_a, out_b, out_c, out_d)
    share = out_a.shape[0]

    def put(n, tile):
        for d, out in enumerate(outs):

            @pl.when(jnp.bitwise_xor(place_ref[3], d) == n // share)
            def _(out=out):
                out[n % share] = tile

    untangle(source, flat, put)


def inside_box(corner_ref, n, place_ref):
    shape = (TILE, 8, 1)
    row = place_ref[1] * TILE + lax.broadcasted_iota(jnp.int32, shape, 0)
    col = place_ref[2] * TILE + lax.broadcasted_iota(jnp.int32, shape, 1)
    hit = (
        (row >= corner_ref[0, n])
        & (row < corner_ref[1, n])
        & (col >= corner_ref[2, n])
        & (col < corner_ref[3, n])
    )
    return jnp.where(hit, 1.0, 0.0)


def mix_kernel(
    place_ref, take_ref, corner_ref, ratio_ref, arrived, own_ref, out_a, out_b, out_c, out_d
):
    count = own_ref.shape[0]
    share = out_a.shape[0]
    for d, out in enumerate((out_a, out_b, out_c, out_d)):

        @pl.loop(0, share)
        def _(i, d=d, out=out):
            n = jnp.bitwise_xor(place_ref[3], d) * share + i
            inside = inside_box(corner_ref, n, place_ref)
            ratio = ratio_ref[n]
            own = own_ref[n].astype(F32)
            blend = arrived[take_ref[n]].astype(F32)
            cut = arrived[take_ref[count + n]].astype(F32)
            mixed = inside * cut + (1.0 - inside) * (ratio * own + (1.0 - ratio) * blend)
            out[i] = mixed.astype(BF)


def split_kernel(
    place_ref, take_ref, corner_ref, ratio_ref, grad_a, grad_b, grad_c, grad_d, out_ref
):
    share = grad_a.shape[0]
    count = 4 * share
    if out_ref.shape[0] > 2 * count:
        out_ref[...] = jnp.zeros(out_ref.shape, BF)
    for d, grad_ref in enumerate((grad_a, grad_b, grad_c, grad_d)):

        @pl.loop(0, share)
        def _(i, d=d, grad_ref=grad_ref):
            n = jnp.bitwise_xor(place_ref[3], d) * share + i
            inside = inside_box(corner_ref, n, place_ref)
            gradient = grad_ref[i].astype(F32)
            cut = inside * gradient
            out_ref[take_ref[n]] = ((1.0 - ratio_ref[n]) * (gradient - cut)).astype(BF)
            out_ref[take_ref[count + n]] = cut.astype(BF)


def join_kernel(
    place_ref,
    index_ref,
    corner_ref,
    ratio_ref,
    grad_a,
    grad_b,
    grad_c,
    grad_d,
    back_ref,
    out_ref,
    total,
):
    count, width = out_ref.shape[2:]
    share = grad_a.shape[0]

    def tile_rows(n):
        return pl.ds(pl.multiple_of(n * PAD, 8), PAD)

    for d, grad_ref in enumerate((grad_a, grad_b, grad_c, grad_d)):

        @pl.loop(0, share)
        def _(i, d=d, grad_ref=grad_ref):
            n = jnp.bitwise_xor(place_ref[3], d) * share + i
            outside = 1.0 - inside_box(corner_ref, n, place_ref)
            kept = ratio_ref[n] * outside * grad_ref[i].astype(F32)
            kept = kept.reshape(PAD, width)
            for lane in range(total.shape[0]):
                total[lane, tile_rows(n), :] = kept[:, lane * 128 : (lane + 1) * 128]

    @pl.loop(0, back_ref.shape[0])
    def _(s):
        piece = back_ref[s].astype(F32).reshape(PAD, width)
        for lane in range(total.shape[0]):
            total[lane, tile_rows(index_ref[s]), :] += piece[:, lane * 128 : (lane + 1) * 128]

    for row in range(TILE):
        for col in range(TILE):
            out_ref[row, col] = jnp.concatenate(
                [
                    total[lane, pl.ds(row * 8 + col, count, stride=PAD), :]
                    for lane in range(total.shape[0])
                ],
                axis=1,
            )


def lay_kernel(place_ref, act_a, act_b, act_c, act_d, out_ref, flat):
    count, width = out_ref.shape[2:]
    share = act_a.shape[0]
    for d, act_ref in enumerate((act_a, act_b, act_c, act_d)):

        @pl.loop(0, share)
        def _(i, d=d, act_ref=act_ref):
            n = jnp.bitwise_xor(place_ref[3], d) * share + i
            tile = act_ref[i].astype(F32).reshape(PAD, width)
            for lane in range(flat.shape[0]):
                flat[lane, pl.ds(pl.multiple_of(n * PAD, 8), PAD), :] = tile[
                    :, lane * 128 : (lane + 1) * 128
                ]

    for row in range(TILE):
        for col in range(TILE):
            out_ref[row, col] = jnp.concatenate(
                [
                    flat[lane, pl.ds(row * 8 + col, count, stride=PAD), :]
                    for lane in range(flat.shape[0])
                ],
                axis=1,
            ).astype(BF)


def unpack_kernel(
    ranks,
    counts,
    place_ref,
    *refs,
):
    pieces, refs = refs[:8], refs[8:]
    outs, (vectors, held, fetch_sem, *buffers, send_sem) = refs[:12], refs[12:]
    copies = [
        pltpu.make_async_copy(piece, held.at[i], fetch_sem.at[i])
        for i, piece in enumerate(pieces)
    ]
    for copy in copies:
        copy.start()
    (
        gain_out,
        shift_out,
        entry_out,
        entry_b_out,
        conv_out,
        conv_b_out,
        exit_out,
        exit_b_out,
        expand_out,
        expand_b_out,
        shrink_out,
        shrink_b_out,
    ) = buffers
    width = exit_out.shape[1]
    units = expand_out.shape[2]
    middle = width // 2

    def squares(out_ref, block, count):
        return [(out_ref, block, 0, part * width, width) for part in range(count)]

    def tall(out_ref, block, count):
        return [(out_ref, block, part * width, 0, width) for part in range(count)]

    plans = (
        squares(expand_out, 1, units // width) + tall(shrink_out, 1, units // width),
        [
            (entry_out, 0, 0, 0, width),
            (entry_out, 0, 0, width, middle),
            (vectors, None, 0, 0, middle),
            (entry_out, 0, middle, width, middle),
            (entry_out, 0, 0, 2 * width, width),
        ],
        squares(entry_out, 1, 3)
        + tall(exit_out, 1, 1)
        + squares(expand_out, 0, units // width)
        + tall(shrink_out, 0, units // width)
        + tall(exit_out, 0, 1),
    )
    for copy in copies:
        copy.wait()
    inner_ranks = ranks // 4
    moves = []
    base = 0
    for plan, count in zip(plans, counts):
        at = 0
        for out_ref, block, first_row, lane, length in plan:
            done = 0
            while done < length:
                step = min(length - done, count - at % count)
                moves.append((out_ref, block, first_row + done, lane, base, count, at, step))
                at += step
                done += step
        base += count
    sent = []
    for target in (expand_out, shrink_out, entry_out, exit_out, vectors):
        for out_ref, block, first_row, lane, base, count, at, step in moves:
            if out_ref is not target:
                continue
            shard, start = at // count, base + at % count
            half, shard = shard // ranks, shard % ranks
            first, inner = shard // inner_ranks, shard % inner_ranks
            piece = 4 * jnp.bitwise_xor(place_ref[2], half) + jnp.bitwise_xor(place_ref[5], first)
            inner = jnp.bitwise_xor(place_ref[6], inner)
            values = held[piece, inner, start : start + step, :].astype(F32)
            place = slice(first_row, first_row + step)
            if block is None:
                out_ref[place, :] = values
            else:
                out_ref[block, place, lane : lane + width] = values
        if target is not vectors:
            i = [j for j, ref in enumerate(buffers) if ref is target][0]
            copy = pltpu.make_async_copy(target, outs[i], send_sem.at[i])
            copy.start()
            sent.append(i)

    def line(n):
        return vectors[n : n + 1, :]

    gain_out[0] = jnp.concatenate([line(33), line(18)], axis=0)
    gain_out[1] = jnp.concatenate([line(11), line(5)], axis=0)
    shift_out[0] = jnp.concatenate([line(34), line(19)], axis=0)
    shift_out[1] = jnp.concatenate([line(12), line(6)], axis=0)
    for part in range(2):
        lanes = slice(part * width, (part + 1) * width)
        entry_b_out[:, lanes] = jnp.concatenate([line(31 + part), line(9 + part)], axis=0)
    for i in range(3):
        for j in range(3):
            conv_out[i, j] = jnp.concatenate(
                [line(35 + 3 * i + j), line(22 + 3 * i + j)], axis=0
            )
    conv_b_out[...] = jnp.concatenate([line(21), line(8)], axis=0)
    exit_b_out[...] = jnp.concatenate([line(20), line(7)], axis=0)
    for part in range(units // width):
        lanes = slice(part * width, (part + 1) * width)
        expand_b_out[:, lanes] = jnp.concatenate([line(14 + part), line(part)], axis=0)
    shrink_b_out[...] = jnp.concatenate([line(13), line(4)], axis=0)
    for i, (buffer, out) in enumerate(zip(buffers, outs)):
        if i not in sent:
            pltpu.make_async_copy(buffer, out, send_sem.at[i]).start()
    for i, (buffer, out) in enumerate(zip(buffers, outs)):
        pltpu.make_async_copy(buffer, out, send_sem.at[i]).wait()


SMEM = pl.BlockSpec(memory_space=pltpu.SMEM)
VMEM = pl.BlockSpec(memory_space=pltpu.VMEM)


ANYWHERE = pl.BlockSpec(memory_space=pl.ANY)
FAR = pl.BlockSpec(memory_space=pltpu.HBM)


def far(values):
    return pltpu.with_memory_space_constraint(values, pltpu.HBM)


class Moves:
    def __init__(self, fetched, sent):
        self.fetched, self.sent = dict(fetched), dict(sent)
        self.waited, self.started = set(), set()

    def copies(self, ref, part):
        copies = self.fetched[id(ref)]
        return [
            ((id(ref), i), copy)
            for i, copy in enumerate(copies)
            if part is None or len(copies) == 1 or i == part
        ]

    def fetch(self, *refs, part=None):
        for ref in refs:
            for key, copy in self.copies(ref, part):
                if key not in self.started:
                    copy.start()
                    self.started.add(key)

    def need(self, *refs, part=None):
        self.fetch(*refs, part=part)
        for ref in refs:
            for key, copy in self.copies(ref, part):
                if key not in self.waited:
                    copy.wait()
                    self.waited.add(key)

    def send(self, *refs):
        for ref in refs:
            self.sent[id(ref)].start()
            self.started.add(id(ref))

    def finish(self):
        for key, copies in self.fetched.items():
            for i, copy in enumerate(copies):
                if (key, i) not in self.started:
                    copy.start()
                if (key, i) not in self.waited:
                    copy.wait()
        for key, copy in self.sent.items():
            if key not in self.started:
                copy.start()
        for copy in self.sent.values():
            copy.wait()


def halves(ref):
    if ref.shape[-2] != WIN:
        return [pl.ds(0, ref.shape[0])]
    count = ref.shape[0] // 2
    return [pl.ds(0, count), pl.ds(count, count)]


def run(
    kernel,
    scalars,
    arrays,
    outs,
    scratch=(),
    flops=0,
    name=None,
    after=(),
    scalar_outs=(),
    lazy=None,
    vmem=16,
    near=((), ()),
):
    outs = list(outs)
    first_in, first_out = (len(arrays), len(outs)) if lazy is None else lazy
    eager, late = list(arrays[:first_in]), list(arrays[first_in:])
    n_in = len(scalars) + len(eager)
    scratch_shapes = [
        kind if dtype is None else pltpu.VMEM(kind, dtype) for kind, dtype in scratch
    ]
    n_own = len(scratch_shapes)
    n_late, n_sent = len(late), len(outs) - first_out
    if lazy is not None:
        scratch_shapes += [pltpu.VMEM(a.shape, a.dtype) for a in late]
        scratch_shapes += [pltpu.VMEM(*out) for out in outs[first_out:]]
        scratch_shapes += [pltpu.SemaphoreType.DMA((n_late, 2)), pltpu.SemaphoreType.DMA((n_sent,))]

    def body(*refs):
        given, refs = refs[:n_in], refs[n_in:]
        sources, refs = refs[:n_late], refs[n_late + len(after) :]
        results, refs = refs[: len(scalar_outs) + first_out], refs[len(scalar_outs) + first_out :]
        targets, refs = refs[:n_sent], refs[n_sent:]
        own, refs = refs[:n_own], refs[n_own:]
        if lazy is None:
            kernel(*given, *results, *own)
            return
        buffers, leaving = refs[:n_late], refs[n_late : n_late + n_sent]
        fetch_sem, send_sem = refs[n_late + n_sent :]
        moves = Moves(
            [
                (
                    id(buffer),
                    [
                        pltpu.make_async_copy(source.at[part], buffer.at[part], fetch_sem.at[i, j])
                        for j, part in enumerate(halves(buffer))
                    ],
                )
                for i, (source, buffer) in enumerate(zip(sources, buffers))
            ],
            [
                (id(buffer), pltpu.make_async_copy(buffer, target, send_sem.at[i]))
                for i, (buffer, target) in enumerate(zip(leaving, targets))
            ],
        )
        kernel(moves, *given, *buffers, *results, *leaving, *own)
        moves.finish()

    out_shape = [jax.ShapeDtypeStruct(shape, dtype) for shape, dtype in scalar_outs] + [
        pltpu.HBM(shape, dtype)
        if lazy is not None and i not in near[1]
        else jax.ShapeDtypeStruct(shape, dtype)
        for i, (shape, dtype) in enumerate(outs)
    ]
    late = [
        a if i in near[0] else far(a)
        for i, a in enumerate(late, first_in)
    ]
    moved = sum(a.size * a.dtype.itemsize for a in arrays)
    return pl.pallas_call(
        body,
        out_shape=out_shape,
        in_specs=[SMEM] * len(scalars)
        + [VMEM] * len(eager)
        + [ANYWHERE if i in near[0] else FAR for i in range(first_in, len(arrays))]
        + [ANYWHERE] * len(after),
        out_specs=[SMEM] * len(scalar_outs)
        + [VMEM] * first_out
        + [ANYWHERE if i in near[1] else FAR for i in range(first_out, len(outs))],
        scratch_shapes=scratch_shapes,
        compiler_params=pltpu.CompilerParams(vmem_limit_bytes=vmem * 1024 * 1024),
        cost_estimate=pl.CostEstimate(flops=flops, bytes_accessed=moved, transcendentals=0),
        name=name,
    )(*scalars, *eager, *late, *after)


def gate(values, after):
    values, after = list(values), list(after)
    return list(lax.optimization_barrier(tuple(values + after)))[: len(values)]


def swap(values, axis):
    return lax.ppermute(values, axis, [(0, 1), (1, 0)])


def added(values, others):
    return (values.astype(F32) + others.astype(F32)).astype(BF)


def shards(values, ranks):
    return values.reshape(ranks, values.shape[0] // ranks, values.shape[1])


def spread_sum(pieces):
    mine = jnp.sum(pieces.astype(F32), axis=0).astype(BF)
    return jnp.broadcast_to(mine[None], pieces.shape)


def across(values, axes, size, mask):
    return lax.ppermute(values, axes, [(i, i ^ mask) for i in range(size)])


def deal(parts):
    return [parts[0]] + [across(parts[d], ("row", "col"), 4, d) for d in (1, 2, 3)]


RANKS = ("dp", "row")


def stages(ranks):
    bits = ranks.bit_length() - 1
    return [(bit, min(2, bits - bit)) for bit in range(0, bits, 2)]


def scatter_send(values, ranks, stage):
    bit, count = stage
    size = 1 << count
    me = (lax.axis_index(RANKS) >> bit) & (size - 1)
    cut = values.reshape(size, values.shape[0] // size, values.shape[1])
    return [lax.dynamic_index_in_dim(cut, me ^ d, 0, keepdims=False) for d in range(size)]


def scatter_move(parts, ranks, stage):
    return [parts[0]] + [
        across(parts[d], RANKS, ranks, d << stage[0]) for d in range(1, len(parts))
    ]


def scatter_sum(parts):
    return sum(part.astype(F32) for part in parts).astype(BF)


def gather(values, ranks, stage):
    return jnp.stack(
        [values]
        + [across(values, RANKS, ranks, d << stage[0]) for d in range(1, 1 << stage[1])]
    )


def rank_order(rank, ranks):
    order = 0
    for bit, count in stages(ranks):
        order = order * (1 << count) + ((rank >> bit) & ((1 << count) - 1))
    return order


def local(
    groups,
    images,
    cotangent,
    mix_partner,
    cut_partner,
    ratios,
    corners,
    drop_masks,
    norm_gains,
    norm_shifts,
    entry_weight,
    entry_bias,
    position_kernel,
    position_bias,
    exit_weight,
    exit_bias,
    expand_weight,
    expand_bias,
    shrink_weight,
    shrink_bias,
):
    images_here = images.shape[0]
    width = images.shape[3]
    units = expand_weight.shape[2]
    row, col = lax.axis_index("row"), lax.axis_index("col")
    share = images_here // 4
    rows = 4 * share * PAD
    ranks = 2 * groups
    capacity = (2 * images_here + groups - 1) // groups
    slots = groups * capacity
    order = rank_order(lax.axis_index(RANKS), ranks)
    place = jnp.stack(
        [
            lax.axis_index("dp"),
            row,
            col,
            2 * row + col,
            order,
            order // (ranks // 4),
            order % (ranks // 4),
        ]
    ).astype(jnp.int32)
    spots = [0] * ranks
    for rank in range(ranks):
        spots[rank_order(rank, ranks)] = rank
    quad = ((share, TILE, 8, width), BF)
    corners = corners.T
    masks = drop_masks.T
    flat = ((width // 128, images_here * PAD, 128), F32)
    index, take, outgoing, own = run(
        pick_kernel,
        [place, mix_partner, cut_partner],
        [images.transpose(1, 2, 0, 3)],
        [((slots, TILE, 8, width), BF), ((images_here, TILE, 8, width), BF)],
        [flat, (pltpu.SMEM((groups,), jnp.int32), None)],
        name="pick",
        vmem=60,
        scalar_outs=(((slots + 8,), jnp.int32), ((2 * images_here,), jnp.int32)),
    )
    arrived = lax.all_to_all(outgoing, "dp", split_axis=0, concat_axis=0, tiled=True)
    cot = deal(
        run(deal_kernel, [place], [cotangent.transpose(1, 2, 0, 3)], [quad] * 4, [flat], name="deal", vmem=60)
    )
    mixed = deal(
        run(
            mix_kernel,
            [place, take, corners, ratios],
            [arrived, own],
            [quad] * 4,
            name="mix",
            after=cot,
        )
    )
    conv_k = position_kernel.transpose(1, 2, 0, 3)
    tall = (rows, width)
    (
        vec1,
        act_a,
        act_b,
        act_c,
        act_d,
        keep1,
        away1,
        active0,
        slope0,
        win0,
        chance0,
        stripe0,
        mid0,
        win1,
        chance1,
        stripe1,
        hidden1,
        grad1,
    ) = run(
        functools.partial(first_kernel, spots),
        [place, masks],
        [
            *mixed,
            norm_gains,
            norm_shifts,
            entry_bias,
            conv_k,
            position_bias,
            exit_bias,
            expand_bias,
            shrink_bias,
            entry_weight,
            exit_weight,
            expand_weight,
            shrink_weight,
            *cot,
        ],
        [
            ((7, 8, width), F32),
            *([quad] * 4),
            ((units, width), BF),
            ((units, width), BF),
            ((rows, units), BF),
            ((rows, units), BF),
            ((4 * share, WIN, 3 * HALF), BF),
            ((4 * share, WIN, LANES), BF),
            (tall, BF),
            (tall, F32),
            ((4 * share, WIN, 3 * HALF), BF),
            ((4 * share, WIN, LANES), BF),
            (tall, BF),
            (tall, F32),
            (tall, F32),
        ],
        [
            (tall, F32),
            ((rows, 3 * width), F32),
            (tall, F32),
            ((rows, units), BF),
            ((rows, units), BF),
            (tall, BF),
            (tall, BF),
        ],
        flops=10 * rows * width * width * 120,
        name="first",
        vmem=46,
        near=((16, 17, 18, 19), (5, 6)),
        lazy=(12, 1),
    )
    sent1 = shards(added(keep1, swap(away1, "col")), ranks)
    pieces1 = lax.all_to_all(sent1, RANKS, split_axis=0, concat_axis=0, tiled=True)
    vec2, conv2, grad0, delta0, keep2, away2 = run(
        second_kernel,
        [place, masks],
        [
            norm_gains,
            norm_shifts,
            conv_k,
            grad1,
            exit_weight,
            win1,
            chance1,
            hidden1,
            entry_weight,
            stripe1,
            mid0,
            shrink_weight,
            slope0,
            expand_weight,
            active0,
            stripe0,
        ],
        [
            ((15, 8, width), F32),
            ((9, 8, width), F32),
            (tall, F32),
            (tall, F32),
            ((13 * width // 2, width), BF),
            ((13 * width // 2, width), BF),
        ],
        [
            (tall, F32),
            (tall, BF),
            ((rows, 3 * width), F32),
            ((rows, 3 * width), BF),
            (tall, BF),
            (tall, BF),
            ((rows, units), BF),
        ],
        flops=6 * rows * width * width * 120,
        name="second",
        vmem=42,
        near=((), (4, 5)),
        after=[sent1],
        lazy=(3, 2),
    )
    act = deal([act_a, act_b, act_c, act_d])
    keep2, away2, grad0, delta0, *act = gate([keep2, away2, grad0, delta0, *act], [pieces1])
    steps = stages(ranks)

    def first_parts(keep, away):
        other = swap(away, "col")
        count = keep.shape[0] // 4
        return [
            added(keep[d * count : (d + 1) * count], other[d * count : (d + 1) * count])
            for d in range(4)
        ]

    parts2 = first_parts(keep2, away2)
    moved2 = scatter_move(parts2, ranks, steps[0])
    *out_tiles, keep3, away3 = run(
        third_kernel,
        [place],
        [
            norm_gains,
            norm_shifts,
            conv_k,
            vec1,
            vec2,
            conv2,
            delta0,
            win0,
            chance0,
            *mixed,
            entry_weight,
            grad0,
        ],
        [quad] * 4 + [((2 * width, width), BF), ((2 * width, width), BF)],
        [
            (tall, F32),
            ((rows, 3 * width), F32),
            ((rows, 3 * width), BF),
            (tall, BF),
            ((4, 8, width), F32),
            ((9, 8, width), F32),
            ((width, width), F32),
        ],
        flops=3 * rows * width * width * 120,
        name="third",
        vmem=36,
        near=((9, 10, 11, 12), range(6)),
        after=parts2,
        lazy=(6, 0),
    )
    *moved2, keep3, away3 = gate([*moved2, keep3, away3], out_tiles)
    gradient = deal(out_tiles)
    (parted,) = run(
        split_kernel,
        [place, take, corners, ratios],
        gradient,
        [((slots, TILE, 8, width), BF)],
        name="split",
    )
    (activations,) = run(
        lay_kernel, [place], [far(a) for a in act], [((TILE, TILE, images_here, width), BF)], [flat], name="lay"
    )
    mine1 = jnp.sum(pieces1.astype(F32), axis=0).astype(BF)
    mine2 = scatter_sum(moved2)
    moved3 = scatter_move(first_parts(keep3, away3), ranks, steps[0])
    mine3 = scatter_sum(gate(moved3, [mine1]))
    cut = mine2.shape[0] * 4 // ranks
    lot = mine3.shape[0] * 4 // ranks
    joint = jnp.concatenate(
        [
            mine3.reshape(ranks // 4, lot, width),
            mine2.reshape(ranks // 4, cut, width),
        ],
        axis=1,
    ).reshape(-1, width)
    for step in steps[1:]:
        joint = scatter_sum(scatter_move(scatter_send(joint, ranks, step), ranks, step))
    joint = jnp.concatenate([mine1, joint], axis=0)
    counts = (mine1.shape[0], lot, cut)
    for step in reversed(steps[1:]):
        joint = gather(joint, ranks, step).reshape(-1, width)
    joint = shards(joint, ranks // 4)
    (parted,) = gate([parted], [joint])
    back = lax.all_to_all(parted, "dp", split_axis=0, concat_axis=0, tiled=True)
    (back,) = gate([back], [activations])
    (input_gradient,) = run(
        join_kernel,
        [place, index, corners, ratios],
        [*gradient, back],
        [((TILE, TILE, images_here, width), F32)],
        [((width // 128, (images_here + 1) * PAD, 128), F32)],
        name="join",
    )
    full = [joint] + [across(joint, RANKS, ranks, d) for d in (1, 2, 3)]
    full[2:] = gate(full[2:], [input_gradient])
    full += [swap(piece, "col") for piece in full]
    shapes = [
        (2, 2, width),
        (2, 2, width),
        (2, width, 3 * width),
        (2, 2 * width),
        (3, 3, 2, width),
        (2, width),
        (2, width, width),
        (2, width),
        (2, width, units),
        (2, units),
        (2, units, width),
        (2, width),
    ]
    gains, shifts, entry, entry_b, conv, conv_b, exit_, exit_b, expand, expand_b, shrink, shrink_b = (
        pl.pallas_call(
            functools.partial(unpack_kernel, ranks, counts),
            out_shape=[jax.ShapeDtypeStruct(shape, F32) for shape in shapes],
            in_specs=[SMEM] + [ANYWHERE] * 8,
            out_specs=[ANYWHERE] * 12,
            scratch_shapes=[
                pltpu.VMEM((width // 2, width), F32),
                pltpu.VMEM((8,) + joint.shape, BF),
                pltpu.SemaphoreType.DMA((8,)),
            ]
            + [pltpu.VMEM(shape, F32) for shape in shapes]
            + [pltpu.SemaphoreType.DMA((12,))],
            compiler_params=pltpu.CompilerParams(vmem_limit_bytes=24 * 1024 * 1024),
            name="unpack",
        )(place, *full)
    )
    return (
        activations.transpose(2, 0, 1, 3),
        input_gradient.transpose(2, 0, 1, 3),
        gains,
        shifts,
        entry,
        entry_b,
        conv.transpose(2, 0, 1, 3),
        conv_b,
        exit_,
        exit_b,
        expand,
        expand_b,
        shrink,
        shrink_b,
    )


def solution(mesh):
    tiles = P("dp", "row", "col", None)
    return jax.shard_map(
        functools.partial(local, mesh.shape["dp"]),
        mesh=mesh,
        in_specs=(tiles, tiles, P(), P(), P("dp"), P("dp", None), P("dp", None)) + (P(),) * 12,
        out_specs=(tiles, tiles) + (P(),) * 12,
        check_vma=False,
    )
```

```python
import functools

import jax
import jax.numpy as jnp
from jax import lax
from jax.experimental import pallas as pl
from jax.experimental.pallas import tpu as pltpu
from jax.sharding import PartitionSpec as P

TILE = 7
PAD = 56
HEAD_DIM = 32
SIDE_HEADS = 4
HALF = 128
WIN = 2 * PAD
CHUNK = 8 * PAD
LANES = SIDE_HEADS * 128
SCALE = HEAD_DIM ** (-0.5)
LOG2E = 1.4426950408889634
EPS = 1e-05
BF = jnp.bfloat16
F32 = jnp.float32


def dot_nn(a, b):
    return lax.dot_general(a, b, (((1,), (0,)), ((), ())), preferred_element_type=F32)


def dot_nt(a, b):
    return lax.dot_general(a, b, (((1,), (1,)), ((), ())), preferred_element_type=F32)


def dot_tn(a, b):
    return lax.dot_general(a, b, (((0,), (0,)), ((), ())), preferred_element_type=F32)


def norm_parts(values):
    centered = values - jnp.mean(values, axis=-1, keepdims=True)
    inverse = lax.rsqrt(jnp.mean(centered * centered, axis=-1, keepdims=True) + EPS)
    return centered * inverse, inverse


def norm_back(delta, hat, inverse, gain):
    scaled = delta * gain
    first = jnp.mean(scaled, axis=-1, keepdims=True)
    second = jnp.mean(scaled * hat, axis=-1, keepdims=True)
    return inverse * (scaled - first - hat * second)


def gelu_parts(values):
    chance = 0.5 + 0.5 * lax.erf(values * (0.5**0.5))
    density = jnp.exp2(values * values * (-0.5 * LOG2E)) * 0.3989422804014327
    return chance, density


def row_sums(values):
    count, width = values.shape
    return jnp.sum(values.reshape(count // 8, 8, width), axis=0)


def scale_rows(place_ref, mask_ref, column):
    scales = [
        mask_ref[column, 4 * place_ref[3] + i].astype(F32) * 1.25 for i in range(4)
    ]
    columns = [jnp.full((PAD, 1), scale, F32) for scale in scales]
    return jnp.concatenate(columns * (CHUNK // (4 * PAD)), axis=0)


def add_row(acc_ref, row, values):
    acc_ref[row] += values


def spread_heads(values):
    lane = lax.broadcasted_iota(jnp.int32, values.shape, 1) // HEAD_DIM
    empty = jnp.zeros((128 - WIN, HALF), F32)
    blocks = []
    for head in range(SIDE_HEADS):
        blocks.append(jnp.where(lane == head, values, 0.0))
        blocks.append(empty)
    return jnp.concatenate(blocks, axis=0).astype(BF)


def over_keys(weights, values):
    weights = fill_rows(weights)
    stacked = jnp.concatenate(
        [weights[:, head * 128 : (head + 1) * 128] for head in range(SIDE_HEADS)], axis=0
    )
    return dot_tn(stacked, spread_heads(values))[:WIN]


def fill_rows(values):
    empty = jnp.zeros((128 - WIN, values.shape[1]), values.dtype)
    return jnp.concatenate([values, empty], axis=0)


def valid_column(shape):
    return lax.broadcasted_iota(jnp.int32, shape, 1) != 7


def valid_rows(shape):
    return lax.broadcasted_iota(jnp.int32, shape, 0) % 8 != 7


def column_shifts(values, across):
    cube = values.reshape(2 * TILE, 8, HALF)
    if not across:
        return (pltpu.roll(cube, 1, 1), cube, pltpu.roll(cube, 7, 1))
    left, right = cube[:TILE], cube[TILE:]
    column = lax.broadcasted_iota(jnp.int32, left.shape, 1)
    before = jnp.concatenate(
        [
            pltpu.roll(left, 1, 1),
            jnp.where(column == 0, pltpu.roll(left, 2, 1), pltpu.roll(right, 1, 1)),
        ],
        axis=0,
    )
    after = jnp.concatenate(
        [
            jnp.where(column == 6, pltpu.roll(right, 6, 1), pltpu.roll(left, 7, 1)),
            pltpu.roll(right, 7, 1),
        ],
        axis=0,
    )
    return (before, cube, after)


def row_shift(cube, step, across):
    if step == 0:
        return cube
    empty = jnp.zeros((1, 8, HALF), F32)

    def move(part):
        if step < 0:
            return jnp.concatenate([empty, part[:-1]], axis=0)
        return jnp.concatenate([part[1:], empty], axis=0)

    if across:
        return jnp.concatenate([move(cube[:TILE]), move(cube[TILE:])], axis=0)
    return move(cube)


def window_conv(shifts, kernel_at, across):
    total = None
    for i in range(3):
        part = None
        for j in range(3):
            term = kernel_at(i, j) * shifts[j]
            part = term if part is None else part + term
        part = row_shift(part, i - 1, across)
        total = part if total is None else total + part
    return total.reshape(WIN, HALF)


def window_rows(across, window):
    side, image = window // 4, window % 4
    if across:
        first, second = 2 * side, 2 * side + 1
    else:
        first, second = side, 2 + side
    return (
        pl.multiple_of((first * 4 + image) * PAD, 8),
        pl.multiple_of((second * 4 + image) * PAD, 8),
    )


def take_window(ref, at, lane):
    return jnp.concatenate(
        [ref[pl.ds(at[0], PAD), lane : lane + HALF], ref[pl.ds(at[1], PAD), lane : lane + HALF]],
        axis=0,
    )


def put_window(ref, at, lane, values):
    ref[pl.ds(at[0], PAD), lane : lane + HALF] = values[:PAD]
    ref[pl.ds(at[1], PAD), lane : lane + HALF] = values[PAD:]


def round_bf(values):
    return values.astype(BF).astype(F32)


def attention_forward(
    block, hidden_ref, gains, shifts, entry_w, entry_b, conv_k, conv_b, wide, stripe, win_out, chance_out
):
    width = hidden_ref.shape[1]

    @pl.loop(0, 2)
    def _(t):
        rows = chunk(t)
        hat, _ = norm_parts(hidden_ref[rows, :])
        normed = (hat * gains[block, 0:1, :] + shifts[block, 0:1, :]).astype(BF)
        for part in range(3):
            out = dot_nn(normed, entry_w[block, :, part * width : (part + 1) * width])
            if part != 1:
                at = 0 if part == 0 else width
                out = out + entry_b[block : block + 1, at : at + width]
            wide[rows, part * width : (part + 1) * width] = round_bf(out)

    for direction in range(2):
        across = direction == 0
        lane = direction * HALF

        @pl.loop(0, 8, unroll=8)
        def _(window, across=across, lane=lane, direction=direction):
            at = window_rows(across, window)
            queries = take_window(wide, at, lane)
            keys = take_window(wide, at, width + lane)
            values = take_window(wide, at, 2 * width + lane)
            keys_bf = keys.astype(BF)
            win_out[direction * 8 + window, :, 0:HALF] = queries.astype(BF)
            win_out[direction * 8 + window, :, HALF : 2 * HALF] = keys_bf
            win_out[direction * 8 + window, :, 2 * HALF : 3 * HALF] = values.astype(BF)
            scores = dot_nt(keys_bf, spread_heads(queries)).reshape(2 * TILE, 8, LANES)
            scores = jnp.where(valid_column((1, 8, LANES)), scores, -1e30)
            top = jnp.max(jnp.max(scores, axis=0), axis=0, keepdims=True)
            lifted = jnp.exp2((scores - top) * (SCALE * LOG2E))
            totals = jnp.sum(jnp.sum(lifted, axis=0), axis=0, keepdims=True)
            chances = (lifted * (1.0 / totals)).reshape(WIN, LANES).astype(BF)
            chance_out[direction * 8 + window] = chances
            attended = over_keys(chances, values)
            clean = jnp.where(valid_rows(values.shape), values, 0.0)
            position = window_conv(
                column_shifts(clean, across),
                lambda i, j: conv_k[i, j, block : block + 1, lane : lane + HALF],
                across,
            )
            put_window(
                stripe, at, lane, attended + position + conv_b[block : block + 1, lane : lane + HALF]
            )


def attention_backward(
    ready,
    block,
    win_in,
    chance_in,
    conv_k,
    stripe_delta,
    wide,
    conv_acc,
):
    width = stripe_delta.shape[1]
    for direction in range(2):
        ready(direction)
        across = direction == 0
        lane = direction * HALF

        @pl.loop(0, 8, unroll=8)
        def _(window, across=across, lane=lane, direction=direction):
            at = window_rows(across, window)
            out_delta = take_window(stripe_delta, at, lane)
            queries = win_in[direction * 8 + window, :, 0:HALF].astype(F32)
            keys = win_in[direction * 8 + window, :, HALF : 2 * HALF].astype(F32)
            values_bf = win_in[direction * 8 + window, :, 2 * HALF : 3 * HALF]
            values = values_bf.astype(F32)
            chances = chance_in[direction * 8 + window]
            delta_spread = spread_heads(out_delta)
            chance_delta = dot_nt(values_bf, delta_spread)
            cubes = (2 * TILE, 8, LANES)
            wide_chances = chances.astype(F32).reshape(cubes)
            weighted = wide_chances * chance_delta.reshape(cubes)
            common = jnp.sum(jnp.sum(weighted, axis=0), axis=0, keepdims=True)
            score_delta = (weighted - wide_chances * common).reshape(WIN, LANES).astype(BF)
            values_delta = dot_nn(chances, delta_spread)
            keys_delta = dot_nn(score_delta, spread_heads(queries)) * SCALE
            query_delta = over_keys(score_delta, keys) * SCALE
            keep = valid_rows(values.shape)
            clean = jnp.where(keep, values, 0.0)
            shifts = column_shifts(clean, across)
            cube = out_delta.reshape(2 * TILE, 8, HALF)
            for i in range(3):
                moved = row_shift(cube, 1 - i, across)
                for j in range(3):
                    conv_acc[3 * i + j, :, lane : lane + HALF] += jnp.sum(moved * shifts[j], axis=0)
            back = window_conv(
                column_shifts(out_delta, across),
                lambda i, j: conv_k[2 - i, 2 - j, block : block + 1, lane : lane + HALF],
                across,
            )
            values_delta = jnp.where(keep, values_delta + back, 0.0)
            put_window(wide, at, lane, query_delta)
            put_window(wide, at, width + lane, keys_delta)
            put_window(wide, at, 2 * width + lane, values_delta)


def chunk(t):
    return pl.ds(pl.multiple_of(t * CHUNK, CHUNK), CHUNK)


class Bundle:
    def __init__(self, place_ref, keep, away, chunks=1, spot=lambda chunk: chunk):
        self.place_ref, self.keep, self.away = place_ref, keep, away
        self.step, self.spot = keep.shape[0] // chunks, spot

    def put(self, at, values):
        values = values.astype(BF)
        half, step = self.keep.shape[0], self.step
        last = at + values.shape[0]
        first = at
        while first < last:
            stop = min(last, (first // step + 1) * step)
            number = first // half
            start = self.spot(first % half // step) * step
            inner, count = first % step, stop - first
            if not isinstance(start, int):
                start = pl.multiple_of(start, step)
            rows = pl.ds(start + inner, count)
            piece = values[first - at : stop - at]

            @pl.when(self.place_ref[2] == number)
            def _(piece=piece, rows=rows):
                self.keep[rows, :] = piece

            @pl.when(self.place_ref[2] != number)
            def _(piece=piece, rows=rows):
                self.away[rows, :] = piece

            first = stop


def put_squares(bundle, at, values, side):
    for part in range(values.shape[1] // side):
        bundle.put(at + part * side, values[:, part * side : (part + 1) * side])


def load_tiles(place_ref, tiles, hidden):
    for d, tile in enumerate(tiles):
        at = jnp.bitwise_xor(place_ref[3], d) * (4 * PAD)
        rows = pl.ds(pl.multiple_of(at, 4 * PAD), 4 * PAD)
        hidden[rows, :] = tile[...].astype(F32).reshape(4 * PAD, hidden.shape[1])


def store_tile(place_ref, tiles, t, values):
    count = CHUNK // (4 * PAD)
    values = values.reshape((count,) + tiles[0].shape).astype(BF)
    for part in range(count):
        for d, tile in enumerate(tiles):

            @pl.when(jnp.bitwise_xor(place_ref[3], d) == count * t + part)
            def _(tile=tile, part=part):
                tile[...] = values[part]


def first_kernel(
    spots,
    moves,
    place_ref,
    mask_ref,
    mixed_a,
    mixed_b,
    mixed_c,
    mixed_d,
    gains,
    shifts,
    entry_b,
    conv_k,
    conv_b,
    exit_b,
    expand_b,
    shrink_b,
    cot_a,
    cot_b,
    cot_c,
    cot_d,
    entry_w,
    exit_w,
    expand_w,
    shrink_w,
    vec_out,
    keep_out,
    away_out,
    act_a,
    act_b,
    act_c,
    act_d,
    active0_out,
    slope0_out,
    win0_out,
    chance0_out,
    stripe0_out,
    mid0_out,
    win1_out,
    chance1_out,
    stripe1_out,
    hidden1_out,
    grad_out,
    hidden,
    wide,
    stripe,
    active1,
    pre1,
    feed1,
    inner1,
):
    width = hidden.shape[1]
    hidden_units = expand_w.shape[2]
    bundle = Bundle(place_ref, keep_out, away_out, len(spots), lambda chunk: spots[chunk])
    vec_out[...] = jnp.zeros(vec_out.shape, F32)
    moves.fetch(entry_w)
    load_tiles(place_ref, (mixed_a, mixed_b, mixed_c, mixed_d), hidden)
    moves.need(entry_w)
    moves.fetch(exit_w, expand_w, shrink_w, cot_a, cot_b, cot_c, cot_d)

    for block in range(2):
        win_out, chance_out, stripe_out = (
            (win0_out, chance0_out, stripe0_out),
            (win1_out, chance1_out, stripe1_out),
        )[block]
        attention_forward(
            block, hidden, gains, shifts, entry_w, entry_b, conv_k, conv_b, wide, stripe, win_out, chance_out
        )
        moves.send(win_out, chance_out)
        moves.need(exit_w, expand_w, shrink_w)
        if block == 1:
            moves.need(cot_a, cot_b, cot_c, cot_d)
            load_tiles(place_ref, (cot_a, cot_b, cot_c, cot_d), grad_out)

        @pl.loop(0, 2)
        def _(t, block=block, stripe_out=stripe_out):
            rows = chunk(t)
            striped = stripe[rows, :].astype(BF)
            stripe_out[rows, :] = striped
            branch = dot_nn(striped, exit_w[block]) + exit_b[block : block + 1, :]
            midway = hidden[rows, :] + scale_rows(place_ref, mask_ref, 2 * block) * branch
            if block == 0:
                mid0_out[rows, :] = midway
            hat, inverse = norm_parts(midway)
            normed = (hat * gains[block, 1:2, :] + shifts[block, 1:2, :]).astype(BF)
            feed_scale = scale_rows(place_ref, mask_ref, 2 * block + 1)
            feed = shrink_b[block : block + 1, :]
            if block == 1:
                inner1[rows, :] = normed
                gradient = grad_out[rows, :]
                feed_delta = (feed_scale * gradient).astype(BF)
                feed1[rows, :] = feed_delta
                add_row(vec_out, 4, row_sums(feed_delta.astype(F32)))
                inner_delta = jnp.zeros((CHUNK, width), F32)
            for part in range(hidden_units // width):
                at = slice(part * width, (part + 1) * width)
                pre_act = dot_nn(normed, expand_w[block, :, at]) + expand_b[block : block + 1, at]
                chance, density = gelu_parts(pre_act)
                active = (pre_act * chance).astype(BF)
                slope = chance + pre_act * density
                if block == 0:
                    active0_out[rows, at] = active
                    slope0_out[rows, at] = slope.astype(BF)
                else:
                    active1[rows, at] = active
                    pre_delta = (dot_nt(feed_delta, shrink_w[block, at, :]) * slope).astype(BF)
                    pre1[rows, at] = pre_delta
                    add_row(vec_out, part, row_sums(pre_delta.astype(F32)))
                    inner_delta = inner_delta + dot_nt(pre_delta, expand_w[block, :, at])
                feed = feed + dot_nn(active, shrink_w[block, at, :])
            output = midway + feed_scale * feed
            if block == 0:
                hidden[rows, :] = output
                hidden1_out[rows, :] = output
            else:
                store_tile(place_ref, (act_a, act_b, act_c, act_d), t, output)
                add_row(vec_out, 5, row_sums(inner_delta * hat))
                add_row(vec_out, 6, row_sums(inner_delta))
                grad_out[rows, :] = gradient + norm_back(
                    inner_delta, hat, inverse, gains[block, 1:2, :]
                )

        moves.send(stripe_out)
        if block == 0:
            moves.send(mid0_out, active0_out, slope0_out, hidden1_out)
        else:
            moves.send(act_a, act_b, act_c, act_d, grad_out)

    put_squares(bundle, 0, dot_tn(inner1[...], pre1[...]), width)
    for part in range(hidden_units // width):
        bundle.put(
            hidden_units + part * width,
            dot_tn(active1[:, part * width : (part + 1) * width], feed1[...]),
        )


def delta_rows(block, place_ref, mask_ref, exit_w, grad_ref, stripe_delta, branch_delta, vec_out, at):
    @pl.loop(0, 2)
    def _(t):
        rows = chunk(t)
        rounded = (scale_rows(place_ref, mask_ref, 2 * block) * grad_ref[rows, :]).astype(BF)
        branch_delta[rows, :] = rounded
        add_row(vec_out, at, row_sums(rounded.astype(F32)))
        out = round_bf(dot_nt(rounded, exit_w[block]))
        stripe_delta[rows, :] = out
        add_row(vec_out, at + 1, row_sums(out))


def entry_backward(block, hidden_ref, gains, shifts, entry_w, grad_ref, wide, wide_bf, normed_bf, vec_out, at, emit):
    width = hidden_ref.shape[1]

    @pl.loop(0, 2)
    def _(t):
        rows = chunk(t)
        hat, inverse = norm_parts(hidden_ref[rows, :])
        normed_bf[rows, :] = (hat * gains[block, 0:1, :] + shifts[block, 0:1, :]).astype(BF)
        delta = jnp.zeros((CHUNK, width), F32)
        for part in range(3):
            lanes = slice(part * width, (part + 1) * width)
            rounded = wide[rows, lanes].astype(BF)
            wide_bf[rows, lanes] = rounded
            if part != 1:
                add_row(vec_out, at + part // 2, row_sums(rounded.astype(F32)))
            delta = delta + dot_nt(rounded, entry_w[block, :, lanes])
        add_row(vec_out, at + 2, row_sums(delta * hat))
        add_row(vec_out, at + 3, row_sums(delta))
        emit(t, rows, grad_ref[rows, :] + norm_back(delta, hat, inverse, gains[block, 0:1, :]))


def second_kernel(
    moves,
    place_ref,
    mask_ref,
    gains,
    shifts,
    conv_k,
    grad_in,
    exit_w,
    win1,
    chance1,
    hidden1,
    entry_w,
    stripe1,
    mid0,
    shrink_w,
    slope0,
    expand_w,
    active0,
    stripe0,
    vec_out,
    conv_out,
    keep_out,
    away_out,
    grad_out,
    stripe_delta_out,
    stripe_delta,
    branch_delta,
    wide,
    wide_bf,
    normed_bf,
    feed0,
    pre0,
):
    grad = grad_out
    width = grad.shape[1]
    hidden_units = expand_w.shape[2]
    bundle = Bundle(
        place_ref, keep_out, away_out, 4, lambda chunk: jnp.bitwise_xor(place_ref[5], chunk)
    )
    vec_out[...] = jnp.zeros(vec_out.shape, F32)
    conv_out[...] = jnp.zeros(conv_out.shape, F32)
    moves.fetch(grad_in, exit_w)
    moves.fetch(win1, chance1, part=0)
    moves.need(grad_in, exit_w)
    moves.fetch(win1, chance1, part=1)
    delta_rows(1, place_ref, mask_ref, exit_w, grad_in, stripe_delta, branch_delta, vec_out, 0)

    def ready(direction):
        moves.need(win1, chance1, part=direction)
        if direction == 0:
            moves.fetch(hidden1, entry_w, stripe1)
        else:
            moves.fetch(mid0, shrink_w, slope0, expand_w, active0, stripe0)

    attention_backward(ready, 1, win1, chance1, conv_k, stripe_delta, wide, conv_out)

    def emit(t, rows, values):
        grad[rows, :] = values

    moves.need(hidden1, entry_w)
    entry_backward(
        1, hidden1, gains, shifts, entry_w, grad_in, wide, wide_bf, normed_bf, vec_out, 2, emit
    )
    put_squares(bundle, 0, dot_tn(normed_bf[...], wide_bf[...]), width)
    moves.need(stripe1)
    bundle.put(3 * width, dot_tn(stripe1[...], branch_delta[...]))
    moves.need(mid0, shrink_w, slope0, expand_w)

    @pl.loop(0, 2)
    def _(t):
        rows = chunk(t)
        gradient = grad[rows, :]
        hat, inverse = norm_parts(mid0[rows, :])
        normed_bf[rows, :] = (hat * gains[0, 1:2, :] + shifts[0, 1:2, :]).astype(BF)
        feed_delta = (scale_rows(place_ref, mask_ref, 1) * gradient).astype(BF)
        feed0[rows, :] = feed_delta
        add_row(vec_out, 6, row_sums(feed_delta.astype(F32)))
        inner_delta = jnp.zeros((CHUNK, width), F32)
        for part in range(hidden_units // width):
            at = slice(part * width, (part + 1) * width)
            pre_delta = (
                dot_nt(feed_delta, shrink_w[0, at, :]) * slope0[rows, at].astype(F32)
            ).astype(BF)
            pre0[rows, at] = pre_delta
            add_row(vec_out, 7 + part, row_sums(pre_delta.astype(F32)))
            inner_delta = inner_delta + dot_nt(pre_delta, expand_w[0, :, at])
        add_row(vec_out, 11, row_sums(inner_delta * hat))
        add_row(vec_out, 12, row_sums(inner_delta))
        grad[rows, :] = gradient + norm_back(inner_delta, hat, inverse, gains[0, 1:2, :])

    delta_rows(0, place_ref, mask_ref, exit_w, grad, stripe_delta_out, branch_delta, vec_out, 13)
    moves.send(grad_out, stripe_delta_out)
    moves.need(active0, stripe0)
    put_squares(bundle, 4 * width, dot_tn(normed_bf[...], pre0[...]), width)
    for part in range(hidden_units // width):
        bundle.put(
            (8 + part) * width,
            dot_tn(active0[:, part * width : (part + 1) * width], feed0[...]),
        )
    bundle.put(12 * width, dot_tn(stripe0[...], branch_delta[...]))


def third_kernel(
    moves,
    place_ref,
    gains,
    shifts,
    conv_k,
    vec1,
    vec2,
    conv2,
    mixed_a,
    mixed_b,
    mixed_c,
    mixed_d,
    stripe_delta,
    win0,
    chance0,
    entry_w,
    grad_in,
    out_a,
    out_b,
    out_c,
    out_d,
    keep_out,
    away_out,
    hidden,
    wide,
    wide_bf,
    normed_bf,
    vec3,
    conv3,
    flat,
):
    width = hidden.shape[1]
    bundle = Bundle(
        place_ref, keep_out, away_out, 4, lambda chunk: jnp.bitwise_xor(place_ref[5], chunk)
    )
    vec3[...] = jnp.zeros(vec3.shape, F32)
    conv3[...] = jnp.zeros(conv3.shape, F32)
    moves.fetch(stripe_delta)
    moves.fetch(win0, chance0, part=0)
    moves.need(stripe_delta)
    moves.fetch(win0, chance0, part=1)

    def ready(direction):
        moves.need(win0, chance0, part=direction)
        if direction == 0:
            moves.fetch(mixed_a, mixed_b, mixed_c, mixed_d, entry_w, grad_in)

    attention_backward(ready, 0, win0, chance0, conv_k, stripe_delta, wide, conv3)

    def emit(t, rows, values):
        store_tile(place_ref, (out_a, out_b, out_c, out_d), t, values)

    moves.need(mixed_a, mixed_b, mixed_c, mixed_d, entry_w, grad_in)
    load_tiles(place_ref, (mixed_a, mixed_b, mixed_c, mixed_d), hidden)
    entry_backward(
        0, hidden, gains, shifts, entry_w, grad_in, wide, wide_bf, normed_bf, vec3, 0, emit
    )
    moves.send(out_a, out_b, out_c, out_d)
    flat[...] = jnp.zeros(flat.shape, F32)
    at = 0
    for ref in (vec1, vec2, conv2, vec3, conv3):
        flat[at : at + ref.shape[0], :] = jnp.sum(ref[...], axis=1)
        at += ref.shape[0]
    spread = dot_tn(normed_bf[...], wide_bf[...])
    half = keep_out.shape[0]
    middle = width // 2
    lots = flat.shape[0] // 2
    bundle.put(0, spread[:, :width])
    bundle.put(width, spread[:middle, width : 2 * width])
    bundle.put(width + middle, flat[:lots, :])
    bundle.put(half, spread[middle:, width : 2 * width])
    bundle.put(half + middle, spread[:, 2 * width :])
    bundle.put(half + middle + width, flat[lots:, :])


def untangle(source, flat, target):
    count, width = source.shape[2:]
    lanes = flat.shape[0]
    for row in range(TILE):
        flat[:, pl.ds(row * 8 + 7, count, stride=PAD), :] = jnp.zeros((lanes, count, 128), F32)
        for col in range(TILE):
            token = source[row, col].astype(F32)
            for lane in range(lanes):
                flat[lane, pl.ds(row * 8 + col, count, stride=PAD), :] = token[
                    :, lane * 128 : (lane + 1) * 128
                ]

    @pl.loop(0, count)
    def _(n):
        rows = pl.ds(pl.multiple_of(n * PAD, 8), PAD)
        tile = jnp.concatenate([flat[lane, rows, :] for lane in range(lanes)], axis=1)
        target(n, tile.reshape(TILE, 8, width).astype(BF))


def owner_of(wanted, count):
    if count & (count - 1) == 0:
        return lax.shift_right_logical(wanted, count.bit_length() - 1)
    return lax.div(wanted, count)


def pick_kernel(
    place_ref, mix_ref, cut_ref, images_ref, index_out, take_out, sent_out, own_out, flat, counts
):
    count = images_ref.shape[2]
    slots = sent_out.shape[0]
    capacity = slots // counts.shape[0]
    me = place_ref[0]

    def put(n, tile):
        own_out[n] = tile

    untangle(images_ref, flat, put)

    @pl.loop(0, slots, unroll=8)
    def _(s):
        index_out[s] = count

    @pl.loop(0, counts.shape[0])
    def _(g):
        counts[g] = 0
        rank = g * capacity
        for ref in (mix_ref, cut_ref):
            for j in range(count):
                wanted = ref[g * count + j]
                owner = owner_of(wanted, count)
                hit = owner == me
                index_out[jnp.where(hit, rank, slots)] = wanted - owner * count
                rank = rank + hit.astype(jnp.int32)

    @pl.loop(0, slots)
    def _(s):
        sent_out[s] = own_out[jnp.minimum(index_out[s], count - 1)]

    for part, ref in enumerate((mix_ref, cut_ref)):

        @pl.loop(0, count)
        def _(j, part=part, ref=ref):
            owner = owner_of(ref[me * count + j], count)
            rank = counts[owner]
            take_out[part * count + j] = owner * capacity + rank
            counts[owner] = rank + 1


def deal_kernel(place_ref, source, out_a, out_b, out_c, out_d, flat):
    outs = (out_a, out_b, out_c, out_d)
    share = out_a.shape[0]

    def put(n, tile):
        for d, out in enumerate(outs):

            @pl.when(jnp.bitwise_xor(place_ref[3], d) == n // share)
            def _(out=out):
                out[n % share] = tile

    untangle(source, flat, put)


def inside_box(corner_ref, n, place_ref):
    shape = (TILE, 8, 1)
    row = place_ref[1] * TILE + lax.broadcasted_iota(jnp.int32, shape, 0)
    col = place_ref[2] * TILE + lax.broadcasted_iota(jnp.int32, shape, 1)
    hit = (
        (row >= corner_ref[0, n])
        & (row < corner_ref[1, n])
        & (col >= corner_ref[2, n])
        & (col < corner_ref[3, n])
    )
    return jnp.where(hit, 1.0, 0.0)


def mix_kernel(
    place_ref, take_ref, corner_ref, ratio_ref, arrived, own_ref, out_a, out_b, out_c, out_d
):
    count = own_ref.shape[0]
    share = out_a.shape[0]
    for d, out in enumerate((out_a, out_b, out_c, out_d)):

        @pl.loop(0, share)
        def _(i, d=d, out=out):
            n = jnp.bitwise_xor(place_ref[3], d) * share + i
            inside = inside_box(corner_ref, n, place_ref)
            ratio = ratio_ref[n]
            own = own_ref[n].astype(F32)
            blend = arrived[take_ref[n]].astype(F32)
            cut = arrived[take_ref[count + n]].astype(F32)
            mixed = inside * cut + (1.0 - inside) * (ratio * own + (1.0 - ratio) * blend)
            out[i] = mixed.astype(BF)


def split_kernel(
    place_ref, take_ref, corner_ref, ratio_ref, grad_a, grad_b, grad_c, grad_d, out_ref
):
    share = grad_a.shape[0]
    count = 4 * share
    if out_ref.shape[0] > 2 * count:
        out_ref[...] = jnp.zeros(out_ref.shape, BF)
    for d, grad_ref in enumerate((grad_a, grad_b, grad_c, grad_d)):

        @pl.loop(0, share)
        def _(i, d=d, grad_ref=grad_ref):
            n = jnp.bitwise_xor(place_ref[3], d) * share + i
            inside = inside_box(corner_ref, n, place_ref)
            gradient = grad_ref[i].astype(F32)
            cut = inside * gradient
            out_ref[take_ref[n]] = ((1.0 - ratio_ref[n]) * (gradient - cut)).astype(BF)
            out_ref[take_ref[count + n]] = cut.astype(BF)


def join_kernel(
    place_ref,
    index_ref,
    corner_ref,
    ratio_ref,
    grad_a,
    grad_b,
    grad_c,
    grad_d,
    back_ref,
    out_ref,
    total,
):
    count, width = out_ref.shape[2:]
    share = grad_a.shape[0]

    def tile_rows(n):
        return pl.ds(pl.multiple_of(n * PAD, 8), PAD)

    for d, grad_ref in enumerate((grad_a, grad_b, grad_c, grad_d)):

        @pl.loop(0, share)
        def _(i, d=d, grad_ref=grad_ref):
            n = jnp.bitwise_xor(place_ref[3], d) * share + i
            outside = 1.0 - inside_box(corner_ref, n, place_ref)
            kept = ratio_ref[n] * outside * grad_ref[i].astype(F32)
            kept = kept.reshape(PAD, width)
            for lane in range(total.shape[0]):
                total[lane, tile_rows(n), :] = kept[:, lane * 128 : (lane + 1) * 128]

    @pl.loop(0, back_ref.shape[0])
    def _(s):
        piece = back_ref[s].astype(F32).reshape(PAD, width)
        for lane in range(total.shape[0]):
            total[lane, tile_rows(index_ref[s]), :] += piece[:, lane * 128 : (lane + 1) * 128]

    for row in range(TILE):
        for col in range(TILE):
            out_ref[row, col] = jnp.concatenate(
                [
                    total[lane, pl.ds(row * 8 + col, count, stride=PAD), :]
                    for lane in range(total.shape[0])
                ],
                axis=1,
            )


def lay_kernel(place_ref, act_a, act_b, act_c, act_d, out_ref, flat):
    count, width = out_ref.shape[2:]
    share = act_a.shape[0]
    for d, act_ref in enumerate((act_a, act_b, act_c, act_d)):

        @pl.loop(0, share)
        def _(i, d=d, act_ref=act_ref):
            n = jnp.bitwise_xor(place_ref[3], d) * share + i
            tile = act_ref[i].astype(F32).reshape(PAD, width)
            for lane in range(flat.shape[0]):
                flat[lane, pl.ds(pl.multiple_of(n * PAD, 8), PAD), :] = tile[
                    :, lane * 128 : (lane + 1) * 128
                ]

    for row in range(TILE):
        for col in range(TILE):
            out_ref[row, col] = jnp.concatenate(
                [
                    flat[lane, pl.ds(row * 8 + col, count, stride=PAD), :]
                    for lane in range(flat.shape[0])
                ],
                axis=1,
            ).astype(BF)


def unpack_kernel(
    ranks,
    counts,
    place_ref,
    *refs,
):
    pieces, refs = refs[:8], refs[8:]
    outs, (vectors, *buffers, send_sem) = refs[:12], refs[12:]
    (
        gain_out,
        shift_out,
        entry_out,
        entry_b_out,
        conv_out,
        conv_b_out,
        exit_out,
        exit_b_out,
        expand_out,
        expand_b_out,
        shrink_out,
        shrink_b_out,
    ) = buffers
    width = exit_out.shape[1]
    units = expand_out.shape[2]
    middle = width // 2

    def squares(out_ref, block, count):
        return [(out_ref, block, 0, part * width, width) for part in range(count)]

    def tall(out_ref, block, count):
        return [(out_ref, block, part * width, 0, width) for part in range(count)]

    plans = (
        squares(expand_out, 1, units // width) + tall(shrink_out, 1, units // width),
        [
            (entry_out, 0, 0, 0, width),
            (entry_out, 0, 0, width, middle),
            (vectors, None, 0, 0, middle),
            (entry_out, 0, middle, width, middle),
            (entry_out, 0, 0, 2 * width, width),
        ],
        squares(entry_out, 1, 3)
        + tall(exit_out, 1, 1)
        + squares(expand_out, 0, units // width)
        + tall(shrink_out, 0, units // width)
        + tall(exit_out, 0, 1),
    )
    inner_ranks = ranks // 4
    moves = []
    base = 0
    for plan, count in zip(plans, counts):
        at = 0
        for out_ref, block, first_row, lane, length in plan:
            done = 0
            while done < length:
                step = min(length - done, count - at % count)
                moves.append((out_ref, block, first_row + done, lane, base, count, at, step))
                at += step
                done += step
        base += count
    big = (expand_out, shrink_out, entry_out, exit_out)
    leaving = []

    def leave(buffer, out):
        copy = pltpu.make_async_copy(buffer, out, send_sem.at[len(leaving)])
        leaving.append(copy)
        return copy

    def place_parts(target, wanted, col, own):
        for out_ref, block, first_row, lane, base, count, at, step in moves:
            if out_ref is not target or block != wanted:
                continue
            shard, start = at // count, base + at % count
            half, shard = shard // ranks, shard % ranks
            first, inner = shard // inner_ranks, shard % inner_ranks
            piece = pieces[4 * (col ^ half) + (own ^ first)]
            inner = jnp.bitwise_xor(place_ref[6], inner)
            values = piece[inner, start : start + step, :].astype(F32)
            place = slice(first_row, first_row + step)
            if block is None:
                out_ref[place, :] = values
            else:
                out_ref[block, place, lane : lane + width] = values

    first_sends = {}
    for block in (1, 0):
        for target in big:
            i = [j for j, ref in enumerate(buffers) if ref is target][0]
            first_sends[block, i] = leave(target.at[block], outs[i].at[block])
    for col in range(2):
        for own in range(4):

            @pl.when((place_ref[2] == col) & (place_ref[5] == own))
            def _(col=col, own=own):
                place_parts(vectors, None, col, own)
                for (block, i), copy in first_sends.items():
                    place_parts(buffers[i], block, col, own)
                    copy.start()

    def line(n):
        return vectors[n : n + 1, :]

    gain_out[0] = jnp.concatenate([line(33), line(18)], axis=0)
    gain_out[1] = jnp.concatenate([line(11), line(5)], axis=0)
    shift_out[0] = jnp.concatenate([line(34), line(19)], axis=0)
    shift_out[1] = jnp.concatenate([line(12), line(6)], axis=0)
    for part in range(2):
        lanes = slice(part * width, (part + 1) * width)
        entry_b_out[:, lanes] = jnp.concatenate([line(31 + part), line(9 + part)], axis=0)
    for i in range(3):
        for j in range(3):
            conv_out[i, j] = jnp.concatenate(
                [line(35 + 3 * i + j), line(22 + 3 * i + j)], axis=0
            )
    conv_b_out[...] = jnp.concatenate([line(21), line(8)], axis=0)
    exit_b_out[...] = jnp.concatenate([line(20), line(7)], axis=0)
    for part in range(units // width):
        lanes = slice(part * width, (part + 1) * width)
        expand_b_out[:, lanes] = jnp.concatenate([line(14 + part), line(part)], axis=0)
    shrink_b_out[...] = jnp.concatenate([line(13), line(4)], axis=0)
    for buffer, out in zip(buffers, outs):
        if not any(buffer is ref for ref in big):
            leave(buffer, out).start()
    for copy in leaving:
        copy.wait()


SMEM = pl.BlockSpec(memory_space=pltpu.SMEM)
VMEM = pl.BlockSpec(memory_space=pltpu.VMEM)


ANYWHERE = pl.BlockSpec(memory_space=pl.ANY)
FAR = pl.BlockSpec(memory_space=pltpu.HBM)


def far(values):
    return pltpu.with_memory_space_constraint(values, pltpu.HBM)


class Moves:
    def __init__(self, fetched, sent):
        self.fetched, self.sent = dict(fetched), dict(sent)
        self.waited, self.started = set(), set()

    def copies(self, ref, part):
        copies = self.fetched.get(id(ref), [])
        return [
            ((id(ref), i), copy)
            for i, copy in enumerate(copies)
            if part is None or len(copies) == 1 or i == part
        ]

    def fetch(self, *refs, part=None):
        for ref in refs:
            for key, copy in self.copies(ref, part):
                if key not in self.started:
                    copy.start()
                    self.started.add(key)

    def need(self, *refs, part=None):
        self.fetch(*refs, part=part)
        for ref in refs:
            for key, copy in self.copies(ref, part):
                if key not in self.waited:
                    copy.wait()
                    self.waited.add(key)

    def send(self, *refs):
        for ref in refs:
            if id(ref) in self.sent:
                self.sent[id(ref)].start()
                self.started.add(id(ref))

    def finish(self):
        for key, copies in self.fetched.items():
            for i, copy in enumerate(copies):
                if (key, i) not in self.started:
                    copy.start()
                if (key, i) not in self.waited:
                    copy.wait()
        for key, copy in self.sent.items():
            if key not in self.started:
                copy.start()
        for copy in self.sent.values():
            copy.wait()


def halves(ref):
    if ref.shape[-2] != WIN:
        return [pl.ds(0, ref.shape[0])]
    count = ref.shape[0] // 2
    return [pl.ds(0, count), pl.ds(count, count)]


def run(
    kernel,
    scalars,
    arrays,
    outs,
    scratch=(),
    flops=0,
    name=None,
    after=(),
    scalar_outs=(),
    lazy=None,
    vmem=16,
    near=((), ()),
):
    outs = list(outs)
    first_in, first_out = (len(arrays), len(outs)) if lazy is None else lazy
    eager, late = list(arrays[:first_in]), list(arrays[first_in:])
    n_in = len(scalars) + len(eager)
    scratch_shapes = [
        kind if dtype is None else pltpu.VMEM(kind, dtype) for kind, dtype in scratch
    ]
    n_own = len(scratch_shapes)
    n_late, n_sent = len(late), len(outs) - first_out
    if lazy is not None:
        scratch_shapes += [pltpu.VMEM(a.shape, a.dtype) for a in late]
        scratch_shapes += [pltpu.VMEM(*out) for out in outs[first_out:]]
        scratch_shapes += [pltpu.SemaphoreType.DMA((n_late, 2)), pltpu.SemaphoreType.DMA((max(n_sent, 1),))]

    def body(*refs):
        given, refs = refs[:n_in], refs[n_in:]
        sources, refs = refs[:n_late], refs[n_late + len(after) :]
        results, refs = refs[: len(scalar_outs) + first_out], refs[len(scalar_outs) + first_out :]
        targets, refs = refs[:n_sent], refs[n_sent:]
        own, refs = refs[:n_own], refs[n_own:]
        if lazy is None:
            kernel(*given, *results, *own)
            return
        buffers, leaving = refs[:n_late], refs[n_late : n_late + n_sent]
        fetch_sem, send_sem = refs[n_late + n_sent :]
        moves = Moves(
            [
                (
                    id(buffer),
                    [
                        pltpu.make_async_copy(source.at[part], buffer.at[part], fetch_sem.at[i, j])
                        for j, part in enumerate(halves(buffer))
                    ],
                )
                for i, (source, buffer) in enumerate(zip(sources, buffers))
            ],
            [
                (id(buffer), pltpu.make_async_copy(buffer, target, send_sem.at[i]))
                for i, (buffer, target) in enumerate(zip(leaving, targets))
            ],
        )
        kernel(moves, *given, *buffers, *results, *leaving, *own)
        moves.finish()

    out_shape = [jax.ShapeDtypeStruct(shape, dtype) for shape, dtype in scalar_outs] + [
        pltpu.HBM(shape, dtype)
        if lazy is not None and i not in near[1]
        else jax.ShapeDtypeStruct(shape, dtype)
        for i, (shape, dtype) in enumerate(outs)
    ]
    late = [
        a if i in near[0] else far(a)
        for i, a in enumerate(late, first_in)
    ]
    moved = sum(a.size * a.dtype.itemsize for a in arrays)
    return pl.pallas_call(
        body,
        out_shape=out_shape,
        in_specs=[SMEM] * len(scalars)
        + [VMEM] * len(eager)
        + [ANYWHERE if i in near[0] else FAR for i in range(first_in, len(arrays))]
        + [ANYWHERE] * len(after),
        out_specs=[SMEM] * len(scalar_outs)
        + [VMEM] * first_out
        + [ANYWHERE if i in near[1] else FAR for i in range(first_out, len(outs))],
        scratch_shapes=scratch_shapes,
        compiler_params=pltpu.CompilerParams(vmem_limit_bytes=vmem * 1024 * 1024),
        cost_estimate=pl.CostEstimate(flops=flops, bytes_accessed=moved, transcendentals=0),
        name=name,
    )(*scalars, *eager, *late, *after)


def gate(values, after):
    values, after = list(values), list(after)
    return list(lax.optimization_barrier(tuple(values + after)))[: len(values)]


def swap(values, axis):
    return lax.ppermute(values, axis, [(0, 1), (1, 0)])


def added(values, others):
    return (values.astype(F32) + others.astype(F32)).astype(BF)


def shards(values, ranks):
    return values.reshape(ranks, values.shape[0] // ranks, values.shape[1])


def spread_sum(pieces):
    mine = jnp.sum(pieces.astype(F32), axis=0).astype(BF)
    return jnp.broadcast_to(mine[None], pieces.shape)


def across(values, axes, size, mask):
    return lax.ppermute(values, axes, [(i, i ^ mask) for i in range(size)])


def deal(parts):
    return [parts[0]] + [across(parts[d], ("row", "col"), 4, d) for d in (1, 2, 3)]


RANKS = ("dp", "row")


def stages(ranks):
    bits = ranks.bit_length() - 1
    return [(bit, min(2, bits - bit)) for bit in range(0, bits, 2)]


def scatter_send(values, ranks, stage):
    bit, count = stage
    size = 1 << count
    me = (lax.axis_index(RANKS) >> bit) & (size - 1)
    cut = values.reshape(size, values.shape[0] // size, values.shape[1])
    return [lax.dynamic_index_in_dim(cut, me ^ d, 0, keepdims=False) for d in range(size)]


def scatter_move(parts, ranks, stage):
    return [parts[0]] + [
        across(parts[d], RANKS, ranks, d << stage[0]) for d in range(1, len(parts))
    ]


def scatter_sum(parts):
    return sum(part.astype(F32) for part in parts).astype(BF)


def gather(values, ranks, stage):
    return jnp.stack(
        [values]
        + [across(values, RANKS, ranks, d << stage[0]) for d in range(1, 1 << stage[1])]
    )


def rank_order(rank, ranks):
    order = 0
    for bit, count in stages(ranks):
        order = order * (1 << count) + ((rank >> bit) & ((1 << count) - 1))
    return order


def local(
    groups,
    images,
    cotangent,
    mix_partner,
    cut_partner,
    ratios,
    corners,
    drop_masks,
    norm_gains,
    norm_shifts,
    entry_weight,
    entry_bias,
    position_kernel,
    position_bias,
    exit_weight,
    exit_bias,
    expand_weight,
    expand_bias,
    shrink_weight,
    shrink_bias,
):
    images_here = images.shape[0]
    width = images.shape[3]
    units = expand_weight.shape[2]
    row, col = lax.axis_index("row"), lax.axis_index("col")
    share = images_here // 4
    rows = 4 * share * PAD
    ranks = 2 * groups
    capacity = (2 * images_here + groups - 1) // groups
    slots = groups * capacity
    order = rank_order(lax.axis_index(RANKS), ranks)
    place = jnp.stack(
        [
            lax.axis_index("dp"),
            row,
            col,
            2 * row + col,
            order,
            order // (ranks // 4),
            order % (ranks // 4),
        ]
    ).astype(jnp.int32)
    spots = [0] * ranks
    for rank in range(ranks):
        spots[rank_order(rank, ranks)] = rank
    quad = ((share, TILE, 8, width), BF)
    corners = corners.T
    masks = drop_masks.T
    flat = ((width // 128, images_here * PAD, 128), F32)
    index, take, outgoing, own = run(
        pick_kernel,
        [place, mix_partner, cut_partner],
        [images.transpose(1, 2, 0, 3)],
        [((slots, TILE, 8, width), BF), ((images_here, TILE, 8, width), BF)],
        [flat, (pltpu.SMEM((groups,), jnp.int32), None)],
        name="pick",
        vmem=60,
        scalar_outs=(((slots + 8,), jnp.int32), ((2 * images_here,), jnp.int32)),
    )
    arrived = lax.all_to_all(outgoing, "dp", split_axis=0, concat_axis=0, tiled=True)
    cot = deal(
        run(deal_kernel, [place], [cotangent.transpose(1, 2, 0, 3)], [quad] * 4, [flat], name="deal", vmem=60)
    )
    mixed = deal(
        run(
            mix_kernel,
            [place, take, corners, ratios],
            [arrived, own],
            [quad] * 4,
            name="mix",
            after=cot,
        )
    )
    conv_k = position_kernel.transpose(1, 2, 0, 3)
    tall = (rows, width)
    (
        vec1,
        keep1,
        away1,
        act_a,
        act_b,
        act_c,
        act_d,
        active0,
        slope0,
        win0,
        chance0,
        stripe0,
        mid0,
        win1,
        chance1,
        stripe1,
        hidden1,
        grad1,
    ) = run(
        functools.partial(first_kernel, spots),
        [place, masks],
        [
            *mixed,
            norm_gains,
            norm_shifts,
            entry_bias,
            conv_k,
            position_bias,
            exit_bias,
            expand_bias,
            shrink_bias,
            *cot,
            entry_weight,
            exit_weight,
            expand_weight,
            shrink_weight,
        ],
        [
            ((7, 8, width), F32),
            ((units, width), BF),
            ((units, width), BF),
            *([quad] * 4),
            ((rows, units), BF),
            ((rows, units), BF),
            ((4 * share, WIN, 3 * HALF), BF),
            ((4 * share, WIN, LANES), BF),
            (tall, BF),
            (tall, F32),
            ((4 * share, WIN, 3 * HALF), BF),
            ((4 * share, WIN, LANES), BF),
            (tall, BF),
            (tall, F32),
            (tall, F32),
        ],
        [
            (tall, F32),
            ((rows, 3 * width), F32),
            (tall, F32),
            ((rows, units), BF),
            ((rows, units), BF),
            (tall, BF),
            (tall, BF),
        ],
        flops=10 * rows * width * width * 120,
        name="first",
        vmem=46,
        near=((), (1, 2)),
        lazy=(17, 3),
    )
    sent1 = shards(added(keep1, swap(away1, "col")), ranks)
    pieces1 = lax.all_to_all(sent1, RANKS, split_axis=0, concat_axis=0, tiled=True)
    vec2, conv2, keep2, away2, grad0, delta0 = run(
        second_kernel,
        [place, masks],
        [
            norm_gains,
            norm_shifts,
            conv_k,
            grad1,
            exit_weight,
            win1,
            chance1,
            hidden1,
            entry_weight,
            stripe1,
            mid0,
            shrink_weight,
            slope0,
            expand_weight,
            active0,
            stripe0,
        ],
        [
            ((15, 8, width), F32),
            ((9, 8, width), F32),
            ((13 * width // 2, width), BF),
            ((13 * width // 2, width), BF),
            (tall, F32),
            (tall, F32),
        ],
        [
            (tall, F32),
            (tall, BF),
            ((rows, 3 * width), F32),
            ((rows, 3 * width), BF),
            (tall, BF),
            (tall, BF),
            ((rows, units), BF),
        ],
        flops=6 * rows * width * width * 120,
        name="second",
        vmem=42,
        near=((), (2, 3)),
        after=[sent1],
        lazy=(3, 4),
    )
    act = deal([act_a, act_b, act_c, act_d])
    keep2, away2, *act = gate([keep2, away2, *act], [pieces1])
    steps = stages(ranks)

    def first_parts(keep, away):
        other = swap(away, "col")
        count = keep.shape[0] // 4
        return [
            added(keep[d * count : (d + 1) * count], other[d * count : (d + 1) * count])
            for d in range(4)
        ]

    parts2 = first_parts(keep2, away2)
    moved2 = scatter_move(parts2, ranks, steps[0])
    *out_tiles, keep3, away3 = run(
        third_kernel,
        [place],
        [
            norm_gains,
            norm_shifts,
            conv_k,
            vec1,
            vec2,
            conv2,
            *mixed,
            delta0,
            win0,
            chance0,
            entry_weight,
            grad0,
        ],
        [quad] * 4 + [((2 * width, width), BF), ((2 * width, width), BF)],
        [
            (tall, F32),
            ((rows, 3 * width), F32),
            ((rows, 3 * width), BF),
            (tall, BF),
            ((4, 8, width), F32),
            ((9, 8, width), F32),
            ((width, width), F32),
        ],
        flops=3 * rows * width * width * 120,
        name="third",
        vmem=36,
        near=((), range(6)),
        after=parts2,
        lazy=(10, 6),
    )
    *moved2, keep3, away3 = gate([*moved2, keep3, away3], out_tiles)
    gradient = deal(out_tiles)
    (parted,) = run(
        split_kernel,
        [place, take, corners, ratios],
        gradient,
        [((slots, TILE, 8, width), BF)],
        name="split",
    )
    mine1 = jnp.sum(pieces1.astype(F32), axis=0).astype(BF)
    mine2 = scatter_sum(moved2)
    moved3 = scatter_move(first_parts(keep3, away3), ranks, steps[0])
    mine3 = scatter_sum(gate(moved3, [mine1]))
    cut = mine2.shape[0] * 4 // ranks
    lot = mine3.shape[0] * 4 // ranks
    joint = jnp.concatenate(
        [
            mine3.reshape(ranks // 4, lot, width),
            mine2.reshape(ranks // 4, cut, width),
        ],
        axis=1,
    ).reshape(-1, width)
    for step in steps[1:]:
        joint = scatter_sum(scatter_move(scatter_send(joint, ranks, step), ranks, step))
    joint = jnp.concatenate([mine1, joint], axis=0)
    counts = (mine1.shape[0], lot, cut)
    for step in reversed(steps[1:]):
        joint = gather(joint, ranks, step).reshape(-1, width)
    joint = shards(joint, ranks // 4)
    (parted,) = gate([parted], [joint])
    (activations,) = run(
        lay_kernel, [place], [far(a) for a in act], [((TILE, TILE, images_here, width), BF)], [flat], name="lay"
    )
    back = lax.all_to_all(parted, "dp", split_axis=0, concat_axis=0, tiled=True)
    (back,) = gate([back], [activations])
    (input_gradient,) = run(
        join_kernel,
        [place, index, corners, ratios],
        [*gradient, back],
        [((TILE, TILE, images_here, width), F32)],
        [((width // 128, (images_here + 1) * PAD, 128), F32)],
        name="join",
    )
    full = [joint] + [across(joint, RANKS, ranks, d) for d in (1, 2, 3)]
    full[2:] = gate(full[2:], [input_gradient])
    full += [swap(piece, "col") for piece in full]
    shapes = [
        (2, 2, width),
        (2, 2, width),
        (2, width, 3 * width),
        (2, 2 * width),
        (3, 3, 2, width),
        (2, width),
        (2, width, width),
        (2, width),
        (2, width, units),
        (2, units),
        (2, units, width),
        (2, width),
    ]
    gains, shifts, entry, entry_b, conv, conv_b, exit_, exit_b, expand, expand_b, shrink, shrink_b = (
        pl.pallas_call(
            functools.partial(unpack_kernel, ranks, counts),
            out_shape=[jax.ShapeDtypeStruct(shape, F32) for shape in shapes],
            in_specs=[SMEM] + [VMEM] * 8,
            out_specs=[ANYWHERE] * 12,
            scratch_shapes=[
                pltpu.VMEM((width // 2, width), F32),
            ]
            + [pltpu.VMEM(shape, F32) for shape in shapes]
            + [pltpu.SemaphoreType.DMA((16,))],
            compiler_params=pltpu.CompilerParams(vmem_limit_bytes=24 * 1024 * 1024),
            name="unpack",
        )(place, *full)
    )
    return (
        activations.transpose(2, 0, 1, 3),
        input_gradient.transpose(2, 0, 1, 3),
        gains,
        shifts,
        entry,
        entry_b,
        conv.transpose(2, 0, 1, 3),
        conv_b,
        exit_,
        exit_b,
        expand,
        expand_b,
        shrink,
        shrink_b,
    )


def solution(mesh):
    tiles = P("dp", "row", "col", None)
    return jax.shard_map(
        functools.partial(local, mesh.shape["dp"]),
        mesh=mesh,
        in_specs=(tiles, tiles, P(), P(), P("dp"), P("dp", None), P("dp", None)) + (P(),) * 12,
        out_specs=(tiles, tiles) + (P(),) * 12,
        check_vma=False,
    )
```

```python
import functools

import jax
import jax.numpy as jnp
from jax import lax
from jax.experimental import pallas as pl
from jax.experimental.pallas import tpu as pltpu
from jax.sharding import PartitionSpec as P

TILE = 7
PAD = 56
HEAD_DIM = 32
SIDE_HEADS = 4
HALF = 128
WIN = 2 * PAD
CHUNK = 8 * PAD
LANES = SIDE_HEADS * 128
SCALE = HEAD_DIM ** (-0.5)
LOG2E = 1.4426950408889634
EPS = 1e-05
BF = jnp.bfloat16
F32 = jnp.float32


def dot_nn(a, b):
    return lax.dot_general(a, b, (((1,), (0,)), ((), ())), preferred_element_type=F32)


def dot_nt(a, b):
    return lax.dot_general(a, b, (((1,), (1,)), ((), ())), preferred_element_type=F32)


def dot_tn(a, b):
    return lax.dot_general(a, b, (((0,), (0,)), ((), ())), preferred_element_type=F32)


def norm_parts(values):
    centered = values - jnp.mean(values, axis=-1, keepdims=True)
    inverse = lax.rsqrt(jnp.mean(centered * centered, axis=-1, keepdims=True) + EPS)
    return centered * inverse, inverse


def norm_back(delta, hat, inverse, gain):
    scaled = delta * gain
    first = jnp.mean(scaled, axis=-1, keepdims=True)
    second = jnp.mean(scaled * hat, axis=-1, keepdims=True)
    return inverse * (scaled - first - hat * second)


def gelu_parts(values):
    chance = 0.5 + 0.5 * lax.erf(values * (0.5**0.5))
    density = jnp.exp2(values * values * (-0.5 * LOG2E)) * 0.3989422804014327
    return chance, density


def row_sums(values):
    count, width = values.shape
    return jnp.sum(values.reshape(count // 8, 8, width), axis=0)


def scale_rows(place_ref, mask_ref, column):
    scales = [
        mask_ref[column, 4 * place_ref[3] + i].astype(F32) * 1.25 for i in range(4)
    ]
    columns = [jnp.full((PAD, 1), scale, F32) for scale in scales]
    return jnp.concatenate(columns * (CHUNK // (4 * PAD)), axis=0)


def add_row(acc_ref, row, values):
    acc_ref[row] += values


def spread_heads(values):
    lane = lax.broadcasted_iota(jnp.int32, values.shape, 1) // HEAD_DIM
    empty = jnp.zeros((128 - WIN, HALF), F32)
    blocks = []
    for head in range(SIDE_HEADS):
        blocks.append(jnp.where(lane == head, values, 0.0))
        blocks.append(empty)
    return jnp.concatenate(blocks, axis=0).astype(BF)


def over_keys(weights, values):
    weights = fill_rows(weights)
    stacked = jnp.concatenate(
        [weights[:, head * 128 : (head + 1) * 128] for head in range(SIDE_HEADS)], axis=0
    )
    return dot_tn(stacked, spread_heads(values))[:WIN]


def fill_rows(values):
    empty = jnp.zeros((128 - WIN, values.shape[1]), values.dtype)
    return jnp.concatenate([values, empty], axis=0)


def valid_column(shape):
    return lax.broadcasted_iota(jnp.int32, shape, 1) != 7


def valid_rows(shape):
    return lax.broadcasted_iota(jnp.int32, shape, 0) % 8 != 7


def column_shifts(values, across):
    cube = values.reshape(2 * TILE, 8, HALF)
    if not across:
        return (pltpu.roll(cube, 1, 1), cube, pltpu.roll(cube, 7, 1))
    left, right = cube[:TILE], cube[TILE:]
    column = lax.broadcasted_iota(jnp.int32, left.shape, 1)
    before = jnp.concatenate(
        [
            pltpu.roll(left, 1, 1),
            jnp.where(column == 0, pltpu.roll(left, 2, 1), pltpu.roll(right, 1, 1)),
        ],
        axis=0,
    )
    after = jnp.concatenate(
        [
            jnp.where(column == 6, pltpu.roll(right, 6, 1), pltpu.roll(left, 7, 1)),
            pltpu.roll(right, 7, 1),
        ],
        axis=0,
    )
    return (before, cube, after)


def row_shift(cube, step, across):
    if step == 0:
        return cube
    empty = jnp.zeros((1, 8, HALF), F32)

    def move(part):
        if step < 0:
            return jnp.concatenate([empty, part[:-1]], axis=0)
        return jnp.concatenate([part[1:], empty], axis=0)

    if across:
        return jnp.concatenate([move(cube[:TILE]), move(cube[TILE:])], axis=0)
    return move(cube)


def window_conv(shifts, kernel_at, across):
    total = None
    for i in range(3):
        part = None
        for j in range(3):
            term = kernel_at(i, j) * shifts[j]
            part = term if part is None else part + term
        part = row_shift(part, i - 1, across)
        total = part if total is None else total + part
    return total.reshape(WIN, HALF)


def window_rows(across, window):
    side, image = window // 4, window % 4
    if across:
        first, second = 2 * side, 2 * side + 1
    else:
        first, second = side, 2 + side
    return (
        pl.multiple_of((first * 4 + image) * PAD, 8),
        pl.multiple_of((second * 4 + image) * PAD, 8),
    )


def take_window(ref, at, lane):
    return jnp.concatenate(
        [ref[pl.ds(at[0], PAD), lane : lane + HALF], ref[pl.ds(at[1], PAD), lane : lane + HALF]],
        axis=0,
    )


def put_window(ref, at, lane, values):
    ref[pl.ds(at[0], PAD), lane : lane + HALF] = values[:PAD]
    ref[pl.ds(at[1], PAD), lane : lane + HALF] = values[PAD:]


def round_bf(values):
    return values.astype(BF).astype(F32)


def attention_forward(
    block, hidden_ref, gains, shifts, entry_w, entry_b, conv_k, conv_b, wide, stripe, win_out, chance_out
):
    width = hidden_ref.shape[1]

    @pl.loop(0, 2)
    def _(t):
        rows = chunk(t)
        hat, _ = norm_parts(hidden_ref[rows, :])
        normed = (hat * gains[block, 0:1, :] + shifts[block, 0:1, :]).astype(BF)
        for part in range(3):
            out = dot_nn(normed, entry_w[block, :, part * width : (part + 1) * width])
            if part != 1:
                at = 0 if part == 0 else width
                out = out + entry_b[block : block + 1, at : at + width]
            wide[rows, part * width : (part + 1) * width] = round_bf(out)

    for direction in range(2):
        across = direction == 0
        lane = direction * HALF

        @pl.loop(0, 8, unroll=4)
        def _(window, across=across, lane=lane, direction=direction):
            at = window_rows(across, window)
            queries = take_window(wide, at, lane)
            keys = take_window(wide, at, width + lane)
            values = take_window(wide, at, 2 * width + lane)
            keys_bf = keys.astype(BF)
            win_out[direction * 8 + window, :, 0:HALF] = queries.astype(BF)
            win_out[direction * 8 + window, :, HALF : 2 * HALF] = keys_bf
            win_out[direction * 8 + window, :, 2 * HALF : 3 * HALF] = values.astype(BF)
            scores = dot_nt(keys_bf, spread_heads(queries)).reshape(2 * TILE, 8, LANES)
            scores = jnp.where(valid_column((1, 8, LANES)), scores, -1e30)
            top = jnp.max(jnp.max(scores, axis=0), axis=0, keepdims=True)
            lifted = jnp.exp2((scores - top) * (SCALE * LOG2E))
            totals = jnp.sum(jnp.sum(lifted, axis=0), axis=0, keepdims=True)
            chances = (lifted * (1.0 / totals)).reshape(WIN, LANES).astype(BF)
            chance_out[direction * 8 + window] = chances
            attended = over_keys(chances, values)
            clean = jnp.where(valid_rows(values.shape), values, 0.0)
            position = window_conv(
                column_shifts(clean, across),
                lambda i, j: conv_k[i, j, block : block + 1, lane : lane + HALF],
                across,
            )
            put_window(
                stripe, at, lane, attended + position + conv_b[block : block + 1, lane : lane + HALF]
            )


def attention_backward(
    ready,
    block,
    win_in,
    chance_in,
    conv_k,
    stripe_delta,
    wide,
    conv_acc,
):
    width = stripe_delta.shape[1]
    for direction in range(2):
        ready(direction)
        across = direction == 0
        lane = direction * HALF

        @pl.loop(0, 8, unroll=4)
        def _(window, across=across, lane=lane, direction=direction):
            at = window_rows(across, window)
            out_delta = take_window(stripe_delta, at, lane)
            queries = win_in[direction * 8 + window, :, 0:HALF].astype(F32)
            keys = win_in[direction * 8 + window, :, HALF : 2 * HALF].astype(F32)
            values_bf = win_in[direction * 8 + window, :, 2 * HALF : 3 * HALF]
            values = values_bf.astype(F32)
            chances = chance_in[direction * 8 + window]
            delta_spread = spread_heads(out_delta)
            chance_delta = dot_nt(values_bf, delta_spread)
            cubes = (2 * TILE, 8, LANES)
            wide_chances = chances.astype(F32).reshape(cubes)
            weighted = wide_chances * chance_delta.reshape(cubes)
            common = jnp.sum(jnp.sum(weighted, axis=0), axis=0, keepdims=True)
            score_delta = (weighted - wide_chances * common).reshape(WIN, LANES).astype(BF)
            values_delta = dot_nn(chances, delta_spread)
            keys_delta = dot_nn(score_delta, spread_heads(queries)) * SCALE
            query_delta = over_keys(score_delta, keys) * SCALE
            keep = valid_rows(values.shape)
            clean = jnp.where(keep, values, 0.0)
            shifts = column_shifts(clean, across)
            cube = out_delta.reshape(2 * TILE, 8, HALF)
            for i in range(3):
                moved = row_shift(cube, 1 - i, across)
                for j in range(3):
                    conv_acc[3 * i + j, :, lane : lane + HALF] += jnp.sum(moved * shifts[j], axis=0)
            back = window_conv(
                column_shifts(out_delta, across),
                lambda i, j: conv_k[2 - i, 2 - j, block : block + 1, lane : lane + HALF],
                across,
            )
            values_delta = jnp.where(keep, values_delta + back, 0.0)
            put_window(wide, at, lane, query_delta)
            put_window(wide, at, width + lane, keys_delta)
            put_window(wide, at, 2 * width + lane, values_delta)


def chunk(t):
    return pl.ds(pl.multiple_of(t * CHUNK, CHUNK), CHUNK)


class Bundle:
    def __init__(self, place_ref, keep, away, chunks=1, spot=lambda chunk: chunk):
        self.place_ref, self.keep, self.away = place_ref, keep, away
        self.step, self.spot = keep.shape[0] // chunks, spot

    def put(self, at, values):
        values = values.astype(BF)
        half, step = self.keep.shape[0], self.step
        last = at + values.shape[0]
        first = at
        while first < last:
            stop = min(last, (first // step + 1) * step)
            number = first // half
            start = self.spot(first % half // step) * step
            inner, count = first % step, stop - first
            if not isinstance(start, int):
                start = pl.multiple_of(start, step)
            rows = pl.ds(start + inner, count)
            piece = values[first - at : stop - at]

            @pl.when(self.place_ref[2] == number)
            def _(piece=piece, rows=rows):
                self.keep[rows, :] = piece

            @pl.when(self.place_ref[2] != number)
            def _(piece=piece, rows=rows):
                self.away[rows, :] = piece

            first = stop


def put_squares(bundle, at, values, side):
    for part in range(values.shape[1] // side):
        bundle.put(at + part * side, values[:, part * side : (part + 1) * side])


def load_tiles(place_ref, tiles, hidden):
    for d, tile in enumerate(tiles):
        at = jnp.bitwise_xor(place_ref[3], d) * (4 * PAD)
        rows = pl.ds(pl.multiple_of(at, 4 * PAD), 4 * PAD)
        hidden[rows, :] = tile[...].astype(F32).reshape(4 * PAD, hidden.shape[1])


def store_tile(place_ref, tiles, t, values):
    count = CHUNK // (4 * PAD)
    values = values.reshape((count,) + tiles[0].shape).astype(BF)
    for part in range(count):
        for d, tile in enumerate(tiles):

            @pl.when(jnp.bitwise_xor(place_ref[3], d) == count * t + part)
            def _(tile=tile, part=part):
                tile[...] = values[part]


def first_kernel(
    spots,
    moves,
    place_ref,
    mask_ref,
    mixed_a,
    mixed_b,
    mixed_c,
    mixed_d,
    gains,
    shifts,
    entry_b,
    conv_k,
    conv_b,
    exit_b,
    expand_b,
    shrink_b,
    cot_a,
    cot_b,
    cot_c,
    cot_d,
    entry_w,
    exit_w,
    expand_w,
    shrink_w,
    vec_out,
    keep_out,
    away_out,
    act_a,
    act_b,
    act_c,
    act_d,
    active0_out,
    slope0_out,
    win0_out,
    chance0_out,
    stripe0_out,
    mid0_out,
    win1_out,
    chance1_out,
    stripe1_out,
    hidden1_out,
    grad_out,
    hidden,
    wide,
    stripe,
    active1,
    pre1,
    feed1,
    inner1,
):
    width = hidden.shape[1]
    hidden_units = expand_w.shape[2]
    bundle = Bundle(place_ref, keep_out, away_out, len(spots), lambda chunk: spots[chunk])
    vec_out[...] = jnp.zeros(vec_out.shape, F32)
    moves.fetch(entry_w)
    load_tiles(place_ref, (mixed_a, mixed_b, mixed_c, mixed_d), hidden)
    moves.need(entry_w)
    moves.fetch(exit_w, expand_w, shrink_w, cot_a, cot_b, cot_c, cot_d)

    for block in range(2):
        win_out, chance_out, stripe_out = (
            (win0_out, chance0_out, stripe0_out),
            (win1_out, chance1_out, stripe1_out),
        )[block]
        attention_forward(
            block, hidden, gains, shifts, entry_w, entry_b, conv_k, conv_b, wide, stripe, win_out, chance_out
        )
        moves.send(win_out, chance_out)
        moves.need(exit_w, expand_w, shrink_w)
        if block == 1:
            moves.need(cot_a, cot_b, cot_c, cot_d)
            load_tiles(place_ref, (cot_a, cot_b, cot_c, cot_d), grad_out)

        @pl.loop(0, 2)
        def _(t, block=block, stripe_out=stripe_out):
            rows = chunk(t)
            striped = stripe[rows, :].astype(BF)
            stripe_out[rows, :] = striped
            branch = dot_nn(striped, exit_w[block]) + exit_b[block : block + 1, :]
            midway = hidden[rows, :] + scale_rows(place_ref, mask_ref, 2 * block) * branch
            if block == 0:
                mid0_out[rows, :] = midway
            hat, inverse = norm_parts(midway)
            normed = (hat * gains[block, 1:2, :] + shifts[block, 1:2, :]).astype(BF)
            feed_scale = scale_rows(place_ref, mask_ref, 2 * block + 1)
            feed = shrink_b[block : block + 1, :]
            if block == 1:
                inner1[rows, :] = normed
                gradient = grad_out[rows, :]
                feed_delta = (feed_scale * gradient).astype(BF)
                feed1[rows, :] = feed_delta
                add_row(vec_out, 4, row_sums(feed_delta.astype(F32)))
                inner_delta = jnp.zeros((CHUNK, width), F32)
            for part in range(hidden_units // width):
                at = slice(part * width, (part + 1) * width)
                pre_act = dot_nn(normed, expand_w[block, :, at]) + expand_b[block : block + 1, at]
                chance, density = gelu_parts(pre_act)
                active = (pre_act * chance).astype(BF)
                slope = chance + pre_act * density
                if block == 0:
                    active0_out[rows, at] = active
                    slope0_out[rows, at] = slope.astype(BF)
                else:
                    active1[rows, at] = active
                    pre_delta = (dot_nt(feed_delta, shrink_w[block, at, :]) * slope).astype(BF)
                    pre1[rows, at] = pre_delta
                    add_row(vec_out, part, row_sums(pre_delta.astype(F32)))
                    inner_delta = inner_delta + dot_nt(pre_delta, expand_w[block, :, at])
                feed = feed + dot_nn(active, shrink_w[block, at, :])
            output = midway + feed_scale * feed
            if block == 0:
                hidden[rows, :] = output
                hidden1_out[rows, :] = output
            else:
                store_tile(place_ref, (act_a, act_b, act_c, act_d), t, output)
                add_row(vec_out, 5, row_sums(inner_delta * hat))
                add_row(vec_out, 6, row_sums(inner_delta))
                grad_out[rows, :] = gradient + norm_back(
                    inner_delta, hat, inverse, gains[block, 1:2, :]
                )

        moves.send(stripe_out)
        if block == 0:
            moves.send(mid0_out, active0_out, slope0_out, hidden1_out)
        else:
            moves.send(act_a, act_b, act_c, act_d, grad_out)

    put_squares(bundle, 0, dot_tn(inner1[...], pre1[...]), width)
    for part in range(hidden_units // width):
        bundle.put(
            hidden_units + part * width,
            dot_tn(active1[:, part * width : (part + 1) * width], feed1[...]),
        )


def delta_rows(block, place_ref, mask_ref, exit_w, grad_ref, stripe_delta, branch_delta, vec_out, at):
    @pl.loop(0, 2)
    def _(t):
        rows = chunk(t)
        rounded = (scale_rows(place_ref, mask_ref, 2 * block) * grad_ref[rows, :]).astype(BF)
        branch_delta[rows, :] = rounded
        add_row(vec_out, at, row_sums(rounded.astype(F32)))
        out = round_bf(dot_nt(rounded, exit_w[block]))
        stripe_delta[rows, :] = out
        add_row(vec_out, at + 1, row_sums(out))


def entry_backward(block, hidden_ref, gains, shifts, entry_w, grad_ref, wide, wide_bf, normed_bf, vec_out, at, emit):
    width = hidden_ref.shape[1]

    @pl.loop(0, 2)
    def _(t):
        rows = chunk(t)
        hat, inverse = norm_parts(hidden_ref[rows, :])
        normed_bf[rows, :] = (hat * gains[block, 0:1, :] + shifts[block, 0:1, :]).astype(BF)
        delta = jnp.zeros((CHUNK, width), F32)
        for part in range(3):
            lanes = slice(part * width, (part + 1) * width)
            rounded = wide[rows, lanes].astype(BF)
            wide_bf[rows, lanes] = rounded
            if part != 1:
                add_row(vec_out, at + part // 2, row_sums(rounded.astype(F32)))
            delta = delta + dot_nt(rounded, entry_w[block, :, lanes])
        add_row(vec_out, at + 2, row_sums(delta * hat))
        add_row(vec_out, at + 3, row_sums(delta))
        emit(t, rows, grad_ref[rows, :] + norm_back(delta, hat, inverse, gains[block, 0:1, :]))


def second_kernel(
    moves,
    place_ref,
    mask_ref,
    gains,
    shifts,
    conv_k,
    grad_in,
    exit_w,
    win1,
    chance1,
    hidden1,
    entry_w,
    stripe1,
    mid0,
    shrink_w,
    slope0,
    expand_w,
    active0,
    stripe0,
    vec_out,
    conv_out,
    keep_out,
    away_out,
    grad_out,
    stripe_delta_out,
    stripe_delta,
    branch_delta,
    wide,
    wide_bf,
    normed_bf,
    feed0,
    pre0,
):
    grad = grad_out
    width = grad.shape[1]
    hidden_units = expand_w.shape[2]
    bundle = Bundle(
        place_ref, keep_out, away_out, 4, lambda chunk: jnp.bitwise_xor(place_ref[5], chunk)
    )
    vec_out[...] = jnp.zeros(vec_out.shape, F32)
    conv_out[...] = jnp.zeros(conv_out.shape, F32)
    moves.fetch(grad_in, exit_w)
    moves.fetch(win1, chance1, part=0)
    moves.need(grad_in, exit_w)
    moves.fetch(win1, chance1, part=1)
    delta_rows(1, place_ref, mask_ref, exit_w, grad_in, stripe_delta, branch_delta, vec_out, 0)

    def ready(direction):
        moves.need(win1, chance1, part=direction)
        if direction == 0:
            moves.fetch(hidden1, entry_w, stripe1)
        else:
            moves.fetch(mid0, shrink_w, slope0, expand_w, active0, stripe0)

    attention_backward(ready, 1, win1, chance1, conv_k, stripe_delta, wide, conv_out)

    def emit(t, rows, values):
        grad[rows, :] = values

    moves.need(hidden1, entry_w)
    entry_backward(
        1, hidden1, gains, shifts, entry_w, grad_in, wide, wide_bf, normed_bf, vec_out, 2, emit
    )
    put_squares(bundle, 0, dot_tn(normed_bf[...], wide_bf[...]), width)
    moves.need(stripe1)
    bundle.put(3 * width, dot_tn(stripe1[...], branch_delta[...]))
    moves.need(mid0, shrink_w, slope0, expand_w)

    @pl.loop(0, 2)
    def _(t):
        rows = chunk(t)
        gradient = grad[rows, :]
        hat, inverse = norm_parts(mid0[rows, :])
        normed_bf[rows, :] = (hat * gains[0, 1:2, :] + shifts[0, 1:2, :]).astype(BF)
        feed_delta = (scale_rows(place_ref, mask_ref, 1) * gradient).astype(BF)
        feed0[rows, :] = feed_delta
        add_row(vec_out, 6, row_sums(feed_delta.astype(F32)))
        inner_delta = jnp.zeros((CHUNK, width), F32)
        for part in range(hidden_units // width):
            at = slice(part * width, (part + 1) * width)
            pre_delta = (
                dot_nt(feed_delta, shrink_w[0, at, :]) * slope0[rows, at].astype(F32)
            ).astype(BF)
            pre0[rows, at] = pre_delta
            add_row(vec_out, 7 + part, row_sums(pre_delta.astype(F32)))
            inner_delta = inner_delta + dot_nt(pre_delta, expand_w[0, :, at])
        add_row(vec_out, 11, row_sums(inner_delta * hat))
        add_row(vec_out, 12, row_sums(inner_delta))
        grad[rows, :] = gradient + norm_back(inner_delta, hat, inverse, gains[0, 1:2, :])

    delta_rows(0, place_ref, mask_ref, exit_w, grad, stripe_delta_out, branch_delta, vec_out, 13)
    moves.send(grad_out, stripe_delta_out)
    moves.need(active0, stripe0)
    put_squares(bundle, 4 * width, dot_tn(normed_bf[...], pre0[...]), width)
    for part in range(hidden_units // width):
        bundle.put(
            (8 + part) * width,
            dot_tn(active0[:, part * width : (part + 1) * width], feed0[...]),
        )
    bundle.put(12 * width, dot_tn(stripe0[...], branch_delta[...]))


def third_kernel(
    moves,
    place_ref,
    gains,
    shifts,
    conv_k,
    vec1,
    vec2,
    conv2,
    mixed_a,
    mixed_b,
    mixed_c,
    mixed_d,
    stripe_delta,
    win0,
    chance0,
    entry_w,
    grad_in,
    out_a,
    out_b,
    out_c,
    out_d,
    keep_out,
    away_out,
    hidden,
    wide,
    wide_bf,
    normed_bf,
    vec3,
    conv3,
    flat,
):
    width = hidden.shape[1]
    bundle = Bundle(
        place_ref, keep_out, away_out, 4, lambda chunk: jnp.bitwise_xor(place_ref[5], chunk)
    )
    vec3[...] = jnp.zeros(vec3.shape, F32)
    conv3[...] = jnp.zeros(conv3.shape, F32)
    moves.fetch(stripe_delta)
    moves.fetch(win0, chance0, part=0)
    moves.need(stripe_delta)
    moves.fetch(win0, chance0, part=1)

    def ready(direction):
        moves.need(win0, chance0, part=direction)
        if direction == 0:
            moves.fetch(mixed_a, mixed_b, mixed_c, mixed_d, entry_w, grad_in)

    attention_backward(ready, 0, win0, chance0, conv_k, stripe_delta, wide, conv3)

    def emit(t, rows, values):
        store_tile(place_ref, (out_a, out_b, out_c, out_d), t, values)

    moves.need(mixed_a, mixed_b, mixed_c, mixed_d, entry_w, grad_in)
    load_tiles(place_ref, (mixed_a, mixed_b, mixed_c, mixed_d), hidden)
    entry_backward(
        0, hidden, gains, shifts, entry_w, grad_in, wide, wide_bf, normed_bf, vec3, 0, emit
    )
    moves.send(out_a, out_b, out_c, out_d)
    flat[...] = jnp.zeros(flat.shape, F32)
    at = 0
    for ref in (vec1, vec2, conv2, vec3, conv3):
        flat[at : at + ref.shape[0], :] = jnp.sum(ref[...], axis=1)
        at += ref.shape[0]
    spread = dot_tn(normed_bf[...], wide_bf[...])
    half = keep_out.shape[0]
    middle = width // 2
    lots = flat.shape[0] // 2
    bundle.put(0, spread[:, :width])
    bundle.put(width, spread[:middle, width : 2 * width])
    bundle.put(width + middle, flat[:lots, :])
    bundle.put(half, spread[middle:, width : 2 * width])
    bundle.put(half + middle, spread[:, 2 * width :])
    bundle.put(half + middle + width, flat[lots:, :])


def untangle(source, flat, target):
    count, width = source.shape[2:]
    lanes = flat.shape[0]
    for row in range(TILE):
        flat[:, pl.ds(row * 8 + 7, count, stride=PAD), :] = jnp.zeros((lanes, count, 128), F32)
        for col in range(TILE):
            token = source[row, col].astype(F32)
            for lane in range(lanes):
                flat[lane, pl.ds(row * 8 + col, count, stride=PAD), :] = token[
                    :, lane * 128 : (lane + 1) * 128
                ]

    @pl.loop(0, count)
    def _(n):
        rows = pl.ds(pl.multiple_of(n * PAD, 8), PAD)
        tile = jnp.concatenate([flat[lane, rows, :] for lane in range(lanes)], axis=1)
        target(n, tile.reshape(TILE, 8, width).astype(BF))


def owner_of(wanted, count):
    if count & (count - 1) == 0:
        return lax.shift_right_logical(wanted, count.bit_length() - 1)
    return lax.div(wanted, count)


def pick_kernel(
    place_ref, mix_ref, cut_ref, images_ref, index_out, take_out, sent_out, own_out, flat, counts
):
    count = images_ref.shape[2]
    slots = sent_out.shape[0]
    capacity = slots // counts.shape[0]
    me = place_ref[0]

    def put(n, tile):
        own_out[n] = tile

    untangle(images_ref, flat, put)

    @pl.loop(0, slots, unroll=8)
    def _(s):
        index_out[s] = count

    @pl.loop(0, counts.shape[0])
    def _(g):
        counts[g] = 0
        rank = g * capacity
        for ref in (mix_ref, cut_ref):
            for j in range(count):
                wanted = ref[g * count + j]
                owner = owner_of(wanted, count)
                hit = owner == me
                index_out[jnp.where(hit, rank, slots)] = wanted - owner * count
                rank = rank + hit.astype(jnp.int32)

    @pl.loop(0, slots)
    def _(s):
        sent_out[s] = own_out[jnp.minimum(index_out[s], count - 1)]

    for part, ref in enumerate((mix_ref, cut_ref)):

        @pl.loop(0, count)
        def _(j, part=part, ref=ref):
            owner = owner_of(ref[me * count + j], count)
            rank = counts[owner]
            take_out[part * count + j] = owner * capacity + rank
            counts[owner] = rank + 1


def deal_kernel(place_ref, source, out_a, out_b, out_c, out_d, flat):
    outs = (out_a, out_b, out_c, out_d)
    share = out_a.shape[0]

    def put(n, tile):
        for d, out in enumerate(outs):

            @pl.when(jnp.bitwise_xor(place_ref[3], d) == n // share)
            def _(out=out):
                out[n % share] = tile

    untangle(source, flat, put)


def inside_box(corner_ref, n, place_ref):
    shape = (TILE, 8, 1)
    row = place_ref[1] * TILE + lax.broadcasted_iota(jnp.int32, shape, 0)
    col = place_ref[2] * TILE + lax.broadcasted_iota(jnp.int32, shape, 1)
    hit = (
        (row >= corner_ref[0, n])
        & (row < corner_ref[1, n])
        & (col >= corner_ref[2, n])
        & (col < corner_ref[3, n])
    )
    return jnp.where(hit, 1.0, 0.0)


def mix_kernel(
    place_ref, take_ref, corner_ref, ratio_ref, arrived, own_ref, out_a, out_b, out_c, out_d
):
    count = own_ref.shape[0]
    share = out_a.shape[0]
    for d, out in enumerate((out_a, out_b, out_c, out_d)):

        @pl.loop(0, share)
        def _(i, d=d, out=out):
            n = jnp.bitwise_xor(place_ref[3], d) * share + i
            inside = inside_box(corner_ref, n, place_ref)
            ratio = ratio_ref[n]
            own = own_ref[n].astype(F32)
            blend = arrived[take_ref[n]].astype(F32)
            cut = arrived[take_ref[count + n]].astype(F32)
            mixed = inside * cut + (1.0 - inside) * (ratio * own + (1.0 - ratio) * blend)
            out[i] = mixed.astype(BF)


def split_kernel(
    place_ref, take_ref, corner_ref, ratio_ref, grad_a, grad_b, grad_c, grad_d, out_ref
):
    share = grad_a.shape[0]
    count = 4 * share
    if out_ref.shape[0] > 2 * count:
        out_ref[...] = jnp.zeros(out_ref.shape, BF)
    for d, grad_ref in enumerate((grad_a, grad_b, grad_c, grad_d)):

        @pl.loop(0, share)
        def _(i, d=d, grad_ref=grad_ref):
            n = jnp.bitwise_xor(place_ref[3], d) * share + i
            inside = inside_box(corner_ref, n, place_ref)
            gradient = grad_ref[i].astype(F32)
            cut = inside * gradient
            out_ref[take_ref[n]] = ((1.0 - ratio_ref[n]) * (gradient - cut)).astype(BF)
            out_ref[take_ref[count + n]] = cut.astype(BF)


def join_kernel(
    place_ref,
    index_ref,
    corner_ref,
    ratio_ref,
    grad_a,
    grad_b,
    grad_c,
    grad_d,
    back_ref,
    out_ref,
    total,
):
    count, width = out_ref.shape[2:]
    share = grad_a.shape[0]

    def tile_rows(n):
        return pl.ds(pl.multiple_of(n * PAD, 8), PAD)

    for d, grad_ref in enumerate((grad_a, grad_b, grad_c, grad_d)):

        @pl.loop(0, share)
        def _(i, d=d, grad_ref=grad_ref):
            n = jnp.bitwise_xor(place_ref[3], d) * share + i
            outside = 1.0 - inside_box(corner_ref, n, place_ref)
            kept = ratio_ref[n] * outside * grad_ref[i].astype(F32)
            kept = kept.reshape(PAD, width)
            for lane in range(total.shape[0]):
                total[lane, tile_rows(n), :] = kept[:, lane * 128 : (lane + 1) * 128]

    @pl.loop(0, back_ref.shape[0])
    def _(s):
        piece = back_ref[s].astype(F32).reshape(PAD, width)
        for lane in range(total.shape[0]):
            total[lane, tile_rows(index_ref[s]), :] += piece[:, lane * 128 : (lane + 1) * 128]

    for row in range(TILE):
        for col in range(TILE):
            out_ref[row, col] = jnp.concatenate(
                [
                    total[lane, pl.ds(row * 8 + col, count, stride=PAD), :]
                    for lane in range(total.shape[0])
                ],
                axis=1,
            )


def lay_kernel(place_ref, act_a, act_b, act_c, act_d, out_ref, flat):
    count, width = out_ref.shape[2:]
    share = act_a.shape[0]
    for d, act_ref in enumerate((act_a, act_b, act_c, act_d)):

        @pl.loop(0, share)
        def _(i, d=d, act_ref=act_ref):
            n = jnp.bitwise_xor(place_ref[3], d) * share + i
            tile = act_ref[i].astype(F32).reshape(PAD, width)
            for lane in range(flat.shape[0]):
                flat[lane, pl.ds(pl.multiple_of(n * PAD, 8), PAD), :] = tile[
                    :, lane * 128 : (lane + 1) * 128
                ]

    for row in range(TILE):
        for col in range(TILE):
            out_ref[row, col] = jnp.concatenate(
                [
                    flat[lane, pl.ds(row * 8 + col, count, stride=PAD), :]
                    for lane in range(flat.shape[0])
                ],
                axis=1,
            ).astype(BF)


def unpack_kernel(
    ranks,
    counts,
    place_ref,
    *refs,
):
    pieces, refs = refs[:8], refs[8:]
    outs, (vectors, *buffers, send_sem) = refs[:12], refs[12:]
    (
        gain_out,
        shift_out,
        entry_out,
        entry_b_out,
        conv_out,
        conv_b_out,
        exit_out,
        exit_b_out,
        expand_out,
        expand_b_out,
        shrink_out,
        shrink_b_out,
    ) = buffers
    width = exit_out.shape[1]
    units = expand_out.shape[2]
    middle = width // 2

    def squares(out_ref, block, count):
        return [(out_ref, block, 0, part * width, width) for part in range(count)]

    def tall(out_ref, block, count):
        return [(out_ref, block, part * width, 0, width) for part in range(count)]

    plans = (
        squares(expand_out, 1, units // width) + tall(shrink_out, 1, units // width),
        [
            (entry_out, 0, 0, 0, width),
            (entry_out, 0, 0, width, middle),
            (vectors, None, 0, 0, middle),
            (entry_out, 0, middle, width, middle),
            (entry_out, 0, 0, 2 * width, width),
        ],
        squares(entry_out, 1, 3)
        + tall(exit_out, 1, 1)
        + squares(expand_out, 0, units // width)
        + tall(shrink_out, 0, units // width)
        + tall(exit_out, 0, 1),
    )
    inner_ranks = ranks // 4
    moves = []
    base = 0
    for plan, count in zip(plans, counts):
        at = 0
        for out_ref, block, first_row, lane, length in plan:
            done = 0
            while done < length:
                step = min(length - done, count - at % count)
                moves.append((out_ref, block, first_row + done, lane, base, count, at, step))
                at += step
                done += step
        base += count
    big = (expand_out, shrink_out, entry_out, exit_out)
    leaving = []

    def leave(buffer, out):
        copy = pltpu.make_async_copy(buffer, out, send_sem.at[len(leaving)])
        leaving.append(copy)
        return copy

    def place_parts(target, wanted, col, own):
        for out_ref, block, first_row, lane, base, count, at, step in moves:
            if out_ref is not target or block != wanted:
                continue
            shard, start = at // count, base + at % count
            half, shard = shard // ranks, shard % ranks
            first, inner = shard // inner_ranks, shard % inner_ranks
            piece = pieces[4 * (col ^ half) + (own ^ first)]
            inner = jnp.bitwise_xor(place_ref[6], inner)
            values = piece[inner, start : start + step, :].astype(F32)
            place = slice(first_row, first_row + step)
            if block is None:
                out_ref[place, :] = values
            else:
                out_ref[block, place, lane : lane + width] = values

    first_sends = {}
    for block in (1, 0):
        for target in big:
            i = [j for j, ref in enumerate(buffers) if ref is target][0]
            first_sends[block, i] = leave(target.at[block], outs[i].at[block])
    for col in range(2):
        for own in range(4):

            @pl.when((place_ref[2] == col) & (place_ref[5] == own))
            def _(col=col, own=own):
                place_parts(vectors, None, col, own)
                for (block, i), copy in first_sends.items():
                    place_parts(buffers[i], block, col, own)
                    copy.start()

    def line(n):
        return vectors[n : n + 1, :]

    gain_out[0] = jnp.concatenate([line(33), line(18)], axis=0)
    gain_out[1] = jnp.concatenate([line(11), line(5)], axis=0)
    shift_out[0] = jnp.concatenate([line(34), line(19)], axis=0)
    shift_out[1] = jnp.concatenate([line(12), line(6)], axis=0)
    for part in range(2):
        lanes = slice(part * width, (part + 1) * width)
        entry_b_out[:, lanes] = jnp.concatenate([line(31 + part), line(9 + part)], axis=0)
    for i in range(3):
        for j in range(3):
            conv_out[i, j] = jnp.concatenate(
                [line(35 + 3 * i + j), line(22 + 3 * i + j)], axis=0
            )
    conv_b_out[...] = jnp.concatenate([line(21), line(8)], axis=0)
    exit_b_out[...] = jnp.concatenate([line(20), line(7)], axis=0)
    for part in range(units // width):
        lanes = slice(part * width, (part + 1) * width)
        expand_b_out[:, lanes] = jnp.concatenate([line(14 + part), line(part)], axis=0)
    shrink_b_out[...] = jnp.concatenate([line(13), line(4)], axis=0)
    for buffer, out in zip(buffers, outs):
        if not any(buffer is ref for ref in big):
            leave(buffer, out).start()
    for copy in leaving:
        copy.wait()


SMEM = pl.BlockSpec(memory_space=pltpu.SMEM)
VMEM = pl.BlockSpec(memory_space=pltpu.VMEM)


ANYWHERE = pl.BlockSpec(memory_space=pl.ANY)
FAR = pl.BlockSpec(memory_space=pltpu.HBM)


def far(values):
    return pltpu.with_memory_space_constraint(values, pltpu.HBM)


class Moves:
    def __init__(self, fetched, sent):
        self.fetched, self.sent = dict(fetched), dict(sent)
        self.waited, self.started = set(), set()

    def copies(self, ref, part):
        copies = self.fetched.get(id(ref), [])
        return [
            ((id(ref), i), copy)
            for i, copy in enumerate(copies)
            if part is None or len(copies) == 1 or i == part
        ]

    def fetch(self, *refs, part=None):
        for ref in refs:
            for key, copy in self.copies(ref, part):
                if key not in self.started:
                    copy.start()
                    self.started.add(key)

    def need(self, *refs, part=None):
        self.fetch(*refs, part=part)
        for ref in refs:
            for key, copy in self.copies(ref, part):
                if key not in self.waited:
                    copy.wait()
                    self.waited.add(key)

    def send(self, *refs):
        for ref in refs:
            if id(ref) in self.sent:
                self.sent[id(ref)].start()
                self.started.add(id(ref))

    def finish(self):
        for key, copies in self.fetched.items():
            for i, copy in enumerate(copies):
                if (key, i) not in self.started:
                    copy.start()
                if (key, i) not in self.waited:
                    copy.wait()
        for key, copy in self.sent.items():
            if key not in self.started:
                copy.start()
        for copy in self.sent.values():
            copy.wait()


def halves(ref):
    if ref.shape[-2] != WIN:
        return [pl.ds(0, ref.shape[0])]
    count = ref.shape[0] // 2
    return [pl.ds(0, count), pl.ds(count, count)]


def run(
    kernel,
    scalars,
    arrays,
    outs,
    scratch=(),
    flops=0,
    name=None,
    after=(),
    scalar_outs=(),
    lazy=None,
    vmem=16,
    near=((), ()),
):
    outs = list(outs)
    first_in, first_out = (len(arrays), len(outs)) if lazy is None else lazy
    eager, late = list(arrays[:first_in]), list(arrays[first_in:])
    n_in = len(scalars) + len(eager)
    scratch_shapes = [
        kind if dtype is None else pltpu.VMEM(kind, dtype) for kind, dtype in scratch
    ]
    n_own = len(scratch_shapes)
    n_late, n_sent = len(late), len(outs) - first_out
    if lazy is not None:
        scratch_shapes += [pltpu.VMEM(a.shape, a.dtype) for a in late]
        scratch_shapes += [pltpu.VMEM(*out) for out in outs[first_out:]]
        scratch_shapes += [pltpu.SemaphoreType.DMA((n_late, 2)), pltpu.SemaphoreType.DMA((max(n_sent, 1),))]

    def body(*refs):
        given, refs = refs[:n_in], refs[n_in:]
        sources, refs = refs[:n_late], refs[n_late + len(after) :]
        results, refs = refs[: len(scalar_outs) + first_out], refs[len(scalar_outs) + first_out :]
        targets, refs = refs[:n_sent], refs[n_sent:]
        own, refs = refs[:n_own], refs[n_own:]
        if lazy is None:
            kernel(*given, *results, *own)
            return
        buffers, leaving = refs[:n_late], refs[n_late : n_late + n_sent]
        fetch_sem, send_sem = refs[n_late + n_sent :]
        moves = Moves(
            [
                (
                    id(buffer),
                    [
                        pltpu.make_async_copy(source.at[part], buffer.at[part], fetch_sem.at[i, j])
                        for j, part in enumerate(halves(buffer))
                    ],
                )
                for i, (source, buffer) in enumerate(zip(sources, buffers))
            ],
            [
                (id(buffer), pltpu.make_async_copy(buffer, target, send_sem.at[i]))
                for i, (buffer, target) in enumerate(zip(leaving, targets))
            ],
        )
        kernel(moves, *given, *buffers, *results, *leaving, *own)
        moves.finish()

    out_shape = [jax.ShapeDtypeStruct(shape, dtype) for shape, dtype in scalar_outs] + [
        pltpu.HBM(shape, dtype)
        if lazy is not None and i not in near[1]
        else jax.ShapeDtypeStruct(shape, dtype)
        for i, (shape, dtype) in enumerate(outs)
    ]
    late = [
        a if i in near[0] else far(a)
        for i, a in enumerate(late, first_in)
    ]
    moved = sum(a.size * a.dtype.itemsize for a in arrays)
    return pl.pallas_call(
        body,
        out_shape=out_shape,
        in_specs=[SMEM] * len(scalars)
        + [VMEM] * len(eager)
        + [ANYWHERE if i in near[0] else FAR for i in range(first_in, len(arrays))]
        + [ANYWHERE] * len(after),
        out_specs=[SMEM] * len(scalar_outs)
        + [VMEM] * first_out
        + [ANYWHERE if i in near[1] else FAR for i in range(first_out, len(outs))],
        scratch_shapes=scratch_shapes,
        compiler_params=pltpu.CompilerParams(vmem_limit_bytes=vmem * 1024 * 1024),
        cost_estimate=pl.CostEstimate(flops=flops, bytes_accessed=moved, transcendentals=0),
        name=name,
    )(*scalars, *eager, *late, *after)


def gate(values, after):
    values, after = list(values), list(after)
    return list(lax.optimization_barrier(tuple(values + after)))[: len(values)]


def swap(values, axis):
    return lax.ppermute(values, axis, [(0, 1), (1, 0)])


def added(values, others):
    return (values.astype(F32) + others.astype(F32)).astype(BF)


def shards(values, ranks):
    return values.reshape(ranks, values.shape[0] // ranks, values.shape[1])


def spread_sum(pieces):
    mine = jnp.sum(pieces.astype(F32), axis=0).astype(BF)
    return jnp.broadcast_to(mine[None], pieces.shape)


def across(values, axes, size, mask):
    return lax.ppermute(values, axes, [(i, i ^ mask) for i in range(size)])


def deal(parts):
    return [parts[0]] + [across(parts[d], ("row", "col"), 4, d) for d in (1, 2, 3)]


RANKS = ("dp", "row")


def stages(ranks):
    bits = ranks.bit_length() - 1
    return [(bit, min(2, bits - bit)) for bit in range(0, bits, 2)]


def scatter_send(values, ranks, stage):
    bit, count = stage
    size = 1 << count
    me = (lax.axis_index(RANKS) >> bit) & (size - 1)
    cut = values.reshape(size, values.shape[0] // size, values.shape[1])
    return [lax.dynamic_index_in_dim(cut, me ^ d, 0, keepdims=False) for d in range(size)]


def scatter_move(parts, ranks, stage):
    return [parts[0]] + [
        across(parts[d], RANKS, ranks, d << stage[0]) for d in range(1, len(parts))
    ]


def scatter_sum(parts):
    return sum(part.astype(F32) for part in parts).astype(BF)


def gather(values, ranks, stage):
    return jnp.stack(
        [values]
        + [across(values, RANKS, ranks, d << stage[0]) for d in range(1, 1 << stage[1])]
    )


def rank_order(rank, ranks):
    order = 0
    for bit, count in stages(ranks):
        order = order * (1 << count) + ((rank >> bit) & ((1 << count) - 1))
    return order


def local(
    groups,
    images,
    cotangent,
    mix_partner,
    cut_partner,
    ratios,
    corners,
    drop_masks,
    norm_gains,
    norm_shifts,
    entry_weight,
    entry_bias,
    position_kernel,
    position_bias,
    exit_weight,
    exit_bias,
    expand_weight,
    expand_bias,
    shrink_weight,
    shrink_bias,
):
    images_here = images.shape[0]
    width = images.shape[3]
    units = expand_weight.shape[2]
    row, col = lax.axis_index("row"), lax.axis_index("col")
    share = images_here // 4
    rows = 4 * share * PAD
    ranks = 2 * groups
    capacity = (2 * images_here + groups - 1) // groups
    slots = groups * capacity
    order = rank_order(lax.axis_index(RANKS), ranks)
    place = jnp.stack(
        [
            lax.axis_index("dp"),
            row,
            col,
            2 * row + col,
            order,
            order // (ranks // 4),
            order % (ranks // 4),
        ]
    ).astype(jnp.int32)
    spots = [0] * ranks
    for rank in range(ranks):
        spots[rank_order(rank, ranks)] = rank
    quad = ((share, TILE, 8, width), BF)
    corners = corners.T
    masks = drop_masks.T
    flat = ((width // 128, images_here * PAD, 128), F32)
    index, take, outgoing, own = run(
        pick_kernel,
        [place, mix_partner, cut_partner],
        [images.transpose(1, 2, 0, 3)],
        [((slots, TILE, 8, width), BF), ((images_here, TILE, 8, width), BF)],
        [flat, (pltpu.SMEM((groups,), jnp.int32), None)],
        name="pick",
        vmem=60,
        scalar_outs=(((slots + 8,), jnp.int32), ((2 * images_here,), jnp.int32)),
    )
    arrived = lax.all_to_all(outgoing, "dp", split_axis=0, concat_axis=0, tiled=True)
    cot = deal(
        run(deal_kernel, [place], [cotangent.transpose(1, 2, 0, 3)], [quad] * 4, [flat], name="deal", vmem=60)
    )
    mixed = deal(
        run(
            mix_kernel,
            [place, take, corners, ratios],
            [arrived, own],
            [quad] * 4,
            name="mix",
            after=cot,
        )
    )
    conv_k = position_kernel.transpose(1, 2, 0, 3)
    tall = (rows, width)
    (
        vec1,
        keep1,
        away1,
        act_a,
        act_b,
        act_c,
        act_d,
        active0,
        slope0,
        win0,
        chance0,
        stripe0,
        mid0,
        win1,
        chance1,
        stripe1,
        hidden1,
        grad1,
    ) = run(
        functools.partial(first_kernel, spots),
        [place, masks],
        [
            *mixed,
            norm_gains,
            norm_shifts,
            entry_bias,
            conv_k,
            position_bias,
            exit_bias,
            expand_bias,
            shrink_bias,
            *cot,
            entry_weight,
            exit_weight,
            expand_weight,
            shrink_weight,
        ],
        [
            ((7, 8, width), F32),
            ((units, width), BF),
            ((units, width), BF),
            *([quad] * 4),
            ((rows, units), BF),
            ((rows, units), BF),
            ((4 * share, WIN, 3 * HALF), BF),
            ((4 * share, WIN, LANES), BF),
            (tall, BF),
            (tall, F32),
            ((4 * share, WIN, 3 * HALF), BF),
            ((4 * share, WIN, LANES), BF),
            (tall, BF),
            (tall, F32),
            (tall, F32),
        ],
        [
            (tall, F32),
            ((rows, 3 * width), F32),
            (tall, F32),
            ((rows, units), BF),
            ((rows, units), BF),
            (tall, BF),
            (tall, BF),
        ],
        flops=10 * rows * width * width * 120,
        name="first",
        vmem=46,
        near=((), (1, 2)),
        lazy=(17, 3),
    )
    sent1 = shards(added(keep1, swap(away1, "col")), ranks)
    pieces1 = lax.all_to_all(sent1, RANKS, split_axis=0, concat_axis=0, tiled=True)
    vec2, conv2, keep2, away2, grad0, delta0 = run(
        second_kernel,
        [place, masks],
        [
            norm_gains,
            norm_shifts,
            conv_k,
            grad1,
            exit_weight,
            win1,
            chance1,
            hidden1,
            entry_weight,
            stripe1,
            mid0,
            shrink_weight,
            slope0,
            expand_weight,
            active0,
            stripe0,
        ],
        [
            ((15, 8, width), F32),
            ((9, 8, width), F32),
            ((13 * width // 2, width), BF),
            ((13 * width // 2, width), BF),
            (tall, F32),
            (tall, F32),
        ],
        [
            (tall, F32),
            (tall, BF),
            ((rows, 3 * width), F32),
            ((rows, 3 * width), BF),
            (tall, BF),
            (tall, BF),
            ((rows, units), BF),
        ],
        flops=6 * rows * width * width * 120,
        name="second",
        vmem=42,
        near=((), (2, 3)),
        after=[sent1],
        lazy=(3, 4),
    )
    act = deal([act_a, act_b, act_c, act_d])
    keep2, away2, *act = gate([keep2, away2, *act], [pieces1])
    steps = stages(ranks)

    def first_parts(keep, away):
        other = swap(away, "col")
        count = keep.shape[0] // 4
        return [
            added(keep[d * count : (d + 1) * count], other[d * count : (d + 1) * count])
            for d in range(4)
        ]

    parts2 = first_parts(keep2, away2)
    moved2 = scatter_move(parts2, ranks, steps[0])
    *out_tiles, keep3, away3 = run(
        third_kernel,
        [place],
        [
            norm_gains,
            norm_shifts,
            conv_k,
            vec1,
            vec2,
            conv2,
            *mixed,
            delta0,
            win0,
            chance0,
            entry_weight,
            grad0,
        ],
        [quad] * 4 + [((2 * width, width), BF), ((2 * width, width), BF)],
        [
            (tall, F32),
            ((rows, 3 * width), F32),
            ((rows, 3 * width), BF),
            (tall, BF),
            ((4, 8, width), F32),
            ((9, 8, width), F32),
            ((width, width), F32),
        ],
        flops=3 * rows * width * width * 120,
        name="third",
        vmem=36,
        near=((), range(6)),
        after=parts2,
        lazy=(10, 6),
    )
    *moved2, keep3, away3 = gate([*moved2, keep3, away3], out_tiles)
    gradient = deal(out_tiles)
    (parted,) = run(
        split_kernel,
        [place, take, corners, ratios],
        gradient,
        [((slots, TILE, 8, width), BF)],
        name="split",
    )
    mine1 = jnp.sum(pieces1.astype(F32), axis=0).astype(BF)
    mine2 = scatter_sum(moved2)
    moved3 = scatter_move(first_parts(keep3, away3), ranks, steps[0])
    mine3 = scatter_sum(gate(moved3, [mine1]))
    cut = mine2.shape[0] * 4 // ranks
    lot = mine3.shape[0] * 4 // ranks
    joint = jnp.concatenate(
        [
            mine3.reshape(ranks // 4, lot, width),
            mine2.reshape(ranks // 4, cut, width),
        ],
        axis=1,
    ).reshape(-1, width)
    for step in steps[1:]:
        joint = scatter_sum(scatter_move(scatter_send(joint, ranks, step), ranks, step))
    joint = jnp.concatenate([mine1, joint], axis=0)
    counts = (mine1.shape[0], lot, cut)
    for step in reversed(steps[1:]):
        joint = gather(joint, ranks, step).reshape(-1, width)
    joint = shards(joint, ranks // 4)
    (parted,) = gate([parted], [joint])
    (activations,) = run(
        lay_kernel, [place], [far(a) for a in act], [((TILE, TILE, images_here, width), BF)], [flat], name="lay"
    )
    back = lax.all_to_all(parted, "dp", split_axis=0, concat_axis=0, tiled=True)
    (back,) = gate([back], [activations])
    (input_gradient,) = run(
        join_kernel,
        [place, index, corners, ratios],
        [*gradient, back],
        [((TILE, TILE, images_here, width), F32)],
        [((width // 128, (images_here + 1) * PAD, 128), F32)],
        name="join",
    )
    full = [joint] + [across(joint, RANKS, ranks, d) for d in (1, 2, 3)]
    full[2:] = gate(full[2:], [input_gradient])
    full += [swap(piece, "col") for piece in full]
    shapes = [
        (2, 2, width),
        (2, 2, width),
        (2, width, 3 * width),
        (2, 2 * width),
        (3, 3, 2, width),
        (2, width),
        (2, width, width),
        (2, width),
        (2, width, units),
        (2, units),
        (2, units, width),
        (2, width),
    ]
    gains, shifts, entry, entry_b, conv, conv_b, exit_, exit_b, expand, expand_b, shrink, shrink_b = (
        pl.pallas_call(
            functools.partial(unpack_kernel, ranks, counts),
            out_shape=[jax.ShapeDtypeStruct(shape, F32) for shape in shapes],
            in_specs=[SMEM] + [VMEM] * 8,
            out_specs=[ANYWHERE] * 12,
            scratch_shapes=[
                pltpu.VMEM((width // 2, width), F32),
            ]
            + [pltpu.VMEM(shape, F32) for shape in shapes]
            + [pltpu.SemaphoreType.DMA((16,))],
            compiler_params=pltpu.CompilerParams(vmem_limit_bytes=24 * 1024 * 1024),
            name="unpack",
        )(place, *full)
    )
    return (
        activations.transpose(2, 0, 1, 3),
        input_gradient.transpose(2, 0, 1, 3),
        gains,
        shifts,
        entry,
        entry_b,
        conv.transpose(2, 0, 1, 3),
        conv_b,
        exit_,
        exit_b,
        expand,
        expand_b,
        shrink,
        shrink_b,
    )


def solution(mesh):
    tiles = P("dp", "row", "col", None)
    return jax.shard_map(
        functools.partial(local, mesh.shape["dp"]),
        mesh=mesh,
        in_specs=(tiles, tiles, P(), P(), P("dp"), P("dp", None), P("dp", None)) + (P(),) * 12,
        out_specs=(tiles, tiles) + (P(),) * 12,
        check_vma=False,
    )
```

```python
import functools

import jax
import jax.numpy as jnp
from jax import lax
from jax.experimental import pallas as pl
from jax.experimental.pallas import tpu as pltpu
from jax.sharding import PartitionSpec as P

TILE = 7
PAD = 56
HEAD_DIM = 32
SIDE_HEADS = 4
HALF = 128
WIN = 2 * PAD
CHUNK = 8 * PAD
LANES = SIDE_HEADS * 128
SCALE = HEAD_DIM ** (-0.5)
LOG2E = 1.4426950408889634
EPS = 1e-05
BF = jnp.bfloat16
F32 = jnp.float32


def dot_nn(a, b):
    return lax.dot_general(a, b, (((1,), (0,)), ((), ())), preferred_element_type=F32)


def dot_nt(a, b):
    return lax.dot_general(a, b, (((1,), (1,)), ((), ())), preferred_element_type=F32)


def dot_tn(a, b):
    return lax.dot_general(a, b, (((0,), (0,)), ((), ())), preferred_element_type=F32)


def norm_parts(values):
    centered = values - jnp.mean(values, axis=-1, keepdims=True)
    inverse = lax.rsqrt(jnp.mean(centered * centered, axis=-1, keepdims=True) + EPS)
    return centered * inverse, inverse


def norm_back(delta, hat, inverse, gain):
    scaled = delta * gain
    first = jnp.mean(scaled, axis=-1, keepdims=True)
    second = jnp.mean(scaled * hat, axis=-1, keepdims=True)
    return inverse * (scaled - first - hat * second)


def gelu_parts(values):
    chance = 0.5 + 0.5 * lax.erf(values * (0.5**0.5))
    density = jnp.exp2(values * values * (-0.5 * LOG2E)) * 0.3989422804014327
    return chance, density


def row_sums(values):
    count, width = values.shape
    return jnp.sum(values.reshape(count // 8, 8, width), axis=0)


def scale_rows(place_ref, mask_ref, column):
    scales = [
        mask_ref[column, 4 * place_ref[3] + i].astype(F32) * 1.25 for i in range(4)
    ]
    columns = [jnp.full((PAD, 1), scale, F32) for scale in scales]
    return jnp.concatenate(columns * (CHUNK // (4 * PAD)), axis=0)


def add_row(acc_ref, row, values):
    acc_ref[row] += values


def spread_heads(values):
    lane = lax.broadcasted_iota(jnp.int32, values.shape, 1) // HEAD_DIM
    empty = jnp.zeros((128 - WIN, HALF), F32)
    blocks = []
    for head in range(SIDE_HEADS):
        blocks.append(jnp.where(lane == head, values, 0.0))
        blocks.append(empty)
    return jnp.concatenate(blocks, axis=0).astype(BF)


def over_keys(weights, values):
    weights = fill_rows(weights)
    stacked = jnp.concatenate(
        [weights[:, head * 128 : (head + 1) * 128] for head in range(SIDE_HEADS)], axis=0
    )
    return dot_tn(stacked, spread_heads(values))[:WIN]


def fill_rows(values):
    empty = jnp.zeros((128 - WIN, values.shape[1]), values.dtype)
    return jnp.concatenate([values, empty], axis=0)


def valid_column(shape):
    return lax.broadcasted_iota(jnp.int32, shape, 1) != 7


def valid_rows(shape):
    return lax.broadcasted_iota(jnp.int32, shape, 0) % 8 != 7


def column_shifts(values, across):
    cube = values.reshape(2 * TILE, 8, HALF)
    if not across:
        return (pltpu.roll(cube, 1, 1), cube, pltpu.roll(cube, 7, 1))
    left, right = cube[:TILE], cube[TILE:]
    column = lax.broadcasted_iota(jnp.int32, left.shape, 1)
    before = jnp.concatenate(
        [
            pltpu.roll(left, 1, 1),
            jnp.where(column == 0, pltpu.roll(left, 2, 1), pltpu.roll(right, 1, 1)),
        ],
        axis=0,
    )
    after = jnp.concatenate(
        [
            jnp.where(column == 6, pltpu.roll(right, 6, 1), pltpu.roll(left, 7, 1)),
            pltpu.roll(right, 7, 1),
        ],
        axis=0,
    )
    return (before, cube, after)


def row_shift(cube, step, across):
    if step == 0:
        return cube
    empty = jnp.zeros((1, 8, HALF), F32)

    def move(part):
        if step < 0:
            return jnp.concatenate([empty, part[:-1]], axis=0)
        return jnp.concatenate([part[1:], empty], axis=0)

    if across:
        return jnp.concatenate([move(cube[:TILE]), move(cube[TILE:])], axis=0)
    return move(cube)


def window_conv(shifts, kernel_at, across):
    total = None
    for i in range(3):
        part = None
        for j in range(3):
            term = kernel_at(i, j) * shifts[j]
            part = term if part is None else part + term
        part = row_shift(part, i - 1, across)
        total = part if total is None else total + part
    return total.reshape(WIN, HALF)


def window_rows(across, window):
    side, image = window // 4, window % 4
    if across:
        first, second = 2 * side, 2 * side + 1
    else:
        first, second = side, 2 + side
    return (
        pl.multiple_of((first * 4 + image) * PAD, 8),
        pl.multiple_of((second * 4 + image) * PAD, 8),
    )


def take_window(ref, at, lane):
    return jnp.concatenate(
        [ref[pl.ds(at[0], PAD), lane : lane + HALF], ref[pl.ds(at[1], PAD), lane : lane + HALF]],
        axis=0,
    )


def put_window(ref, at, lane, values):
    ref[pl.ds(at[0], PAD), lane : lane + HALF] = values[:PAD]
    ref[pl.ds(at[1], PAD), lane : lane + HALF] = values[PAD:]


def round_bf(values):
    return values.astype(BF).astype(F32)


def attention_forward(
    block, hidden_ref, gains, shifts, entry_w, entry_b, conv_k, conv_b, wide, stripe, win_out, chance_out
):
    width = hidden_ref.shape[1]

    @pl.loop(0, 2)
    def _(t):
        rows = chunk(t)
        hat, _ = norm_parts(hidden_ref[rows, :])
        normed = (hat * gains[block, 0:1, :] + shifts[block, 0:1, :]).astype(BF)
        for part in range(3):
            out = dot_nn(normed, entry_w[block, :, part * width : (part + 1) * width])
            if part != 1:
                at = 0 if part == 0 else width
                out = out + entry_b[block : block + 1, at : at + width]
            wide[rows, part * width : (part + 1) * width] = round_bf(out)

    for direction in range(2):
        across = direction == 0
        lane = direction * HALF

        @pl.loop(0, 8, unroll=4)
        def _(window, across=across, lane=lane, direction=direction):
            at = window_rows(across, window)
            queries = take_window(wide, at, lane)
            keys = take_window(wide, at, width + lane)
            values = take_window(wide, at, 2 * width + lane)
            keys_bf = keys.astype(BF)
            win_out[direction * 8 + window, :, 0:HALF] = queries.astype(BF)
            win_out[direction * 8 + window, :, HALF : 2 * HALF] = keys_bf
            win_out[direction * 8 + window, :, 2 * HALF : 3 * HALF] = values.astype(BF)
            scores = dot_nt(keys_bf, spread_heads(queries)).reshape(2 * TILE, 8, LANES)
            scores = jnp.where(valid_column((1, 8, LANES)), scores, -1e30)
            top = jnp.max(jnp.max(scores, axis=0), axis=0, keepdims=True)
            lifted = jnp.exp2((scores - top) * (SCALE * LOG2E))
            totals = jnp.sum(jnp.sum(lifted, axis=0), axis=0, keepdims=True)
            chances = (lifted * (1.0 / totals)).reshape(WIN, LANES).astype(BF)
            chance_out[direction * 8 + window] = chances
            attended = over_keys(chances, values)
            clean = jnp.where(valid_rows(values.shape), values, 0.0)
            position = window_conv(
                column_shifts(clean, across),
                lambda i, j: conv_k[i, j, block : block + 1, lane : lane + HALF],
                across,
            )
            put_window(
                stripe, at, lane, attended + position + conv_b[block : block + 1, lane : lane + HALF]
            )


def attention_backward(
    ready,
    block,
    win_in,
    chance_in,
    conv_k,
    stripe_delta,
    wide,
    conv_acc,
):
    width = stripe_delta.shape[1]
    for direction in range(2):
        ready(direction)
        across = direction == 0
        lane = direction * HALF

        @pl.loop(0, 8, unroll=4)
        def _(window, across=across, lane=lane, direction=direction):
            at = window_rows(across, window)
            out_delta = take_window(stripe_delta, at, lane)
            queries = win_in[direction * 8 + window, :, 0:HALF].astype(F32)
            keys = win_in[direction * 8 + window, :, HALF : 2 * HALF].astype(F32)
            values_bf = win_in[direction * 8 + window, :, 2 * HALF : 3 * HALF]
            values = values_bf.astype(F32)
            chances = chance_in[direction * 8 + window]
            delta_spread = spread_heads(out_delta)
            chance_delta = dot_nt(values_bf, delta_spread)
            cubes = (2 * TILE, 8, LANES)
            wide_chances = chances.astype(F32).reshape(cubes)
            weighted = wide_chances * chance_delta.reshape(cubes)
            common = jnp.sum(jnp.sum(weighted, axis=0), axis=0, keepdims=True)
            score_delta = (weighted - wide_chances * common).reshape(WIN, LANES).astype(BF)
            values_delta = dot_nn(chances, delta_spread)
            keys_delta = dot_nn(score_delta, spread_heads(queries)) * SCALE
            query_delta = over_keys(score_delta, keys) * SCALE
            keep = valid_rows(values.shape)
            clean = jnp.where(keep, values, 0.0)
            shifts = column_shifts(clean, across)
            cube = out_delta.reshape(2 * TILE, 8, HALF)
            for i in range(3):
                moved = row_shift(cube, 1 - i, across)
                for j in range(3):
                    conv_acc[3 * i + j, :, lane : lane + HALF] += jnp.sum(moved * shifts[j], axis=0)
            back = window_conv(
                column_shifts(out_delta, across),
                lambda i, j: conv_k[2 - i, 2 - j, block : block + 1, lane : lane + HALF],
                across,
            )
            values_delta = jnp.where(keep, values_delta + back, 0.0)
            put_window(wide, at, lane, query_delta)
            put_window(wide, at, width + lane, keys_delta)
            put_window(wide, at, 2 * width + lane, values_delta)


def chunk(t):
    return pl.ds(pl.multiple_of(t * CHUNK, CHUNK), CHUNK)


class Bundle:
    def __init__(self, place_ref, keep, away, chunks=1, spot=lambda chunk: chunk):
        self.place_ref, self.keep, self.away = place_ref, keep, away
        self.step, self.spot = keep.shape[0] // chunks, spot

    def put(self, at, values):
        values = values.astype(BF)
        half, step = self.keep.shape[0], self.step
        last = at + values.shape[0]
        first = at
        while first < last:
            stop = min(last, (first // step + 1) * step)
            number = first // half
            start = self.spot(first % half // step) * step
            inner, count = first % step, stop - first
            if not isinstance(start, int):
                start = pl.multiple_of(start, step)
            rows = pl.ds(start + inner, count)
            piece = values[first - at : stop - at]

            @pl.when(self.place_ref[2] == number)
            def _(piece=piece, rows=rows):
                self.keep[rows, :] = piece

            @pl.when(self.place_ref[2] != number)
            def _(piece=piece, rows=rows):
                self.away[rows, :] = piece

            first = stop


def put_squares(bundle, at, values, side):
    for part in range(values.shape[1] // side):
        bundle.put(at + part * side, values[:, part * side : (part + 1) * side])


def load_tiles(place_ref, tiles, hidden):
    for d, tile in enumerate(tiles):
        at = jnp.bitwise_xor(place_ref[3], d) * (4 * PAD)
        rows = pl.ds(pl.multiple_of(at, 4 * PAD), 4 * PAD)
        hidden[rows, :] = tile[...].astype(F32).reshape(4 * PAD, hidden.shape[1])


def store_tile(place_ref, tiles, t, values):
    count = CHUNK // (4 * PAD)
    values = values.reshape((count,) + tiles[0].shape).astype(BF)
    for part in range(count):
        for d, tile in enumerate(tiles):

            @pl.when(jnp.bitwise_xor(place_ref[3], d) == count * t + part)
            def _(tile=tile, part=part):
                tile[...] = values[part]


def first_kernel(
    spots,
    moves,
    place_ref,
    mask_ref,
    mixed_a,
    mixed_b,
    mixed_c,
    mixed_d,
    gains,
    shifts,
    entry_b,
    conv_k,
    conv_b,
    exit_b,
    expand_b,
    shrink_b,
    cot_a,
    cot_b,
    cot_c,
    cot_d,
    entry_w,
    exit_w,
    expand_w,
    shrink_w,
    vec_out,
    keep_out,
    away_out,
    act_a,
    act_b,
    act_c,
    act_d,
    active0_out,
    slope0_out,
    win0_out,
    chance0_out,
    stripe0_out,
    mid0_out,
    win1_out,
    chance1_out,
    stripe1_out,
    hidden1_out,
    grad_out,
    hidden,
    wide,
    stripe,
    active1,
    pre1,
    feed1,
    inner1,
):
    width = hidden.shape[1]
    hidden_units = expand_w.shape[2]
    bundle = Bundle(place_ref, keep_out, away_out, len(spots), lambda chunk: spots[chunk])
    vec_out[...] = jnp.zeros(vec_out.shape, F32)
    moves.fetch(entry_w)
    load_tiles(place_ref, (mixed_a, mixed_b, mixed_c, mixed_d), hidden)
    moves.need(entry_w)
    moves.fetch(exit_w, expand_w, shrink_w, cot_a, cot_b, cot_c, cot_d)

    for block in range(2):
        win_out, chance_out, stripe_out = (
            (win0_out, chance0_out, stripe0_out),
            (win1_out, chance1_out, stripe1_out),
        )[block]
        attention_forward(
            block, hidden, gains, shifts, entry_w, entry_b, conv_k, conv_b, wide, stripe, win_out, chance_out
        )
        moves.send(win_out, chance_out)
        moves.need(exit_w, expand_w, shrink_w)
        if block == 1:
            moves.need(cot_a, cot_b, cot_c, cot_d)
            load_tiles(place_ref, (cot_a, cot_b, cot_c, cot_d), grad_out)

        @pl.loop(0, 2)
        def _(t, block=block, stripe_out=stripe_out):
            rows = chunk(t)
            striped = stripe[rows, :].astype(BF)
            stripe_out[rows, :] = striped
            branch = dot_nn(striped, exit_w[block]) + exit_b[block : block + 1, :]
            midway = hidden[rows, :] + scale_rows(place_ref, mask_ref, 2 * block) * branch
            if block == 0:
                mid0_out[rows, :] = midway
            hat, inverse = norm_parts(midway)
            normed = (hat * gains[block, 1:2, :] + shifts[block, 1:2, :]).astype(BF)
            feed_scale = scale_rows(place_ref, mask_ref, 2 * block + 1)
            feed = shrink_b[block : block + 1, :]
            if block == 1:
                inner1[rows, :] = normed
                gradient = grad_out[rows, :]
                feed_delta = (feed_scale * gradient).astype(BF)
                feed1[rows, :] = feed_delta
                add_row(vec_out, 4, row_sums(feed_delta.astype(F32)))
                inner_delta = jnp.zeros((CHUNK, width), F32)
            for part in range(hidden_units // width):
                at = slice(part * width, (part + 1) * width)
                pre_act = dot_nn(normed, expand_w[block, :, at]) + expand_b[block : block + 1, at]
                chance, density = gelu_parts(pre_act)
                active = (pre_act * chance).astype(BF)
                slope = chance + pre_act * density
                if block == 0:
                    active0_out[rows, at] = active
                    slope0_out[rows, at] = slope.astype(BF)
                else:
                    active1[rows, at] = active
                    pre_delta = (dot_nt(feed_delta, shrink_w[block, at, :]) * slope).astype(BF)
                    pre1[rows, at] = pre_delta
                    add_row(vec_out, part, row_sums(pre_delta.astype(F32)))
                    inner_delta = inner_delta + dot_nt(pre_delta, expand_w[block, :, at])
                feed = feed + dot_nn(active, shrink_w[block, at, :])
            output = midway + feed_scale * feed
            if block == 0:
                hidden[rows, :] = output
                hidden1_out[rows, :] = output
            else:
                store_tile(place_ref, (act_a, act_b, act_c, act_d), t, output)
                add_row(vec_out, 5, row_sums(inner_delta * hat))
                add_row(vec_out, 6, row_sums(inner_delta))
                grad_out[rows, :] = gradient + norm_back(
                    inner_delta, hat, inverse, gains[block, 1:2, :]
                )

        moves.send(stripe_out)
        if block == 0:
            moves.send(mid0_out, active0_out, slope0_out, hidden1_out)
        else:
            moves.send(act_a, act_b, act_c, act_d, grad_out)

    put_squares(bundle, 0, dot_tn(inner1[...], pre1[...]), width)
    for part in range(hidden_units // width):
        bundle.put(
            hidden_units + part * width,
            dot_tn(active1[:, part * width : (part + 1) * width], feed1[...]),
        )


def delta_rows(block, place_ref, mask_ref, exit_w, grad_ref, stripe_delta, branch_delta, vec_out, at):
    @pl.loop(0, 2)
    def _(t):
        rows = chunk(t)
        rounded = (scale_rows(place_ref, mask_ref, 2 * block) * grad_ref[rows, :]).astype(BF)
        branch_delta[rows, :] = rounded
        add_row(vec_out, at, row_sums(rounded.astype(F32)))
        out = round_bf(dot_nt(rounded, exit_w[block]))
        stripe_delta[rows, :] = out
        add_row(vec_out, at + 1, row_sums(out))


def entry_backward(block, hidden_ref, gains, shifts, entry_w, grad_ref, wide, wide_bf, normed_bf, vec_out, at, emit):
    width = hidden_ref.shape[1]

    @pl.loop(0, 2)
    def _(t):
        rows = chunk(t)
        hat, inverse = norm_parts(hidden_ref[rows, :])
        normed_bf[rows, :] = (hat * gains[block, 0:1, :] + shifts[block, 0:1, :]).astype(BF)
        delta = jnp.zeros((CHUNK, width), F32)
        for part in range(3):
            lanes = slice(part * width, (part + 1) * width)
            rounded = wide[rows, lanes].astype(BF)
            wide_bf[rows, lanes] = rounded
            if part != 1:
                add_row(vec_out, at + part // 2, row_sums(rounded.astype(F32)))
            delta = delta + dot_nt(rounded, entry_w[block, :, lanes])
        add_row(vec_out, at + 2, row_sums(delta * hat))
        add_row(vec_out, at + 3, row_sums(delta))
        emit(t, rows, grad_ref[rows, :] + norm_back(delta, hat, inverse, gains[block, 0:1, :]))


def second_kernel(
    moves,
    place_ref,
    mask_ref,
    gains,
    shifts,
    conv_k,
    grad_in,
    exit_w,
    win1,
    chance1,
    hidden1,
    entry_w,
    stripe1,
    mid0,
    shrink_w,
    slope0,
    expand_w,
    active0,
    stripe0,
    vec_out,
    conv_out,
    keep_out,
    away_out,
    grad_out,
    stripe_delta_out,
    stripe_delta,
    branch_delta,
    wide,
    wide_bf,
    normed_bf,
    feed0,
    pre0,
):
    grad = grad_out
    width = grad.shape[1]
    hidden_units = expand_w.shape[2]
    bundle = Bundle(
        place_ref, keep_out, away_out, 4, lambda chunk: jnp.bitwise_xor(place_ref[5], chunk)
    )
    vec_out[...] = jnp.zeros(vec_out.shape, F32)
    conv_out[...] = jnp.zeros(conv_out.shape, F32)
    moves.fetch(grad_in, exit_w)
    moves.fetch(win1, chance1, part=0)
    moves.need(grad_in, exit_w)
    moves.fetch(win1, chance1, part=1)
    delta_rows(1, place_ref, mask_ref, exit_w, grad_in, stripe_delta, branch_delta, vec_out, 0)

    def ready(direction):
        moves.need(win1, chance1, part=direction)
        if direction == 0:
            moves.fetch(hidden1, entry_w, stripe1)
        else:
            moves.fetch(mid0, shrink_w, slope0, expand_w, active0, stripe0)

    attention_backward(ready, 1, win1, chance1, conv_k, stripe_delta, wide, conv_out)

    def emit(t, rows, values):
        grad[rows, :] = values

    moves.need(hidden1, entry_w)
    entry_backward(
        1, hidden1, gains, shifts, entry_w, grad_in, wide, wide_bf, normed_bf, vec_out, 2, emit
    )
    put_squares(bundle, 0, dot_tn(normed_bf[...], wide_bf[...]), width)
    moves.need(stripe1)
    bundle.put(3 * width, dot_tn(stripe1[...], branch_delta[...]))
    moves.need(mid0, shrink_w, slope0, expand_w)

    @pl.loop(0, 2)
    def _(t):
        rows = chunk(t)
        gradient = grad[rows, :]
        hat, inverse = norm_parts(mid0[rows, :])
        normed_bf[rows, :] = (hat * gains[0, 1:2, :] + shifts[0, 1:2, :]).astype(BF)
        feed_delta = (scale_rows(place_ref, mask_ref, 1) * gradient).astype(BF)
        feed0[rows, :] = feed_delta
        add_row(vec_out, 6, row_sums(feed_delta.astype(F32)))
        inner_delta = jnp.zeros((CHUNK, width), F32)
        for part in range(hidden_units // width):
            at = slice(part * width, (part + 1) * width)
            pre_delta = (
                dot_nt(feed_delta, shrink_w[0, at, :]) * slope0[rows, at].astype(F32)
            ).astype(BF)
            pre0[rows, at] = pre_delta
            add_row(vec_out, 7 + part, row_sums(pre_delta.astype(F32)))
            inner_delta = inner_delta + dot_nt(pre_delta, expand_w[0, :, at])
        add_row(vec_out, 11, row_sums(inner_delta * hat))
        add_row(vec_out, 12, row_sums(inner_delta))
        grad[rows, :] = gradient + norm_back(inner_delta, hat, inverse, gains[0, 1:2, :])

    delta_rows(0, place_ref, mask_ref, exit_w, grad, stripe_delta_out, branch_delta, vec_out, 13)
    moves.send(grad_out, stripe_delta_out)
    moves.need(active0, stripe0)
    put_squares(bundle, 4 * width, dot_tn(normed_bf[...], pre0[...]), width)
    for part in range(hidden_units // width):
        bundle.put(
            (8 + part) * width,
            dot_tn(active0[:, part * width : (part + 1) * width], feed0[...]),
        )
    bundle.put(12 * width, dot_tn(stripe0[...], branch_delta[...]))


def third_kernel(
    moves,
    place_ref,
    gains,
    shifts,
    conv_k,
    vec1,
    vec2,
    conv2,
    mixed_a,
    mixed_b,
    mixed_c,
    mixed_d,
    stripe_delta,
    win0,
    chance0,
    entry_w,
    grad_in,
    out_a,
    out_b,
    out_c,
    out_d,
    keep_out,
    away_out,
    hidden,
    wide,
    wide_bf,
    normed_bf,
    vec3,
    conv3,
    flat,
):
    width = hidden.shape[1]
    bundle = Bundle(
        place_ref, keep_out, away_out, 4, lambda chunk: jnp.bitwise_xor(place_ref[5], chunk)
    )
    vec3[...] = jnp.zeros(vec3.shape, F32)
    conv3[...] = jnp.zeros(conv3.shape, F32)
    moves.fetch(stripe_delta)
    moves.fetch(win0, chance0, part=0)
    moves.need(stripe_delta)
    moves.fetch(win0, chance0, part=1)

    def ready(direction):
        moves.need(win0, chance0, part=direction)
        if direction == 0:
            moves.fetch(mixed_a, mixed_b, mixed_c, mixed_d, entry_w, grad_in)

    attention_backward(ready, 0, win0, chance0, conv_k, stripe_delta, wide, conv3)

    def emit(t, rows, values):
        store_tile(place_ref, (out_a, out_b, out_c, out_d), t, values)

    moves.need(mixed_a, mixed_b, mixed_c, mixed_d, entry_w, grad_in)
    load_tiles(place_ref, (mixed_a, mixed_b, mixed_c, mixed_d), hidden)
    entry_backward(
        0, hidden, gains, shifts, entry_w, grad_in, wide, wide_bf, normed_bf, vec3, 0, emit
    )
    moves.send(out_a, out_b, out_c, out_d)
    flat[...] = jnp.zeros(flat.shape, F32)
    at = 0
    for ref in (vec1, vec2, conv2, vec3, conv3):
        flat[at : at + ref.shape[0], :] = jnp.sum(ref[...], axis=1)
        at += ref.shape[0]
    spread = dot_tn(normed_bf[...], wide_bf[...])
    half = keep_out.shape[0]
    middle = width // 2
    lots = flat.shape[0] // 2
    bundle.put(0, spread[:, :width])
    bundle.put(width, spread[:middle, width : 2 * width])
    bundle.put(width + middle, flat[:lots, :])
    bundle.put(half, spread[middle:, width : 2 * width])
    bundle.put(half + middle, spread[:, 2 * width :])
    bundle.put(half + middle + width, flat[lots:, :])


def untangle(source, flat, target):
    count, width = source.shape[2:]
    lanes = flat.shape[0]
    for row in range(TILE):
        flat[:, pl.ds(row * 8 + 7, count, stride=PAD), :] = jnp.zeros((lanes, count, 128), F32)
        for col in range(TILE):
            token = source[row, col].astype(F32)
            for lane in range(lanes):
                flat[lane, pl.ds(row * 8 + col, count, stride=PAD), :] = token[
                    :, lane * 128 : (lane + 1) * 128
                ]

    @pl.loop(0, count)
    def _(n):
        rows = pl.ds(pl.multiple_of(n * PAD, 8), PAD)
        tile = jnp.concatenate([flat[lane, rows, :] for lane in range(lanes)], axis=1)
        target(n, tile.reshape(TILE, 8, width).astype(BF))


def owner_of(wanted, count):
    if count & (count - 1) == 0:
        return lax.shift_right_logical(wanted, count.bit_length() - 1)
    return lax.div(wanted, count)


def pick_kernel(
    moves, mix_ref, cut_ref, images_ref, index_out, take_out, sent_out, own_out, flat, counts
):
    moves.fetch(images_ref)
    count = images_ref.shape[2]
    slots = sent_out.shape[0]
    capacity = slots // counts.shape[0]
    me = lax.axis_index("dp")

    def put(n, tile):
        own_out[n] = tile

    @pl.loop(0, slots, unroll=8)
    def _(s):
        index_out[s] = count

    @pl.loop(0, counts.shape[0])
    def _(g):
        counts[g] = 0
        rank = g * capacity
        for ref in (mix_ref, cut_ref):
            for j in range(count):
                wanted = ref[g * count + j]
                owner = owner_of(wanted, count)
                hit = owner == me
                index_out[jnp.where(hit, rank, slots)] = wanted - owner * count
                rank = rank + hit.astype(jnp.int32)

    for part, ref in enumerate((mix_ref, cut_ref)):

        @pl.loop(0, count)
        def _(j, part=part, ref=ref):
            owner = owner_of(ref[me * count + j], count)
            rank = counts[owner]
            take_out[part * count + j] = owner * capacity + rank
            counts[owner] = rank + 1

    moves.need(images_ref)
    untangle(images_ref, flat, put)

    @pl.loop(0, slots, unroll=4)
    def _(s):
        sent_out[s] = own_out[jnp.minimum(index_out[s], count - 1)]


def deal_kernel(place_ref, source, out_a, out_b, out_c, out_d, flat):
    outs = (out_a, out_b, out_c, out_d)
    share = out_a.shape[0]

    def put(n, tile):
        for d, out in enumerate(outs):

            @pl.when(jnp.bitwise_xor(place_ref[3], d) == n // share)
            def _(out=out):
                out[n % share] = tile

    untangle(source, flat, put)


def inside_box(corner_ref, n, place_ref):
    shape = (TILE, 8, 1)
    row = place_ref[1] * TILE + lax.broadcasted_iota(jnp.int32, shape, 0)
    col = place_ref[2] * TILE + lax.broadcasted_iota(jnp.int32, shape, 1)
    hit = (
        (row >= corner_ref[0, n])
        & (row < corner_ref[1, n])
        & (col >= corner_ref[2, n])
        & (col < corner_ref[3, n])
    )
    return jnp.where(hit, 1.0, 0.0)


def mix_kernel(
    place_ref, take_ref, corner_ref, ratio_ref, arrived, own_ref, out_a, out_b, out_c, out_d
):
    count = own_ref.shape[0]
    share = out_a.shape[0]
    for d, out in enumerate((out_a, out_b, out_c, out_d)):

        @pl.loop(0, share)
        def _(i, d=d, out=out):
            n = jnp.bitwise_xor(place_ref[3], d) * share + i
            inside = inside_box(corner_ref, n, place_ref)
            ratio = ratio_ref[n]
            own = own_ref[n].astype(F32)
            blend = arrived[take_ref[n]].astype(F32)
            cut = arrived[take_ref[count + n]].astype(F32)
            mixed = inside * cut + (1.0 - inside) * (ratio * own + (1.0 - ratio) * blend)
            out[i] = mixed.astype(BF)


def split_kernel(
    place_ref, take_ref, corner_ref, ratio_ref, grad_a, grad_b, grad_c, grad_d, out_ref
):
    share = grad_a.shape[0]
    count = 4 * share
    if out_ref.shape[0] > 2 * count:
        out_ref[...] = jnp.zeros(out_ref.shape, BF)
    for d, grad_ref in enumerate((grad_a, grad_b, grad_c, grad_d)):

        @pl.loop(0, share)
        def _(i, d=d, grad_ref=grad_ref):
            n = jnp.bitwise_xor(place_ref[3], d) * share + i
            inside = inside_box(corner_ref, n, place_ref)
            gradient = grad_ref[i].astype(F32)
            cut = inside * gradient
            out_ref[take_ref[n]] = ((1.0 - ratio_ref[n]) * (gradient - cut)).astype(BF)
            out_ref[take_ref[count + n]] = cut.astype(BF)


def join_kernel(
    place_ref,
    index_ref,
    corner_ref,
    ratio_ref,
    grad_a,
    grad_b,
    grad_c,
    grad_d,
    back_ref,
    out_ref,
    total,
):
    count, width = out_ref.shape[2:]
    share = grad_a.shape[0]

    def tile_rows(n):
        return pl.ds(pl.multiple_of(n * PAD, 8), PAD)

    for d, grad_ref in enumerate((grad_a, grad_b, grad_c, grad_d)):

        @pl.loop(0, share)
        def _(i, d=d, grad_ref=grad_ref):
            n = jnp.bitwise_xor(place_ref[3], d) * share + i
            outside = 1.0 - inside_box(corner_ref, n, place_ref)
            kept = ratio_ref[n] * outside * grad_ref[i].astype(F32)
            kept = kept.reshape(PAD, width)
            for lane in range(total.shape[0]):
                total[lane, tile_rows(n), :] = kept[:, lane * 128 : (lane + 1) * 128]

    @pl.loop(0, back_ref.shape[0])
    def _(s):
        piece = back_ref[s].astype(F32).reshape(PAD, width)
        for lane in range(total.shape[0]):
            total[lane, tile_rows(index_ref[s]), :] += piece[:, lane * 128 : (lane + 1) * 128]

    for row in range(TILE):
        for col in range(TILE):
            out_ref[row, col] = jnp.concatenate(
                [
                    total[lane, pl.ds(row * 8 + col, count, stride=PAD), :]
                    for lane in range(total.shape[0])
                ],
                axis=1,
            )


def lay_kernel(place_ref, act_a, act_b, act_c, act_d, out_ref, flat):
    count, width = out_ref.shape[2:]
    share = act_a.shape[0]
    for d, act_ref in enumerate((act_a, act_b, act_c, act_d)):

        @pl.loop(0, share)
        def _(i, d=d, act_ref=act_ref):
            n = jnp.bitwise_xor(place_ref[3], d) * share + i
            tile = act_ref[i].astype(F32).reshape(PAD, width)
            for lane in range(flat.shape[0]):
                flat[lane, pl.ds(pl.multiple_of(n * PAD, 8), PAD), :] = tile[
                    :, lane * 128 : (lane + 1) * 128
                ]

    for row in range(TILE):
        for col in range(TILE):
            out_ref[row, col] = jnp.concatenate(
                [
                    flat[lane, pl.ds(row * 8 + col, count, stride=PAD), :]
                    for lane in range(flat.shape[0])
                ],
                axis=1,
            ).astype(BF)


def unpack_kernel(
    ranks,
    counts,
    place_ref,
    *refs,
):
    pieces, refs = refs[:8], refs[8:]
    outs, (vectors, *buffers, send_sem) = refs[:12], refs[12:]
    (
        gain_out,
        shift_out,
        entry_out,
        entry_b_out,
        conv_out,
        conv_b_out,
        exit_out,
        exit_b_out,
        expand_out,
        expand_b_out,
        shrink_out,
        shrink_b_out,
    ) = buffers
    width = exit_out.shape[1]
    units = expand_out.shape[2]
    middle = width // 2

    def squares(out_ref, block, count):
        return [(out_ref, block, 0, part * width, width) for part in range(count)]

    def tall(out_ref, block, count):
        return [(out_ref, block, part * width, 0, width) for part in range(count)]

    plans = (
        squares(expand_out, 1, units // width) + tall(shrink_out, 1, units // width),
        [
            (entry_out, 0, 0, 0, width),
            (entry_out, 0, 0, width, middle),
            (vectors, None, 0, 0, middle),
            (entry_out, 0, middle, width, middle),
            (entry_out, 0, 0, 2 * width, width),
        ],
        squares(entry_out, 1, 3)
        + tall(exit_out, 1, 1)
        + squares(expand_out, 0, units // width)
        + tall(shrink_out, 0, units // width)
        + tall(exit_out, 0, 1),
    )
    inner_ranks = ranks // 4
    moves = []
    base = 0
    for plan, count in zip(plans, counts):
        at = 0
        for out_ref, block, first_row, lane, length in plan:
            done = 0
            while done < length:
                step = min(length - done, count - at % count)
                moves.append((out_ref, block, first_row + done, lane, base, count, at, step))
                at += step
                done += step
        base += count
    big = (expand_out, shrink_out, entry_out, exit_out)
    leaving = []

    def leave(buffer, out):
        copy = pltpu.make_async_copy(buffer, out, send_sem.at[len(leaving)])
        leaving.append(copy)
        return copy

    def place_parts(target, wanted, col, own):
        for out_ref, block, first_row, lane, base, count, at, step in moves:
            if out_ref is not target or block != wanted:
                continue
            shard, start = at // count, base + at % count
            half, shard = shard // ranks, shard % ranks
            first, inner = shard // inner_ranks, shard % inner_ranks
            piece = pieces[4 * (col ^ half) + (own ^ first)]
            inner = jnp.bitwise_xor(place_ref[6], inner)
            values = piece[inner, start : start + step, :].astype(F32)
            place = slice(first_row, first_row + step)
            if block is None:
                out_ref[place, :] = values
            else:
                out_ref[block, place, lane : lane + width] = values

    first_sends = {}
    for block in (1, 0):
        for target in big:
            i = [j for j, ref in enumerate(buffers) if ref is target][0]
            first_sends[block, i] = leave(target.at[block], outs[i].at[block])
    for col in range(2):
        for own in range(4):

            @pl.when((place_ref[2] == col) & (place_ref[5] == own))
            def _(col=col, own=own):
                place_parts(vectors, None, col, own)
                for (block, i), copy in first_sends.items():
                    place_parts(buffers[i], block, col, own)
                    copy.start()

    def line(n):
        return vectors[n : n + 1, :]

    gain_out[0] = jnp.concatenate([line(33), line(18)], axis=0)
    gain_out[1] = jnp.concatenate([line(11), line(5)], axis=0)
    shift_out[0] = jnp.concatenate([line(34), line(19)], axis=0)
    shift_out[1] = jnp.concatenate([line(12), line(6)], axis=0)
    for part in range(2):
        lanes = slice(part * width, (part + 1) * width)
        entry_b_out[:, lanes] = jnp.concatenate([line(31 + part), line(9 + part)], axis=0)
    for i in range(3):
        for j in range(3):
            conv_out[i, j] = jnp.concatenate(
                [line(35 + 3 * i + j), line(22 + 3 * i + j)], axis=0
            )
    conv_b_out[...] = jnp.concatenate([line(21), line(8)], axis=0)
    exit_b_out[...] = jnp.concatenate([line(20), line(7)], axis=0)
    for part in range(units // width):
        lanes = slice(part * width, (part + 1) * width)
        expand_b_out[:, lanes] = jnp.concatenate([line(14 + part), line(part)], axis=0)
    shrink_b_out[...] = jnp.concatenate([line(13), line(4)], axis=0)
    for buffer, out in zip(buffers, outs):
        if not any(buffer is ref for ref in big):
            leave(buffer, out).start()
    for copy in leaving:
        copy.wait()


SMEM = pl.BlockSpec(memory_space=pltpu.SMEM)
VMEM = pl.BlockSpec(memory_space=pltpu.VMEM)


ANYWHERE = pl.BlockSpec(memory_space=pl.ANY)
FAR = pl.BlockSpec(memory_space=pltpu.HBM)


def far(values):
    return pltpu.with_memory_space_constraint(values, pltpu.HBM)


class Here:
    def __init__(self, ranks):
        self.ranks = ranks

    def seat(self):
        group, row, col = (lax.axis_index(axis) for axis in ("dp", "row", "col"))
        bits = self.ranks.bit_length() - 1
        rank = 2 * group + row
        order = jnp.int32(0)
        for bit in range(0, bits, 2):
            count = min(2, bits - bit)
            part = jnp.bitwise_and(lax.shift_right_logical(rank, bit), (1 << count) - 1)
            order = order * (1 << count) + part
        rest = self.ranks // 4
        first = jnp.bitwise_and(rank, 3)
        return (group, row, col, 2 * row + col, order, first, order - first * rest)


class Moves:
    def __init__(self, fetched, sent):
        self.fetched, self.sent = dict(fetched), dict(sent)
        self.waited, self.started = set(), set()

    def copies(self, ref, part):
        copies = self.fetched.get(id(ref), [])
        return [
            ((id(ref), i), copy)
            for i, copy in enumerate(copies)
            if part is None or len(copies) == 1 or i == part
        ]

    def fetch(self, *refs, part=None):
        for ref in refs:
            for key, copy in self.copies(ref, part):
                if key not in self.started:
                    copy.start()
                    self.started.add(key)

    def need(self, *refs, part=None):
        self.fetch(*refs, part=part)
        for ref in refs:
            for key, copy in self.copies(ref, part):
                if key not in self.waited:
                    copy.wait()
                    self.waited.add(key)

    def send(self, *refs):
        for ref in refs:
            if id(ref) in self.sent:
                self.sent[id(ref)].start()
                self.started.add(id(ref))

    def finish(self):
        for key, copies in self.fetched.items():
            for i, copy in enumerate(copies):
                if (key, i) not in self.started:
                    copy.start()
                if (key, i) not in self.waited:
                    copy.wait()
        for key, copy in self.sent.items():
            if key not in self.started:
                copy.start()
        for copy in self.sent.values():
            copy.wait()


def halves(ref):
    if ref.shape[-2] != WIN:
        return [pl.ds(0, ref.shape[0])]
    count = ref.shape[0] // 2
    return [pl.ds(0, count), pl.ds(count, count)]


def run(
    kernel,
    scalars,
    arrays,
    outs,
    scratch=(),
    flops=0,
    name=None,
    after=(),
    scalar_outs=(),
    lazy=None,
    vmem=16,
    near=((), ()),
):
    outs = list(outs)
    here = None
    if scalars and isinstance(scalars[0], Here):
        here, scalars = scalars[0], scalars[1:]
    first_in, first_out = (len(arrays), len(outs)) if lazy is None else lazy
    eager, late = list(arrays[:first_in]), list(arrays[first_in:])
    n_in = len(scalars) + len(eager)
    scratch_shapes = [
        kind if dtype is None else pltpu.VMEM(kind, dtype) for kind, dtype in scratch
    ]
    n_own = len(scratch_shapes)
    n_late, n_sent = len(late), len(outs) - first_out
    if lazy is not None:
        scratch_shapes += [pltpu.VMEM(a.shape, a.dtype) for a in late]
        scratch_shapes += [pltpu.VMEM(*out) for out in outs[first_out:]]
        scratch_shapes += [pltpu.SemaphoreType.DMA((n_late, 2)), pltpu.SemaphoreType.DMA((max(n_sent, 1),))]

    def body(*refs):
        given, refs = refs[:n_in], refs[n_in:]
        sources, refs = refs[:n_late], refs[n_late + len(after) :]
        results, refs = refs[: len(scalar_outs) + first_out], refs[len(scalar_outs) + first_out :]
        targets, refs = refs[:n_sent], refs[n_sent:]
        own, refs = refs[:n_own], refs[n_own:]
        if here is not None:
            given = (here.seat(),) + tuple(given)
        if lazy is None:
            kernel(*given, *results, *own)
            return
        buffers, leaving = refs[:n_late], refs[n_late : n_late + n_sent]
        fetch_sem, send_sem = refs[n_late + n_sent :]
        moves = Moves(
            [
                (
                    id(buffer),
                    [
                        pltpu.make_async_copy(source.at[part], buffer.at[part], fetch_sem.at[i, j])
                        for j, part in enumerate(halves(buffer))
                    ],
                )
                for i, (source, buffer) in enumerate(zip(sources, buffers))
            ],
            [
                (id(buffer), pltpu.make_async_copy(buffer, target, send_sem.at[i]))
                for i, (buffer, target) in enumerate(zip(leaving, targets))
            ],
        )
        kernel(moves, *given, *buffers, *results, *leaving, *own)
        moves.finish()

    out_shape = [jax.ShapeDtypeStruct(shape, dtype) for shape, dtype in scalar_outs] + [
        pltpu.HBM(shape, dtype)
        if lazy is not None and i not in near[1]
        else jax.ShapeDtypeStruct(shape, dtype)
        for i, (shape, dtype) in enumerate(outs)
    ]
    late = [
        a if i in near[0] else far(a)
        for i, a in enumerate(late, first_in)
    ]
    moved = sum(a.size * a.dtype.itemsize for a in arrays)
    return pl.pallas_call(
        body,
        out_shape=out_shape,
        in_specs=[SMEM] * len(scalars)
        + [VMEM] * len(eager)
        + [ANYWHERE if i in near[0] else FAR for i in range(first_in, len(arrays))]
        + [ANYWHERE] * len(after),
        out_specs=[SMEM] * len(scalar_outs)
        + [VMEM] * first_out
        + [ANYWHERE if i in near[1] else FAR for i in range(first_out, len(outs))],
        scratch_shapes=scratch_shapes,
        compiler_params=pltpu.CompilerParams(vmem_limit_bytes=vmem * 1024 * 1024),
        cost_estimate=pl.CostEstimate(flops=flops, bytes_accessed=moved, transcendentals=0),
        name=name,
    )(*scalars, *eager, *late, *after)


def gate(values, after):
    values, after = list(values), list(after)
    return list(lax.optimization_barrier(tuple(values + after)))[: len(values)]


def swap(values, axis):
    return lax.ppermute(values, axis, [(0, 1), (1, 0)])


def added(values, others):
    return (values.astype(F32) + others.astype(F32)).astype(BF)


def shards(values, ranks):
    return values.reshape(ranks, values.shape[0] // ranks, values.shape[1])


def spread_sum(pieces):
    mine = jnp.sum(pieces.astype(F32), axis=0).astype(BF)
    return jnp.broadcast_to(mine[None], pieces.shape)


def across(values, axes, size, mask):
    return lax.ppermute(values, axes, [(i, i ^ mask) for i in range(size)])


def deal(parts):
    return [parts[0]] + [across(parts[d], ("row", "col"), 4, d) for d in (1, 2, 3)]


RANKS = ("dp", "row")


def stages(ranks):
    bits = ranks.bit_length() - 1
    return [(bit, min(2, bits - bit)) for bit in range(0, bits, 2)]


def scatter_send(values, ranks, stage):
    bit, count = stage
    size = 1 << count
    me = (lax.axis_index(RANKS) >> bit) & (size - 1)
    cut = values.reshape(size, values.shape[0] // size, values.shape[1])
    return [lax.dynamic_index_in_dim(cut, me ^ d, 0, keepdims=False) for d in range(size)]


def scatter_move(parts, ranks, stage):
    return [parts[0]] + [
        across(parts[d], RANKS, ranks, d << stage[0]) for d in range(1, len(parts))
    ]


def scatter_sum(parts):
    return sum(part.astype(F32) for part in parts).astype(BF)


def gather(values, ranks, stage):
    return jnp.stack(
        [values]
        + [across(values, RANKS, ranks, d << stage[0]) for d in range(1, 1 << stage[1])]
    )


def rank_order(rank, ranks):
    order = 0
    for bit, count in stages(ranks):
        order = order * (1 << count) + ((rank >> bit) & ((1 << count) - 1))
    return order


def local(
    groups,
    images,
    cotangent,
    mix_partner,
    cut_partner,
    ratios,
    corners,
    drop_masks,
    norm_gains,
    norm_shifts,
    entry_weight,
    entry_bias,
    position_kernel,
    position_bias,
    exit_weight,
    exit_bias,
    expand_weight,
    expand_bias,
    shrink_weight,
    shrink_bias,
):
    images_here = images.shape[0]
    width = images.shape[3]
    units = expand_weight.shape[2]
    share = images_here // 4
    rows = 4 * share * PAD
    ranks = 2 * groups
    capacity = (2 * images_here + groups - 1) // groups
    slots = groups * capacity
    place = Here(ranks)
    spots = [0] * ranks
    for rank in range(ranks):
        spots[rank_order(rank, ranks)] = rank
    quad = ((share, TILE, 8, width), BF)
    corners = corners.T
    masks = drop_masks.T
    flat = ((width // 128, images_here * PAD, 128), F32)
    index, take, outgoing, own = run(
        pick_kernel,
        [mix_partner, cut_partner],
        [images.transpose(1, 2, 0, 3)],
        [((slots, TILE, 8, width), BF), ((images_here, TILE, 8, width), BF)],
        [flat, (pltpu.SMEM((groups,), jnp.int32), None)],
        name="pick",
        vmem=60,
        lazy=(0, 2),
        near=((), (0, 1)),
        scalar_outs=(((slots + 8,), jnp.int32), ((2 * images_here,), jnp.int32)),
    )
    arrived = lax.all_to_all(outgoing, "dp", split_axis=0, concat_axis=0, tiled=True)
    cot = deal(
        run(deal_kernel, [place], [cotangent.transpose(1, 2, 0, 3)], [quad] * 4, [flat], name="deal")
    )
    mixed = deal(
        run(
            mix_kernel,
            [place, take, corners, ratios],
            [arrived, own],
            [quad] * 4,
            name="mix",
            after=cot,
        )
    )
    conv_k = position_kernel.transpose(1, 2, 0, 3)
    tall = (rows, width)
    (
        vec1,
        keep1,
        away1,
        act_a,
        act_b,
        act_c,
        act_d,
        active0,
        slope0,
        win0,
        chance0,
        stripe0,
        mid0,
        win1,
        chance1,
        stripe1,
        hidden1,
        grad1,
    ) = run(
        functools.partial(first_kernel, spots),
        [place, masks],
        [
            *mixed,
            norm_gains,
            norm_shifts,
            entry_bias,
            conv_k,
            position_bias,
            exit_bias,
            expand_bias,
            shrink_bias,
            *cot,
            entry_weight,
            exit_weight,
            expand_weight,
            shrink_weight,
        ],
        [
            ((7, 8, width), F32),
            ((units, width), BF),
            ((units, width), BF),
            *([quad] * 4),
            ((rows, units), BF),
            ((rows, units), BF),
            ((4 * share, WIN, 3 * HALF), BF),
            ((4 * share, WIN, LANES), BF),
            (tall, BF),
            (tall, F32),
            ((4 * share, WIN, 3 * HALF), BF),
            ((4 * share, WIN, LANES), BF),
            (tall, BF),
            (tall, F32),
            (tall, F32),
        ],
        [
            (tall, F32),
            ((rows, 3 * width), F32),
            (tall, F32),
            ((rows, units), BF),
            ((rows, units), BF),
            (tall, BF),
            (tall, BF),
        ],
        flops=10 * rows * width * width * 120,
        name="first",
        vmem=46,
        near=((), (1, 2)),
        lazy=(17, 3),
    )
    sent1 = shards(added(keep1, swap(away1, "col")), ranks)
    pieces1 = lax.all_to_all(sent1, RANKS, split_axis=0, concat_axis=0, tiled=True)
    vec2, conv2, keep2, away2, grad0, delta0 = run(
        second_kernel,
        [place, masks],
        [
            norm_gains,
            norm_shifts,
            conv_k,
            grad1,
            exit_weight,
            win1,
            chance1,
            hidden1,
            entry_weight,
            stripe1,
            mid0,
            shrink_weight,
            slope0,
            expand_weight,
            active0,
            stripe0,
        ],
        [
            ((15, 8, width), F32),
            ((9, 8, width), F32),
            ((13 * width // 2, width), BF),
            ((13 * width // 2, width), BF),
            (tall, F32),
            (tall, F32),
        ],
        [
            (tall, F32),
            (tall, BF),
            ((rows, 3 * width), F32),
            ((rows, 3 * width), BF),
            (tall, BF),
            (tall, BF),
            ((rows, units), BF),
        ],
        flops=6 * rows * width * width * 120,
        name="second",
        vmem=42,
        near=((), (2, 3)),
        after=[sent1],
        lazy=(3, 4),
    )
    act = deal([act_a, act_b, act_c, act_d])
    keep2, away2, *act = gate([keep2, away2, *act], [pieces1])
    steps = stages(ranks)

    def first_parts(keep, away):
        other = swap(away, "col")
        count = keep.shape[0] // 4
        return [
            added(keep[d * count : (d + 1) * count], other[d * count : (d + 1) * count])
            for d in range(4)
        ]

    parts2 = first_parts(keep2, away2)
    moved2 = scatter_move(parts2, ranks, steps[0])
    *out_tiles, keep3, away3 = run(
        third_kernel,
        [place],
        [
            norm_gains,
            norm_shifts,
            conv_k,
            vec1,
            vec2,
            conv2,
            *mixed,
            delta0,
            win0,
            chance0,
            entry_weight,
            grad0,
        ],
        [quad] * 4 + [((2 * width, width), BF), ((2 * width, width), BF)],
        [
            (tall, F32),
            ((rows, 3 * width), F32),
            ((rows, 3 * width), BF),
            (tall, BF),
            ((4, 8, width), F32),
            ((9, 8, width), F32),
            ((width, width), F32),
        ],
        flops=3 * rows * width * width * 120,
        name="third",
        vmem=36,
        near=((), range(6)),
        after=parts2,
        lazy=(10, 6),
    )
    *moved2, keep3, away3 = gate([*moved2, keep3, away3], out_tiles)
    gradient = deal(out_tiles)
    (parted,) = run(
        split_kernel,
        [place, take, corners, ratios],
        gradient,
        [((slots, TILE, 8, width), BF)],
        name="split",
    )
    mine1 = jnp.sum(pieces1.astype(F32), axis=0).astype(BF)
    mine2 = scatter_sum(moved2)
    moved3 = scatter_move(first_parts(keep3, away3), ranks, steps[0])
    mine3 = scatter_sum(gate(moved3, [mine1]))
    cut = mine2.shape[0] * 4 // ranks
    lot = mine3.shape[0] * 4 // ranks
    joint = jnp.concatenate(
        [
            mine3.reshape(ranks // 4, lot, width),
            mine2.reshape(ranks // 4, cut, width),
        ],
        axis=1,
    ).reshape(-1, width)
    for step in steps[1:]:
        joint = scatter_sum(scatter_move(scatter_send(joint, ranks, step), ranks, step))
    joint = jnp.concatenate([mine1, joint], axis=0)
    counts = (mine1.shape[0], lot, cut)
    for step in reversed(steps[1:]):
        joint = gather(joint, ranks, step).reshape(-1, width)
    joint = shards(joint, ranks // 4)
    (parted,) = gate([parted], [joint])
    (activations,) = run(
        lay_kernel, [place], [far(a) for a in act], [((TILE, TILE, images_here, width), BF)], [flat], name="lay"
    )
    back = lax.all_to_all(parted, "dp", split_axis=0, concat_axis=0, tiled=True)
    (back,) = gate([back], [activations])
    (input_gradient,) = run(
        join_kernel,
        [place, index, corners, ratios],
        [*gradient, back],
        [((TILE, TILE, images_here, width), F32)],
        [((width // 128, (images_here + 1) * PAD, 128), F32)],
        name="join",
    )
    full = [joint] + [across(joint, RANKS, ranks, d) for d in (1, 2, 3)]
    full[2:] = gate(full[2:], [input_gradient])
    full += [swap(piece, "col") for piece in full]
    shapes = [
        (2, 2, width),
        (2, 2, width),
        (2, width, 3 * width),
        (2, 2 * width),
        (3, 3, 2, width),
        (2, width),
        (2, width, width),
        (2, width),
        (2, width, units),
        (2, units),
        (2, units, width),
        (2, width),
    ]
    gains, shifts, entry, entry_b, conv, conv_b, exit_, exit_b, expand, expand_b, shrink, shrink_b = (
        pl.pallas_call(
            lambda *refs: unpack_kernel(ranks, counts, place.seat(), *refs),
            out_shape=[jax.ShapeDtypeStruct(shape, F32) for shape in shapes],
            in_specs=[VMEM] * 8,
            out_specs=[ANYWHERE] * 12,
            scratch_shapes=[
                pltpu.VMEM((width // 2, width), F32),
            ]
            + [pltpu.VMEM(shape, F32) for shape in shapes]
            + [pltpu.SemaphoreType.DMA((16,))],
            compiler_params=pltpu.CompilerParams(vmem_limit_bytes=24 * 1024 * 1024),
            name="unpack",
        )(*full)
    )
    return (
        activations.transpose(2, 0, 1, 3),
        input_gradient.transpose(2, 0, 1, 3),
        gains,
        shifts,
        entry,
        entry_b,
        conv.transpose(2, 0, 1, 3),
        conv_b,
        exit_,
        exit_b,
        expand,
        expand_b,
        shrink,
        shrink_b,
    )


def solution(mesh):
    tiles = P("dp", "row", "col", None)
    return jax.shard_map(
        functools.partial(local, mesh.shape["dp"]),
        mesh=mesh,
        in_specs=(tiles, tiles, P(), P(), P("dp"), P("dp", None), P("dp", None)) + (P(),) * 12,
        out_specs=(tiles, tiles) + (P(),) * 12,
        check_vma=False,
    )
```

```python
import functools

import jax
import jax.numpy as jnp
from jax import lax
from jax.experimental import pallas as pl
from jax.experimental.pallas import tpu as pltpu
from jax.sharding import PartitionSpec as P

TILE = 7
PAD = 56
HEAD_DIM = 32
SIDE_HEADS = 4
HALF = 128
WIN = 2 * PAD
CHUNK = 8 * PAD
LANES = SIDE_HEADS * 128
SCALE = HEAD_DIM ** (-0.5)
LOG2E = 1.4426950408889634
EPS = 1e-05
BF = jnp.bfloat16
F32 = jnp.float32


def dot_nn(a, b):
    return lax.dot_general(a, b, (((1,), (0,)), ((), ())), preferred_element_type=F32)


def dot_nt(a, b):
    return lax.dot_general(a, b, (((1,), (1,)), ((), ())), preferred_element_type=F32)


def dot_tn(a, b):
    return lax.dot_general(a, b, (((0,), (0,)), ((), ())), preferred_element_type=F32)


def norm_parts(values):
    centered = values - jnp.mean(values, axis=-1, keepdims=True)
    inverse = lax.rsqrt(jnp.mean(centered * centered, axis=-1, keepdims=True) + EPS)
    return centered * inverse, inverse


def norm_back(delta, hat, inverse, gain):
    scaled = delta * gain
    first = jnp.mean(scaled, axis=-1, keepdims=True)
    second = jnp.mean(scaled * hat, axis=-1, keepdims=True)
    return inverse * (scaled - first - hat * second)


def gelu_parts(values):
    chance = 0.5 + 0.5 * lax.erf(values * (0.5**0.5))
    density = jnp.exp2(values * values * (-0.5 * LOG2E)) * 0.3989422804014327
    return chance, density


def row_sums(values):
    count, width = values.shape
    return jnp.sum(values.reshape(count // 8, 8, width), axis=0)


def scale_rows(place_ref, mask_ref, column):
    scales = [
        mask_ref[column, 4 * place_ref[3] + i].astype(F32) * 1.25 for i in range(4)
    ]
    columns = [jnp.full((PAD, 1), scale, F32) for scale in scales]
    return jnp.concatenate(columns * (CHUNK // (4 * PAD)), axis=0)


def add_row(acc_ref, row, values):
    acc_ref[row] += values


def spread_heads(values):
    lane = lax.broadcasted_iota(jnp.int32, values.shape, 1) // HEAD_DIM
    empty = jnp.zeros((128 - WIN, HALF), F32)
    blocks = []
    for head in range(SIDE_HEADS):
        blocks.append(jnp.where(lane == head, values, 0.0))
        blocks.append(empty)
    return jnp.concatenate(blocks, axis=0).astype(BF)


def over_keys(weights, values):
    weights = fill_rows(weights)
    stacked = jnp.concatenate(
        [weights[:, head * 128 : (head + 1) * 128] for head in range(SIDE_HEADS)], axis=0
    )
    return dot_tn(stacked, spread_heads(values))[:WIN]


def fill_rows(values):
    empty = jnp.zeros((128 - WIN, values.shape[1]), values.dtype)
    return jnp.concatenate([values, empty], axis=0)


def valid_column(shape):
    return lax.broadcasted_iota(jnp.int32, shape, 1) != 7


def valid_rows(shape):
    return lax.broadcasted_iota(jnp.int32, shape, 0) % 8 != 7


def column_shifts(values, across):
    cube = values.reshape(2 * TILE, 8, HALF)
    if not across:
        return (pltpu.roll(cube, 1, 1), cube, pltpu.roll(cube, 7, 1))
    left, right = cube[:TILE], cube[TILE:]
    column = lax.broadcasted_iota(jnp.int32, left.shape, 1)
    before = jnp.concatenate(
        [
            pltpu.roll(left, 1, 1),
            jnp.where(column == 0, pltpu.roll(left, 2, 1), pltpu.roll(right, 1, 1)),
        ],
        axis=0,
    )
    after = jnp.concatenate(
        [
            jnp.where(column == 6, pltpu.roll(right, 6, 1), pltpu.roll(left, 7, 1)),
            pltpu.roll(right, 7, 1),
        ],
        axis=0,
    )
    return (before, cube, after)


def row_shift(cube, step, across):
    if step == 0:
        return cube
    empty = jnp.zeros((1, 8, HALF), F32)

    def move(part):
        if step < 0:
            return jnp.concatenate([empty, part[:-1]], axis=0)
        return jnp.concatenate([part[1:], empty], axis=0)

    if across:
        return jnp.concatenate([move(cube[:TILE]), move(cube[TILE:])], axis=0)
    return move(cube)


def window_conv(shifts, kernel_at, across):
    total = None
    for i in range(3):
        part = None
        for j in range(3):
            term = kernel_at(i, j) * shifts[j]
            part = term if part is None else part + term
        part = row_shift(part, i - 1, across)
        total = part if total is None else total + part
    return total.reshape(WIN, HALF)


def window_rows(across, window):
    side, image = window // 4, window % 4
    if across:
        first, second = 2 * side, 2 * side + 1
    else:
        first, second = side, 2 + side
    return (
        pl.multiple_of((first * 4 + image) * PAD, 8),
        pl.multiple_of((second * 4 + image) * PAD, 8),
    )


def take_window(ref, at, lane):
    return jnp.concatenate(
        [ref[pl.ds(at[0], PAD), lane : lane + HALF], ref[pl.ds(at[1], PAD), lane : lane + HALF]],
        axis=0,
    )


def put_window(ref, at, lane, values):
    ref[pl.ds(at[0], PAD), lane : lane + HALF] = values[:PAD]
    ref[pl.ds(at[1], PAD), lane : lane + HALF] = values[PAD:]


def round_bf(values):
    return values.astype(BF).astype(F32)


def attention_forward(
    block, hidden_ref, gains, shifts, entry_w, entry_b, conv_k, conv_b, wide, stripe, win_out, chance_out
):
    width = hidden_ref.shape[1]

    @pl.loop(0, 2)
    def _(t):
        rows = chunk(t)
        hat, _ = norm_parts(hidden_ref[rows, :])
        normed = (hat * gains[block, 0:1, :] + shifts[block, 0:1, :]).astype(BF)
        for part in range(3):
            out = dot_nn(normed, entry_w[block, :, part * width : (part + 1) * width])
            if part != 1:
                at = 0 if part == 0 else width
                out = out + entry_b[block : block + 1, at : at + width]
            wide[rows, part * width : (part + 1) * width] = round_bf(out)

    for direction in range(2):
        across = direction == 0
        lane = direction * HALF

        @pl.loop(0, 8, unroll=8)
        def _(window, across=across, lane=lane, direction=direction):
            at = window_rows(across, window)
            queries = take_window(wide, at, lane)
            keys = take_window(wide, at, width + lane)
            values = take_window(wide, at, 2 * width + lane)
            keys_bf = keys.astype(BF)
            win_out[direction * 8 + window, :, 0:HALF] = queries.astype(BF)
            win_out[direction * 8 + window, :, HALF : 2 * HALF] = keys_bf
            win_out[direction * 8 + window, :, 2 * HALF : 3 * HALF] = values.astype(BF)
            scores = dot_nt(keys_bf, spread_heads(queries)).reshape(2 * TILE, 8, LANES)
            scores = jnp.where(valid_column((1, 8, LANES)), scores, -1e30)
            top = jnp.max(jnp.max(scores, axis=0), axis=0, keepdims=True)
            lifted = jnp.exp2((scores - top) * (SCALE * LOG2E))
            totals = jnp.sum(jnp.sum(lifted, axis=0), axis=0, keepdims=True)
            chances = (lifted * (1.0 / totals)).reshape(WIN, LANES).astype(BF)
            chance_out[direction * 8 + window] = chances
            attended = over_keys(chances, values)
            clean = jnp.where(valid_rows(values.shape), values, 0.0)
            position = window_conv(
                column_shifts(clean, across),
                lambda i, j: conv_k[i, j, block : block + 1, lane : lane + HALF],
                across,
            )
            put_window(
                stripe, at, lane, attended + position + conv_b[block : block + 1, lane : lane + HALF]
            )


def attention_backward(
    ready,
    block,
    win_in,
    chance_in,
    conv_k,
    stripe_delta,
    wide,
    conv_acc,
):
    width = stripe_delta.shape[1]
    for direction in range(2):
        ready(direction)
        across = direction == 0
        lane = direction * HALF

        @pl.loop(0, 8, unroll=4)
        def _(window, across=across, lane=lane, direction=direction):
            at = window_rows(across, window)
            out_delta = take_window(stripe_delta, at, lane)
            queries = win_in[direction * 8 + window, :, 0:HALF].astype(F32)
            keys = win_in[direction * 8 + window, :, HALF : 2 * HALF].astype(F32)
            values_bf = win_in[direction * 8 + window, :, 2 * HALF : 3 * HALF]
            values = values_bf.astype(F32)
            chances = chance_in[direction * 8 + window]
            delta_spread = spread_heads(out_delta)
            chance_delta = dot_nt(values_bf, delta_spread)
            cubes = (2 * TILE, 8, LANES)
            wide_chances = chances.astype(F32).reshape(cubes)
            weighted = wide_chances * chance_delta.reshape(cubes)
            common = jnp.sum(jnp.sum(weighted, axis=0), axis=0, keepdims=True)
            score_delta = (weighted - wide_chances * common).reshape(WIN, LANES).astype(BF)
            values_delta = dot_nn(chances, delta_spread)
            keys_delta = dot_nn(score_delta, spread_heads(queries)) * SCALE
            query_delta = over_keys(score_delta, keys) * SCALE
            keep = valid_rows(values.shape)
            clean = jnp.where(keep, values, 0.0)
            shifts = column_shifts(clean, across)
            cube = out_delta.reshape(2 * TILE, 8, HALF)
            for i in range(3):
                moved = row_shift(cube, 1 - i, across)
                for j in range(3):
                    conv_acc[3 * i + j, :, lane : lane + HALF] += jnp.sum(moved * shifts[j], axis=0)
            back = window_conv(
                column_shifts(out_delta, across),
                lambda i, j: conv_k[2 - i, 2 - j, block : block + 1, lane : lane + HALF],
                across,
            )
            values_delta = jnp.where(keep, values_delta + back, 0.0)
            put_window(wide, at, lane, query_delta)
            put_window(wide, at, width + lane, keys_delta)
            put_window(wide, at, 2 * width + lane, values_delta)


def chunk(t):
    return pl.ds(pl.multiple_of(t * CHUNK, CHUNK), CHUNK)


class Bundle:
    def __init__(self, place_ref, keep, away, chunks=1, spot=lambda chunk: chunk):
        self.place_ref, self.keep, self.away = place_ref, keep, away
        self.step, self.spot = keep.shape[0] // chunks, spot

    def put(self, at, values):
        values = values.astype(BF)
        half, step = self.keep.shape[0], self.step
        last = at + values.shape[0]
        first = at
        while first < last:
            stop = min(last, (first // step + 1) * step)
            number = first // half
            start = self.spot(first % half // step) * step
            inner, count = first % step, stop - first
            if not isinstance(start, int):
                start = pl.multiple_of(start, step)
            rows = pl.ds(start + inner, count)
            piece = values[first - at : stop - at]

            @pl.when(self.place_ref[2] == number)
            def _(piece=piece, rows=rows):
                self.keep[rows, :] = piece

            @pl.when(self.place_ref[2] != number)
            def _(piece=piece, rows=rows):
                self.away[rows, :] = piece

            first = stop


def put_squares(bundle, at, values, side):
    for part in range(values.shape[1] // side):
        bundle.put(at + part * side, values[:, part * side : (part + 1) * side])


def load_tiles(place_ref, tiles, hidden):
    for d, tile in enumerate(tiles):
        at = jnp.bitwise_xor(place_ref[3], d) * (4 * PAD)
        rows = pl.ds(pl.multiple_of(at, 4 * PAD), 4 * PAD)
        hidden[rows, :] = tile[...].astype(F32).reshape(4 * PAD, hidden.shape[1])


def store_tile(place_ref, tiles, t, values):
    count = CHUNK // (4 * PAD)
    values = values.reshape((count,) + tiles[0].shape).astype(BF)
    for part in range(count):
        for d, tile in enumerate(tiles):

            @pl.when(jnp.bitwise_xor(place_ref[3], d) == count * t + part)
            def _(tile=tile, part=part):
                tile[...] = values[part]


def first_kernel(
    spots,
    moves,
    place_ref,
    mask_ref,
    mixed_a,
    mixed_b,
    mixed_c,
    mixed_d,
    gains,
    shifts,
    entry_b,
    conv_k,
    conv_b,
    exit_b,
    expand_b,
    shrink_b,
    cot_a,
    cot_b,
    cot_c,
    cot_d,
    entry_w,
    exit_w,
    expand_w,
    shrink_w,
    vec_out,
    keep_out,
    away_out,
    act_a,
    act_b,
    act_c,
    act_d,
    active0_out,
    slope0_out,
    win0_out,
    chance0_out,
    stripe0_out,
    mid0_out,
    win1_out,
    chance1_out,
    stripe1_out,
    hidden1_out,
    grad_out,
    hidden,
    wide,
    stripe,
    active1,
    pre1,
    feed1,
    inner1,
):
    width = hidden.shape[1]
    hidden_units = expand_w.shape[2]
    bundle = Bundle(place_ref, keep_out, away_out, len(spots), lambda chunk: spots[chunk])
    vec_out[...] = jnp.zeros(vec_out.shape, F32)
    moves.fetch(entry_w)
    load_tiles(place_ref, (mixed_a, mixed_b, mixed_c, mixed_d), hidden)
    moves.need(entry_w)
    moves.fetch(exit_w, expand_w, shrink_w, cot_a, cot_b, cot_c, cot_d)

    for block in range(2):
        win_out, chance_out, stripe_out = (
            (win0_out, chance0_out, stripe0_out),
            (win1_out, chance1_out, stripe1_out),
        )[block]
        attention_forward(
            block, hidden, gains, shifts, entry_w, entry_b, conv_k, conv_b, wide, stripe, win_out, chance_out
        )
        moves.send(win_out, chance_out)
        moves.need(exit_w, expand_w, shrink_w)
        if block == 1:
            moves.need(cot_a, cot_b, cot_c, cot_d)
            load_tiles(place_ref, (cot_a, cot_b, cot_c, cot_d), grad_out)

        @pl.loop(0, 2)
        def _(t, block=block, stripe_out=stripe_out):
            rows = chunk(t)
            striped = stripe[rows, :].astype(BF)
            stripe_out[rows, :] = striped
            branch = dot_nn(striped, exit_w[block]) + exit_b[block : block + 1, :]
            midway = hidden[rows, :] + scale_rows(place_ref, mask_ref, 2 * block) * branch
            if block == 0:
                mid0_out[rows, :] = midway
            hat, inverse = norm_parts(midway)
            normed = (hat * gains[block, 1:2, :] + shifts[block, 1:2, :]).astype(BF)
            feed_scale = scale_rows(place_ref, mask_ref, 2 * block + 1)
            feed = shrink_b[block : block + 1, :]
            if block == 1:
                inner1[rows, :] = normed
                gradient = grad_out[rows, :]
                feed_delta = (feed_scale * gradient).astype(BF)
                feed1[rows, :] = feed_delta
                add_row(vec_out, 4, row_sums(feed_delta.astype(F32)))
                inner_delta = jnp.zeros((CHUNK, width), F32)
            for part in range(hidden_units // width):
                at = slice(part * width, (part + 1) * width)
                pre_act = dot_nn(normed, expand_w[block, :, at]) + expand_b[block : block + 1, at]
                chance, density = gelu_parts(pre_act)
                active = (pre_act * chance).astype(BF)
                slope = chance + pre_act * density
                if block == 0:
                    active0_out[rows, at] = active
                    slope0_out[rows, at] = slope.astype(BF)
                else:
                    active1[rows, at] = active
                    pre_delta = (dot_nt(feed_delta, shrink_w[block, at, :]) * slope).astype(BF)
                    pre1[rows, at] = pre_delta
                    add_row(vec_out, part, row_sums(pre_delta.astype(F32)))
                    inner_delta = inner_delta + dot_nt(pre_delta, expand_w[block, :, at])
                feed = feed + dot_nn(active, shrink_w[block, at, :])
            output = midway + feed_scale * feed
            if block == 0:
                hidden[rows, :] = output
                hidden1_out[rows, :] = output
            else:
                store_tile(place_ref, (act_a, act_b, act_c, act_d), t, output)
                add_row(vec_out, 5, row_sums(inner_delta * hat))
                add_row(vec_out, 6, row_sums(inner_delta))
                grad_out[rows, :] = gradient + norm_back(
                    inner_delta, hat, inverse, gains[block, 1:2, :]
                )

        moves.send(stripe_out)
        if block == 0:
            moves.send(mid0_out, active0_out, slope0_out, hidden1_out)
        else:
            moves.send(act_a, act_b, act_c, act_d, grad_out)

    put_squares(bundle, 0, dot_tn(inner1[...], pre1[...]), width)
    for part in range(hidden_units // width):
        bundle.put(
            hidden_units + part * width,
            dot_tn(active1[:, part * width : (part + 1) * width], feed1[...]),
        )


def delta_rows(block, place_ref, mask_ref, exit_w, grad_ref, stripe_delta, branch_delta, vec_out, at):
    @pl.loop(0, 2)
    def _(t):
        rows = chunk(t)
        rounded = (scale_rows(place_ref, mask_ref, 2 * block) * grad_ref[rows, :]).astype(BF)
        branch_delta[rows, :] = rounded
        add_row(vec_out, at, row_sums(rounded.astype(F32)))
        out = round_bf(dot_nt(rounded, exit_w[block]))
        stripe_delta[rows, :] = out
        add_row(vec_out, at + 1, row_sums(out))


def entry_backward(block, hidden_ref, gains, shifts, entry_w, grad_ref, wide, wide_bf, normed_bf, vec_out, at, emit):
    width = hidden_ref.shape[1]

    @pl.loop(0, 2)
    def _(t):
        rows = chunk(t)
        hat, inverse = norm_parts(hidden_ref[rows, :])
        normed_bf[rows, :] = (hat * gains[block, 0:1, :] + shifts[block, 0:1, :]).astype(BF)
        delta = jnp.zeros((CHUNK, width), F32)
        for part in range(3):
            lanes = slice(part * width, (part + 1) * width)
            rounded = wide[rows, lanes].astype(BF)
            wide_bf[rows, lanes] = rounded
            if part != 1:
                add_row(vec_out, at + part // 2, row_sums(rounded.astype(F32)))
            delta = delta + dot_nt(rounded, entry_w[block, :, lanes])
        add_row(vec_out, at + 2, row_sums(delta * hat))
        add_row(vec_out, at + 3, row_sums(delta))
        emit(t, rows, grad_ref[rows, :] + norm_back(delta, hat, inverse, gains[block, 0:1, :]))


def second_kernel(
    moves,
    place_ref,
    mask_ref,
    gains,
    shifts,
    conv_k,
    grad_in,
    exit_w,
    win1,
    chance1,
    hidden1,
    entry_w,
    stripe1,
    mid0,
    shrink_w,
    slope0,
    expand_w,
    active0,
    stripe0,
    vec_out,
    conv_out,
    keep_out,
    away_out,
    grad_out,
    stripe_delta_out,
    stripe_delta,
    branch_delta,
    wide,
    wide_bf,
    normed_bf,
    feed0,
    pre0,
):
    grad = grad_out
    width = grad.shape[1]
    hidden_units = expand_w.shape[2]
    bundle = Bundle(
        place_ref, keep_out, away_out, 4, lambda chunk: jnp.bitwise_xor(place_ref[5], chunk)
    )
    vec_out[...] = jnp.zeros(vec_out.shape, F32)
    conv_out[...] = jnp.zeros(conv_out.shape, F32)
    moves.fetch(grad_in, exit_w)
    moves.fetch(win1, chance1, part=0)
    moves.need(grad_in, exit_w)
    moves.fetch(win1, chance1, part=1)
    delta_rows(1, place_ref, mask_ref, exit_w, grad_in, stripe_delta, branch_delta, vec_out, 0)

    def ready(direction):
        moves.need(win1, chance1, part=direction)
        if direction == 0:
            moves.fetch(hidden1, entry_w, stripe1)
        else:
            moves.fetch(mid0, shrink_w, slope0, expand_w, active0, stripe0)

    attention_backward(ready, 1, win1, chance1, conv_k, stripe_delta, wide, conv_out)

    def emit(t, rows, values):
        grad[rows, :] = values

    moves.need(hidden1, entry_w)
    entry_backward(
        1, hidden1, gains, shifts, entry_w, grad_in, wide, wide_bf, normed_bf, vec_out, 2, emit
    )
    put_squares(bundle, 0, dot_tn(normed_bf[...], wide_bf[...]), width)
    moves.need(stripe1)
    bundle.put(3 * width, dot_tn(stripe1[...], branch_delta[...]))
    moves.need(mid0, shrink_w, slope0, expand_w)

    @pl.loop(0, 2)
    def _(t):
        rows = chunk(t)
        gradient = grad[rows, :]
        hat, inverse = norm_parts(mid0[rows, :])
        normed_bf[rows, :] = (hat * gains[0, 1:2, :] + shifts[0, 1:2, :]).astype(BF)
        feed_delta = (scale_rows(place_ref, mask_ref, 1) * gradient).astype(BF)
        feed0[rows, :] = feed_delta
        add_row(vec_out, 6, row_sums(feed_delta.astype(F32)))
        inner_delta = jnp.zeros((CHUNK, width), F32)
        for part in range(hidden_units // width):
            at = slice(part * width, (part + 1) * width)
            pre_delta = (
                dot_nt(feed_delta, shrink_w[0, at, :]) * slope0[rows, at].astype(F32)
            ).astype(BF)
            pre0[rows, at] = pre_delta
            add_row(vec_out, 7 + part, row_sums(pre_delta.astype(F32)))
            inner_delta = inner_delta + dot_nt(pre_delta, expand_w[0, :, at])
        add_row(vec_out, 11, row_sums(inner_delta * hat))
        add_row(vec_out, 12, row_sums(inner_delta))
        grad[rows, :] = gradient + norm_back(inner_delta, hat, inverse, gains[0, 1:2, :])

    delta_rows(0, place_ref, mask_ref, exit_w, grad, stripe_delta_out, branch_delta, vec_out, 13)
    moves.send(grad_out, stripe_delta_out)
    moves.need(active0, stripe0)
    put_squares(bundle, 4 * width, dot_tn(normed_bf[...], pre0[...]), width)
    for part in range(hidden_units // width):
        bundle.put(
            (8 + part) * width,
            dot_tn(active0[:, part * width : (part + 1) * width], feed0[...]),
        )
    bundle.put(12 * width, dot_tn(stripe0[...], branch_delta[...]))


def third_kernel(
    moves,
    place_ref,
    gains,
    shifts,
    conv_k,
    vec1,
    vec2,
    conv2,
    mixed_a,
    mixed_b,
    mixed_c,
    mixed_d,
    stripe_delta,
    win0,
    chance0,
    entry_w,
    grad_in,
    out_a,
    out_b,
    out_c,
    out_d,
    keep_out,
    away_out,
    hidden,
    wide,
    wide_bf,
    normed_bf,
    vec3,
    conv3,
    flat,
):
    width = hidden.shape[1]
    bundle = Bundle(
        place_ref, keep_out, away_out, 4, lambda chunk: jnp.bitwise_xor(place_ref[5], chunk)
    )
    vec3[...] = jnp.zeros(vec3.shape, F32)
    conv3[...] = jnp.zeros(conv3.shape, F32)
    moves.fetch(stripe_delta)
    moves.fetch(win0, chance0, part=0)
    moves.need(stripe_delta)
    moves.fetch(win0, chance0, part=1)

    def ready(direction):
        moves.need(win0, chance0, part=direction)
        if direction == 0:
            moves.fetch(mixed_a, mixed_b, mixed_c, mixed_d, entry_w, grad_in)

    attention_backward(ready, 0, win0, chance0, conv_k, stripe_delta, wide, conv3)

    def emit(t, rows, values):
        store_tile(place_ref, (out_a, out_b, out_c, out_d), t, values)

    moves.need(mixed_a, mixed_b, mixed_c, mixed_d, entry_w, grad_in)
    load_tiles(place_ref, (mixed_a, mixed_b, mixed_c, mixed_d), hidden)
    entry_backward(
        0, hidden, gains, shifts, entry_w, grad_in, wide, wide_bf, normed_bf, vec3, 0, emit
    )
    moves.send(out_a, out_b, out_c, out_d)
    flat[...] = jnp.zeros(flat.shape, F32)
    at = 0
    for ref in (vec1, vec2, conv2, vec3, conv3):
        flat[at : at + ref.shape[0], :] = jnp.sum(ref[...], axis=1)
        at += ref.shape[0]
    spread = dot_tn(normed_bf[...], wide_bf[...])
    half = keep_out.shape[0]
    middle = width // 2
    lots = flat.shape[0] // 2
    bundle.put(0, spread[:, :width])
    bundle.put(width, spread[:middle, width : 2 * width])
    bundle.put(width + middle, flat[:lots, :])
    bundle.put(half, spread[middle:, width : 2 * width])
    bundle.put(half + middle, spread[:, 2 * width :])
    bundle.put(half + middle + width, flat[lots:, :])


def untangle(source, flat, target):
    count, width = source.shape[2:]
    lanes = flat.shape[0]
    for row in range(TILE):
        flat[:, pl.ds(row * 8 + 7, count, stride=PAD), :] = jnp.zeros((lanes, count, 128), F32)
        for col in range(TILE):
            token = source[row, col].astype(F32)
            for lane in range(lanes):
                flat[lane, pl.ds(row * 8 + col, count, stride=PAD), :] = token[
                    :, lane * 128 : (lane + 1) * 128
                ]

    @pl.loop(0, count)
    def _(n):
        rows = pl.ds(pl.multiple_of(n * PAD, 8), PAD)
        tile = jnp.concatenate([flat[lane, rows, :] for lane in range(lanes)], axis=1)
        target(n, tile.reshape(TILE, 8, width).astype(BF))


def owner_of(wanted, count):
    if count & (count - 1) == 0:
        return lax.shift_right_logical(wanted, count.bit_length() - 1)
    return lax.div(wanted, count)


def pick_kernel(
    moves, mix_ref, cut_ref, images_ref, index_out, take_out, sent_out, own_out, flat, counts
):
    moves.fetch(images_ref)
    count = images_ref.shape[2]
    slots = sent_out.shape[0]
    capacity = slots // counts.shape[0]
    me = lax.axis_index("dp")

    def put(n, tile):
        own_out[n] = tile

    @pl.loop(0, slots, unroll=8)
    def _(s):
        index_out[s] = count

    @pl.loop(0, counts.shape[0])
    def _(g):
        counts[g] = 0
        rank = g * capacity
        for ref in (mix_ref, cut_ref):
            for j in range(count):
                wanted = ref[g * count + j]
                owner = owner_of(wanted, count)
                hit = owner == me
                index_out[jnp.where(hit, rank, slots)] = wanted - owner * count
                rank = rank + hit.astype(jnp.int32)

    for part, ref in enumerate((mix_ref, cut_ref)):

        @pl.loop(0, count)
        def _(j, part=part, ref=ref):
            owner = owner_of(ref[me * count + j], count)
            rank = counts[owner]
            take_out[part * count + j] = owner * capacity + rank
            counts[owner] = rank + 1

    moves.need(images_ref)
    untangle(images_ref, flat, put)

    @pl.loop(0, slots, unroll=4)
    def _(s):
        sent_out[s] = own_out[jnp.minimum(index_out[s], count - 1)]


def deal_kernel(place_ref, source, out_a, out_b, out_c, out_d, flat):
    outs = (out_a, out_b, out_c, out_d)
    share = out_a.shape[0]

    def put(n, tile):
        for d, out in enumerate(outs):

            @pl.when(jnp.bitwise_xor(place_ref[3], d) == n // share)
            def _(out=out):
                out[n % share] = tile

    untangle(source, flat, put)


def inside_box(corner_ref, n, place_ref):
    shape = (TILE, 8, 1)
    row = place_ref[1] * TILE + lax.broadcasted_iota(jnp.int32, shape, 0)
    col = place_ref[2] * TILE + lax.broadcasted_iota(jnp.int32, shape, 1)
    hit = (
        (row >= corner_ref[0, n])
        & (row < corner_ref[1, n])
        & (col >= corner_ref[2, n])
        & (col < corner_ref[3, n])
    )
    return jnp.where(hit, 1.0, 0.0)


def mix_kernel(
    place_ref, take_ref, corner_ref, ratio_ref, arrived, own_ref, out_a, out_b, out_c, out_d
):
    count = own_ref.shape[0]
    share = out_a.shape[0]
    for d, out in enumerate((out_a, out_b, out_c, out_d)):

        @pl.loop(0, share)
        def _(i, d=d, out=out):
            n = jnp.bitwise_xor(place_ref[3], d) * share + i
            inside = inside_box(corner_ref, n, place_ref)
            ratio = ratio_ref[n]
            own = own_ref[n].astype(F32)
            blend = arrived[take_ref[n]].astype(F32)
            cut = arrived[take_ref[count + n]].astype(F32)
            mixed = inside * cut + (1.0 - inside) * (ratio * own + (1.0 - ratio) * blend)
            out[i] = mixed.astype(BF)


def split_kernel(
    place_ref, take_ref, corner_ref, ratio_ref, grad_a, grad_b, grad_c, grad_d, out_ref
):
    share = grad_a.shape[0]
    count = 4 * share
    if out_ref.shape[0] > 2 * count:
        out_ref[...] = jnp.zeros(out_ref.shape, BF)
    for d, grad_ref in enumerate((grad_a, grad_b, grad_c, grad_d)):

        @pl.loop(0, share)
        def _(i, d=d, grad_ref=grad_ref):
            n = jnp.bitwise_xor(place_ref[3], d) * share + i
            inside = inside_box(corner_ref, n, place_ref)
            gradient = grad_ref[i].astype(F32)
            cut = inside * gradient
            out_ref[take_ref[n]] = ((1.0 - ratio_ref[n]) * (gradient - cut)).astype(BF)
            out_ref[take_ref[count + n]] = cut.astype(BF)


def join_kernel(
    place_ref,
    index_ref,
    corner_ref,
    ratio_ref,
    grad_a,
    grad_b,
    grad_c,
    grad_d,
    back_ref,
    out_ref,
    total,
):
    count, width = out_ref.shape[2:]
    share = grad_a.shape[0]

    def tile_rows(n):
        return pl.ds(pl.multiple_of(n * PAD, 8), PAD)

    for d, grad_ref in enumerate((grad_a, grad_b, grad_c, grad_d)):

        @pl.loop(0, share)
        def _(i, d=d, grad_ref=grad_ref):
            n = jnp.bitwise_xor(place_ref[3], d) * share + i
            outside = 1.0 - inside_box(corner_ref, n, place_ref)
            kept = ratio_ref[n] * outside * grad_ref[i].astype(F32)
            kept = kept.reshape(PAD, width)
            for lane in range(total.shape[0]):
                total[lane, tile_rows(n), :] = kept[:, lane * 128 : (lane + 1) * 128]

    @pl.loop(0, back_ref.shape[0])
    def _(s):
        piece = back_ref[s].astype(F32).reshape(PAD, width)
        for lane in range(total.shape[0]):
            total[lane, tile_rows(index_ref[s]), :] += piece[:, lane * 128 : (lane + 1) * 128]

    for row in range(TILE):
        for col in range(TILE):
            out_ref[row, col] = jnp.concatenate(
                [
                    total[lane, pl.ds(row * 8 + col, count, stride=PAD), :]
                    for lane in range(total.shape[0])
                ],
                axis=1,
            )


def lay_kernel(place_ref, act_a, act_b, act_c, act_d, out_ref, flat):
    count, width = out_ref.shape[2:]
    share = act_a.shape[0]
    for d, act_ref in enumerate((act_a, act_b, act_c, act_d)):

        @pl.loop(0, share)
        def _(i, d=d, act_ref=act_ref):
            n = jnp.bitwise_xor(place_ref[3], d) * share + i
            tile = act_ref[i].astype(F32).reshape(PAD, width)
            for lane in range(flat.shape[0]):
                flat[lane, pl.ds(pl.multiple_of(n * PAD, 8), PAD), :] = tile[
                    :, lane * 128 : (lane + 1) * 128
                ]

    for row in range(TILE):
        for col in range(TILE):
            out_ref[row, col] = jnp.concatenate(
                [
                    flat[lane, pl.ds(row * 8 + col, count, stride=PAD), :]
                    for lane in range(flat.shape[0])
                ],
                axis=1,
            ).astype(BF)


def unpack_kernel(
    ranks,
    counts,
    place_ref,
    *refs,
):
    pieces, refs = refs[:8], refs[8:]
    outs, (vectors, *buffers, send_sem) = refs[:12], refs[12:]
    (
        gain_out,
        shift_out,
        entry_out,
        entry_b_out,
        conv_out,
        conv_b_out,
        exit_out,
        exit_b_out,
        expand_out,
        expand_b_out,
        shrink_out,
        shrink_b_out,
    ) = buffers
    width = exit_out.shape[1]
    units = expand_out.shape[2]
    middle = width // 2

    def squares(out_ref, block, count):
        return [(out_ref, block, 0, part * width, width) for part in range(count)]

    def tall(out_ref, block, count):
        return [(out_ref, block, part * width, 0, width) for part in range(count)]

    plans = (
        squares(expand_out, 1, units // width) + tall(shrink_out, 1, units // width),
        [
            (entry_out, 0, 0, 0, width),
            (entry_out, 0, 0, width, middle),
            (vectors, None, 0, 0, middle),
            (entry_out, 0, middle, width, middle),
            (entry_out, 0, 0, 2 * width, width),
        ],
        squares(entry_out, 1, 3)
        + tall(exit_out, 1, 1)
        + squares(expand_out, 0, units // width)
        + tall(shrink_out, 0, units // width)
        + tall(exit_out, 0, 1),
    )
    inner_ranks = ranks // 4
    moves = []
    base = 0
    for plan, count in zip(plans, counts):
        at = 0
        for out_ref, block, first_row, lane, length in plan:
            done = 0
            while done < length:
                step = min(length - done, count - at % count)
                moves.append((out_ref, block, first_row + done, lane, base, count, at, step))
                at += step
                done += step
        base += count
    big = (expand_out, shrink_out, entry_out, exit_out)
    leaving = []

    def leave(buffer, out):
        copy = pltpu.make_async_copy(buffer, out, send_sem.at[len(leaving)])
        leaving.append(copy)
        return copy

    def place_parts(target, wanted, col, own):
        for out_ref, block, first_row, lane, base, count, at, step in moves:
            if out_ref is not target or block != wanted:
                continue
            shard, start = at // count, base + at % count
            half, shard = shard // ranks, shard % ranks
            first, inner = shard // inner_ranks, shard % inner_ranks
            piece = pieces[4 * (col ^ half) + (own ^ first)]
            inner = jnp.bitwise_xor(place_ref[6], inner)
            values = piece[inner, start : start + step, :].astype(F32)
            place = slice(first_row, first_row + step)
            if block is None:
                out_ref[place, :] = values
            else:
                out_ref[block, place, lane : lane + width] = values

    first_sends = {}
    for block in (1, 0):
        for target in big:
            i = [j for j, ref in enumerate(buffers) if ref is target][0]
            first_sends[block, i] = leave(target.at[block], outs[i].at[block])
    for col in range(2):
        for own in range(4):

            @pl.when((place_ref[2] == col) & (place_ref[5] == own))
            def _(col=col, own=own):
                place_parts(vectors, None, col, own)
                for (block, i), copy in first_sends.items():
                    place_parts(buffers[i], block, col, own)
                    copy.start()

    def line(n):
        return vectors[n : n + 1, :]

    gain_out[0] = jnp.concatenate([line(33), line(18)], axis=0)
    gain_out[1] = jnp.concatenate([line(11), line(5)], axis=0)
    shift_out[0] = jnp.concatenate([line(34), line(19)], axis=0)
    shift_out[1] = jnp.concatenate([line(12), line(6)], axis=0)
    for part in range(2):
        lanes = slice(part * width, (part + 1) * width)
        entry_b_out[:, lanes] = jnp.concatenate([line(31 + part), line(9 + part)], axis=0)
    for i in range(3):
        for j in range(3):
            conv_out[i, j] = jnp.concatenate(
                [line(35 + 3 * i + j), line(22 + 3 * i + j)], axis=0
            )
    conv_b_out[...] = jnp.concatenate([line(21), line(8)], axis=0)
    exit_b_out[...] = jnp.concatenate([line(20), line(7)], axis=0)
    for part in range(units // width):
        lanes = slice(part * width, (part + 1) * width)
        expand_b_out[:, lanes] = jnp.concatenate([line(14 + part), line(part)], axis=0)
    shrink_b_out[...] = jnp.concatenate([line(13), line(4)], axis=0)
    for buffer, out in zip(buffers, outs):
        if not any(buffer is ref for ref in big):
            leave(buffer, out).start()
    for copy in leaving:
        copy.wait()


SMEM = pl.BlockSpec(memory_space=pltpu.SMEM)
VMEM = pl.BlockSpec(memory_space=pltpu.VMEM)


ANYWHERE = pl.BlockSpec(memory_space=pl.ANY)
FAR = pl.BlockSpec(memory_space=pltpu.HBM)


def far(values):
    return pltpu.with_memory_space_constraint(values, pltpu.HBM)


class Here:
    def __init__(self, ranks):
        self.ranks = ranks

    def seat(self):
        group, row, col = (lax.axis_index(axis) for axis in ("dp", "row", "col"))
        bits = self.ranks.bit_length() - 1
        rank = 2 * group + row
        order = jnp.int32(0)
        for bit in range(0, bits, 2):
            count = min(2, bits - bit)
            part = jnp.bitwise_and(lax.shift_right_logical(rank, bit), (1 << count) - 1)
            order = order * (1 << count) + part
        rest = self.ranks // 4
        first = jnp.bitwise_and(rank, 3)
        return (group, row, col, 2 * row + col, order, first, order - first * rest)


class Moves:
    def __init__(self, fetched, sent):
        self.fetched, self.sent = dict(fetched), dict(sent)
        self.waited, self.started = set(), set()

    def copies(self, ref, part):
        copies = self.fetched.get(id(ref), [])
        return [
            ((id(ref), i), copy)
            for i, copy in enumerate(copies)
            if part is None or len(copies) == 1 or i == part
        ]

    def fetch(self, *refs, part=None):
        for ref in refs:
            for key, copy in self.copies(ref, part):
                if key not in self.started:
                    copy.start()
                    self.started.add(key)

    def need(self, *refs, part=None):
        self.fetch(*refs, part=part)
        for ref in refs:
            for key, copy in self.copies(ref, part):
                if key not in self.waited:
                    copy.wait()
                    self.waited.add(key)

    def send(self, *refs):
        for ref in refs:
            if id(ref) in self.sent:
                self.sent[id(ref)].start()
                self.started.add(id(ref))

    def finish(self):
        for key, copies in self.fetched.items():
            for i, copy in enumerate(copies):
                if (key, i) not in self.started:
                    copy.start()
                if (key, i) not in self.waited:
                    copy.wait()
        for key, copy in self.sent.items():
            if key not in self.started:
                copy.start()
        for copy in self.sent.values():
            copy.wait()


def halves(ref):
    if ref.shape[-2] != WIN:
        return [pl.ds(0, ref.shape[0])]
    count = ref.shape[0] // 2
    return [pl.ds(0, count), pl.ds(count, count)]


def run(
    kernel,
    scalars,
    arrays,
    outs,
    scratch=(),
    flops=0,
    name=None,
    after=(),
    scalar_outs=(),
    lazy=None,
    vmem=16,
    near=((), ()),
):
    outs = list(outs)
    here = None
    if scalars and isinstance(scalars[0], Here):
        here, scalars = scalars[0], scalars[1:]
    first_in, first_out = (len(arrays), len(outs)) if lazy is None else lazy
    eager, late = list(arrays[:first_in]), list(arrays[first_in:])
    n_in = len(scalars) + len(eager)
    scratch_shapes = [
        kind if dtype is None else pltpu.VMEM(kind, dtype) for kind, dtype in scratch
    ]
    n_own = len(scratch_shapes)
    n_late, n_sent = len(late), len(outs) - first_out
    if lazy is not None:
        scratch_shapes += [pltpu.VMEM(a.shape, a.dtype) for a in late]
        scratch_shapes += [pltpu.VMEM(*out) for out in outs[first_out:]]
        scratch_shapes += [pltpu.SemaphoreType.DMA((n_late, 2)), pltpu.SemaphoreType.DMA((max(n_sent, 1),))]

    def body(*refs):
        given, refs = refs[:n_in], refs[n_in:]
        sources, refs = refs[:n_late], refs[n_late + len(after) :]
        results, refs = refs[: len(scalar_outs) + first_out], refs[len(scalar_outs) + first_out :]
        targets, refs = refs[:n_sent], refs[n_sent:]
        own, refs = refs[:n_own], refs[n_own:]
        if here is not None:
            given = (here.seat(),) + tuple(given)
        if lazy is None:
            kernel(*given, *results, *own)
            return
        buffers, leaving = refs[:n_late], refs[n_late : n_late + n_sent]
        fetch_sem, send_sem = refs[n_late + n_sent :]
        moves = Moves(
            [
                (
                    id(buffer),
                    [
                        pltpu.make_async_copy(source.at[part], buffer.at[part], fetch_sem.at[i, j])
                        for j, part in enumerate(halves(buffer))
                    ],
                )
                for i, (source, buffer) in enumerate(zip(sources, buffers))
            ],
            [
                (id(buffer), pltpu.make_async_copy(buffer, target, send_sem.at[i]))
                for i, (buffer, target) in enumerate(zip(leaving, targets))
            ],
        )
        kernel(moves, *given, *buffers, *results, *leaving, *own)
        moves.finish()

    out_shape = [jax.ShapeDtypeStruct(shape, dtype) for shape, dtype in scalar_outs] + [
        pltpu.HBM(shape, dtype)
        if lazy is not None and i not in near[1]
        else jax.ShapeDtypeStruct(shape, dtype)
        for i, (shape, dtype) in enumerate(outs)
    ]
    late = [
        a if i in near[0] else far(a)
        for i, a in enumerate(late, first_in)
    ]
    moved = sum(a.size * a.dtype.itemsize for a in arrays)
    return pl.pallas_call(
        body,
        out_shape=out_shape,
        in_specs=[SMEM] * len(scalars)
        + [VMEM] * len(eager)
        + [ANYWHERE if i in near[0] else FAR for i in range(first_in, len(arrays))]
        + [ANYWHERE] * len(after),
        out_specs=[SMEM] * len(scalar_outs)
        + [VMEM] * first_out
        + [ANYWHERE if i in near[1] else FAR for i in range(first_out, len(outs))],
        scratch_shapes=scratch_shapes,
        compiler_params=pltpu.CompilerParams(vmem_limit_bytes=vmem * 1024 * 1024),
        cost_estimate=pl.CostEstimate(flops=flops, bytes_accessed=moved, transcendentals=0),
        name=name,
    )(*scalars, *eager, *late, *after)


def gate(values, after):
    values, after = list(values), list(after)
    return list(lax.optimization_barrier(tuple(values + after)))[: len(values)]


def swap(values, axis):
    return lax.ppermute(values, axis, [(0, 1), (1, 0)])


def added(values, others):
    return (values.astype(F32) + others.astype(F32)).astype(BF)


def shards(values, ranks):
    return values.reshape(ranks, values.shape[0] // ranks, values.shape[1])


def spread_sum(pieces):
    mine = jnp.sum(pieces.astype(F32), axis=0).astype(BF)
    return jnp.broadcast_to(mine[None], pieces.shape)


def across(values, axes, size, mask):
    return lax.ppermute(values, axes, [(i, i ^ mask) for i in range(size)])


def deal(parts):
    return [parts[0]] + [across(parts[d], ("row", "col"), 4, d) for d in (1, 2, 3)]


RANKS = ("dp", "row")


def stages(ranks):
    bits = ranks.bit_length() - 1
    return [(bit, min(2, bits - bit)) for bit in range(0, bits, 2)]


def scatter_send(values, ranks, stage):
    bit, count = stage
    size = 1 << count
    me = (lax.axis_index(RANKS) >> bit) & (size - 1)
    cut = values.reshape(size, values.shape[0] // size, values.shape[1])
    return [lax.dynamic_index_in_dim(cut, me ^ d, 0, keepdims=False) for d in range(size)]


def scatter_move(parts, ranks, stage):
    return [parts[0]] + [
        across(parts[d], RANKS, ranks, d << stage[0]) for d in range(1, len(parts))
    ]


def scatter_sum(parts):
    return sum(part.astype(F32) for part in parts).astype(BF)


def gather(values, ranks, stage):
    return jnp.stack(
        [values]
        + [across(values, RANKS, ranks, d << stage[0]) for d in range(1, 1 << stage[1])]
    )


def rank_order(rank, ranks):
    order = 0
    for bit, count in stages(ranks):
        order = order * (1 << count) + ((rank >> bit) & ((1 << count) - 1))
    return order


def local(
    groups,
    images,
    cotangent,
    mix_partner,
    cut_partner,
    ratios,
    corners,
    drop_masks,
    norm_gains,
    norm_shifts,
    entry_weight,
    entry_bias,
    position_kernel,
    position_bias,
    exit_weight,
    exit_bias,
    expand_weight,
    expand_bias,
    shrink_weight,
    shrink_bias,
):
    images_here = images.shape[0]
    width = images.shape[3]
    units = expand_weight.shape[2]
    share = images_here // 4
    rows = 4 * share * PAD
    ranks = 2 * groups
    capacity = (2 * images_here + groups - 1) // groups
    slots = groups * capacity
    place = Here(ranks)
    spots = [0] * ranks
    for rank in range(ranks):
        spots[rank_order(rank, ranks)] = rank
    quad = ((share, TILE, 8, width), BF)
    corners = corners.T
    masks = drop_masks.T
    flat = ((width // 128, images_here * PAD, 128), F32)
    index, take, outgoing, own = run(
        pick_kernel,
        [mix_partner, cut_partner],
        [images.transpose(1, 2, 0, 3)],
        [((slots, TILE, 8, width), BF), ((images_here, TILE, 8, width), BF)],
        [flat, (pltpu.SMEM((groups,), jnp.int32), None)],
        name="pick",
        vmem=60,
        lazy=(0, 2),
        near=((), (0, 1)),
        scalar_outs=(((slots + 8,), jnp.int32), ((2 * images_here,), jnp.int32)),
    )
    arrived = lax.all_to_all(outgoing, "dp", split_axis=0, concat_axis=0, tiled=True)
    cot = deal(
        run(deal_kernel, [place], [cotangent.transpose(1, 2, 0, 3)], [quad] * 4, [flat], name="deal")
    )
    mixed = deal(
        run(
            mix_kernel,
            [place, take, corners, ratios],
            [arrived, own],
            [quad] * 4,
            name="mix",
            after=cot,
        )
    )
    conv_k = position_kernel.transpose(1, 2, 0, 3)
    tall = (rows, width)
    (
        vec1,
        keep1,
        away1,
        act_a,
        act_b,
        act_c,
        act_d,
        active0,
        slope0,
        win0,
        chance0,
        stripe0,
        mid0,
        win1,
        chance1,
        stripe1,
        hidden1,
        grad1,
    ) = run(
        functools.partial(first_kernel, spots),
        [place, masks],
        [
            *mixed,
            norm_gains,
            norm_shifts,
            entry_bias,
            conv_k,
            position_bias,
            exit_bias,
            expand_bias,
            shrink_bias,
            *cot,
            entry_weight,
            exit_weight,
            expand_weight,
            shrink_weight,
        ],
        [
            ((7, 8, width), F32),
            ((units, width), BF),
            ((units, width), BF),
            *([quad] * 4),
            ((rows, units), BF),
            ((rows, units), BF),
            ((4 * share, WIN, 3 * HALF), BF),
            ((4 * share, WIN, LANES), BF),
            (tall, BF),
            (tall, F32),
            ((4 * share, WIN, 3 * HALF), BF),
            ((4 * share, WIN, LANES), BF),
            (tall, BF),
            (tall, F32),
            (tall, F32),
        ],
        [
            (tall, F32),
            ((rows, 3 * width), F32),
            (tall, F32),
            ((rows, units), BF),
            ((rows, units), BF),
            (tall, BF),
            (tall, BF),
        ],
        flops=10 * rows * width * width * 120,
        name="first",
        vmem=46,
        near=((), (1, 2)),
        lazy=(17, 3),
    )
    sent1 = shards(added(keep1, swap(away1, "col")), ranks)
    pieces1 = lax.all_to_all(sent1, RANKS, split_axis=0, concat_axis=0, tiled=True)
    vec2, conv2, keep2, away2, grad0, delta0 = run(
        second_kernel,
        [place, masks],
        [
            norm_gains,
            norm_shifts,
            conv_k,
            grad1,
            exit_weight,
            win1,
            chance1,
            hidden1,
            entry_weight,
            stripe1,
            mid0,
            shrink_weight,
            slope0,
            expand_weight,
            active0,
            stripe0,
        ],
        [
            ((15, 8, width), F32),
            ((9, 8, width), F32),
            ((13 * width // 2, width), BF),
            ((13 * width // 2, width), BF),
            (tall, F32),
            (tall, F32),
        ],
        [
            (tall, F32),
            (tall, BF),
            ((rows, 3 * width), F32),
            ((rows, 3 * width), BF),
            (tall, BF),
            (tall, BF),
            ((rows, units), BF),
        ],
        flops=6 * rows * width * width * 120,
        name="second",
        vmem=42,
        near=((), (2, 3)),
        after=[sent1],
        lazy=(3, 4),
    )
    act = deal([act_a, act_b, act_c, act_d])
    keep2, away2, *act = gate([keep2, away2, *act], [pieces1])
    steps = stages(ranks)

    def first_parts(keep, away):
        other = swap(away, "col")
        count = keep.shape[0] // 4
        return [
            added(keep[d * count : (d + 1) * count], other[d * count : (d + 1) * count])
            for d in range(4)
        ]

    parts2 = first_parts(keep2, away2)
    moved2 = scatter_move(parts2, ranks, steps[0])
    *out_tiles, keep3, away3 = run(
        third_kernel,
        [place],
        [
            norm_gains,
            norm_shifts,
            conv_k,
            vec1,
            vec2,
            conv2,
            *mixed,
            delta0,
            win0,
            chance0,
            entry_weight,
            grad0,
        ],
        [quad] * 4 + [((2 * width, width), BF), ((2 * width, width), BF)],
        [
            (tall, F32),
            ((rows, 3 * width), F32),
            ((rows, 3 * width), BF),
            (tall, BF),
            ((4, 8, width), F32),
            ((9, 8, width), F32),
            ((width, width), F32),
        ],
        flops=3 * rows * width * width * 120,
        name="third",
        vmem=36,
        near=((), range(6)),
        after=parts2,
        lazy=(10, 6),
    )
    *moved2, keep3, away3 = gate([*moved2, keep3, away3], out_tiles)
    gradient = deal(out_tiles)
    (parted,) = run(
        split_kernel,
        [place, take, corners, ratios],
        gradient,
        [((slots, TILE, 8, width), BF)],
        name="split",
    )
    mine1 = jnp.sum(pieces1.astype(F32), axis=0).astype(BF)
    mine2 = scatter_sum(moved2)
    moved3 = scatter_move(first_parts(keep3, away3), ranks, steps[0])
    mine3 = scatter_sum(gate(moved3, [mine1]))
    cut = mine2.shape[0] * 4 // ranks
    lot = mine3.shape[0] * 4 // ranks
    joint = jnp.concatenate(
        [
            mine3.reshape(ranks // 4, lot, width),
            mine2.reshape(ranks // 4, cut, width),
        ],
        axis=1,
    ).reshape(-1, width)
    for step in steps[1:]:
        joint = scatter_sum(scatter_move(scatter_send(joint, ranks, step), ranks, step))
    joint = jnp.concatenate([mine1, joint], axis=0)
    counts = (mine1.shape[0], lot, cut)
    for step in reversed(steps[1:]):
        joint = gather(joint, ranks, step).reshape(-1, width)
    joint = shards(joint, ranks // 4)
    (parted,) = gate([parted], [joint])
    (activations,) = run(
        lay_kernel, [place], [far(a) for a in act], [((TILE, TILE, images_here, width), BF)], [flat], name="lay"
    )
    back = lax.all_to_all(parted, "dp", split_axis=0, concat_axis=0, tiled=True)
    (back,) = gate([back], [activations])
    (input_gradient,) = run(
        join_kernel,
        [place, index, corners, ratios],
        [*gradient, back],
        [((TILE, TILE, images_here, width), F32)],
        [((width // 128, (images_here + 1) * PAD, 128), F32)],
        name="join",
    )
    full = [joint] + [across(joint, RANKS, ranks, d) for d in (1, 2, 3)]
    full[2:] = gate(full[2:], [input_gradient])
    full += [swap(piece, "col") for piece in full]
    shapes = [
        (2, 2, width),
        (2, 2, width),
        (2, width, 3 * width),
        (2, 2 * width),
        (3, 3, 2, width),
        (2, width),
        (2, width, width),
        (2, width),
        (2, width, units),
        (2, units),
        (2, units, width),
        (2, width),
    ]
    gains, shifts, entry, entry_b, conv, conv_b, exit_, exit_b, expand, expand_b, shrink, shrink_b = (
        pl.pallas_call(
            lambda *refs: unpack_kernel(ranks, counts, place.seat(), *refs),
            out_shape=[jax.ShapeDtypeStruct(shape, F32) for shape in shapes],
            in_specs=[VMEM] * 8,
            out_specs=[ANYWHERE] * 12,
            scratch_shapes=[
                pltpu.VMEM((width // 2, width), F32),
            ]
            + [pltpu.VMEM(shape, F32) for shape in shapes]
            + [pltpu.SemaphoreType.DMA((16,))],
            compiler_params=pltpu.CompilerParams(vmem_limit_bytes=24 * 1024 * 1024),
            name="unpack",
        )(*full)
    )
    return (
        activations.transpose(2, 0, 1, 3),
        input_gradient.transpose(2, 0, 1, 3),
        gains,
        shifts,
        entry,
        entry_b,
        conv.transpose(2, 0, 1, 3),
        conv_b,
        exit_,
        exit_b,
        expand,
        expand_b,
        shrink,
        shrink_b,
    )


def solution(mesh):
    tiles = P("dp", "row", "col", None)
    return jax.shard_map(
        functools.partial(local, mesh.shape["dp"]),
        mesh=mesh,
        in_specs=(tiles, tiles, P(), P(), P("dp"), P("dp", None), P("dp", None)) + (P(),) * 12,
        out_specs=(tiles, tiles) + (P(),) * 12,
        check_vma=False,
    )
```

```python
import functools

import jax
import jax.numpy as jnp
from jax import lax
from jax.experimental import pallas as pl
from jax.experimental.pallas import tpu as pltpu
from jax.sharding import PartitionSpec as P

TILE = 7
PAD = 56
HEAD_DIM = 32
SIDE_HEADS = 4
HALF = 128
WIN = 2 * PAD
CHUNK = 8 * PAD
LANES = SIDE_HEADS * 128
SCALE = HEAD_DIM ** (-0.5)
LOG2E = 1.4426950408889634
EPS = 1e-05
BF = jnp.bfloat16
F32 = jnp.float32


def dot_nn(a, b):
    return lax.dot_general(a, b, (((1,), (0,)), ((), ())), preferred_element_type=F32)


def dot_nt(a, b):
    return lax.dot_general(a, b, (((1,), (1,)), ((), ())), preferred_element_type=F32)


def dot_tn(a, b):
    return lax.dot_general(a, b, (((0,), (0,)), ((), ())), preferred_element_type=F32)


def norm_parts(values):
    centered = values - jnp.mean(values, axis=-1, keepdims=True)
    inverse = lax.rsqrt(jnp.mean(centered * centered, axis=-1, keepdims=True) + EPS)
    return centered * inverse, inverse


def norm_back(delta, hat, inverse, gain):
    scaled = delta * gain
    first = jnp.mean(scaled, axis=-1, keepdims=True)
    second = jnp.mean(scaled * hat, axis=-1, keepdims=True)
    return inverse * (scaled - first - hat * second)


def gelu_parts(values):
    chance = 0.5 + 0.5 * lax.erf(values * (0.5**0.5))
    density = jnp.exp2(values * values * (-0.5 * LOG2E)) * 0.3989422804014327
    return chance, density


def row_sums(values):
    count, width = values.shape
    return jnp.sum(values.reshape(count // 8, 8, width), axis=0)


def scale_rows(place_ref, mask_ref, column):
    scales = [
        mask_ref[column, 4 * place_ref[3] + i].astype(F32) * 1.25 for i in range(4)
    ]
    columns = [jnp.full((PAD, 1), scale, F32) for scale in scales]
    return jnp.concatenate(columns * (CHUNK // (4 * PAD)), axis=0)


def add_row(acc_ref, row, values):
    acc_ref[row] += values


def spread_heads(values):
    lane = lax.broadcasted_iota(jnp.int32, values.shape, 1) // HEAD_DIM
    empty = jnp.zeros((128 - WIN, HALF), F32)
    blocks = []
    for head in range(SIDE_HEADS):
        blocks.append(jnp.where(lane == head, values, 0.0))
        blocks.append(empty)
    return jnp.concatenate(blocks, axis=0).astype(BF)


def over_keys(weights, values):
    weights = fill_rows(weights)
    stacked = jnp.concatenate(
        [weights[:, head * 128 : (head + 1) * 128] for head in range(SIDE_HEADS)], axis=0
    )
    return dot_tn(stacked, spread_heads(values))[:WIN]


def fill_rows(values):
    empty = jnp.zeros((128 - WIN, values.shape[1]), values.dtype)
    return jnp.concatenate([values, empty], axis=0)


def valid_column(shape):
    return lax.broadcasted_iota(jnp.int32, shape, 1) != 7


def valid_rows(shape):
    return lax.broadcasted_iota(jnp.int32, shape, 0) % 8 != 7


def column_shifts(values, across):
    cube = values.reshape(2 * TILE, 8, HALF)
    if not across:
        return (pltpu.roll(cube, 1, 1), cube, pltpu.roll(cube, 7, 1))
    left, right = cube[:TILE], cube[TILE:]
    column = lax.broadcasted_iota(jnp.int32, left.shape, 1)
    before = jnp.concatenate(
        [
            pltpu.roll(left, 1, 1),
            jnp.where(column == 0, pltpu.roll(left, 2, 1), pltpu.roll(right, 1, 1)),
        ],
        axis=0,
    )
    after = jnp.concatenate(
        [
            jnp.where(column == 6, pltpu.roll(right, 6, 1), pltpu.roll(left, 7, 1)),
            pltpu.roll(right, 7, 1),
        ],
        axis=0,
    )
    return (before, cube, after)


def row_shift(cube, step, across):
    if step == 0:
        return cube
    empty = jnp.zeros((1, 8, HALF), F32)

    def move(part):
        if step < 0:
            return jnp.concatenate([empty, part[:-1]], axis=0)
        return jnp.concatenate([part[1:], empty], axis=0)

    if across:
        return jnp.concatenate([move(cube[:TILE]), move(cube[TILE:])], axis=0)
    return move(cube)


def window_conv(shifts, kernel_at, across):
    total = None
    for i in range(3):
        part = None
        for j in range(3):
            term = kernel_at(i, j) * shifts[j]
            part = term if part is None else part + term
        part = row_shift(part, i - 1, across)
        total = part if total is None else total + part
    return total.reshape(WIN, HALF)


def window_rows(across, window):
    side, image = window // 4, window % 4
    if across:
        first, second = 2 * side, 2 * side + 1
    else:
        first, second = side, 2 + side
    return (
        pl.multiple_of((first * 4 + image) * PAD, 8),
        pl.multiple_of((second * 4 + image) * PAD, 8),
    )


def take_window(ref, at, lane):
    return jnp.concatenate(
        [ref[pl.ds(at[0], PAD), lane : lane + HALF], ref[pl.ds(at[1], PAD), lane : lane + HALF]],
        axis=0,
    )


def put_window(ref, at, lane, values):
    ref[pl.ds(at[0], PAD), lane : lane + HALF] = values[:PAD]
    ref[pl.ds(at[1], PAD), lane : lane + HALF] = values[PAD:]


def round_bf(values):
    return values.astype(BF).astype(F32)


def attention_forward(
    block, hidden_ref, gains, shifts, entry_w, entry_b, conv_k, conv_b, wide, stripe, win_out, chance_out
):
    width = hidden_ref.shape[1]

    @pl.loop(0, 2)
    def _(t):
        rows = chunk(t)
        hat, _ = norm_parts(hidden_ref[rows, :])
        normed = (hat * gains[block, 0:1, :] + shifts[block, 0:1, :]).astype(BF)
        for part in range(3):
            out = dot_nn(normed, entry_w[block, :, part * width : (part + 1) * width])
            if part != 1:
                at = 0 if part == 0 else width
                out = out + entry_b[block : block + 1, at : at + width]
            wide[rows, part * width : (part + 1) * width] = round_bf(out)

    for direction in range(2):
        across = direction == 0
        lane = direction * HALF

        @pl.loop(0, 8, unroll=8)
        def _(window, across=across, lane=lane, direction=direction):
            at = window_rows(across, window)
            queries = take_window(wide, at, lane)
            keys = take_window(wide, at, width + lane)
            values = take_window(wide, at, 2 * width + lane)
            keys_bf = keys.astype(BF)
            win_out[direction * 8 + window, :, 0:HALF] = queries.astype(BF)
            win_out[direction * 8 + window, :, HALF : 2 * HALF] = keys_bf
            win_out[direction * 8 + window, :, 2 * HALF : 3 * HALF] = values.astype(BF)
            scores = dot_nt(keys_bf, spread_heads(queries)).reshape(2 * TILE, 8, LANES)
            scores = jnp.where(valid_column((1, 8, LANES)), scores, -1e30)
            top = jnp.max(jnp.max(scores, axis=0), axis=0, keepdims=True)
            lifted = jnp.exp2((scores - top) * (SCALE * LOG2E))
            totals = jnp.sum(jnp.sum(lifted, axis=0), axis=0, keepdims=True)
            chances = (lifted * (1.0 / totals)).reshape(WIN, LANES).astype(BF)
            chance_out[direction * 8 + window] = chances
            attended = over_keys(chances, values)
            clean = jnp.where(valid_rows(values.shape), values, 0.0)
            position = window_conv(
                column_shifts(clean, across),
                lambda i, j: conv_k[i, j, block : block + 1, lane : lane + HALF],
                across,
            )
            put_window(
                stripe, at, lane, attended + position + conv_b[block : block + 1, lane : lane + HALF]
            )


def attention_backward(
    ready,
    block,
    win_in,
    chance_in,
    conv_k,
    stripe_delta,
    wide,
    conv_acc,
):
    width = stripe_delta.shape[1]
    for direction in range(2):
        ready(direction)
        across = direction == 0
        lane = direction * HALF

        @pl.loop(0, 8, unroll=4)
        def _(window, across=across, lane=lane, direction=direction):
            at = window_rows(across, window)
            out_delta = take_window(stripe_delta, at, lane)
            queries = win_in[direction * 8 + window, :, 0:HALF].astype(F32)
            keys = win_in[direction * 8 + window, :, HALF : 2 * HALF].astype(F32)
            values_bf = win_in[direction * 8 + window, :, 2 * HALF : 3 * HALF]
            values = values_bf.astype(F32)
            chances = chance_in[direction * 8 + window]
            delta_spread = spread_heads(out_delta)
            chance_delta = dot_nt(values_bf, delta_spread)
            cubes = (2 * TILE, 8, LANES)
            wide_chances = chances.astype(F32).reshape(cubes)
            weighted = wide_chances * chance_delta.reshape(cubes)
            common = jnp.sum(jnp.sum(weighted, axis=0), axis=0, keepdims=True)
            score_delta = (weighted - wide_chances * common).reshape(WIN, LANES).astype(BF)
            values_delta = dot_nn(chances, delta_spread)
            keys_delta = dot_nn(score_delta, spread_heads(queries)) * SCALE
            query_delta = over_keys(score_delta, keys) * SCALE
            keep = valid_rows(values.shape)
            clean = jnp.where(keep, values, 0.0)
            shifts = column_shifts(clean, across)
            cube = out_delta.reshape(2 * TILE, 8, HALF)
            for i in range(3):
                moved = row_shift(cube, 1 - i, across)
                for j in range(3):
                    conv_acc[3 * i + j, :, lane : lane + HALF] += jnp.sum(moved * shifts[j], axis=0)
            back = window_conv(
                column_shifts(out_delta, across),
                lambda i, j: conv_k[2 - i, 2 - j, block : block + 1, lane : lane + HALF],
                across,
            )
            values_delta = jnp.where(keep, values_delta + back, 0.0)
            put_window(wide, at, lane, query_delta)
            put_window(wide, at, width + lane, keys_delta)
            put_window(wide, at, 2 * width + lane, values_delta)


def chunk(t):
    return pl.ds(pl.multiple_of(t * CHUNK, CHUNK), CHUNK)


class Bundle:
    def __init__(self, place_ref, keep, away, chunks=1, spot=lambda chunk: chunk):
        self.place_ref, self.keep, self.away = place_ref, keep, away
        self.step, self.spot = keep.shape[0] // chunks, spot

    def put(self, at, values):
        values = values.astype(BF)
        half, step = self.keep.shape[0], self.step
        last = at + values.shape[0]
        first = at
        while first < last:
            stop = min(last, (first // step + 1) * step)
            number = first // half
            start = self.spot(first % half // step) * step
            inner, count = first % step, stop - first
            if not isinstance(start, int):
                start = pl.multiple_of(start, step)
            rows = pl.ds(start + inner, count)
            piece = values[first - at : stop - at]

            @pl.when(self.place_ref[2] == number)
            def _(piece=piece, rows=rows):
                self.keep[rows, :] = piece

            @pl.when(self.place_ref[2] != number)
            def _(piece=piece, rows=rows):
                self.away[rows, :] = piece

            first = stop


def put_squares(bundle, at, values, side):
    for part in range(values.shape[1] // side):
        bundle.put(at + part * side, values[:, part * side : (part + 1) * side])


def load_tiles(place_ref, tiles, hidden):
    for d, tile in enumerate(tiles):
        at = jnp.bitwise_xor(place_ref[3], d) * (4 * PAD)
        rows = pl.ds(pl.multiple_of(at, 4 * PAD), 4 * PAD)
        hidden[rows, :] = tile[...].astype(F32).reshape(4 * PAD, hidden.shape[1])


def store_tile(place_ref, tiles, t, values):
    count = CHUNK // (4 * PAD)
    values = values.reshape((count,) + tiles[0].shape).astype(BF)
    for part in range(count):
        for d, tile in enumerate(tiles):

            @pl.when(jnp.bitwise_xor(place_ref[3], d) == count * t + part)
            def _(tile=tile, part=part):
                tile[...] = values[part]


def first_kernel(
    spots,
    moves,
    place_ref,
    mask_ref,
    mixed_a,
    mixed_b,
    mixed_c,
    mixed_d,
    gains,
    shifts,
    entry_b,
    conv_k,
    conv_b,
    exit_b,
    expand_b,
    shrink_b,
    cot_a,
    cot_b,
    cot_c,
    cot_d,
    entry_w,
    exit_w,
    expand_w,
    shrink_w,
    vec_out,
    keep_out,
    away_out,
    act_a,
    act_b,
    act_c,
    act_d,
    active0_out,
    slope0_out,
    win0_out,
    chance0_out,
    stripe0_out,
    mid0_out,
    win1_out,
    chance1_out,
    stripe1_out,
    hidden1_out,
    grad_out,
    hidden,
    wide,
    stripe,
    active1,
    pre1,
    feed1,
    inner1,
):
    width = hidden.shape[1]
    hidden_units = expand_w.shape[2]
    bundle = Bundle(place_ref, keep_out, away_out, len(spots), lambda chunk: spots[chunk])
    vec_out[...] = jnp.zeros(vec_out.shape, F32)
    moves.fetch(entry_w)
    load_tiles(place_ref, (mixed_a, mixed_b, mixed_c, mixed_d), hidden)
    moves.need(entry_w)
    moves.fetch(exit_w, expand_w, shrink_w, cot_a, cot_b, cot_c, cot_d)

    for block in range(2):
        win_out, chance_out, stripe_out = (
            (win0_out, chance0_out, stripe0_out),
            (win1_out, chance1_out, stripe1_out),
        )[block]
        attention_forward(
            block, hidden, gains, shifts, entry_w, entry_b, conv_k, conv_b, wide, stripe, win_out, chance_out
        )
        moves.send(win_out, chance_out)
        moves.need(exit_w, expand_w, shrink_w)
        if block == 1:
            moves.need(cot_a, cot_b, cot_c, cot_d)
            load_tiles(place_ref, (cot_a, cot_b, cot_c, cot_d), grad_out)

        @pl.loop(0, 2)
        def _(t, block=block, stripe_out=stripe_out):
            rows = chunk(t)
            striped = stripe[rows, :].astype(BF)
            stripe_out[rows, :] = striped
            branch = dot_nn(striped, exit_w[block]) + exit_b[block : block + 1, :]
            midway = hidden[rows, :] + scale_rows(place_ref, mask_ref, 2 * block) * branch
            if block == 0:
                mid0_out[rows, :] = midway
            hat, inverse = norm_parts(midway)
            normed = (hat * gains[block, 1:2, :] + shifts[block, 1:2, :]).astype(BF)
            feed_scale = scale_rows(place_ref, mask_ref, 2 * block + 1)
            feed = shrink_b[block : block + 1, :]
            if block == 1:
                inner1[rows, :] = normed
                gradient = grad_out[rows, :]
                feed_delta = (feed_scale * gradient).astype(BF)
                feed1[rows, :] = feed_delta
                add_row(vec_out, 4, row_sums(feed_delta.astype(F32)))
                inner_delta = jnp.zeros((CHUNK, width), F32)
            for part in range(hidden_units // width):
                at = slice(part * width, (part + 1) * width)
                pre_act = dot_nn(normed, expand_w[block, :, at]) + expand_b[block : block + 1, at]
                chance, density = gelu_parts(pre_act)
                active = (pre_act * chance).astype(BF)
                slope = chance + pre_act * density
                if block == 0:
                    active0_out[rows, at] = active
                    slope0_out[rows, at] = slope.astype(BF)
                else:
                    active1[rows, at] = active
                    pre_delta = (dot_nt(feed_delta, shrink_w[block, at, :]) * slope).astype(BF)
                    pre1[rows, at] = pre_delta
                    add_row(vec_out, part, row_sums(pre_delta.astype(F32)))
                    inner_delta = inner_delta + dot_nt(pre_delta, expand_w[block, :, at])
                feed = feed + dot_nn(active, shrink_w[block, at, :])
            output = midway + feed_scale * feed
            if block == 0:
                hidden[rows, :] = output
                hidden1_out[rows, :] = output
            else:
                store_tile(place_ref, (act_a, act_b, act_c, act_d), t, output)
                add_row(vec_out, 5, row_sums(inner_delta * hat))
                add_row(vec_out, 6, row_sums(inner_delta))
                grad_out[rows, :] = gradient + norm_back(
                    inner_delta, hat, inverse, gains[block, 1:2, :]
                )

        moves.send(stripe_out)
        if block == 0:
            moves.send(mid0_out, active0_out, slope0_out, hidden1_out)
        else:
            moves.send(act_a, act_b, act_c, act_d, grad_out)

    put_squares(bundle, 0, dot_tn(inner1[...], pre1[...]), width)
    for part in range(hidden_units // width):
        bundle.put(
            hidden_units + part * width,
            dot_tn(active1[:, part * width : (part + 1) * width], feed1[...]),
        )


def delta_rows(block, place_ref, mask_ref, exit_w, grad_ref, stripe_delta, branch_delta, vec_out, at):
    @pl.loop(0, 2)
    def _(t):
        rows = chunk(t)
        rounded = (scale_rows(place_ref, mask_ref, 2 * block) * grad_ref[rows, :]).astype(BF)
        branch_delta[rows, :] = rounded
        add_row(vec_out, at, row_sums(rounded.astype(F32)))
        out = round_bf(dot_nt(rounded, exit_w[block]))
        stripe_delta[rows, :] = out
        add_row(vec_out, at + 1, row_sums(out))


def entry_backward(block, hidden_ref, gains, shifts, entry_w, grad_ref, wide, wide_bf, normed_bf, vec_out, at, emit):
    width = hidden_ref.shape[1]

    @pl.loop(0, 2)
    def _(t):
        rows = chunk(t)
        hat, inverse = norm_parts(hidden_ref[rows, :])
        normed_bf[rows, :] = (hat * gains[block, 0:1, :] + shifts[block, 0:1, :]).astype(BF)
        delta = jnp.zeros((CHUNK, width), F32)
        for part in range(3):
            lanes = slice(part * width, (part + 1) * width)
            rounded = wide[rows, lanes].astype(BF)
            wide_bf[rows, lanes] = rounded
            if part != 1:
                add_row(vec_out, at + part // 2, row_sums(rounded.astype(F32)))
            delta = delta + dot_nt(rounded, entry_w[block, :, lanes])
        add_row(vec_out, at + 2, row_sums(delta * hat))
        add_row(vec_out, at + 3, row_sums(delta))
        emit(t, rows, grad_ref[rows, :] + norm_back(delta, hat, inverse, gains[block, 0:1, :]))


def second_kernel(
    moves,
    place_ref,
    mask_ref,
    gains,
    shifts,
    conv_k,
    grad_in,
    exit_w,
    win1,
    chance1,
    hidden1,
    entry_w,
    stripe1,
    mid0,
    shrink_w,
    slope0,
    expand_w,
    active0,
    stripe0,
    vec_out,
    conv_out,
    keep_out,
    away_out,
    grad_out,
    stripe_delta_out,
    stripe_delta,
    branch_delta,
    wide,
    wide_bf,
    normed_bf,
    feed0,
    pre0,
):
    grad = grad_out
    width = grad.shape[1]
    hidden_units = expand_w.shape[2]
    bundle = Bundle(
        place_ref, keep_out, away_out, 4, lambda chunk: jnp.bitwise_xor(place_ref[5], chunk)
    )
    vec_out[...] = jnp.zeros(vec_out.shape, F32)
    conv_out[...] = jnp.zeros(conv_out.shape, F32)
    moves.fetch(grad_in, exit_w)
    moves.fetch(win1, chance1, part=0)
    moves.need(grad_in, exit_w)
    moves.fetch(win1, chance1, part=1)
    delta_rows(1, place_ref, mask_ref, exit_w, grad_in, stripe_delta, branch_delta, vec_out, 0)

    def ready(direction):
        moves.need(win1, chance1, part=direction)
        if direction == 0:
            moves.fetch(hidden1, entry_w, stripe1)
        else:
            moves.fetch(mid0, shrink_w, slope0, expand_w, active0, stripe0)

    attention_backward(ready, 1, win1, chance1, conv_k, stripe_delta, wide, conv_out)

    def emit(t, rows, values):
        grad[rows, :] = values

    moves.need(hidden1, entry_w)
    entry_backward(
        1, hidden1, gains, shifts, entry_w, grad_in, wide, wide_bf, normed_bf, vec_out, 2, emit
    )
    put_squares(bundle, 0, dot_tn(normed_bf[...], wide_bf[...]), width)
    moves.need(stripe1)
    bundle.put(3 * width, dot_tn(stripe1[...], branch_delta[...]))
    moves.need(mid0, shrink_w, slope0, expand_w)

    @pl.loop(0, 2)
    def _(t):
        rows = chunk(t)
        gradient = grad[rows, :]
        hat, inverse = norm_parts(mid0[rows, :])
        normed_bf[rows, :] = (hat * gains[0, 1:2, :] + shifts[0, 1:2, :]).astype(BF)
        feed_delta = (scale_rows(place_ref, mask_ref, 1) * gradient).astype(BF)
        feed0[rows, :] = feed_delta
        add_row(vec_out, 6, row_sums(feed_delta.astype(F32)))
        inner_delta = jnp.zeros((CHUNK, width), F32)
        for part in range(hidden_units // width):
            at = slice(part * width, (part + 1) * width)
            pre_delta = (
                dot_nt(feed_delta, shrink_w[0, at, :]) * slope0[rows, at].astype(F32)
            ).astype(BF)
            pre0[rows, at] = pre_delta
            add_row(vec_out, 7 + part, row_sums(pre_delta.astype(F32)))
            inner_delta = inner_delta + dot_nt(pre_delta, expand_w[0, :, at])
        add_row(vec_out, 11, row_sums(inner_delta * hat))
        add_row(vec_out, 12, row_sums(inner_delta))
        grad[rows, :] = gradient + norm_back(inner_delta, hat, inverse, gains[0, 1:2, :])

    delta_rows(0, place_ref, mask_ref, exit_w, grad, stripe_delta_out, branch_delta, vec_out, 13)
    moves.send(grad_out, stripe_delta_out)
    moves.need(active0, stripe0)
    put_squares(bundle, 4 * width, dot_tn(normed_bf[...], pre0[...]), width)
    for part in range(hidden_units // width):
        bundle.put(
            (8 + part) * width,
            dot_tn(active0[:, part * width : (part + 1) * width], feed0[...]),
        )
    bundle.put(12 * width, dot_tn(stripe0[...], branch_delta[...]))


def third_kernel(
    moves,
    place_ref,
    gains,
    shifts,
    conv_k,
    vec1,
    vec2,
    conv2,
    mixed_a,
    mixed_b,
    mixed_c,
    mixed_d,
    stripe_delta,
    win0,
    chance0,
    entry_w,
    grad_in,
    out_a,
    out_b,
    out_c,
    out_d,
    keep_out,
    away_out,
    hidden,
    wide,
    wide_bf,
    normed_bf,
    vec3,
    conv3,
    flat,
):
    width = hidden.shape[1]
    bundle = Bundle(
        place_ref, keep_out, away_out, 4, lambda chunk: jnp.bitwise_xor(place_ref[5], chunk)
    )
    vec3[...] = jnp.zeros(vec3.shape, F32)
    conv3[...] = jnp.zeros(conv3.shape, F32)
    moves.fetch(stripe_delta)
    moves.fetch(win0, chance0, part=0)
    moves.need(stripe_delta)
    moves.fetch(win0, chance0, part=1)

    def ready(direction):
        moves.need(win0, chance0, part=direction)
        if direction == 0:
            moves.fetch(mixed_a, mixed_b, mixed_c, mixed_d, entry_w, grad_in)

    attention_backward(ready, 0, win0, chance0, conv_k, stripe_delta, wide, conv3)

    def emit(t, rows, values):
        store_tile(place_ref, (out_a, out_b, out_c, out_d), t, values)

    moves.need(mixed_a, mixed_b, mixed_c, mixed_d, entry_w, grad_in)
    load_tiles(place_ref, (mixed_a, mixed_b, mixed_c, mixed_d), hidden)
    entry_backward(
        0, hidden, gains, shifts, entry_w, grad_in, wide, wide_bf, normed_bf, vec3, 0, emit
    )
    moves.send(out_a, out_b, out_c, out_d)
    flat[...] = jnp.zeros(flat.shape, F32)
    at = 0
    for ref in (vec1, vec2, conv2, vec3, conv3):
        flat[at : at + ref.shape[0], :] = jnp.sum(ref[...], axis=1)
        at += ref.shape[0]
    spread = dot_tn(normed_bf[...], wide_bf[...])
    half = keep_out.shape[0]
    middle = width // 2
    lots = flat.shape[0] // 2
    bundle.put(0, spread[:, :width])
    bundle.put(width, spread[:middle, width : 2 * width])
    bundle.put(width + middle, flat[:lots, :])
    bundle.put(half, spread[middle:, width : 2 * width])
    bundle.put(half + middle, spread[:, 2 * width :])
    bundle.put(half + middle + width, flat[lots:, :])


def untangle(source, flat, target):
    count, width = source.shape[2:]
    lanes = flat.shape[0]
    for row in range(TILE):
        flat[:, pl.ds(row * 8 + 7, count, stride=PAD), :] = jnp.zeros((lanes, count, 128), F32)
        for col in range(TILE):
            token = source[row, col].astype(F32)
            for lane in range(lanes):
                flat[lane, pl.ds(row * 8 + col, count, stride=PAD), :] = token[
                    :, lane * 128 : (lane + 1) * 128
                ]

    @pl.loop(0, count)
    def _(n):
        rows = pl.ds(pl.multiple_of(n * PAD, 8), PAD)
        tile = jnp.concatenate([flat[lane, rows, :] for lane in range(lanes)], axis=1)
        target(n, tile.reshape(TILE, 8, width).astype(BF))


def owner_of(wanted, count):
    if count & (count - 1) == 0:
        return lax.shift_right_logical(wanted, count.bit_length() - 1)
    return lax.div(wanted, count)


def pick_kernel(
    moves, mix_ref, cut_ref, images_ref, index_out, take_out, sent_out, own_out, flat, counts
):
    moves.fetch(images_ref)
    count = images_ref.shape[2]
    slots = sent_out.shape[0]
    capacity = slots // counts.shape[0]
    me = lax.axis_index("dp")

    def put(n, tile):
        own_out[n] = tile

    @pl.loop(0, slots, unroll=8)
    def _(s):
        index_out[s] = count

    @pl.loop(0, counts.shape[0])
    def _(g):
        counts[g] = 0
        rank = g * capacity
        for ref in (mix_ref, cut_ref):
            for j in range(count):
                wanted = ref[g * count + j]
                owner = owner_of(wanted, count)
                hit = owner == me
                index_out[jnp.where(hit, rank, slots)] = wanted - owner * count
                rank = rank + hit.astype(jnp.int32)

    for part, ref in enumerate((mix_ref, cut_ref)):

        @pl.loop(0, count)
        def _(j, part=part, ref=ref):
            owner = owner_of(ref[me * count + j], count)
            rank = counts[owner]
            take_out[part * count + j] = owner * capacity + rank
            counts[owner] = rank + 1

    moves.need(images_ref)
    untangle(images_ref, flat, put)

    @pl.loop(0, slots, unroll=4)
    def _(s):
        sent_out[s] = own_out[jnp.minimum(index_out[s], count - 1)]


def deal_kernel(place_ref, source, out_a, out_b, out_c, out_d, flat):
    outs = (out_a, out_b, out_c, out_d)
    share = out_a.shape[0]

    def put(n, tile):
        for d, out in enumerate(outs):

            @pl.when(jnp.bitwise_xor(place_ref[3], d) == n // share)
            def _(out=out):
                out[n % share] = tile

    untangle(source, flat, put)


def inside_box(corner_ref, n, place_ref):
    shape = (TILE, 8, 1)
    row = place_ref[1] * TILE + lax.broadcasted_iota(jnp.int32, shape, 0)
    col = place_ref[2] * TILE + lax.broadcasted_iota(jnp.int32, shape, 1)
    hit = (
        (row >= corner_ref[0, n])
        & (row < corner_ref[1, n])
        & (col >= corner_ref[2, n])
        & (col < corner_ref[3, n])
    )
    return jnp.where(hit, 1.0, 0.0)


def mix_kernel(
    place_ref, take_ref, corner_ref, ratio_ref, arrived, own_ref, out_a, out_b, out_c, out_d
):
    count = own_ref.shape[0]
    share = out_a.shape[0]
    for d, out in enumerate((out_a, out_b, out_c, out_d)):

        @pl.loop(0, share)
        def _(i, d=d, out=out):
            n = jnp.bitwise_xor(place_ref[3], d) * share + i
            inside = inside_box(corner_ref, n, place_ref)
            ratio = ratio_ref[n]
            own = own_ref[n].astype(F32)
            blend = arrived[take_ref[n]].astype(F32)
            cut = arrived[take_ref[count + n]].astype(F32)
            mixed = inside * cut + (1.0 - inside) * (ratio * own + (1.0 - ratio) * blend)
            out[i] = mixed.astype(BF)


def split_kernel(
    place_ref, take_ref, corner_ref, ratio_ref, grad_a, grad_b, grad_c, grad_d, out_ref
):
    share = grad_a.shape[0]
    count = 4 * share
    if out_ref.shape[0] > 2 * count:
        out_ref[...] = jnp.zeros(out_ref.shape, BF)
    for d, grad_ref in enumerate((grad_a, grad_b, grad_c, grad_d)):

        @pl.loop(0, share)
        def _(i, d=d, grad_ref=grad_ref):
            n = jnp.bitwise_xor(place_ref[3], d) * share + i
            inside = inside_box(corner_ref, n, place_ref)
            gradient = grad_ref[i].astype(F32)
            cut = inside * gradient
            out_ref[take_ref[n]] = ((1.0 - ratio_ref[n]) * (gradient - cut)).astype(BF)
            out_ref[take_ref[count + n]] = cut.astype(BF)


def join_kernel(
    place_ref,
    index_ref,
    corner_ref,
    ratio_ref,
    grad_a,
    grad_b,
    grad_c,
    grad_d,
    back_ref,
    out_ref,
    total,
):
    count, width = out_ref.shape[2:]
    share = grad_a.shape[0]

    def tile_rows(n):
        return pl.ds(pl.multiple_of(n * PAD, 8), PAD)

    for d, grad_ref in enumerate((grad_a, grad_b, grad_c, grad_d)):

        @pl.loop(0, share)
        def _(i, d=d, grad_ref=grad_ref):
            n = jnp.bitwise_xor(place_ref[3], d) * share + i
            outside = 1.0 - inside_box(corner_ref, n, place_ref)
            kept = ratio_ref[n] * outside * grad_ref[i].astype(F32)
            kept = kept.reshape(PAD, width)
            for lane in range(total.shape[0]):
                total[lane, tile_rows(n), :] = kept[:, lane * 128 : (lane + 1) * 128]

    @pl.loop(0, back_ref.shape[0])
    def _(s):
        piece = back_ref[s].astype(F32).reshape(PAD, width)
        for lane in range(total.shape[0]):
            total[lane, tile_rows(index_ref[s]), :] += piece[:, lane * 128 : (lane + 1) * 128]

    for row in range(TILE):
        for col in range(TILE):
            out_ref[row, col] = jnp.concatenate(
                [
                    total[lane, pl.ds(row * 8 + col, count, stride=PAD), :]
                    for lane in range(total.shape[0])
                ],
                axis=1,
            )


def lay_kernel(place_ref, act_a, act_b, act_c, act_d, out_ref, flat):
    count, width = out_ref.shape[2:]
    share = act_a.shape[0]
    for d, act_ref in enumerate((act_a, act_b, act_c, act_d)):

        @pl.loop(0, share)
        def _(i, d=d, act_ref=act_ref):
            n = jnp.bitwise_xor(place_ref[3], d) * share + i
            tile = act_ref[i].astype(F32).reshape(PAD, width)
            for lane in range(flat.shape[0]):
                flat[lane, pl.ds(pl.multiple_of(n * PAD, 8), PAD), :] = tile[
                    :, lane * 128 : (lane + 1) * 128
                ]

    for row in range(TILE):
        for col in range(TILE):
            out_ref[row, col] = jnp.concatenate(
                [
                    flat[lane, pl.ds(row * 8 + col, count, stride=PAD), :]
                    for lane in range(flat.shape[0])
                ],
                axis=1,
            ).astype(BF)


def unpack_kernel(
    ranks,
    counts,
    place_ref,
    *refs,
):
    pieces, refs = refs[:8], refs[8:]
    outs, (vectors, *buffers, send_sem) = refs[:12], refs[12:]
    (
        gain_out,
        shift_out,
        entry_out,
        entry_b_out,
        conv_out,
        conv_b_out,
        exit_out,
        exit_b_out,
        expand_out,
        expand_b_out,
        shrink_out,
        shrink_b_out,
    ) = buffers
    width = exit_out.shape[1]
    units = expand_out.shape[2]
    middle = width // 2

    def squares(out_ref, block, count):
        return [(out_ref, block, 0, part * width, width) for part in range(count)]

    def tall(out_ref, block, count):
        return [(out_ref, block, part * width, 0, width) for part in range(count)]

    plans = (
        squares(expand_out, 1, units // width) + tall(shrink_out, 1, units // width),
        [
            (entry_out, 0, 0, 0, width),
            (entry_out, 0, 0, width, middle),
            (vectors, None, 0, 0, middle),
            (entry_out, 0, middle, width, middle),
            (entry_out, 0, 0, 2 * width, width),
            (None, None, 0, 0, middle),
        ],
        squares(entry_out, 1, 3)
        + tall(exit_out, 1, 1)
        + squares(expand_out, 0, units // width)
        + tall(shrink_out, 0, units // width)
        + tall(exit_out, 0, 1),
    )
    moves = []
    base = 0
    for plan, count in zip(plans, counts):
        lump = sum(part[4] for part in plan) // 8
        at = 0
        for out_ref, block, first_row, lane, length in plan:
            done = 0
            while done < length:
                inside = at % lump
                step = min(length - done, count - inside % count, lump - inside)
                where = (at // lump, inside // count, base + inside % count)
                moves.append((out_ref, block, first_row + done, lane, where, step))
                at += step
                done += step
        base += count
    big = (expand_out, shrink_out, entry_out, exit_out)
    leaving = []

    def leave(buffer, out):
        copy = pltpu.make_async_copy(buffer, out, send_sem.at[len(leaving)])
        leaving.append(copy)
        return copy

    def place_parts(target, wanted, col, own):
        for out_ref, block, first_row, lane, (number, inner, start), step in moves:
            if out_ref is not target or block != wanted:
                continue
            piece = pieces[4 * (col ^ (number // 4)) + (own ^ (number % 4))]
            inner = jnp.bitwise_xor(place_ref[6], inner)
            values = piece[inner, start : start + step, :].astype(F32)
            place = slice(first_row, first_row + step)
            if block is None:
                out_ref[place, :] = values
            else:
                out_ref[block, place, lane : lane + width] = values

    first_sends = {}
    for block in (1, 0):
        for target in big:
            i = [j for j, ref in enumerate(buffers) if ref is target][0]
            first_sends[block, i] = leave(target.at[block], outs[i].at[block])
    for col in range(2):
        for own in range(4):

            @pl.when((place_ref[2] == col) & (place_ref[5] == own))
            def _(col=col, own=own):
                place_parts(vectors, None, col, own)
                for (block, i), copy in first_sends.items():
                    place_parts(buffers[i], block, col, own)
                    copy.start()

    def line(n):
        return vectors[n : n + 1, :]

    gain_out[0] = jnp.concatenate([line(33), line(18)], axis=0)
    gain_out[1] = jnp.concatenate([line(11), line(5)], axis=0)
    shift_out[0] = jnp.concatenate([line(34), line(19)], axis=0)
    shift_out[1] = jnp.concatenate([line(12), line(6)], axis=0)
    for part in range(2):
        lanes = slice(part * width, (part + 1) * width)
        entry_b_out[:, lanes] = jnp.concatenate([line(31 + part), line(9 + part)], axis=0)
    for i in range(3):
        for j in range(3):
            conv_out[i, j] = jnp.concatenate(
                [line(35 + 3 * i + j), line(22 + 3 * i + j)], axis=0
            )
    conv_b_out[...] = jnp.concatenate([line(21), line(8)], axis=0)
    exit_b_out[...] = jnp.concatenate([line(20), line(7)], axis=0)
    for part in range(units // width):
        lanes = slice(part * width, (part + 1) * width)
        expand_b_out[:, lanes] = jnp.concatenate([line(14 + part), line(part)], axis=0)
    shrink_b_out[...] = jnp.concatenate([line(13), line(4)], axis=0)
    for buffer, out in zip(buffers, outs):
        if not any(buffer is ref for ref in big):
            leave(buffer, out).start()
    for copy in leaving:
        copy.wait()


SMEM = pl.BlockSpec(memory_space=pltpu.SMEM)
VMEM = pl.BlockSpec(memory_space=pltpu.VMEM)


ANYWHERE = pl.BlockSpec(memory_space=pl.ANY)
FAR = pl.BlockSpec(memory_space=pltpu.HBM)


def far(values):
    return pltpu.with_memory_space_constraint(values, pltpu.HBM)


class Here:
    def __init__(self, ranks):
        self.ranks = ranks

    def seat(self):
        group, row, col = (lax.axis_index(axis) for axis in ("dp", "row", "col"))
        bits = self.ranks.bit_length() - 1
        rank = 2 * group + row
        order = jnp.int32(0)
        for bit in range(0, bits, 2):
            count = min(2, bits - bit)
            part = jnp.bitwise_and(lax.shift_right_logical(rank, bit), (1 << count) - 1)
            order = order * (1 << count) + part
        rest = self.ranks // 4
        first = jnp.bitwise_and(rank, 3)
        return (group, row, col, 2 * row + col, order, first, order - first * rest)


class Moves:
    def __init__(self, fetched, sent):
        self.fetched, self.sent = dict(fetched), dict(sent)
        self.waited, self.started = set(), set()

    def copies(self, ref, part):
        copies = self.fetched.get(id(ref), [])
        return [
            ((id(ref), i), copy)
            for i, copy in enumerate(copies)
            if part is None or len(copies) == 1 or i == part
        ]

    def fetch(self, *refs, part=None):
        for ref in refs:
            for key, copy in self.copies(ref, part):
                if key not in self.started:
                    copy.start()
                    self.started.add(key)

    def need(self, *refs, part=None):
        self.fetch(*refs, part=part)
        for ref in refs:
            for key, copy in self.copies(ref, part):
                if key not in self.waited:
                    copy.wait()
                    self.waited.add(key)

    def send(self, *refs):
        for ref in refs:
            if id(ref) in self.sent:
                self.sent[id(ref)].start()
                self.started.add(id(ref))

    def finish(self):
        for key, copies in self.fetched.items():
            for i, copy in enumerate(copies):
                if (key, i) not in self.started:
                    copy.start()
                if (key, i) not in self.waited:
                    copy.wait()
        for key, copy in self.sent.items():
            if key not in self.started:
                copy.start()
        for copy in self.sent.values():
            copy.wait()


def halves(ref):
    if ref.shape[-2] != WIN:
        return [pl.ds(0, ref.shape[0])]
    count = ref.shape[0] // 2
    return [pl.ds(0, count), pl.ds(count, count)]


def run(
    kernel,
    scalars,
    arrays,
    outs,
    scratch=(),
    flops=0,
    name=None,
    after=(),
    scalar_outs=(),
    lazy=None,
    vmem=16,
    near=((), ()),
):
    outs = list(outs)
    here = None
    if scalars and isinstance(scalars[0], Here):
        here, scalars = scalars[0], scalars[1:]
    first_in, first_out = (len(arrays), len(outs)) if lazy is None else lazy
    eager, late = list(arrays[:first_in]), list(arrays[first_in:])
    n_in = len(scalars) + len(eager)
    scratch_shapes = [
        kind if dtype is None else pltpu.VMEM(kind, dtype) for kind, dtype in scratch
    ]
    n_own = len(scratch_shapes)
    n_late, n_sent = len(late), len(outs) - first_out
    if lazy is not None:
        scratch_shapes += [pltpu.VMEM(a.shape, a.dtype) for a in late]
        scratch_shapes += [pltpu.VMEM(*out) for out in outs[first_out:]]
        scratch_shapes += [pltpu.SemaphoreType.DMA((n_late, 2)), pltpu.SemaphoreType.DMA((max(n_sent, 1),))]

    def body(*refs):
        given, refs = refs[:n_in], refs[n_in:]
        sources, refs = refs[:n_late], refs[n_late + len(after) :]
        results, refs = refs[: len(scalar_outs) + first_out], refs[len(scalar_outs) + first_out :]
        targets, refs = refs[:n_sent], refs[n_sent:]
        own, refs = refs[:n_own], refs[n_own:]
        if here is not None:
            given = (here.seat(),) + tuple(given)
        if lazy is None:
            kernel(*given, *results, *own)
            return
        buffers, leaving = refs[:n_late], refs[n_late : n_late + n_sent]
        fetch_sem, send_sem = refs[n_late + n_sent :]
        moves = Moves(
            [
                (
                    id(buffer),
                    [
                        pltpu.make_async_copy(source.at[part], buffer.at[part], fetch_sem.at[i, j])
                        for j, part in enumerate(halves(buffer))
                    ],
                )
                for i, (source, buffer) in enumerate(zip(sources, buffers))
            ],
            [
                (id(buffer), pltpu.make_async_copy(buffer, target, send_sem.at[i]))
                for i, (buffer, target) in enumerate(zip(leaving, targets))
            ],
        )
        kernel(moves, *given, *buffers, *results, *leaving, *own)
        moves.finish()

    out_shape = [jax.ShapeDtypeStruct(shape, dtype) for shape, dtype in scalar_outs] + [
        pltpu.HBM(shape, dtype)
        if lazy is not None and i not in near[1]
        else jax.ShapeDtypeStruct(shape, dtype)
        for i, (shape, dtype) in enumerate(outs)
    ]
    late = [
        a if i in near[0] else far(a)
        for i, a in enumerate(late, first_in)
    ]
    moved = sum(a.size * a.dtype.itemsize for a in arrays)
    return pl.pallas_call(
        body,
        out_shape=out_shape,
        in_specs=[SMEM] * len(scalars)
        + [VMEM] * len(eager)
        + [ANYWHERE if i in near[0] else FAR for i in range(first_in, len(arrays))]
        + [ANYWHERE] * len(after),
        out_specs=[SMEM] * len(scalar_outs)
        + [VMEM] * first_out
        + [ANYWHERE if i in near[1] else FAR for i in range(first_out, len(outs))],
        scratch_shapes=scratch_shapes,
        compiler_params=pltpu.CompilerParams(vmem_limit_bytes=vmem * 1024 * 1024),
        cost_estimate=pl.CostEstimate(flops=flops, bytes_accessed=moved, transcendentals=0),
        name=name,
    )(*scalars, *eager, *late, *after)


def gate(values, after):
    values, after = list(values), list(after)
    return list(lax.optimization_barrier(tuple(values + after)))[: len(values)]


def swap(values, axis):
    return lax.ppermute(values, axis, [(0, 1), (1, 0)])


def added(values, others):
    return (values.astype(F32) + others.astype(F32)).astype(BF)


def shards(values, ranks):
    return values.reshape(ranks, values.shape[0] // ranks, values.shape[1])


def spread_sum(pieces):
    mine = jnp.sum(pieces.astype(F32), axis=0).astype(BF)
    return jnp.broadcast_to(mine[None], pieces.shape)


def across(values, axes, size, mask):
    return lax.ppermute(values, axes, [(i, i ^ mask) for i in range(size)])


def deal(parts):
    return [parts[0]] + [across(parts[d], ("row", "col"), 4, d) for d in (1, 2, 3)]


RANKS = ("dp", "row")


def stages(ranks):
    bits = ranks.bit_length() - 1
    return [(bit, min(2, bits - bit)) for bit in range(0, bits, 2)]


def scatter_send(values, ranks, stage):
    bit, count = stage
    size = 1 << count
    me = (lax.axis_index(RANKS) >> bit) & (size - 1)
    cut = values.reshape(size, values.shape[0] // size, values.shape[1])
    return [lax.dynamic_index_in_dim(cut, me ^ d, 0, keepdims=False) for d in range(size)]


def scatter_move(parts, ranks, stage):
    return [parts[0]] + [
        across(parts[d], RANKS, ranks, d << stage[0]) for d in range(1, len(parts))
    ]


def scatter_sum(parts):
    return sum(part.astype(F32) for part in parts).astype(BF)


def gather(values, ranks, stage):
    return jnp.stack(
        [values]
        + [across(values, RANKS, ranks, d << stage[0]) for d in range(1, 1 << stage[1])]
    )


def rank_order(rank, ranks):
    order = 0
    for bit, count in stages(ranks):
        order = order * (1 << count) + ((rank >> bit) & ((1 << count) - 1))
    return order


def local(
    groups,
    images,
    cotangent,
    mix_partner,
    cut_partner,
    ratios,
    corners,
    drop_masks,
    norm_gains,
    norm_shifts,
    entry_weight,
    entry_bias,
    position_kernel,
    position_bias,
    exit_weight,
    exit_bias,
    expand_weight,
    expand_bias,
    shrink_weight,
    shrink_bias,
):
    images_here = images.shape[0]
    width = images.shape[3]
    units = expand_weight.shape[2]
    share = images_here // 4
    rows = 4 * share * PAD
    ranks = 2 * groups
    capacity = (2 * images_here + groups - 1) // groups
    slots = groups * capacity
    place = Here(ranks)
    spots = [0] * ranks
    for rank in range(ranks):
        spots[rank_order(rank, ranks)] = rank
    quad = ((share, TILE, 8, width), BF)
    corners = corners.T
    masks = drop_masks.T
    flat = ((width // 128, images_here * PAD, 128), F32)
    index, take, outgoing, own = run(
        pick_kernel,
        [mix_partner, cut_partner],
        [images.transpose(1, 2, 0, 3)],
        [((slots, TILE, 8, width), BF), ((images_here, TILE, 8, width), BF)],
        [flat, (pltpu.SMEM((groups,), jnp.int32), None)],
        name="pick",
        vmem=60,
        lazy=(0, 2),
        near=((), (0, 1)),
        scalar_outs=(((slots + 8,), jnp.int32), ((2 * images_here,), jnp.int32)),
    )
    arrived = lax.all_to_all(outgoing, "dp", split_axis=0, concat_axis=0, tiled=True)
    cot = deal(
        run(deal_kernel, [place], [cotangent.transpose(1, 2, 0, 3)], [quad] * 4, [flat], name="deal")
    )
    mixed = deal(
        run(
            mix_kernel,
            [place, take, corners, ratios],
            [arrived, own],
            [quad] * 4,
            name="mix",
            after=cot,
        )
    )
    conv_k = position_kernel.transpose(1, 2, 0, 3)
    tall = (rows, width)
    (
        vec1,
        keep1,
        away1,
        act_a,
        act_b,
        act_c,
        act_d,
        active0,
        slope0,
        win0,
        chance0,
        stripe0,
        mid0,
        win1,
        chance1,
        stripe1,
        hidden1,
        grad1,
    ) = run(
        functools.partial(first_kernel, spots),
        [place, masks],
        [
            *mixed,
            norm_gains,
            norm_shifts,
            entry_bias,
            conv_k,
            position_bias,
            exit_bias,
            expand_bias,
            shrink_bias,
            *cot,
            entry_weight,
            exit_weight,
            expand_weight,
            shrink_weight,
        ],
        [
            ((7, 8, width), F32),
            ((units, width), BF),
            ((units, width), BF),
            *([quad] * 4),
            ((rows, units), BF),
            ((rows, units), BF),
            ((4 * share, WIN, 3 * HALF), BF),
            ((4 * share, WIN, LANES), BF),
            (tall, BF),
            (tall, F32),
            ((4 * share, WIN, 3 * HALF), BF),
            ((4 * share, WIN, LANES), BF),
            (tall, BF),
            (tall, F32),
            (tall, F32),
        ],
        [
            (tall, F32),
            ((rows, 3 * width), F32),
            (tall, F32),
            ((rows, units), BF),
            ((rows, units), BF),
            (tall, BF),
            (tall, BF),
        ],
        flops=10 * rows * width * width * 120,
        name="first",
        vmem=46,
        near=((), (1, 2)),
        lazy=(17, 3),
    )
    sent1 = shards(added(keep1, swap(away1, "col")), ranks)
    pieces1 = lax.all_to_all(sent1, RANKS, split_axis=0, concat_axis=0, tiled=True)
    vec2, conv2, keep2, away2, grad0, delta0 = run(
        second_kernel,
        [place, masks],
        [
            norm_gains,
            norm_shifts,
            conv_k,
            grad1,
            exit_weight,
            win1,
            chance1,
            hidden1,
            entry_weight,
            stripe1,
            mid0,
            shrink_weight,
            slope0,
            expand_weight,
            active0,
            stripe0,
        ],
        [
            ((15, 8, width), F32),
            ((9, 8, width), F32),
            ((13 * width // 2, width), BF),
            ((13 * width // 2, width), BF),
            (tall, F32),
            (tall, F32),
        ],
        [
            (tall, F32),
            (tall, BF),
            ((rows, 3 * width), F32),
            ((rows, 3 * width), BF),
            (tall, BF),
            (tall, BF),
            ((rows, units), BF),
        ],
        flops=6 * rows * width * width * 120,
        name="second",
        vmem=42,
        near=((), (2, 3)),
        after=[sent1],
        lazy=(3, 4),
    )
    act = deal([act_a, act_b, act_c, act_d])
    keep2, away2, *act = gate([keep2, away2, *act], [pieces1])
    steps = stages(ranks)

    def first_parts(keep, away):
        other = swap(away, "col")
        count = keep.shape[0] // 4
        return [
            added(keep[d * count : (d + 1) * count], other[d * count : (d + 1) * count])
            for d in range(4)
        ]

    parts2 = first_parts(keep2, away2)
    moved2 = scatter_move(parts2, ranks, steps[0])
    *out_tiles, keep3, away3 = run(
        third_kernel,
        [place],
        [
            norm_gains,
            norm_shifts,
            conv_k,
            vec1,
            vec2,
            conv2,
            *mixed,
            delta0,
            win0,
            chance0,
            entry_weight,
            grad0,
        ],
        [quad] * 4 + [((2 * width, width), BF), ((2 * width, width), BF)],
        [
            (tall, F32),
            ((rows, 3 * width), F32),
            ((rows, 3 * width), BF),
            (tall, BF),
            ((4, 8, width), F32),
            ((9, 8, width), F32),
            ((width, width), F32),
        ],
        flops=3 * rows * width * width * 120,
        name="third",
        vmem=36,
        near=((), range(6)),
        after=parts2,
        lazy=(10, 6),
    )
    *moved2, keep3, away3 = gate([*moved2, keep3, away3], out_tiles)
    gradient = deal(out_tiles)
    (parted,) = run(
        split_kernel,
        [place, take, corners, ratios],
        gradient,
        [((slots, TILE, 8, width), BF)],
        name="split",
    )
    mine1 = jnp.sum(pieces1.astype(F32), axis=0).astype(BF)
    mine2 = scatter_sum(moved2)
    moved3 = scatter_move(first_parts(keep3, away3), ranks, steps[0])
    mine3 = scatter_sum(gate(moved3, [mine1]))
    mine2, mine3 = (
        jnp.pad(values, ((0, -values.shape[0] % (4 * ranks)), (0, 0))) for values in (mine2, mine3)
    )
    cut = mine2.shape[0] * 4 // ranks
    lot = mine3.shape[0] * 4 // ranks
    joint = jnp.concatenate(
        [
            mine3.reshape(ranks // 4, lot, width),
            mine2.reshape(ranks // 4, cut, width),
        ],
        axis=1,
    ).reshape(-1, width)
    for step in steps[1:]:
        joint = scatter_sum(scatter_move(scatter_send(joint, ranks, step), ranks, step))
    joint = jnp.concatenate([mine1, joint], axis=0)
    counts = (mine1.shape[0], lot, cut)
    for step in reversed(steps[1:]):
        joint = gather(joint, ranks, step).reshape(-1, width)
    joint = shards(joint, ranks // 4)
    (parted,) = gate([parted], [joint])
    (activations,) = run(
        lay_kernel, [place], [far(a) for a in act], [((TILE, TILE, images_here, width), BF)], [flat], name="lay"
    )
    back = lax.all_to_all(parted, "dp", split_axis=0, concat_axis=0, tiled=True)
    (back,) = gate([back], [activations])
    (input_gradient,) = run(
        join_kernel,
        [place, index, corners, ratios],
        [*gradient, back],
        [((TILE, TILE, images_here, width), F32)],
        [((width // 128, (images_here + 1) * PAD, 128), F32)],
        name="join",
    )
    full = [joint] + [across(joint, RANKS, ranks, d) for d in (1, 2, 3)]
    full[2:] = gate(full[2:], [input_gradient])
    full += [swap(piece, "col") for piece in full]
    shapes = [
        (2, 2, width),
        (2, 2, width),
        (2, width, 3 * width),
        (2, 2 * width),
        (3, 3, 2, width),
        (2, width),
        (2, width, width),
        (2, width),
        (2, width, units),
        (2, units),
        (2, units, width),
        (2, width),
    ]
    gains, shifts, entry, entry_b, conv, conv_b, exit_, exit_b, expand, expand_b, shrink, shrink_b = (
        pl.pallas_call(
            lambda *refs: unpack_kernel(ranks, counts, place.seat(), *refs),
            out_shape=[jax.ShapeDtypeStruct(shape, F32) for shape in shapes],
            in_specs=[VMEM] * 8,
            out_specs=[ANYWHERE] * 12,
            scratch_shapes=[
                pltpu.VMEM((width // 2, width), F32),
            ]
            + [pltpu.VMEM(shape, F32) for shape in shapes]
            + [pltpu.SemaphoreType.DMA((16,))],
            compiler_params=pltpu.CompilerParams(vmem_limit_bytes=24 * 1024 * 1024),
            name="unpack",
        )(*full)
    )
    return (
        activations.transpose(2, 0, 1, 3),
        input_gradient.transpose(2, 0, 1, 3),
        gains,
        shifts,
        entry,
        entry_b,
        conv.transpose(2, 0, 1, 3),
        conv_b,
        exit_,
        exit_b,
        expand,
        expand_b,
        shrink,
        shrink_b,
    )


def solution(mesh):
    tiles = P("dp", "row", "col", None)
    return jax.shard_map(
        functools.partial(local, mesh.shape["dp"]),
        mesh=mesh,
        in_specs=(tiles, tiles, P(), P(), P("dp"), P("dp", None), P("dp", None)) + (P(),) * 12,
        out_specs=(tiles, tiles) + (P(),) * 12,
        check_vma=False,
    )
```

```python
import functools

import jax
import jax.numpy as jnp
from jax import lax
from jax.experimental import pallas as pl
from jax.experimental.pallas import tpu as pltpu
from jax.sharding import PartitionSpec as P

TILE = 7
PAD = 56
HEAD_DIM = 32
SIDE_HEADS = 4
HALF = 128
WIN = 2 * PAD
CHUNK = 8 * PAD
LANES = SIDE_HEADS * 128
SCALE = HEAD_DIM ** (-0.5)
LOG2E = 1.4426950408889634
EPS = 1e-05
BF = jnp.bfloat16
F32 = jnp.float32


def dot_nn(a, b):
    return lax.dot_general(a, b, (((1,), (0,)), ((), ())), preferred_element_type=F32)


def dot_nt(a, b):
    return lax.dot_general(a, b, (((1,), (1,)), ((), ())), preferred_element_type=F32)


def dot_tn(a, b):
    return lax.dot_general(a, b, (((0,), (0,)), ((), ())), preferred_element_type=F32)


def norm_parts(values):
    centered = values - jnp.mean(values, axis=-1, keepdims=True)
    inverse = lax.rsqrt(jnp.mean(centered * centered, axis=-1, keepdims=True) + EPS)
    return centered * inverse, inverse


def norm_back(delta, hat, inverse, gain):
    scaled = delta * gain
    first = jnp.mean(scaled, axis=-1, keepdims=True)
    second = jnp.mean(scaled * hat, axis=-1, keepdims=True)
    return inverse * (scaled - first - hat * second)


def gelu_parts(values):
    chance = 0.5 + 0.5 * lax.erf(values * (0.5**0.5))
    density = jnp.exp2(values * values * (-0.5 * LOG2E)) * 0.3989422804014327
    return chance, density


def row_sums(values):
    count, width = values.shape
    return jnp.sum(values.reshape(count // 8, 8, width), axis=0)


def scale_rows(place_ref, mask_ref, column):
    scales = [
        mask_ref[column, 4 * place_ref[3] + i].astype(F32) * 1.25 for i in range(4)
    ]
    columns = [jnp.full((PAD, 1), scale, F32) for scale in scales]
    return jnp.concatenate(columns * (CHUNK // (4 * PAD)), axis=0)


def add_row(acc_ref, row, values):
    acc_ref[row] += values


def spread_heads(values):
    lane = lax.broadcasted_iota(jnp.int32, values.shape, 1) // HEAD_DIM
    empty = jnp.zeros((128 - WIN, HALF), F32)
    blocks = []
    for head in range(SIDE_HEADS):
        blocks.append(jnp.where(lane == head, values, 0.0))
        blocks.append(empty)
    return jnp.concatenate(blocks, axis=0).astype(BF)


def over_keys(weights, values):
    weights = fill_rows(weights)
    stacked = jnp.concatenate(
        [weights[:, head * 128 : (head + 1) * 128] for head in range(SIDE_HEADS)], axis=0
    )
    return dot_tn(stacked, spread_heads(values))[:WIN]


def fill_rows(values):
    empty = jnp.zeros((128 - WIN, values.shape[1]), values.dtype)
    return jnp.concatenate([values, empty], axis=0)


def valid_column(shape):
    return lax.broadcasted_iota(jnp.int32, shape, 1) != 7


def valid_rows(shape):
    return lax.broadcasted_iota(jnp.int32, shape, 0) % 8 != 7


def column_shifts(values, across):
    cube = values.reshape(2 * TILE, 8, HALF)
    if not across:
        return (pltpu.roll(cube, 1, 1), cube, pltpu.roll(cube, 7, 1))
    left, right = cube[:TILE], cube[TILE:]
    column = lax.broadcasted_iota(jnp.int32, left.shape, 1)
    before = jnp.concatenate(
        [
            pltpu.roll(left, 1, 1),
            jnp.where(column == 0, pltpu.roll(left, 2, 1), pltpu.roll(right, 1, 1)),
        ],
        axis=0,
    )
    after = jnp.concatenate(
        [
            jnp.where(column == 6, pltpu.roll(right, 6, 1), pltpu.roll(left, 7, 1)),
            pltpu.roll(right, 7, 1),
        ],
        axis=0,
    )
    return (before, cube, after)


def row_shift(cube, step, across):
    if step == 0:
        return cube
    empty = jnp.zeros((1, 8, HALF), F32)

    def move(part):
        if step < 0:
            return jnp.concatenate([empty, part[:-1]], axis=0)
        return jnp.concatenate([part[1:], empty], axis=0)

    if across:
        return jnp.concatenate([move(cube[:TILE]), move(cube[TILE:])], axis=0)
    return move(cube)


def window_conv(shifts, kernel_at, across):
    total = None
    for i in range(3):
        part = None
        for j in range(3):
            term = kernel_at(i, j) * shifts[j]
            part = term if part is None else part + term
        part = row_shift(part, i - 1, across)
        total = part if total is None else total + part
    return total.reshape(WIN, HALF)


def window_rows(across, window):
    side, image = window // 4, window % 4
    if across:
        first, second = 2 * side, 2 * side + 1
    else:
        first, second = side, 2 + side
    return (
        pl.multiple_of((first * 4 + image) * PAD, 8),
        pl.multiple_of((second * 4 + image) * PAD, 8),
    )


def take_window(ref, at, lane):
    return jnp.concatenate(
        [ref[pl.ds(at[0], PAD), lane : lane + HALF], ref[pl.ds(at[1], PAD), lane : lane + HALF]],
        axis=0,
    )


def put_window(ref, at, lane, values):
    ref[pl.ds(at[0], PAD), lane : lane + HALF] = values[:PAD]
    ref[pl.ds(at[1], PAD), lane : lane + HALF] = values[PAD:]


def round_bf(values):
    return values.astype(BF).astype(F32)


def attention_forward(
    block, hidden_ref, gains, shifts, entry_w, entry_b, conv_k, conv_b, wide, stripe, win_out, chance_out
):
    width = hidden_ref.shape[1]

    @pl.loop(0, 2)
    def _(t):
        rows = chunk(t)
        hat, _ = norm_parts(hidden_ref[rows, :])
        normed = (hat * gains[block, 0:1, :] + shifts[block, 0:1, :]).astype(BF)
        for part in range(3):
            out = dot_nn(normed, entry_w[block, :, part * width : (part + 1) * width])
            if part != 1:
                at = 0 if part == 0 else width
                out = out + entry_b[block : block + 1, at : at + width]
            wide[rows, part * width : (part + 1) * width] = round_bf(out)

    for direction in range(2):
        across = direction == 0
        lane = direction * HALF

        @pl.loop(0, 8, unroll=8)
        def _(window, across=across, lane=lane, direction=direction):
            at = window_rows(across, window)
            queries = take_window(wide, at, lane)
            keys = take_window(wide, at, width + lane)
            values = take_window(wide, at, 2 * width + lane)
            keys_bf = keys.astype(BF)
            win_out[direction * 8 + window, :, 0:HALF] = queries.astype(BF)
            win_out[direction * 8 + window, :, HALF : 2 * HALF] = keys_bf
            win_out[direction * 8 + window, :, 2 * HALF : 3 * HALF] = values.astype(BF)
            scores = dot_nt(keys_bf, spread_heads(queries)).reshape(2 * TILE, 8, LANES)
            scores = jnp.where(valid_column((1, 8, LANES)), scores, -1e30)
            top = jnp.max(jnp.max(scores, axis=0), axis=0, keepdims=True)
            lifted = jnp.exp2((scores - top) * (SCALE * LOG2E))
            totals = jnp.sum(jnp.sum(lifted, axis=0), axis=0, keepdims=True)
            chances = (lifted * (1.0 / totals)).reshape(WIN, LANES).astype(BF)
            chance_out[direction * 8 + window] = chances
            attended = over_keys(chances, values)
            clean = jnp.where(valid_rows(values.shape), values, 0.0)
            position = window_conv(
                column_shifts(clean, across),
                lambda i, j: conv_k[i, j, block : block + 1, lane : lane + HALF],
                across,
            )
            put_window(
                stripe, at, lane, attended + position + conv_b[block : block + 1, lane : lane + HALF]
            )


def attention_backward(
    ready,
    block,
    win_in,
    chance_in,
    conv_k,
    stripe_delta,
    wide,
    conv_acc,
):
    width = stripe_delta.shape[1]
    for direction in range(2):
        ready(direction)
        across = direction == 0
        lane = direction * HALF

        @pl.loop(0, 8, unroll=4)
        def _(window, across=across, lane=lane, direction=direction):
            at = window_rows(across, window)
            out_delta = take_window(stripe_delta, at, lane)
            queries = win_in[direction * 8 + window, :, 0:HALF].astype(F32)
            keys = win_in[direction * 8 + window, :, HALF : 2 * HALF].astype(F32)
            values_bf = win_in[direction * 8 + window, :, 2 * HALF : 3 * HALF]
            values = values_bf.astype(F32)
            chances = chance_in[direction * 8 + window]
            delta_spread = spread_heads(out_delta)
            chance_delta = dot_nt(values_bf, delta_spread)
            cubes = (2 * TILE, 8, LANES)
            wide_chances = chances.astype(F32).reshape(cubes)
            weighted = wide_chances * chance_delta.reshape(cubes)
            common = jnp.sum(jnp.sum(weighted, axis=0), axis=0, keepdims=True)
            score_delta = (weighted - wide_chances * common).reshape(WIN, LANES).astype(BF)
            values_delta = dot_nn(chances, delta_spread)
            keys_delta = dot_nn(score_delta, spread_heads(queries)) * SCALE
            query_delta = over_keys(score_delta, keys) * SCALE
            keep = valid_rows(values.shape)
            clean = jnp.where(keep, values, 0.0)
            shifts = column_shifts(clean, across)
            cube = out_delta.reshape(2 * TILE, 8, HALF)
            for i in range(3):
                moved = row_shift(cube, 1 - i, across)
                for j in range(3):
                    conv_acc[3 * i + j, :, lane : lane + HALF] += jnp.sum(moved * shifts[j], axis=0)
            back = window_conv(
                column_shifts(out_delta, across),
                lambda i, j: conv_k[2 - i, 2 - j, block : block + 1, lane : lane + HALF],
                across,
            )
            values_delta = jnp.where(keep, values_delta + back, 0.0)
            put_window(wide, at, lane, query_delta)
            put_window(wide, at, width + lane, keys_delta)
            put_window(wide, at, 2 * width + lane, values_delta)


def chunk(t):
    return pl.ds(pl.multiple_of(t * CHUNK, CHUNK), CHUNK)


class Bundle:
    def __init__(self, place_ref, keep, away, chunks=1, spot=lambda chunk: chunk):
        self.place_ref, self.keep, self.away = place_ref, keep, away
        self.step, self.spot = keep.shape[0] // chunks, spot

    def put(self, at, values):
        values = values.astype(BF)
        half, step = self.keep.shape[0], self.step
        last = at + values.shape[0]
        first = at
        while first < last:
            stop = min(last, (first // step + 1) * step)
            number = first // half
            start = self.spot(first % half // step) * step
            inner, count = first % step, stop - first
            if not isinstance(start, int):
                start = pl.multiple_of(start, step)
            rows = pl.ds(start + inner, count)
            piece = values[first - at : stop - at]

            @pl.when(self.place_ref[2] == number)
            def _(piece=piece, rows=rows):
                self.keep[rows, :] = piece

            @pl.when(self.place_ref[2] != number)
            def _(piece=piece, rows=rows):
                self.away[rows, :] = piece

            first = stop


def put_squares(bundle, at, values, side):
    for part in range(values.shape[1] // side):
        bundle.put(at + part * side, values[:, part * side : (part + 1) * side])


def load_tiles(place_ref, tiles, hidden):
    for d, tile in enumerate(tiles):
        at = jnp.bitwise_xor(place_ref[3], d) * (4 * PAD)
        rows = pl.ds(pl.multiple_of(at, 4 * PAD), 4 * PAD)
        hidden[rows, :] = tile[...].astype(F32).reshape(4 * PAD, hidden.shape[1])


def store_tile(place_ref, tiles, t, values):
    count = CHUNK // (4 * PAD)
    values = values.reshape((count,) + tiles[0].shape).astype(BF)
    for part in range(count):
        for d, tile in enumerate(tiles):

            @pl.when(jnp.bitwise_xor(place_ref[3], d) == count * t + part)
            def _(tile=tile, part=part):
                tile[...] = values[part]


def first_kernel(
    spots,
    moves,
    place_ref,
    mask_ref,
    mixed_a,
    mixed_b,
    mixed_c,
    mixed_d,
    gains,
    shifts,
    entry_b,
    conv_k,
    conv_b,
    exit_b,
    expand_b,
    shrink_b,
    cot_a,
    cot_b,
    cot_c,
    cot_d,
    entry_w,
    exit_w,
    expand_w,
    shrink_w,
    vec_out,
    keep_out,
    away_out,
    act_a,
    act_b,
    act_c,
    act_d,
    active0_out,
    slope0_out,
    win0_out,
    chance0_out,
    stripe0_out,
    mid0_out,
    win1_out,
    chance1_out,
    stripe1_out,
    hidden1_out,
    grad_out,
    hidden,
    wide,
    stripe,
    active1,
    pre1,
    feed1,
    inner1,
):
    width = hidden.shape[1]
    hidden_units = expand_w.shape[2]
    bundle = Bundle(place_ref, keep_out, away_out, len(spots), lambda chunk: spots[chunk])
    vec_out[...] = jnp.zeros(vec_out.shape, F32)
    moves.fetch(entry_w)
    load_tiles(place_ref, (mixed_a, mixed_b, mixed_c, mixed_d), hidden)
    moves.need(entry_w)
    moves.fetch(exit_w, expand_w, shrink_w, cot_a, cot_b, cot_c, cot_d)

    for block in range(2):
        win_out, chance_out, stripe_out = (
            (win0_out, chance0_out, stripe0_out),
            (win1_out, chance1_out, stripe1_out),
        )[block]
        attention_forward(
            block, hidden, gains, shifts, entry_w, entry_b, conv_k, conv_b, wide, stripe, win_out, chance_out
        )
        moves.send(win_out, chance_out)
        moves.need(exit_w, expand_w, shrink_w)
        if block == 1:
            moves.need(cot_a, cot_b, cot_c, cot_d)
            load_tiles(place_ref, (cot_a, cot_b, cot_c, cot_d), grad_out)

        @pl.loop(0, 2)
        def _(t, block=block, stripe_out=stripe_out):
            rows = chunk(t)
            striped = stripe[rows, :].astype(BF)
            stripe_out[rows, :] = striped
            branch = dot_nn(striped, exit_w[block]) + exit_b[block : block + 1, :]
            midway = hidden[rows, :] + scale_rows(place_ref, mask_ref, 2 * block) * branch
            if block == 0:
                mid0_out[rows, :] = midway
            hat, inverse = norm_parts(midway)
            normed = (hat * gains[block, 1:2, :] + shifts[block, 1:2, :]).astype(BF)
            feed_scale = scale_rows(place_ref, mask_ref, 2 * block + 1)
            feed = shrink_b[block : block + 1, :]
            if block == 1:
                inner1[rows, :] = normed
                gradient = grad_out[rows, :]
                feed_delta = (feed_scale * gradient).astype(BF)
                feed1[rows, :] = feed_delta
                add_row(vec_out, 4, row_sums(feed_delta.astype(F32)))
                inner_delta = jnp.zeros((CHUNK, width), F32)
            for part in range(hidden_units // width):
                at = slice(part * width, (part + 1) * width)
                pre_act = dot_nn(normed, expand_w[block, :, at]) + expand_b[block : block + 1, at]
                chance, density = gelu_parts(pre_act)
                active = (pre_act * chance).astype(BF)
                slope = chance + pre_act * density
                if block == 0:
                    active0_out[rows, at] = active
                    slope0_out[rows, at] = slope.astype(BF)
                else:
                    active1[rows, at] = active
                    pre_delta = (dot_nt(feed_delta, shrink_w[block, at, :]) * slope).astype(BF)
                    pre1[rows, at] = pre_delta
                    add_row(vec_out, part, row_sums(pre_delta.astype(F32)))
                    inner_delta = inner_delta + dot_nt(pre_delta, expand_w[block, :, at])
                feed = feed + dot_nn(active, shrink_w[block, at, :])
            output = midway + feed_scale * feed
            if block == 0:
                hidden[rows, :] = output
                hidden1_out[rows, :] = output
            else:
                store_tile(place_ref, (act_a, act_b, act_c, act_d), t, output)
                add_row(vec_out, 5, row_sums(inner_delta * hat))
                add_row(vec_out, 6, row_sums(inner_delta))
                grad_out[rows, :] = gradient + norm_back(
                    inner_delta, hat, inverse, gains[block, 1:2, :]
                )

        moves.send(stripe_out)
        if block == 0:
            moves.send(mid0_out, active0_out, slope0_out, hidden1_out)
        else:
            moves.send(act_a, act_b, act_c, act_d, grad_out)

    put_squares(bundle, 0, dot_tn(inner1[...], pre1[...]), width)
    for part in range(hidden_units // width):
        bundle.put(
            hidden_units + part * width,
            dot_tn(active1[:, part * width : (part + 1) * width], feed1[...]),
        )


def delta_rows(block, place_ref, mask_ref, exit_w, grad_ref, stripe_delta, branch_delta, vec_out, at):
    @pl.loop(0, 2)
    def _(t):
        rows = chunk(t)
        rounded = (scale_rows(place_ref, mask_ref, 2 * block) * grad_ref[rows, :]).astype(BF)
        branch_delta[rows, :] = rounded
        add_row(vec_out, at, row_sums(rounded.astype(F32)))
        out = round_bf(dot_nt(rounded, exit_w[block]))
        stripe_delta[rows, :] = out
        add_row(vec_out, at + 1, row_sums(out))


def entry_backward(block, hidden_ref, gains, shifts, entry_w, grad_ref, wide, wide_bf, normed_bf, vec_out, at, emit):
    width = hidden_ref.shape[1]

    @pl.loop(0, 2)
    def _(t):
        rows = chunk(t)
        hat, inverse = norm_parts(hidden_ref[rows, :])
        normed_bf[rows, :] = (hat * gains[block, 0:1, :] + shifts[block, 0:1, :]).astype(BF)
        delta = jnp.zeros((CHUNK, width), F32)
        for part in range(3):
            lanes = slice(part * width, (part + 1) * width)
            rounded = wide[rows, lanes].astype(BF)
            wide_bf[rows, lanes] = rounded
            if part != 1:
                add_row(vec_out, at + part // 2, row_sums(rounded.astype(F32)))
            delta = delta + dot_nt(rounded, entry_w[block, :, lanes])
        add_row(vec_out, at + 2, row_sums(delta * hat))
        add_row(vec_out, at + 3, row_sums(delta))
        emit(t, rows, grad_ref[rows, :] + norm_back(delta, hat, inverse, gains[block, 0:1, :]))


def second_kernel(
    moves,
    place_ref,
    mask_ref,
    gains,
    shifts,
    conv_k,
    grad_in,
    exit_w,
    win1,
    chance1,
    hidden1,
    entry_w,
    stripe1,
    mid0,
    shrink_w,
    slope0,
    expand_w,
    active0,
    stripe0,
    vec_out,
    conv_out,
    keep_out,
    away_out,
    grad_out,
    stripe_delta_out,
    stripe_delta,
    branch_delta,
    wide,
    wide_bf,
    normed_bf,
    feed0,
    pre0,
):
    grad = grad_out
    width = grad.shape[1]
    hidden_units = expand_w.shape[2]
    bundle = Bundle(
        place_ref, keep_out, away_out, 4, lambda chunk: jnp.bitwise_xor(place_ref[5], chunk)
    )
    vec_out[...] = jnp.zeros(vec_out.shape, F32)
    conv_out[...] = jnp.zeros(conv_out.shape, F32)
    moves.fetch(grad_in, exit_w)
    moves.fetch(win1, chance1, part=0)
    moves.need(grad_in, exit_w)
    moves.fetch(win1, chance1, part=1)
    delta_rows(1, place_ref, mask_ref, exit_w, grad_in, stripe_delta, branch_delta, vec_out, 0)

    def ready(direction):
        moves.need(win1, chance1, part=direction)
        if direction == 0:
            moves.fetch(hidden1, entry_w, stripe1)
        else:
            moves.fetch(mid0, shrink_w, slope0, expand_w, active0, stripe0)

    attention_backward(ready, 1, win1, chance1, conv_k, stripe_delta, wide, conv_out)

    def emit(t, rows, values):
        grad[rows, :] = values

    moves.need(hidden1, entry_w)
    entry_backward(
        1, hidden1, gains, shifts, entry_w, grad_in, wide, wide_bf, normed_bf, vec_out, 2, emit
    )
    put_squares(bundle, 0, dot_tn(normed_bf[...], wide_bf[...]), width)
    moves.need(stripe1)
    bundle.put(3 * width, dot_tn(stripe1[...], branch_delta[...]))
    moves.need(mid0, shrink_w, slope0, expand_w)

    @pl.loop(0, 2)
    def _(t):
        rows = chunk(t)
        gradient = grad[rows, :]
        hat, inverse = norm_parts(mid0[rows, :])
        normed_bf[rows, :] = (hat * gains[0, 1:2, :] + shifts[0, 1:2, :]).astype(BF)
        feed_delta = (scale_rows(place_ref, mask_ref, 1) * gradient).astype(BF)
        feed0[rows, :] = feed_delta
        add_row(vec_out, 6, row_sums(feed_delta.astype(F32)))
        inner_delta = jnp.zeros((CHUNK, width), F32)
        for part in range(hidden_units // width):
            at = slice(part * width, (part + 1) * width)
            pre_delta = (
                dot_nt(feed_delta, shrink_w[0, at, :]) * slope0[rows, at].astype(F32)
            ).astype(BF)
            pre0[rows, at] = pre_delta
            add_row(vec_out, 7 + part, row_sums(pre_delta.astype(F32)))
            inner_delta = inner_delta + dot_nt(pre_delta, expand_w[0, :, at])
        add_row(vec_out, 11, row_sums(inner_delta * hat))
        add_row(vec_out, 12, row_sums(inner_delta))
        grad[rows, :] = gradient + norm_back(inner_delta, hat, inverse, gains[0, 1:2, :])

    delta_rows(0, place_ref, mask_ref, exit_w, grad, stripe_delta_out, branch_delta, vec_out, 13)
    moves.send(grad_out, stripe_delta_out)
    moves.need(active0, stripe0)
    put_squares(bundle, 4 * width, dot_tn(normed_bf[...], pre0[...]), width)
    for part in range(hidden_units // width):
        bundle.put(
            (8 + part) * width,
            dot_tn(active0[:, part * width : (part + 1) * width], feed0[...]),
        )
    bundle.put(12 * width, dot_tn(stripe0[...], branch_delta[...]))


def third_kernel(
    moves,
    place_ref,
    gains,
    shifts,
    conv_k,
    vec1,
    vec2,
    conv2,
    mixed_a,
    mixed_b,
    mixed_c,
    mixed_d,
    stripe_delta,
    win0,
    chance0,
    entry_w,
    grad_in,
    out_a,
    out_b,
    out_c,
    out_d,
    keep_out,
    away_out,
    hidden,
    wide,
    wide_bf,
    normed_bf,
    vec3,
    conv3,
    flat,
):
    width = hidden.shape[1]
    bundle = Bundle(
        place_ref, keep_out, away_out, 4, lambda chunk: jnp.bitwise_xor(place_ref[5], chunk)
    )
    vec3[...] = jnp.zeros(vec3.shape, F32)
    conv3[...] = jnp.zeros(conv3.shape, F32)
    moves.fetch(stripe_delta)
    moves.fetch(win0, chance0, part=0)
    moves.need(stripe_delta)
    moves.fetch(win0, chance0, part=1)

    def ready(direction):
        moves.need(win0, chance0, part=direction)
        if direction == 0:
            moves.fetch(mixed_a, mixed_b, mixed_c, mixed_d, entry_w, grad_in)

    attention_backward(ready, 0, win0, chance0, conv_k, stripe_delta, wide, conv3)

    def emit(t, rows, values):
        store_tile(place_ref, (out_a, out_b, out_c, out_d), t, values)

    moves.need(mixed_a, mixed_b, mixed_c, mixed_d, entry_w, grad_in)
    load_tiles(place_ref, (mixed_a, mixed_b, mixed_c, mixed_d), hidden)
    entry_backward(
        0, hidden, gains, shifts, entry_w, grad_in, wide, wide_bf, normed_bf, vec3, 0, emit
    )
    moves.send(out_a, out_b, out_c, out_d)
    flat[...] = jnp.zeros(flat.shape, F32)
    at = 0
    for ref in (vec1, vec2, conv2, vec3, conv3):
        flat[at : at + ref.shape[0], :] = jnp.sum(ref[...], axis=1)
        at += ref.shape[0]
    spread = dot_tn(normed_bf[...], wide_bf[...])
    half = keep_out.shape[0]
    middle = width // 2
    lots = flat.shape[0] // 2
    bundle.put(0, spread[:, :width])
    bundle.put(width, spread[:middle, width : 2 * width])
    bundle.put(width + middle, flat[:lots, :])
    bundle.put(half, spread[middle:, width : 2 * width])
    bundle.put(half + middle, spread[:, 2 * width :])
    bundle.put(half + middle + width, flat[lots:, :])


def untangle(source, flat, target):
    count, width = source.shape[2:]
    lanes = flat.shape[0]
    for row in range(TILE):
        flat[:, pl.ds(row * 8 + 7, count, stride=PAD), :] = jnp.zeros((lanes, count, 128), F32)
        for col in range(TILE):
            token = source[row, col].astype(F32)
            for lane in range(lanes):
                flat[lane, pl.ds(row * 8 + col, count, stride=PAD), :] = token[
                    :, lane * 128 : (lane + 1) * 128
                ]

    @pl.loop(0, count, unroll=4)
    def _(n):
        rows = pl.ds(pl.multiple_of(n * PAD, 8), PAD)
        tile = jnp.concatenate([flat[lane, rows, :] for lane in range(lanes)], axis=1)
        target(n, tile.reshape(TILE, 8, width).astype(BF))


def owner_of(wanted, count):
    if count & (count - 1) == 0:
        return lax.shift_right_logical(wanted, count.bit_length() - 1)
    return lax.div(wanted, count)


def pick_kernel(
    groups, moves, mix_ref, cut_ref, images_ref, index_out, sent_out, own_out, flat
):
    moves.fetch(images_ref)
    count = images_ref.shape[2]
    slots = sent_out.shape[0]
    capacity = slots // groups
    me = lax.axis_index("dp")

    def put(n, tile):
        own_out[n] = tile

    @pl.loop(0, slots, unroll=8)
    def _(s):
        index_out[s] = count

    @pl.loop(0, groups)
    def _(g):
        rank = g * capacity
        for ref in (mix_ref, cut_ref):
            for j in range(count):
                wanted = ref[g * count + j]
                owner = owner_of(wanted, count)
                hit = owner == me
                index_out[jnp.where(hit, rank, slots)] = wanted - owner * count
                rank = rank + hit.astype(jnp.int32)

    moves.need(images_ref)
    untangle(images_ref, flat, put)

    @pl.loop(0, slots, unroll=4)
    def _(s):
        sent_out[s] = own_out[jnp.minimum(index_out[s], count - 1)]


def deal_kernel(
    capacity, place_ref, mix_ref, cut_ref, source, take_out, out_a, out_b, out_c, out_d, flat, counts
):
    outs = (out_a, out_b, out_c, out_d)
    share = out_a.shape[0]

    def put(n, tile):
        for d, out in enumerate(outs):

            @pl.when(jnp.bitwise_xor(place_ref[3], d) == n // share)
            def _(out=out):
                out[n % share] = tile

    count = source.shape[2]
    me = place_ref[0]

    @pl.loop(0, counts.shape[0])
    def _(g):
        counts[g] = 0

    for part, ref in enumerate((mix_ref, cut_ref)):

        @pl.loop(0, count)
        def _(j, part=part, ref=ref):
            owner = owner_of(ref[me * count + j], count)
            rank = counts[owner]
            take_out[part * count + j] = owner * capacity + rank
            counts[owner] = rank + 1

    untangle(source, flat, put)


def inside_box(corner_ref, n, place_ref):
    shape = (TILE, 8, 1)
    row = place_ref[1] * TILE + lax.broadcasted_iota(jnp.int32, shape, 0)
    col = place_ref[2] * TILE + lax.broadcasted_iota(jnp.int32, shape, 1)
    hit = (
        (row >= corner_ref[0, n])
        & (row < corner_ref[1, n])
        & (col >= corner_ref[2, n])
        & (col < corner_ref[3, n])
    )
    return jnp.where(hit, 1.0, 0.0)


def mix_kernel(
    place_ref, take_ref, corner_ref, ratio_ref, arrived, own_ref, out_a, out_b, out_c, out_d
):
    count = own_ref.shape[0]
    share = out_a.shape[0]
    for d, out in enumerate((out_a, out_b, out_c, out_d)):

        @pl.loop(0, share, unroll=2)
        def _(i, d=d, out=out):
            n = jnp.bitwise_xor(place_ref[3], d) * share + i
            inside = inside_box(corner_ref, n, place_ref)
            ratio = ratio_ref[n]
            own = own_ref[n].astype(F32)
            blend = arrived[take_ref[n]].astype(F32)
            cut = arrived[take_ref[count + n]].astype(F32)
            mixed = inside * cut + (1.0 - inside) * (ratio * own + (1.0 - ratio) * blend)
            out[i] = mixed.astype(BF)


def split_kernel(
    place_ref, take_ref, corner_ref, ratio_ref, grad_a, grad_b, grad_c, grad_d, out_ref
):
    share = grad_a.shape[0]
    count = 4 * share
    if out_ref.shape[0] > 2 * count:
        out_ref[...] = jnp.zeros(out_ref.shape, BF)
    for d, grad_ref in enumerate((grad_a, grad_b, grad_c, grad_d)):

        @pl.loop(0, share)
        def _(i, d=d, grad_ref=grad_ref):
            n = jnp.bitwise_xor(place_ref[3], d) * share + i
            inside = inside_box(corner_ref, n, place_ref)
            gradient = grad_ref[i].astype(F32)
            cut = inside * gradient
            out_ref[take_ref[n]] = ((1.0 - ratio_ref[n]) * (gradient - cut)).astype(BF)
            out_ref[take_ref[count + n]] = cut.astype(BF)


def join_kernel(
    place_ref,
    index_ref,
    corner_ref,
    ratio_ref,
    grad_a,
    grad_b,
    grad_c,
    grad_d,
    back_ref,
    out_ref,
    total,
):
    count, width = out_ref.shape[2:]
    share = grad_a.shape[0]

    def tile_rows(n):
        return pl.ds(pl.multiple_of(n * PAD, 8), PAD)

    for d, grad_ref in enumerate((grad_a, grad_b, grad_c, grad_d)):

        @pl.loop(0, share)
        def _(i, d=d, grad_ref=grad_ref):
            n = jnp.bitwise_xor(place_ref[3], d) * share + i
            outside = 1.0 - inside_box(corner_ref, n, place_ref)
            kept = ratio_ref[n] * outside * grad_ref[i].astype(F32)
            kept = kept.reshape(PAD, width)
            for lane in range(total.shape[0]):
                total[lane, tile_rows(n), :] = kept[:, lane * 128 : (lane + 1) * 128]

    @pl.loop(0, back_ref.shape[0])
    def _(s):
        piece = back_ref[s].astype(F32).reshape(PAD, width)
        for lane in range(total.shape[0]):
            total[lane, tile_rows(index_ref[s]), :] += piece[:, lane * 128 : (lane + 1) * 128]

    for row in range(TILE):
        for col in range(TILE):
            out_ref[row, col] = jnp.concatenate(
                [
                    total[lane, pl.ds(row * 8 + col, count, stride=PAD), :]
                    for lane in range(total.shape[0])
                ],
                axis=1,
            )


def lay_kernel(place_ref, act_a, act_b, act_c, act_d, out_ref, flat):
    count, width = out_ref.shape[2:]
    share = act_a.shape[0]
    for d, act_ref in enumerate((act_a, act_b, act_c, act_d)):

        @pl.loop(0, share)
        def _(i, d=d, act_ref=act_ref):
            n = jnp.bitwise_xor(place_ref[3], d) * share + i
            tile = act_ref[i].astype(F32).reshape(PAD, width)
            for lane in range(flat.shape[0]):
                flat[lane, pl.ds(pl.multiple_of(n * PAD, 8), PAD), :] = tile[
                    :, lane * 128 : (lane + 1) * 128
                ]

    for row in range(TILE):
        for col in range(TILE):
            out_ref[row, col] = jnp.concatenate(
                [
                    flat[lane, pl.ds(row * 8 + col, count, stride=PAD), :]
                    for lane in range(flat.shape[0])
                ],
                axis=1,
            ).astype(BF)


def unpack_kernel(
    ranks,
    counts,
    place_ref,
    *refs,
):
    pieces, refs = refs[:8], refs[8:]
    outs, (vectors, *buffers, send_sem) = refs[:12], refs[12:]
    (
        gain_out,
        shift_out,
        entry_out,
        entry_b_out,
        conv_out,
        conv_b_out,
        exit_out,
        exit_b_out,
        expand_out,
        expand_b_out,
        shrink_out,
        shrink_b_out,
    ) = buffers
    width = exit_out.shape[1]
    units = expand_out.shape[2]
    middle = width // 2

    def squares(out_ref, block, count):
        return [(out_ref, block, 0, part * width, width) for part in range(count)]

    def tall(out_ref, block, count):
        return [(out_ref, block, part * width, 0, width) for part in range(count)]

    plans = (
        squares(expand_out, 1, units // width) + tall(shrink_out, 1, units // width),
        [
            (entry_out, 0, 0, 0, width),
            (entry_out, 0, 0, width, middle),
            (vectors, None, 0, 0, middle),
            (entry_out, 0, middle, width, middle),
            (entry_out, 0, 0, 2 * width, width),
        ],
        squares(entry_out, 1, 3)
        + tall(exit_out, 1, 1)
        + squares(expand_out, 0, units // width)
        + tall(shrink_out, 0, units // width)
        + tall(exit_out, 0, 1),
    )
    inner_ranks = ranks // 4
    moves = []
    base = 0
    for plan, count in zip(plans, counts):
        at = 0
        for out_ref, block, first_row, lane, length in plan:
            done = 0
            while done < length:
                step = min(length - done, count - at % count)
                moves.append((out_ref, block, first_row + done, lane, base, count, at, step))
                at += step
                done += step
        base += count
    big = (expand_out, shrink_out, entry_out, exit_out)
    leaving = []

    def leave(buffer, out):
        copy = pltpu.make_async_copy(buffer, out, send_sem.at[len(leaving)])
        leaving.append(copy)
        return copy

    def place_parts(target, wanted, col, own):
        for out_ref, block, first_row, lane, base, count, at, step in moves:
            if out_ref is not target or block != wanted:
                continue
            shard, start = at // count, base + at % count
            half, shard = shard // ranks, shard % ranks
            first, inner = shard // inner_ranks, shard % inner_ranks
            piece = pieces[4 * (col ^ half) + (own ^ first)]
            inner = jnp.bitwise_xor(place_ref[6], inner)
            values = piece[inner, start : start + step, :].astype(F32)
            place = slice(first_row, first_row + step)
            if block is None:
                out_ref[place, :] = values
            else:
                out_ref[block, place, lane : lane + width] = values

    first_sends = {}
    for block in (1, 0):
        for target in big:
            i = [j for j, ref in enumerate(buffers) if ref is target][0]
            first_sends[block, i] = leave(target.at[block], outs[i].at[block])
    for col in range(2):
        for own in range(4):

            @pl.when((place_ref[2] == col) & (place_ref[5] == own))
            def _(col=col, own=own):
                place_parts(vectors, None, col, own)
                for (block, i), copy in first_sends.items():
                    place_parts(buffers[i], block, col, own)
                    copy.start()

    def line(n):
        return vectors[n : n + 1, :]

    gain_out[0] = jnp.concatenate([line(33), line(18)], axis=0)
    gain_out[1] = jnp.concatenate([line(11), line(5)], axis=0)
    shift_out[0] = jnp.concatenate([line(34), line(19)], axis=0)
    shift_out[1] = jnp.concatenate([line(12), line(6)], axis=0)
    for part in range(2):
        lanes = slice(part * width, (part + 1) * width)
        entry_b_out[:, lanes] = jnp.concatenate([line(31 + part), line(9 + part)], axis=0)
    for i in range(3):
        for j in range(3):
            conv_out[i, j] = jnp.concatenate(
                [line(35 + 3 * i + j), line(22 + 3 * i + j)], axis=0
            )
    conv_b_out[...] = jnp.concatenate([line(21), line(8)], axis=0)
    exit_b_out[...] = jnp.concatenate([line(20), line(7)], axis=0)
    for part in range(units // width):
        lanes = slice(part * width, (part + 1) * width)
        expand_b_out[:, lanes] = jnp.concatenate([line(14 + part), line(part)], axis=0)
    shrink_b_out[...] = jnp.concatenate([line(13), line(4)], axis=0)
    for buffer, out in zip(buffers, outs):
        if not any(buffer is ref for ref in big):
            leave(buffer, out).start()
    for copy in leaving:
        copy.wait()


SMEM = pl.BlockSpec(memory_space=pltpu.SMEM)
VMEM = pl.BlockSpec(memory_space=pltpu.VMEM)


ANYWHERE = pl.BlockSpec(memory_space=pl.ANY)
FAR = pl.BlockSpec(memory_space=pltpu.HBM)


def far(values):
    return pltpu.with_memory_space_constraint(values, pltpu.HBM)


class Here:
    def __init__(self, ranks):
        self.ranks = ranks

    def seat(self):
        group, row, col = (lax.axis_index(axis) for axis in ("dp", "row", "col"))
        bits = self.ranks.bit_length() - 1
        rank = 2 * group + row
        order = jnp.int32(0)
        for bit in range(0, bits, 2):
            count = min(2, bits - bit)
            part = jnp.bitwise_and(lax.shift_right_logical(rank, bit), (1 << count) - 1)
            order = order * (1 << count) + part
        rest = self.ranks // 4
        first = jnp.bitwise_and(rank, 3)
        return (group, row, col, 2 * row + col, order, first, order - first * rest)


class Moves:
    def __init__(self, fetched, sent):
        self.fetched, self.sent = dict(fetched), dict(sent)
        self.waited, self.started = set(), set()

    def copies(self, ref, part):
        copies = self.fetched.get(id(ref), [])
        return [
            ((id(ref), i), copy)
            for i, copy in enumerate(copies)
            if part is None or len(copies) == 1 or i == part
        ]

    def fetch(self, *refs, part=None):
        for ref in refs:
            for key, copy in self.copies(ref, part):
                if key not in self.started:
                    copy.start()
                    self.started.add(key)

    def need(self, *refs, part=None):
        self.fetch(*refs, part=part)
        for ref in refs:
            for key, copy in self.copies(ref, part):
                if key not in self.waited:
                    copy.wait()
                    self.waited.add(key)

    def send(self, *refs):
        for ref in refs:
            if id(ref) in self.sent:
                self.sent[id(ref)].start()
                self.started.add(id(ref))

    def finish(self):
        for key, copies in self.fetched.items():
            for i, copy in enumerate(copies):
                if (key, i) not in self.started:
                    copy.start()
                if (key, i) not in self.waited:
                    copy.wait()
        for key, copy in self.sent.items():
            if key not in self.started:
                copy.start()
        for copy in self.sent.values():
            copy.wait()


def halves(ref):
    if ref.shape[-2] != WIN:
        return [pl.ds(0, ref.shape[0])]
    count = ref.shape[0] // 2
    return [pl.ds(0, count), pl.ds(count, count)]


def run(
    kernel,
    scalars,
    arrays,
    outs,
    scratch=(),
    flops=0,
    name=None,
    after=(),
    scalar_outs=(),
    lazy=None,
    vmem=16,
    near=((), ()),
):
    outs = list(outs)
    here = None
    if scalars and isinstance(scalars[0], Here):
        here, scalars = scalars[0], scalars[1:]
    first_in, first_out = (len(arrays), len(outs)) if lazy is None else lazy
    eager, late = list(arrays[:first_in]), list(arrays[first_in:])
    n_in = len(scalars) + len(eager)
    scratch_shapes = [
        kind if dtype is None else pltpu.VMEM(kind, dtype) for kind, dtype in scratch
    ]
    n_own = len(scratch_shapes)
    n_late, n_sent = len(late), len(outs) - first_out
    if lazy is not None:
        scratch_shapes += [pltpu.VMEM(a.shape, a.dtype) for a in late]
        scratch_shapes += [pltpu.VMEM(*out) for out in outs[first_out:]]
        scratch_shapes += [pltpu.SemaphoreType.DMA((n_late, 2)), pltpu.SemaphoreType.DMA((max(n_sent, 1),))]

    def body(*refs):
        given, refs = refs[:n_in], refs[n_in:]
        sources, refs = refs[:n_late], refs[n_late + len(after) :]
        results, refs = refs[: len(scalar_outs) + first_out], refs[len(scalar_outs) + first_out :]
        targets, refs = refs[:n_sent], refs[n_sent:]
        own, refs = refs[:n_own], refs[n_own:]
        if here is not None:
            given = (here.seat(),) + tuple(given)
        if lazy is None:
            kernel(*given, *results, *own)
            return
        buffers, leaving = refs[:n_late], refs[n_late : n_late + n_sent]
        fetch_sem, send_sem = refs[n_late + n_sent :]
        moves = Moves(
            [
                (
                    id(buffer),
                    [
                        pltpu.make_async_copy(source.at[part], buffer.at[part], fetch_sem.at[i, j])
                        for j, part in enumerate(halves(buffer))
                    ],
                )
                for i, (source, buffer) in enumerate(zip(sources, buffers))
            ],
            [
                (id(buffer), pltpu.make_async_copy(buffer, target, send_sem.at[i]))
                for i, (buffer, target) in enumerate(zip(leaving, targets))
            ],
        )
        kernel(moves, *given, *buffers, *results, *leaving, *own)
        moves.finish()

    out_shape = [jax.ShapeDtypeStruct(shape, dtype) for shape, dtype in scalar_outs] + [
        pltpu.HBM(shape, dtype)
        if lazy is not None and i not in near[1]
        else jax.ShapeDtypeStruct(shape, dtype)
        for i, (shape, dtype) in enumerate(outs)
    ]
    late = [
        a if i in near[0] else far(a)
        for i, a in enumerate(late, first_in)
    ]
    moved = sum(a.size * a.dtype.itemsize for a in arrays)
    return pl.pallas_call(
        body,
        out_shape=out_shape,
        in_specs=[SMEM] * len(scalars)
        + [VMEM] * len(eager)
        + [ANYWHERE if i in near[0] else FAR for i in range(first_in, len(arrays))]
        + [ANYWHERE] * len(after),
        out_specs=[SMEM] * len(scalar_outs)
        + [VMEM] * first_out
        + [ANYWHERE if i in near[1] else FAR for i in range(first_out, len(outs))],
        scratch_shapes=scratch_shapes,
        compiler_params=pltpu.CompilerParams(vmem_limit_bytes=vmem * 1024 * 1024),
        cost_estimate=pl.CostEstimate(flops=flops, bytes_accessed=moved, transcendentals=0),
        name=name,
    )(*scalars, *eager, *late, *after)


def gate(values, after):
    values, after = list(values), list(after)
    return list(lax.optimization_barrier(tuple(values + after)))[: len(values)]


def swap(values, axis):
    return lax.ppermute(values, axis, [(0, 1), (1, 0)])


def added(values, others):
    return (values.astype(F32) + others.astype(F32)).astype(BF)


def shards(values, ranks):
    return values.reshape(ranks, values.shape[0] // ranks, values.shape[1])


def spread_sum(pieces):
    mine = jnp.sum(pieces.astype(F32), axis=0).astype(BF)
    return jnp.broadcast_to(mine[None], pieces.shape)


def across(values, axes, size, mask):
    return lax.ppermute(values, axes, [(i, i ^ mask) for i in range(size)])


def deal(parts):
    return [parts[0]] + [across(parts[d], ("row", "col"), 4, d) for d in (1, 2, 3)]


RANKS = ("dp", "row")


def stages(ranks):
    bits = ranks.bit_length() - 1
    return [(bit, min(2, bits - bit)) for bit in range(0, bits, 2)]


def scatter_send(values, ranks, stage):
    bit, count = stage
    size = 1 << count
    me = (lax.axis_index(RANKS) >> bit) & (size - 1)
    cut = values.reshape(size, values.shape[0] // size, values.shape[1])
    return [lax.dynamic_index_in_dim(cut, me ^ d, 0, keepdims=False) for d in range(size)]


def scatter_move(parts, ranks, stage):
    return [parts[0]] + [
        across(parts[d], RANKS, ranks, d << stage[0]) for d in range(1, len(parts))
    ]


def scatter_sum(parts):
    return sum(part.astype(F32) for part in parts).astype(BF)


def gather(values, ranks, stage):
    return jnp.stack(
        [values]
        + [across(values, RANKS, ranks, d << stage[0]) for d in range(1, 1 << stage[1])]
    )


def rank_order(rank, ranks):
    order = 0
    for bit, count in stages(ranks):
        order = order * (1 << count) + ((rank >> bit) & ((1 << count) - 1))
    return order


def local(
    groups,
    images,
    cotangent,
    mix_partner,
    cut_partner,
    ratios,
    corners,
    drop_masks,
    norm_gains,
    norm_shifts,
    entry_weight,
    entry_bias,
    position_kernel,
    position_bias,
    exit_weight,
    exit_bias,
    expand_weight,
    expand_bias,
    shrink_weight,
    shrink_bias,
):
    images_here = images.shape[0]
    width = images.shape[3]
    units = expand_weight.shape[2]
    share = images_here // 4
    rows = 4 * share * PAD
    ranks = 2 * groups
    capacity = (2 * images_here + groups - 1) // groups
    slots = groups * capacity
    place = Here(ranks)
    spots = [0] * ranks
    for rank in range(ranks):
        spots[rank_order(rank, ranks)] = rank
    quad = ((share, TILE, 8, width), BF)
    corners = corners.T
    masks = drop_masks.T
    flat = ((width // 128, images_here * PAD, 128), F32)
    index, outgoing, own = run(
        functools.partial(pick_kernel, groups),
        [mix_partner, cut_partner],
        [images.transpose(1, 2, 0, 3)],
        [((slots, TILE, 8, width), BF), ((images_here, TILE, 8, width), BF)],
        [flat],
        name="pick",
        vmem=60,
        lazy=(0, 2),
        near=((), (0, 1)),
        scalar_outs=(((slots + 8,), jnp.int32),),
    )
    arrived = lax.all_to_all(outgoing, "dp", split_axis=0, concat_axis=0, tiled=True)
    take, *cot = run(
        functools.partial(deal_kernel, capacity),
        [place, mix_partner, cut_partner],
        [cotangent.transpose(1, 2, 0, 3)],
        [quad] * 4,
        [flat, (pltpu.SMEM((groups,), jnp.int32), None)],
        name="deal",
        scalar_outs=(((2 * images_here,), jnp.int32),),
    )
    cot = deal(cot)
    mixed = deal(
        run(
            mix_kernel,
            [place, take, corners, ratios],
            [arrived, own],
            [quad] * 4,
            name="mix",
            after=cot,
        )
    )
    conv_k = position_kernel.transpose(1, 2, 0, 3)
    tall = (rows, width)
    (
        vec1,
        keep1,
        away1,
        act_a,
        act_b,
        act_c,
        act_d,
        active0,
        slope0,
        win0,
        chance0,
        stripe0,
        mid0,
        win1,
        chance1,
        stripe1,
        hidden1,
        grad1,
    ) = run(
        functools.partial(first_kernel, spots),
        [place, masks],
        [
            *mixed,
            norm_gains,
            norm_shifts,
            entry_bias,
            conv_k,
            position_bias,
            exit_bias,
            expand_bias,
            shrink_bias,
            *cot,
            entry_weight,
            exit_weight,
            expand_weight,
            shrink_weight,
        ],
        [
            ((7, 8, width), F32),
            ((units, width), BF),
            ((units, width), BF),
            *([quad] * 4),
            ((rows, units), BF),
            ((rows, units), BF),
            ((4 * share, WIN, 3 * HALF), BF),
            ((4 * share, WIN, LANES), BF),
            (tall, BF),
            (tall, F32),
            ((4 * share, WIN, 3 * HALF), BF),
            ((4 * share, WIN, LANES), BF),
            (tall, BF),
            (tall, F32),
            (tall, F32),
        ],
        [
            (tall, F32),
            ((rows, 3 * width), F32),
            (tall, F32),
            ((rows, units), BF),
            ((rows, units), BF),
            (tall, BF),
            (tall, BF),
        ],
        flops=10 * rows * width * width * 120,
        name="first",
        vmem=46,
        near=((), (1, 2)),
        lazy=(17, 3),
    )
    sent1 = shards(added(keep1, swap(away1, "col")), ranks)
    pieces1 = lax.all_to_all(sent1, RANKS, split_axis=0, concat_axis=0, tiled=True)
    vec2, conv2, keep2, away2, grad0, delta0 = run(
        second_kernel,
        [place, masks],
        [
            norm_gains,
            norm_shifts,
            conv_k,
            grad1,
            exit_weight,
            win1,
            chance1,
            hidden1,
            entry_weight,
            stripe1,
            mid0,
            shrink_weight,
            slope0,
            expand_weight,
            active0,
            stripe0,
        ],
        [
            ((15, 8, width), F32),
            ((9, 8, width), F32),
            ((13 * width // 2, width), BF),
            ((13 * width // 2, width), BF),
            (tall, F32),
            (tall, F32),
        ],
        [
            (tall, F32),
            (tall, BF),
            ((rows, 3 * width), F32),
            ((rows, 3 * width), BF),
            (tall, BF),
            (tall, BF),
            ((rows, units), BF),
        ],
        flops=6 * rows * width * width * 120,
        name="second",
        vmem=42,
        near=((), (2, 3)),
        after=[sent1],
        lazy=(3, 4),
    )
    act = deal([act_a, act_b, act_c, act_d])
    keep2, away2, *act = gate([keep2, away2, *act], [pieces1])
    steps = stages(ranks)

    def first_parts(keep, away):
        other = swap(away, "col")
        count = keep.shape[0] // 4
        return [
            added(keep[d * count : (d + 1) * count], other[d * count : (d + 1) * count])
            for d in range(4)
        ]

    parts2 = first_parts(keep2, away2)
    moved2 = scatter_move(parts2, ranks, steps[0])
    *out_tiles, keep3, away3 = run(
        third_kernel,
        [place],
        [
            norm_gains,
            norm_shifts,
            conv_k,
            vec1,
            vec2,
            conv2,
            *mixed,
            delta0,
            win0,
            chance0,
            entry_weight,
            grad0,
        ],
        [quad] * 4 + [((2 * width, width), BF), ((2 * width, width), BF)],
        [
            (tall, F32),
            ((rows, 3 * width), F32),
            ((rows, 3 * width), BF),
            (tall, BF),
            ((4, 8, width), F32),
            ((9, 8, width), F32),
            ((width, width), F32),
        ],
        flops=3 * rows * width * width * 120,
        name="third",
        vmem=36,
        near=((), range(6)),
        after=parts2,
        lazy=(10, 6),
    )
    *moved2, keep3, away3 = gate([*moved2, keep3, away3], out_tiles)
    gradient = deal(out_tiles)
    (parted,) = run(
        split_kernel,
        [place, take, corners, ratios],
        gradient,
        [((slots, TILE, 8, width), BF)],
        name="split",
    )
    mine1 = jnp.sum(pieces1.astype(F32), axis=0).astype(BF)
    mine2 = scatter_sum(moved2)
    moved3 = scatter_move(first_parts(keep3, away3), ranks, steps[0])
    mine3 = scatter_sum(gate(moved3, [mine1]))
    cut = mine2.shape[0] * 4 // ranks
    lot = mine3.shape[0] * 4 // ranks
    joint = jnp.concatenate(
        [
            mine3.reshape(ranks // 4, lot, width),
            mine2.reshape(ranks // 4, cut, width),
        ],
        axis=1,
    ).reshape(-1, width)
    for step in steps[1:]:
        joint = scatter_sum(scatter_move(scatter_send(joint, ranks, step), ranks, step))
    joint = jnp.concatenate([mine1, joint], axis=0)
    counts = (mine1.shape[0], lot, cut)
    for step in reversed(steps[1:]):
        joint = gather(joint, ranks, step).reshape(-1, width)
    joint = shards(joint, ranks // 4)
    (parted,) = gate([parted], [joint])
    (activations,) = run(
        lay_kernel, [place], [far(a) for a in act], [((TILE, TILE, images_here, width), BF)], [flat], name="lay"
    )
    back = lax.all_to_all(parted, "dp", split_axis=0, concat_axis=0, tiled=True)
    (back,) = gate([back], [activations])
    (input_gradient,) = run(
        join_kernel,
        [place, index, corners, ratios],
        [*gradient, back],
        [((TILE, TILE, images_here, width), F32)],
        [((width // 128, (images_here + 1) * PAD, 128), F32)],
        name="join",
    )
    full = [joint] + [across(joint, RANKS, ranks, d) for d in (1, 2, 3)]
    full[2:] = gate(full[2:], [input_gradient])
    full += [swap(piece, "col") for piece in full]
    shapes = [
        (2, 2, width),
        (2, 2, width),
        (2, width, 3 * width),
        (2, 2 * width),
        (3, 3, 2, width),
        (2, width),
        (2, width, width),
        (2, width),
        (2, width, units),
        (2, units),
        (2, units, width),
        (2, width),
    ]
    gains, shifts, entry, entry_b, conv, conv_b, exit_, exit_b, expand, expand_b, shrink, shrink_b = (
        pl.pallas_call(
            lambda *refs: unpack_kernel(ranks, counts, place.seat(), *refs),
            out_shape=[jax.ShapeDtypeStruct(shape, F32) for shape in shapes],
            in_specs=[VMEM] * 8,
            out_specs=[ANYWHERE] * 12,
            scratch_shapes=[
                pltpu.VMEM((width // 2, width), F32),
            ]
            + [pltpu.VMEM(shape, F32) for shape in shapes]
            + [pltpu.SemaphoreType.DMA((16,))],
            compiler_params=pltpu.CompilerParams(vmem_limit_bytes=24 * 1024 * 1024),
            name="unpack",
        )(*full)
    )
    return (
        activations.transpose(2, 0, 1, 3),
        input_gradient.transpose(2, 0, 1, 3),
        gains,
        shifts,
        entry,
        entry_b,
        conv.transpose(2, 0, 1, 3),
        conv_b,
        exit_,
        exit_b,
        expand,
        expand_b,
        shrink,
        shrink_b,
    )


def solution(mesh):
    tiles = P("dp", "row", "col", None)
    return jax.shard_map(
        functools.partial(local, mesh.shape["dp"]),
        mesh=mesh,
        in_specs=(tiles, tiles, P(), P(), P("dp"), P("dp", None), P("dp", None)) + (P(),) * 12,
        out_specs=(tiles, tiles) + (P(),) * 12,
        check_vma=False,
    )
```
